32 devices in a mesh: seq: 8 (over y, x, core), tp: 4 (over z).
Axes of the slice: x: 2, y: 2, z: 4, core: 2. Of those that a mesh axis runs over, the one named last changes fastest.
Arguments:
- tokens: bfloat16 [3584, 768], P('seq'), may hold values from -6 to 6
- gain_one: float32 [768], replicated, may hold values from 0.5 to 1.5
- w_qkv: bfloat16 [768, 3, 768], P(None, None, 'tp'), may hold values from -0.21875 to 0.21875
- w_out: bfloat16 [768, 768], P('tp'), may hold values from -4 to 4
- gain_two: float32 [768], replicated, may hold values from 0.5 to 1.5
- w_in: bfloat16 [768, 2, 1152], P(None, None, 'tp'), may hold values from -0.21875 to 0.21875
- w_down: bfloat16 [1152, 768], P('tp'), may hold values from -0.1875 to 0.1875
- cotangent: bfloat16 [3584, 768], P('seq'), may hold values from -6 to 6
- doc_lengths: int32 [4], replicated, may hold values from 1 to 1792, as said below
- roster: int32 [8], replicated, may hold values from 0 to 7, as said below
Outputs:
- layer_out: bfloat16 [3584, 768], P('seq')
- input_grad: bfloat16 [3584, 768], P('seq')
- grad_gain_one: float32 [768], replicated
- grad_qkv: float32 [768, 3, 768], P(None, None, 'tp')
- grad_out: float32 [768, 768], P('tp')
- grad_gain_two: float32 [768], replicated
- grad_in: float32 [768, 2, 1152], P(None, None, 'tp')
- grad_down: float32 [1152, 768], P('tp')
The draws below stay inside these ranges and needn't reach their ends.
Inputs may be any that keep to these rules, and one draw needn't show every extreme that they name: `doc_lengths`: 4 positive lengths that sum to 3584; the largest is exactly 1792. A permutation; rows i * 448 to (i + 1) * 448 - 1 of tokens and cotangent hold the packed positions from roster[i] * 448 on.
All inputs are finite; a program needn't handle non-finite values.
Results may differ from the reference program's by a relative error of at most 0.024.
Values may be sent and summed in bfloat16 or wider, within the bound.
No kernel may reach another device: no remote copies, remote signals or barrier semaphores. Data moves between devices by JAX's collectives and lax.ppermute only.
A program may use at most 192 MiB of HBM per device.

```python
import functools
import math
import jax
import jax.numpy as jnp
from jax import lax

D = 768
HEADS = 12
HDIM = 64
FF = 1152
TOK_DEV = 448
DOCS = 4
TOKENS = 3584
MOST = 1792
N_SEQ = 8


def document_plan(key):
    key_weights, key_longest, key_order = jax.random.split(key, 3)
    weights = jax.random.randint(key_weights, (DOCS - 1,), 3, 5).astype(jnp.int32)
    remainder = TOKENS - MOST
    bounds = ((remainder - (DOCS - 1)) * jnp.cumsum(weights) // jnp.sum(weights)).astype(jnp.int32)
    others = jnp.diff(jnp.concatenate([jnp.zeros((1,), jnp.int32), bounds])) + 1
    longest = jax.random.randint(key_longest, (), 0, DOCS).astype(jnp.int32)
    places = jnp.arange(DOCS, dtype=jnp.int32)
    lower = others[jnp.clip(places, 0, DOCS - 2)]
    upper = others[jnp.clip(places - 1, 0, DOCS - 2)]
    lengths = jnp.where(places < longest, lower, jnp.where(places == longest, MOST, upper)).astype(jnp.int32)
    before = jnp.sum(jnp.where(places < longest, lengths, 0)).astype(jnp.int32)
    first_block = (before + TOK_DEV - 1) // TOK_DEV
    shuffled = jax.random.permutation(key_order, N_SEQ - 2).astype(jnp.int32)
    middle = jnp.where(shuffled < first_block, shuffled, shuffled + 2)
    roster = jnp.concatenate([first_block[None], middle, first_block[None] + 1]).astype(jnp.int32)
    return (lengths, roster)


def draw_doc_lengths(key, part):
    lengths, unused = document_plan(key)
    return lengths


def draw_roster(key, part):
    unused, roster = document_plan(key)
    return roster


def level_of(stream_key, dims, cuts, least, high):
    def one(position, shards_of):
        steps = jax.random.uniform(jax.random.fold_in(jax.random.fold_in(stream_key, 6), position), (shards_of,), jnp.float32, least / len(cuts), high / len(cuts))
        return jnp.repeat(jnp.exp(steps), dims[position] // shards_of).reshape((-1,) + (1,) * (len(dims) - position - 1))

    level = one(*cuts[0])
    for cut in cuts[1:]:
        level = level * one(*cut)
    return level


def centred(rng, shape, deviation, bound, cuts=(), held_as=jnp.bfloat16):
    level = level_of(rng, shape, cuts, -0.22, 0.18) if cuts else 1.0
    entries = jax.random.normal(rng, shape, jnp.float32) * deviation * level
    return jnp.minimum(jnp.maximum(entries, -bound), bound).astype(held_as)


def setup_inputs(seed: int = 0) -> dict:
    key_of = jax.random.split(jax.random.key(seed), 11)
    tokens = centred(key_of[0], (TOKENS, D), 1.0, 6.0, ((0, 8),))
    gain_one = jnp.clip(1.0 + 0.1 * jax.random.normal(key_of[1], (D,), jnp.float32), 0.5, 1.5)
    w_qkv = centred(key_of[2], (D, 3, D), D ** -0.5, 0.21875, ((2, 4),))
    w_out = centred(key_of[3], (D, D), (0.036 * (TOKENS // (3 * DOCS) + 1) ** 0.5), 4.0, ((0, 4),))
    gain_two = jnp.clip(1.0 + 0.1 * jax.random.normal(key_of[4], (D,), jnp.float32), 0.5, 1.5)
    w_in = centred(key_of[5], (D, 2, FF), D ** -0.5, 0.21875, ((2, 4),))
    w_down = centred(key_of[6], (FF, D), FF ** -0.5, 0.1875, ((0, 4),))
    cotangent = centred(key_of[7], (TOKENS, D), 1.0, 6.0, ((0, 8),))
    doc_lengths = draw_doc_lengths(jax.random.fold_in(key_of[10], 71), 0)
    roster = draw_roster(jax.random.fold_in(key_of[10], 71), 0)
    return dict(tokens=tokens, gain_one=gain_one, w_qkv=w_qkv, w_out=w_out, gain_two=gain_two, w_in=w_in, w_down=w_down, cotangent=cotangent, doc_lengths=doc_lengths, roster=roster)


EPSILON = 1e-05
ROPE_THETA = 160000.0
MASKED = -1e+30
HIGHEST = lax.Precision.HIGHEST

@jax.custom_vjp
def low(v):
    return lax.optimization_barrier(v.astype(jnp.bfloat16)).astype(jnp.float32)

@jax.custom_vjp
def low_back(v):
    return v

def low_keep(v):
    return (low(v), None)

def low_pass(kept, grad):
    return (grad,)

def back_keep(v):
    return (v, None)

def back_low(kept, grad):
    return (low(grad),)
low.defvjp(low_keep, low_pass)
low_back.defvjp(back_keep, back_low)

def layer_norm(values, gain):
    centre = lax.optimization_barrier(jnp.mean(values, axis=-1, keepdims=True))
    shifted = values - centre
    spread = lax.optimization_barrier(jnp.mean(shifted * shifted, axis=-1, keepdims=True))
    return shifted * lax.rsqrt(spread + EPSILON) * gain

def token_layout(doc_lengths, roster, first_row, row_total, tok_dev):
    row_ids = first_row + jnp.arange(row_total).astype(jnp.int32)
    owners = row_ids // tok_dev
    picked = owners[:, None] == jnp.arange(roster.shape[0]).astype(jnp.int32)[None, :]
    blocks = lax.optimization_barrier(jnp.sum(jnp.where(picked, roster[None, :], 0), axis=1)).astype(jnp.int32)
    packed = blocks * tok_dev + row_ids % tok_dev
    doc_ends = jnp.cumsum(doc_lengths).astype(jnp.int32)
    starts = doc_ends - doc_lengths
    segment = lax.optimization_barrier(jnp.sum((packed[:, None] >= doc_ends[None, :]).astype(jnp.int32), axis=1)).astype(jnp.int32)
    within = segment[:, None] == jnp.arange(doc_lengths.shape[0]).astype(jnp.int32)[None, :]
    in_doc = packed - lax.optimization_barrier(jnp.sum(jnp.where(within, starts[None, :], 0), axis=1)).astype(jnp.int32)
    return (segment, in_doc)

def rotary_tables(in_doc, head_dim):
    half_dim = head_dim // 2
    frequency = ROPE_THETA ** (-(jnp.arange(half_dim).astype(jnp.float32) * (2.0 / head_dim)))
    angles = in_doc.astype(jnp.float32)[:, None] * frequency[None, :]
    cos_table = jnp.cos(angles)
    sin_table = jnp.sin(angles)
    return (jnp.concatenate([cos_table, cos_table], axis=1), jnp.concatenate([sin_table, sin_table], axis=1))

def rotate(vectors, cos_table, sin_table):
    half_dim = vectors.shape[-1] // 2
    turned = jnp.concatenate([-vectors[..., half_dim:], vectors[..., :half_dim]], axis=-1)
    return vectors * cos_table[:, None, :] + turned * sin_table[:, None, :]

def attend_block(query_block, query_segment, key_rows, value_rows, key_segment):
    raw_scores = low_back(jnp.einsum('qhd,khd->hqk', query_block, key_rows, precision=HIGHEST))
    same_doc = (query_segment[:, None] == key_segment[None, :])[None]
    scores = jnp.where(same_doc, raw_scores * HDIM ** (-0.5), MASKED)
    log_total = jax.nn.logsumexp(scores, axis=2, keepdims=True)
    attn_probs = jnp.where(same_doc, jnp.exp(scores - log_total), 0.0)
    return jnp.einsum('hqk,khd->qhd', low(attn_probs), value_rows, precision=HIGHEST)

def layer_forward(segment, cos_table, sin_table, tokens, gain_one, w_qkv, w_out, gain_two, w_in, w_down):
    h_one = low(layer_norm(tokens, gain_one))
    projected = low_back(jnp.einsum('td,dkc->tkc', h_one, w_qkv, precision=HIGHEST))
    queries = low(rotate(projected[:, 0].reshape(TOKENS, HEADS, HDIM), cos_table, sin_table))
    key_rows = low(rotate(projected[:, 1].reshape(TOKENS, HEADS, HDIM), cos_table, sin_table))
    value_rows = low(projected[:, 2].reshape(TOKENS, HEADS, HDIM))
    block_rows = math.gcd(TOKENS, 512)
    grouped = queries.reshape(TOKENS // block_rows, block_rows, HEADS, HDIM)
    seg_grouped = segment.reshape(TOKENS // block_rows, block_rows)

    def one_block(inputs):
        return attend_block(inputs[0], inputs[1], key_rows, value_rows, segment)
    attended = lax.map(jax.checkpoint(one_block), (grouped, seg_grouped)).reshape(TOKENS, HEADS * HDIM)
    out_b = low(low_back(attended))
    branch_one = low_back(jnp.dot(out_b, w_out, precision=HIGHEST))
    middle = tokens + branch_one
    h_two = low(layer_norm(middle, gain_two))
    gate_up = low_back(jnp.einsum('td,dkf->tkf', h_two, w_in, precision=HIGHEST))
    mixed = low(jax.nn.gelu(gate_up[:, 0], approximate=False) * gate_up[:, 1])
    branch_two = low_back(jnp.dot(mixed, w_down, precision=HIGHEST))
    return middle + branch_two

def reference(tokens, gain_one, w_qkv, w_out, gain_two, w_in, w_down, cotangent, doc_lengths, roster):
    segment, in_doc = token_layout(doc_lengths, roster, 0, TOKENS, TOK_DEV)
    cos_table, sin_table = rotary_tables(in_doc, HDIM)
    forward = functools.partial(layer_forward, segment, cos_table, sin_table)
    result, pullback = jax.vjp(forward, tokens.astype(jnp.float32), gain_one.astype(jnp.float32), w_qkv.astype(jnp.float32), w_out.astype(jnp.float32), gain_two.astype(jnp.float32), w_in.astype(jnp.float32), w_down.astype(jnp.float32))
    gradients = pullback(cotangent.astype(jnp.float32))
    return (result.astype(jnp.bfloat16), gradients[0].astype(jnp.bfloat16), gradients[1], gradients[2], gradients[3], gradients[4], gradients[5], gradients[6])
```

```python
import functools

import jax
import jax.numpy as jnp
from jax import lax
from jax.experimental import pallas as pl
from jax.experimental.pallas import tpu as pltpu
from jax.sharding import PartitionSpec as P

HDIM = 64
HALF = HDIM // 2
EPSILON = 1e-05
ROPE_THETA = 160000.0
MASKED = -1e30
AUG = 80
F32 = jnp.float32
BF16 = jnp.bfloat16
ANY = pl.BlockSpec(memory_space=pl.ANY)
VMEM = pl.BlockSpec(memory_space=pltpu.VMEM)
SMEM = pl.BlockSpec(memory_space=pltpu.SMEM)

NN = (((1,), (0,)), ((), ()))
NT = (((1,), (1,)), ((), ()))
TN = (((0,), (0,)), ((), ()))


def mm(a, b, dims):
    return lax.dot_general(a, b, dims, preferred_element_type=F32)


def swap(x, axis, hop, count):
    return lax.ppermute(x, axis, [(i, i ^ hop) for i in range(count)])


def doc_bounds(len_ref):
    ends, total = [], jnp.int32(0)
    for d in range(len_ref.shape[0]):
        total = total + len_ref[d]
        ends.append(total)
    return ends


def doc_of(ends, position):
    found = jnp.int32(0)
    for end in ends:
        found = found + (end <= position).astype(jnp.int32)
    return found


def meet(ends, base_a, base_b, rows):
    low = jnp.maximum(doc_of(ends, base_a), doc_of(ends, base_b))
    high = jnp.minimum(doc_of(ends, base_a + rows - 1), doc_of(ends, base_b + rows - 1))
    return low <= high


def doc_rows(ends, base, rows):
    spot = base + lax.broadcasted_iota(jnp.int32, (16, rows), 1)
    line = lax.broadcasted_iota(jnp.int32, (16, rows), 0)
    held = jnp.zeros((16, rows), F32)
    start = jnp.int32(0)
    for d, end in enumerate(ends):
        inside = (line == d) & (spot >= start) & (spot < end)
        held = jnp.where(inside, 1.0, held)
        start = end
    return held


def ban_rows(ends, base, rows):
    line = lax.broadcasted_iota(jnp.int32, (16, rows), 0)
    held = doc_rows(ends, base, rows)
    return jnp.where((held > 0.5) | (line >= len(ends)), 0.0, MASKED)


def key_row(block, seq_index):
    return seq_index ^ (2 * block)


def forward_kernel(count, heads, len_ref, roster_ref, q_own, q_pair, *refs):
    kv_refs = refs[:count]
    own_out, pair_out = refs[count : count + 2]
    kv, q_aug, state, sems = refs[count + 2 :]
    rows = q_own.shape[1]
    width = heads * HDIM
    me = lax.axis_index("seq")
    copies = [pltpu.make_async_copy(kv_refs[j], kv.at[j], sems.at[j]) for j in range(count)]
    for copy in copies:
        copy.start()
    ends = doc_bounds(len_ref)
    bases = (roster_ref[me] * rows, roster_ref[me ^ 1] * rows)
    for g, q_ref in enumerate((q_own, q_pair)):
        mark = doc_rows(ends, bases[g], rows).astype(BF16)
        for h in range(heads):
            q_aug[g * heads + h, :HDIM, :] = q_ref[h * HDIM : (h + 1) * HDIM, :]
            q_aug[g * heads + h, HDIM:, :] = mark
    line = lax.broadcasted_iota(jnp.int32, (2 * heads, AUG, rows), 1)
    state[...] = jnp.where(line >= 72, MASKED, 0.0)
    for copy in copies:
        copy.wait()

    first = lax.broadcasted_iota(jnp.int32, (16, rows), 0) == 0
    ones = jnp.where(first, 1.0, 0.0).astype(BF16)

    def block(j, carry):
        key_base = roster_ref[key_row(j, me)] * rows
        ban = ban_rows(ends, key_base, rows).astype(BF16)
        for g in range(2):

            @pl.when(meet(ends, bases[g], key_base, rows))
            def _():
                for h in range(heads):
                    at = g * heads + h
                    keys = jnp.concatenate([kv[j, h * HDIM : (h + 1) * HDIM, :], ban], axis=0)
                    vals = jnp.concatenate(
                        [kv[j, width + h * HDIM : width + (h + 1) * HDIM, :], ones], axis=0
                    )
                    scores = mm(keys, q_aug[at], TN)
                    old = state[at, 72:73, :]
                    new = jnp.maximum(old, jnp.max(scores, axis=0, keepdims=True))
                    probs = jnp.exp(scores - new).astype(BF16)
                    part = mm(vals, probs, NN)
                    fade = jnp.exp(old - new)
                    state[at, :72, :] = state[at, :72, :] * fade + part[:72]
                    state[at, 72:, :] = jnp.broadcast_to(new, (8, rows))

        return carry

    lax.fori_loop(0, count, block, 0)
    own_out[...] = state[:heads]
    pair_out[...] = state[heads:]


def attention_forward(doc_lengths, roster, q_own, q_pair, blocks):
    width, rows = q_own.shape
    heads = width // HDIM
    count = len(blocks)
    shape = jax.ShapeDtypeStruct((heads, AUG, rows), F32)
    return pl.pallas_call(
        functools.partial(forward_kernel, count, heads),
        out_shape=(shape, shape),
        in_specs=[SMEM, SMEM, VMEM, VMEM] + [ANY] * count,
        out_specs=(VMEM, VMEM),
        scratch_shapes=[
            pltpu.VMEM((count, 2 * width, rows), BF16),
            pltpu.VMEM((2 * heads, AUG, rows), BF16),
            pltpu.VMEM((2 * heads, AUG, rows), F32),
            pltpu.SemaphoreType.DMA((count,)),
        ],
        compiler_params=pltpu.CompilerParams(vmem_limit_bytes=56 * 2**20),
    )(doc_lengths, roster, q_own, q_pair, *blocks)


def backward_kernel(count, heads, len_ref, roster_ref, *refs):
    q_own, q_pair, g_own, g_pair, o_own, o_pair, t_own, t_pair = refs[:8]
    kv_refs = refs[8 : 8 + count]
    dq_own, dq_pair = refs[8 + count : 10 + count]
    dkv_refs = refs[10 + count : 10 + 2 * count]
    kv, q_aug, delta, dq, dkv, sems = refs[10 + 2 * count :]
    rows = q_own.shape[1]
    width = heads * HDIM
    me = lax.axis_index("seq")
    copies = [pltpu.make_async_copy(kv_refs[j], kv.at[j], sems.at[j]) for j in range(count)]
    for copy in copies:
        copy.start()
    ends = doc_bounds(len_ref)
    bases = (roster_ref[me] * rows, roster_ref[me ^ 1] * rows)
    for g, (q_ref, g_ref, o_ref) in enumerate(((q_own, g_own, o_own), (q_pair, g_pair, o_pair))):
        mark = doc_rows(ends, bases[g], rows).astype(BF16)
        for h in range(heads):
            part = slice(h * HDIM, (h + 1) * HDIM)
            q_aug[g * heads + h, :HDIM, :] = q_ref[part, :]
            q_aug[g * heads + h, HDIM:, :] = mark
            product = g_ref[part, :].astype(F32) * o_ref[part, :].astype(F32)
            delta[g * heads + h] = jnp.broadcast_to(
                jnp.sum(product, axis=0, keepdims=True), (8, rows)
            )
    dq[...] = jnp.zeros_like(dq)
    for copy in copies:
        copy.wait()

    def block(j, carry):
        key_base = roster_ref[key_row(j, me)] * rows
        ban = ban_rows(ends, key_base, rows).astype(BF16)
        dkv[j] = jnp.zeros((2 * width, rows), F32)
        for g, (g_ref, t_ref) in enumerate(((g_own, t_own), (g_pair, t_pair))):

            @pl.when(meet(ends, bases[g], key_base, rows))
            def _():
                for h in range(heads):
                    at = g * heads + h
                    part = slice(h * HDIM, (h + 1) * HDIM)
                    late = slice(width + h * HDIM, width + (h + 1) * HDIM)
                    keys = kv[j, part, :]
                    scores = mm(jnp.concatenate([keys, ban], axis=0), q_aug[at], TN)
                    probs = jnp.exp(scores - t_ref[h, 0:1, :])
                    prob_grads = mm(kv[j, late, :], g_ref[part, :], TN)
                    score_grad = (probs * (prob_grads - delta[at, 0:1, :])).astype(BF16)
                    dkv[j, late, :] += mm(g_ref[part, :], probs.astype(BF16), NT)
                    dkv[j, part, :] += mm(q_aug[at, :HDIM, :], score_grad, NT)
                    dq[at] += mm(keys, score_grad, NN)

        return carry

    lax.fori_loop(0, count, block, 0)
    for h in range(heads):
        part = slice(h * HDIM, (h + 1) * HDIM)
        dq_own[part, :] = (dq[h] * HDIM**-0.5).astype(dq_own.dtype)
        dq_pair[part, :] = (dq[heads + h] * HDIM**-0.5).astype(dq_pair.dtype)
    for j in range(count):
        dkv_refs[j][...] = dkv[j].astype(dkv_refs[j].dtype)


def attention_backward(doc_lengths, roster, queries, grads, outs, totals, blocks):
    width, rows = queries[0].shape
    heads = width // HDIM
    count = len(blocks)
    grad_shape = jax.ShapeDtypeStruct((width, rows), F32)
    pair_shape = jax.ShapeDtypeStruct((width, rows), BF16)
    first = jax.ShapeDtypeStruct((2 * width, rows), F32)
    other = jax.ShapeDtypeStruct((2 * width, rows), BF16)
    return pl.pallas_call(
        functools.partial(backward_kernel, count, heads),
        out_shape=(grad_shape, pair_shape, first) + (other,) * (count - 1),
        in_specs=[SMEM, SMEM] + [VMEM] * 8 + [ANY] * count,
        out_specs=(VMEM,) * (2 + count),
        scratch_shapes=[
            pltpu.VMEM((count, 2 * width, rows), BF16),
            pltpu.VMEM((2 * heads, AUG, rows), BF16),
            pltpu.VMEM((2 * heads, 8, rows), F32),
            pltpu.VMEM((2 * heads, HDIM, rows), F32),
            pltpu.VMEM((count, 2 * width, rows), F32),
            pltpu.SemaphoreType.DMA((count,)),
        ],
        compiler_params=pltpu.CompilerParams(vmem_limit_bytes=60 * 2**20),
    )(doc_lengths, roster, *queries, *grads, *outs, *totals, *blocks)


def normed(values):
    centre = jnp.mean(values, axis=-1, keepdims=True)
    shifted = values - centre
    spread = jnp.mean(shifted * shifted, axis=-1, keepdims=True)
    scale = lax.rsqrt(spread + EPSILON)
    return shifted * scale, scale


def norm_back(unit, scale, grad, gain):
    u = grad * gain
    mean_u = jnp.mean(u, axis=-1, keepdims=True)
    mean_un = jnp.mean(u * unit, axis=-1, keepdims=True)
    return scale * (u - mean_u - unit * mean_un)


def own_tables(doc_lengths, roster, me, rows):
    base = jnp.sum(jnp.where(jnp.arange(roster.shape[0]) == me, roster, 0)) * rows
    packed = base + jnp.arange(rows, dtype=jnp.int32)
    doc_ends = jnp.cumsum(doc_lengths)
    passed = packed[None, :] >= doc_ends[:, None]
    start = jnp.max(jnp.where(passed, doc_ends[:, None], 0), axis=0)
    place = packed - start
    frequency = ROPE_THETA ** (-(jnp.arange(HALF).astype(F32) * (2.0 / HDIM)))
    angles = place.astype(F32)[None, :] * frequency[:, None]
    return jnp.cos(angles), jnp.sin(angles)


def rotate(vectors, cos_table, sin_table):
    width, rows = vectors.shape
    split = vectors.reshape(width // HDIM, 2, HALF, rows)
    low, high = split[:, 0], split[:, 1]
    return jnp.stack(
        [low * cos_table - high * sin_table, high * cos_table + low * sin_table], axis=1
    ).reshape(width, rows)


def rotate_back(vectors, cos_table, sin_table):
    width, rows = vectors.shape
    split = vectors.reshape(width // HDIM, 2, HALF, rows)
    low, high = split[:, 0], split[:, 1]
    return jnp.stack(
        [low * cos_table + high * sin_table, high * cos_table - low * sin_table], axis=1
    ).reshape(width, rows)


def body(
    n_seq,
    n_tp,
    tokens,
    gain_one,
    w_qkv,
    w_out,
    gain_two,
    w_in,
    w_down,
    cotangent,
    doc_lengths,
    roster,
):
    rows, model = tokens.shape
    width = w_qkv.shape[2]
    heads = width // HDIM
    units = w_in.shape[2]
    part_rows = rows // n_tp
    count = n_seq // 2
    me = lax.axis_index("seq")
    tp = lax.axis_index("tp")
    qkv_t = w_qkv.transpose(1, 2, 0).reshape(3 * width, model)
    in_t = w_in.transpose(1, 2, 0).reshape(2 * units, model)

    def own_part(x, hop=0):
        return lax.dynamic_slice_in_dim(x, (tp ^ hop) * part_rows, part_rows, 0)

    cos_table, sin_table = own_tables(doc_lengths, roster, me, rows)
    inputs = tokens.astype(F32)
    unit_one, scale_one = normed(inputs)
    h_one = (unit_one * gain_one).astype(BF16)
    projected = mm(qkv_t, h_one, NT)
    queries = rotate(projected[:width], cos_table, sin_table).astype(BF16)
    queries = queries * jnp.asarray(HDIM**-0.5, BF16)
    keys = rotate(projected[width : 2 * width], cos_table, sin_table).astype(BF16)
    kv = jnp.concatenate([keys, projected[2 * width :].astype(BF16)], axis=0)
    blocks = [kv] + [swap(kv, "seq", 2 * j, n_seq) for j in range(1, count)]
    q_pair = swap(queries, "seq", 1, n_seq)
    w_outs = [w_out] + [swap(w_out, "tp", k, n_tp) for k in range(1, n_tp)]

    state_own, state_pair = attention_forward(doc_lengths, roster, queries, q_pair, blocks)
    state_back = swap(state_pair, "seq", 1, n_seq)
    top = jnp.maximum(state_own[:, 72:73], state_back[:, 72:73])
    fade_own = jnp.exp(state_own[:, 72:73] - top)
    fade_back = jnp.exp(state_back[:, 72:73] - top)
    mixed_state = state_own[:, :72] * fade_own + state_back[:, :72] * fade_back
    total = mixed_state[:, 64:65]
    log_total = top + jnp.log(total)
    out_b = (mixed_state[:, :64] / total).astype(BF16).reshape(width, rows)
    outs = [out_b] + [swap(out_b, "tp", k, n_tp) for k in range(1, n_tp)]
    out_pair = swap(out_b, "seq", 1, n_seq)
    totals = jnp.broadcast_to(log_total, (heads, 8, rows))
    totals_pair = swap(totals, "seq", 1, n_seq)

    middle = inputs
    for out, weight in zip(outs, w_outs):
        middle = middle + mm(out, weight, TN)
    unit_two, scale_two = normed(middle)
    h_two = (unit_two * gain_two).astype(BF16)
    gate_up = mm(in_t, h_two, NT)
    gate, up = gate_up[:units], gate_up[units:]
    erf_part = 0.5 * (1.0 + lax.erf(gate * (2.0**-0.5)))
    activated = gate * erf_part
    slope = erf_part + gate * jnp.exp(-0.5 * gate * gate) * ((2.0 * jnp.pi) ** -0.5)
    mixed = (activated * up).astype(BF16)
    mixed_grad = mm(w_down, cotangent, NT)
    gate_grad = jnp.concatenate(
        [mixed_grad * up * slope, mixed_grad * activated], axis=0
    ).astype(BF16)
    h_two_grad = mm(gate_grad, in_t, TN)
    gain_two_part = jnp.sum(h_two_grad * unit_two, axis=0, keepdims=True)
    h_two_low = h_two_grad.astype(BF16)
    arrived = own_part(h_two_grad)
    for k in range(1, n_tp):
        arrived = arrived + swap(own_part(h_two_low, k), "tp", k, n_tp).astype(F32)

    branch_two = mm(mixed, w_down, TN).astype(BF16)
    grad_down = mm(mixed, cotangent, NN)
    grad_in = mm(gate_grad, h_two, NN)

    middle_part = own_part(middle)
    unit_part, scale_part = normed(middle_part)
    middle_grad = own_part(cotangent).astype(F32) + norm_back(
        unit_part, scale_part, arrived, gain_two
    )
    branch_grad = middle_grad.astype(BF16)
    pieces = [mm(branch_grad, w_outs[0], NT).astype(BF16)] + [
        swap(mm(branch_grad, w_outs[k], NT).astype(BF16), "tp", k, n_tp) for k in range(1, n_tp)
    ]
    out_grad = jnp.zeros((rows, width), BF16)
    for k in range(n_tp):
        out_grad = lax.dynamic_update_slice_in_dim(out_grad, pieces[k], (tp ^ k) * part_rows, 0)
    out_grad = out_grad.T
    grad_pair = swap(out_grad, "seq", 1, n_seq)

    results = attention_backward(
        doc_lengths,
        roster,
        (queries, q_pair),
        (out_grad, grad_pair),
        (out_b, out_pair),
        (totals, totals_pair),
        blocks,
    )
    dq_own, dq_pair = results[:2]
    dkv = results[2]
    for j in range(1, count):
        dkv = dkv + swap(results[2 + j], "seq", 2 * j, n_seq).astype(F32)
    dq = dq_own + swap(dq_pair, "seq", 1, n_seq).astype(F32)

    branch_full = jnp.zeros((rows, model), BF16)
    for k in range(n_tp):
        piece = swap(branch_grad, "tp", k, n_tp) if k else branch_grad
        branch_full = lax.dynamic_update_slice_in_dim(branch_full, piece, (tp ^ k) * part_rows, 0)
    grad_out = mm(out_b, branch_full, NN)

    proj_grad = jnp.concatenate(
        [
            rotate_back(dq, cos_table, sin_table),
            rotate_back(dkv[:width], cos_table, sin_table),
            dkv[width:],
        ],
        axis=0,
    ).astype(BF16)
    h_one_grad = mm(proj_grad, qkv_t, TN)
    gain_one_part = jnp.sum(h_one_grad * unit_one, axis=0, keepdims=True)
    h_one_low = h_one_grad.astype(BF16)
    arrived = own_part(h_one_grad)
    for k in range(1, n_tp):
        arrived = arrived + swap(own_part(h_one_low, k), "tp", k, n_tp).astype(F32)
    unit_part, scale_part = normed(own_part(tokens).astype(F32))
    input_part = (middle_grad + norm_back(unit_part, scale_part, arrived, gain_one)).astype(BF16)
    input_grad = jnp.zeros((rows, model), BF16)
    for k in range(n_tp):
        piece = swap(input_part, "tp", k, n_tp) if k else input_part
        input_grad = lax.dynamic_update_slice_in_dim(input_grad, piece, (tp ^ k) * part_rows, 0)
    grad_qkv = mm(proj_grad, h_one, NN)

    layer_out = (middle + lax.psum(branch_two, "tp").astype(F32)).astype(BF16)
    low = lambda x: x.astype(BF16)
    gains = jnp.concatenate([gain_one_part, gain_two_part], axis=0)
    early = lax.psum((low(grad_down), low(grad_in)), "seq")
    late = lax.psum((low(grad_out), low(grad_qkv)), "seq")
    gains = lax.psum(gains, ("seq", "tp"))
    f = lambda x: x.astype(F32)
    back = lambda x, n: f(x).reshape(-1, n, model).transpose(2, 0, 1)
    return (
        layer_out,
        input_grad,
        gains[0],
        back(late[1], width),
        f(late[0]),
        gains[1],
        back(early[1], units),
        f(early[0]),
    )


def solution(mesh):
    placed = (
        P("seq", None),
        P(),
        P(None, None, "tp"),
        P("tp", None),
        P(),
        P(None, None, "tp"),
        P("tp", None),
        P("seq", None),
        P(),
        P(),
    )
    return jax.shard_map(
        functools.partial(body, mesh.shape["seq"], mesh.shape["tp"]),
        mesh=mesh,
        in_specs=placed,
        out_specs=(
            P("seq", None),
            P("seq", None),
            P(),
            P(None, None, "tp"),
            P("tp", None),
            P(),
            P(None, None, "tp"),
            P("tp", None),
        ),
        check_vma=False,
    )
```

```python
import functools

import jax
import jax.numpy as jnp
from jax import lax
from jax.experimental import pallas as pl
from jax.experimental.pallas import tpu as pltpu
from jax.sharding import PartitionSpec as P

HDIM = 64
HALF = HDIM // 2
EPSILON = 1e-05
ROPE_THETA = 160000.0
MASKED = -1e30
AUG = 80
STRIP = 64
F32 = jnp.float32
BF16 = jnp.bfloat16
ANY = pl.BlockSpec(memory_space=pl.ANY)
VMEM = pl.BlockSpec(memory_space=pltpu.VMEM)
SMEM = pl.BlockSpec(memory_space=pltpu.SMEM)

NN = (((1,), (0,)), ((), ()))
NT = (((1,), (1,)), ((), ()))
TN = (((0,), (0,)), ((), ()))


def params(mib):
    return pltpu.CompilerParams(vmem_limit_bytes=mib * 2**20)


def shaped(shape, dtype):
    return jax.ShapeDtypeStruct(shape, dtype)


def mm(a, b, dims):
    return lax.dot_general(a, b, dims, preferred_element_type=F32)


def swap(x, axis, hop, count):
    return lax.ppermute(x, axis, [(i, i ^ hop) for i in range(count)])


def doc_bounds(len_ref):
    ends, total = [], jnp.int32(0)
    for d in range(len_ref.shape[0]):
        total = total + len_ref[d]
        ends.append(total)
    return ends


def doc_of(ends, position):
    found = jnp.int32(0)
    for end in ends:
        found = found + (end <= position).astype(jnp.int32)
    return found


def meet(ends, base_a, base_b, rows):
    low = jnp.maximum(doc_of(ends, base_a), doc_of(ends, base_b))
    high = jnp.minimum(doc_of(ends, base_a + rows - 1), doc_of(ends, base_b + rows - 1))
    return low <= high


def doc_rows(ends, base, rows):
    spot = base + lax.broadcasted_iota(jnp.int32, (16, rows), 1)
    line = lax.broadcasted_iota(jnp.int32, (16, rows), 0)
    held = jnp.zeros((16, rows), F32)
    start = jnp.int32(0)
    for d, end in enumerate(ends):
        inside = (line == d) & (spot >= start) & (spot < end)
        held = jnp.where(inside, 1.0, held)
        start = end
    return held


def ban_rows(ends, base, rows):
    line = lax.broadcasted_iota(jnp.int32, (16, rows), 0)
    held = doc_rows(ends, base, rows)
    return jnp.where((held > 0.5) | (line >= len(ends)), 0.0, MASKED)


def key_row(block, seq_index):
    return seq_index ^ (2 * block)


def place_row(ends, base, rows):
    spot = base + lax.broadcasted_iota(jnp.int32, (1, rows), 1)
    start = jnp.zeros((1, rows), jnp.int32)
    for end in ends:
        start = jnp.where(spot >= end, end, start)
    return (spot - start).astype(F32)


def normed(values):
    centre = jnp.mean(values, axis=-1, keepdims=True)
    shifted = values - centre
    spread = jnp.mean(shifted * shifted, axis=-1, keepdims=True)
    scale = lax.rsqrt(spread + EPSILON)
    return shifted * scale, scale


def norm_back(unit, scale, grad, gain):
    u = grad * gain
    mean_u = jnp.mean(u, axis=-1, keepdims=True)
    mean_un = jnp.mean(u * unit, axis=-1, keepdims=True)
    return scale * (u - mean_u - unit * mean_un)


def project_kernel(width, len_ref, roster_ref, x_ref, gain_ref, w_ref, freq_ref, *refs):
    q_out, kv_out, h_out, cos_out, sin_out, proj = refs
    rows = x_ref.shape[0]

    def strip(i, carry):
        at = pl.ds(i * STRIP, STRIP)
        unit, unused = normed(x_ref[at, :].astype(F32))
        h_out[at, :] = (unit * gain_ref[...]).astype(BF16)
        return carry

    lax.fori_loop(0, rows // STRIP, strip, 0)
    proj[...] = mm(w_ref[...], h_out[...], NT)
    ends = doc_bounds(len_ref)
    place = place_row(ends, roster_ref[lax.axis_index("seq")] * rows, rows)
    angles = place * freq_ref[...]
    cos_table = jnp.cos(angles)
    sin_table = jnp.sin(angles)
    cos_out[...] = cos_table
    sin_out[...] = sin_table
    for at in range(0, 2 * width, HDIM):
        low = proj[at : at + HALF, :]
        high = proj[at + HALF : at + HDIM, :]
        turned_low = (low * cos_table - high * sin_table).astype(BF16)
        turned_high = (high * cos_table + low * sin_table).astype(BF16)
        if at < width:
            q_out[at : at + HALF, :] = (turned_low.astype(F32) * HDIM**-0.5).astype(BF16)
            q_out[at + HALF : at + HDIM, :] = (turned_high.astype(F32) * HDIM**-0.5).astype(BF16)
        else:
            kv_out[at - width : at - width + HALF, :] = turned_low
            kv_out[at - width + HALF : at - width + HDIM, :] = turned_high
    kv_out[width:, :] = proj[2 * width :, :].astype(BF16)


def project(doc_lengths, roster, tokens, gain, qkv_t):
    rows, model = tokens.shape
    width = qkv_t.shape[0] // 3
    freq = ROPE_THETA ** (-(jnp.arange(HALF).astype(F32) * (2.0 / HDIM)))
    table = shaped((HALF, rows), F32)
    return pl.pallas_call(
        functools.partial(project_kernel, width),
        out_shape=(
            shaped((width, rows), BF16),
            shaped((2 * width, rows), BF16),
            shaped((rows, model), BF16),
            table,
            table,
        ),
        in_specs=[SMEM, SMEM] + [VMEM] * 4,
        out_specs=(VMEM,) * 5,
        scratch_shapes=[pltpu.VMEM((3 * width, rows), F32)],
        compiler_params=params(24),
    )(doc_lengths, roster, tokens, gain, qkv_t, freq[:, None])


def forward_kernel(count, heads, len_ref, roster_ref, q_own, q_pair, *refs):
    kv_refs = refs[:count]
    own_out, pair_out = refs[count : count + 2]
    kv, q_aug, state, sems = refs[count + 2 :]
    rows = q_own.shape[1]
    width = heads * HDIM
    me = lax.axis_index("seq")
    copies = [pltpu.make_async_copy(kv_refs[j], kv.at[j], sems.at[j]) for j in range(count)]
    for copy in copies:
        copy.start()
    ends = doc_bounds(len_ref)
    bases = (roster_ref[me] * rows, roster_ref[me ^ 1] * rows)
    for g, q_ref in enumerate((q_own, q_pair)):
        mark = doc_rows(ends, bases[g], rows).astype(BF16)
        for h in range(heads):
            q_aug[g * heads + h, :HDIM, :] = q_ref[h * HDIM : (h + 1) * HDIM, :]
            q_aug[g * heads + h, HDIM:, :] = mark
    line = lax.broadcasted_iota(jnp.int32, (2 * heads, AUG, rows), 1)
    state[...] = jnp.where(line >= 72, MASKED, 0.0)
    for copy in copies:
        copy.wait()

    first = lax.broadcasted_iota(jnp.int32, (16, rows), 0) == 0
    ones = jnp.where(first, 1.0, 0.0).astype(BF16)

    def block(j, carry):
        key_base = roster_ref[key_row(j, me)] * rows
        ban = ban_rows(ends, key_base, rows).astype(BF16)
        for g in range(2):

            @pl.when(meet(ends, bases[g], key_base, rows))
            def _():
                for h in range(heads):
                    at = g * heads + h
                    keys = jnp.concatenate([kv[j, h * HDIM : (h + 1) * HDIM, :], ban], axis=0)
                    vals = jnp.concatenate(
                        [kv[j, width + h * HDIM : width + (h + 1) * HDIM, :], ones], axis=0
                    )
                    scores = mm(keys, q_aug[at], TN)
                    old = state[at, 72:73, :]
                    new = jnp.maximum(old, jnp.max(scores, axis=0, keepdims=True))
                    probs = jnp.exp(scores - new).astype(BF16)
                    part = mm(vals, probs, NN)
                    fade = jnp.exp(old - new)
                    state[at, :72, :] = state[at, :72, :] * fade + part[:72]
                    state[at, 72:, :] = jnp.broadcast_to(new, (8, rows))

        return carry

    lax.fori_loop(0, count, block, 0)
    own_out[...] = state[:heads]
    pair_out[...] = state[heads:]


def attention_forward(doc_lengths, roster, q_own, q_pair, blocks):
    width, rows = q_own.shape
    heads = width // HDIM
    count = len(blocks)
    shape = jax.ShapeDtypeStruct((heads, AUG, rows), F32)
    return pl.pallas_call(
        functools.partial(forward_kernel, count, heads),
        out_shape=(shape, shape),
        in_specs=[SMEM, SMEM, VMEM, VMEM] + [ANY] * count,
        out_specs=(VMEM, VMEM),
        scratch_shapes=[
            pltpu.VMEM((count, 2 * width, rows), BF16),
            pltpu.VMEM((2 * heads, AUG, rows), BF16),
            pltpu.VMEM((2 * heads, AUG, rows), F32),
            pltpu.SemaphoreType.DMA((count,)),
        ],
        compiler_params=pltpu.CompilerParams(vmem_limit_bytes=56 * 2**20),
    )(doc_lengths, roster, q_own, q_pair, *blocks)


def backward_kernel(count, heads, len_ref, roster_ref, *refs):
    q_own, q_pair, g_own, g_pair, o_own, o_pair, t_own, t_pair = refs[:8]
    kv_refs = refs[8 : 8 + count]
    dq_own, dq_pair = refs[8 + count : 10 + count]
    dkv_refs = refs[10 + count : 10 + 2 * count]
    kv, q_aug, delta, dq, dkv, sems = refs[10 + 2 * count :]
    rows = q_own.shape[1]
    width = heads * HDIM
    me = lax.axis_index("seq")
    copies = [pltpu.make_async_copy(kv_refs[j], kv.at[j], sems.at[j]) for j in range(count)]
    for copy in copies:
        copy.start()
    ends = doc_bounds(len_ref)
    bases = (roster_ref[me] * rows, roster_ref[me ^ 1] * rows)
    for g, (q_ref, g_ref, o_ref) in enumerate(((q_own, g_own, o_own), (q_pair, g_pair, o_pair))):
        mark = doc_rows(ends, bases[g], rows).astype(BF16)
        for h in range(heads):
            part = slice(h * HDIM, (h + 1) * HDIM)
            q_aug[g * heads + h, :HDIM, :] = q_ref[part, :]
            q_aug[g * heads + h, HDIM:, :] = mark
            product = g_ref[part, :].astype(F32) * o_ref[part, :].astype(F32)
            delta[g * heads + h] = jnp.broadcast_to(
                jnp.sum(product, axis=0, keepdims=True), (8, rows)
            )
    dq[...] = jnp.zeros_like(dq)
    for copy in copies:
        copy.wait()

    def block(j, carry):
        key_base = roster_ref[key_row(j, me)] * rows
        ban = ban_rows(ends, key_base, rows).astype(BF16)
        dkv[j] = jnp.zeros((2 * width, rows), F32)
        for g, (g_ref, t_ref) in enumerate(((g_own, t_own), (g_pair, t_pair))):

            @pl.when(meet(ends, bases[g], key_base, rows))
            def _():
                for h in range(heads):
                    at = g * heads + h
                    part = slice(h * HDIM, (h + 1) * HDIM)
                    late = slice(width + h * HDIM, width + (h + 1) * HDIM)
                    keys = kv[j, part, :]
                    scores = mm(jnp.concatenate([keys, ban], axis=0), q_aug[at], TN)
                    probs = jnp.exp(scores - t_ref[h, 0:1, :])
                    prob_grads = mm(kv[j, late, :], g_ref[part, :], TN)
                    score_grad = (probs * (prob_grads - delta[at, 0:1, :])).astype(BF16)
                    dkv[j, late, :] += mm(g_ref[part, :], probs.astype(BF16), NT)
                    dkv[j, part, :] += mm(q_aug[at, :HDIM, :], score_grad, NT)
                    dq[at] += mm(keys, score_grad, NN)

        return carry

    lax.fori_loop(0, count, block, 0)
    for h in range(heads):
        part = slice(h * HDIM, (h + 1) * HDIM)
        dq_own[part, :] = (dq[h] * HDIM**-0.5).astype(dq_own.dtype)
        dq_pair[part, :] = (dq[heads + h] * HDIM**-0.5).astype(dq_pair.dtype)
    for j in range(count):
        dkv_refs[j][...] = dkv[j].astype(dkv_refs[j].dtype)


def attention_backward(doc_lengths, roster, queries, grads, outs, totals, blocks):
    width, rows = queries[0].shape
    heads = width // HDIM
    count = len(blocks)
    grad_shape = jax.ShapeDtypeStruct((width, rows), F32)
    pair_shape = jax.ShapeDtypeStruct((width, rows), BF16)
    first = jax.ShapeDtypeStruct((2 * width, rows), F32)
    other = jax.ShapeDtypeStruct((2 * width, rows), BF16)
    return pl.pallas_call(
        functools.partial(backward_kernel, count, heads),
        out_shape=(grad_shape, pair_shape, first) + (other,) * (count - 1),
        in_specs=[SMEM, SMEM] + [VMEM] * 8 + [ANY] * count,
        out_specs=(VMEM,) * (2 + count),
        scratch_shapes=[
            pltpu.VMEM((count, 2 * width, rows), BF16),
            pltpu.VMEM((2 * heads, AUG, rows), BF16),
            pltpu.VMEM((2 * heads, 8, rows), F32),
            pltpu.VMEM((2 * heads, HDIM, rows), F32),
            pltpu.VMEM((count, 2 * width, rows), F32),
            pltpu.SemaphoreType.DMA((count,)),
        ],
        compiler_params=pltpu.CompilerParams(vmem_limit_bytes=60 * 2**20),
    )(doc_lengths, roster, *queries, *grads, *outs, *totals, *blocks)


def join_kernel(heads, own_ref, back_ref, out_ref, total_ref):
    rows = own_ref.shape[2]
    for h in range(heads):
        top_own = own_ref[h, 72:73, :]
        top_back = back_ref[h, 72:73, :]
        top = jnp.maximum(top_own, top_back)
        fade_own = jnp.exp(top_own - top)
        fade_back = jnp.exp(top_back - top)
        total = own_ref[h, 64:65, :] * fade_own + back_ref[h, 64:65, :] * fade_back
        share_own = fade_own / total
        share_back = fade_back / total
        value = own_ref[h, :HDIM, :] * share_own + back_ref[h, :HDIM, :] * share_back
        out_ref[h * HDIM : (h + 1) * HDIM, :] = value.astype(BF16)
        total_ref[h] = jnp.broadcast_to(top + jnp.log(total), (8, rows))


def join(own, back):
    heads, unused, rows = own.shape
    return pl.pallas_call(
        functools.partial(join_kernel, heads),
        out_shape=(shaped((heads * HDIM, rows), BF16), shaped((heads, 8, rows), F32)),
        in_specs=[VMEM, VMEM],
        out_specs=(VMEM, VMEM),
        compiler_params=params(16),
    )(own, back)


def feed_kernel(n_tp, x_ref, cot_ref, gain_ref, in_ref, down_ref, *refs):
    out_refs = refs[:n_tp]
    w_refs = refs[n_tp : 2 * n_tp]
    middle_out, h_out, mixed_out, gate_out, gain_out = refs[2 * n_tp : 2 * n_tp + 5]
    part_refs = refs[2 * n_tp + 5 : 3 * n_tp + 5]
    outs, weights, unit, gate_up, mixed_grad, grad = refs[3 * n_tp + 5 :]
    rows = x_ref.shape[0]
    part = rows // n_tp
    units = down_ref.shape[0]
    width = out_refs[0].shape[0]
    tp = lax.axis_index("tp")
    for k in range(n_tp):
        outs[k * width : (k + 1) * width, :] = out_refs[k][...]
        weights[k * width : (k + 1) * width, :] = w_refs[k][...]
    middle_out[...] = mm(outs[...], weights[...], TN)
    mixed_grad[...] = mm(down_ref[...], cot_ref[...], NT)

    def strip(i, carry):
        at = pl.ds(i * STRIP, STRIP)
        middle = middle_out[at, :] + x_ref[at, :].astype(F32)
        middle_out[at, :] = middle
        held, unused = normed(middle)
        unit[at, :] = held
        h_out[at, :] = (held * gain_ref[...]).astype(BF16)
        return carry

    lax.fori_loop(0, rows // STRIP, strip, 0)
    gate_up[...] = mm(in_ref[...], h_out[...], NT)

    def wave(i, carry):
        at = pl.ds(i * 32, 32)
        late = pl.ds(units + i * 32, 32)
        gate = gate_up[at, :]
        up = gate_up[late, :]
        back = mixed_grad[at, :]
        bell = 0.5 * (1.0 + lax.erf(gate * (2.0**-0.5)))
        active = gate * bell
        slope = bell + gate * jnp.exp(-0.5 * gate * gate) * ((2.0 * jnp.pi) ** -0.5)
        mixed_out[at, :] = (active * up).astype(BF16)
        gate_out[at, :] = (back * up * slope).astype(BF16)
        gate_out[late, :] = (back * active).astype(BF16)
        return carry

    lax.fori_loop(0, units // 32, wave, 0)
    grad[...] = mm(gate_out[...], in_ref[...], TN)

    def gains(i, carry):
        at = pl.ds(i * STRIP, STRIP)
        product = grad[at, :] * unit[at, :]
        return carry + jnp.sum(product.reshape(STRIP // 8, 8, -1), axis=0)

    gain_out[...] = lax.fori_loop(0, rows // STRIP, gains, jnp.zeros(gain_out.shape, F32))
    for k in range(n_tp):
        at = pl.ds(pl.multiple_of((tp ^ k) * part, part), part)
        part_refs[k][...] = grad[at, :].astype(part_refs[k].dtype)


def feed(tokens, cotangent, gain, in_t, w_down, outs, w_outs):
    rows, model = tokens.shape
    n_tp = len(outs)
    units = w_down.shape[0]
    part = rows // n_tp
    return pl.pallas_call(
        functools.partial(feed_kernel, n_tp),
        out_shape=(
            shaped((rows, model), F32),
            shaped((rows, model), BF16),
            shaped((units, rows), BF16),
            shaped((2 * units, rows), BF16),
            shaped((8, model), F32),
            shaped((part, model), F32),
        )
        + (shaped((part, model), BF16),) * (n_tp - 1),
        in_specs=[VMEM] * (5 + 2 * n_tp),
        out_specs=(VMEM,) * (5 + n_tp),
        scratch_shapes=[
            pltpu.VMEM((n_tp * outs[0].shape[0], rows), BF16),
            pltpu.VMEM((n_tp * outs[0].shape[0], model), BF16),
            pltpu.VMEM((rows, model), F32),
            pltpu.VMEM((2 * units, rows), F32),
            pltpu.VMEM((units, rows), F32),
            pltpu.VMEM((rows, model), F32),
        ],
        compiler_params=params(32),
    )(tokens, cotangent, gain, in_t, w_down, *outs, *w_outs)


def branch_kernel(n_tp, middle_ref, cot_ref, gain_ref, *refs):
    arrived = refs[:n_tp]
    w_refs = refs[n_tp : 2 * n_tp]
    grad_out, branch_out = refs[2 * n_tp : 2 * n_tp + 2]
    piece_refs = refs[2 * n_tp + 2 :]
    part = arrived[0].shape[0]
    tp = lax.axis_index("tp")
    at = pl.ds(pl.multiple_of(tp * part, part), part)
    total = arrived[0][...]
    for ref in arrived[1:]:
        total = total + ref[...].astype(F32)
    unit, scale = normed(middle_ref[at, :])
    value = cot_ref[at, :].astype(F32) + norm_back(unit, scale, total, gain_ref[...])
    grad_out[...] = value
    branch_out[...] = value.astype(BF16)
    for k in range(n_tp):
        piece_refs[k][...] = mm(branch_out[...], w_refs[k][...], NT).astype(BF16)


def branch(middle, cotangent, gain, arrived, w_outs):
    part, model = arrived[0].shape
    n_tp = len(arrived)
    width = w_outs[0].shape[0]
    return pl.pallas_call(
        functools.partial(branch_kernel, n_tp),
        out_shape=(shaped((part, model), F32), shaped((part, model), BF16))
        + (shaped((part, width), BF16),) * n_tp,
        in_specs=[VMEM] * (3 + 2 * n_tp),
        out_specs=(VMEM,) * (2 + n_tp),
        compiler_params=params(24),
    )(middle, cotangent, gain, *arrived, *w_outs)


def lay_kernel(n_tp, *refs):
    out_ref, held = refs[n_tp:]
    part = refs[0].shape[0]
    tp = lax.axis_index("tp")
    for k in range(n_tp):
        at = pl.ds(pl.multiple_of((tp ^ k) * part, part), part)
        held[at, :] = refs[k][...].astype(F32)
    out_ref[...] = held[...].T.astype(BF16)


def lay_turned(pieces):
    part, width = pieces[0].shape
    rows = part * len(pieces)
    return pl.pallas_call(
        functools.partial(lay_kernel, len(pieces)),
        out_shape=shaped((width, rows), BF16),
        in_specs=[VMEM] * len(pieces),
        out_specs=VMEM,
        scratch_shapes=[pltpu.VMEM((rows, width), F32)],
        compiler_params=params(16),
    )(*pieces)


def stack_kernel(n_tp, *refs):
    out_ref = refs[n_tp]
    part = refs[0].shape[0]
    tp = lax.axis_index("tp")
    for k in range(n_tp):
        at = pl.ds(pl.multiple_of((tp ^ k) * part, part), part)
        out_ref[at, :] = refs[k][...]


def stack_parts(pieces):
    part, model = pieces[0].shape
    return pl.pallas_call(
        functools.partial(stack_kernel, len(pieces)),
        out_shape=shaped((part * len(pieces), model), pieces[0].dtype),
        in_specs=[VMEM] * len(pieces),
        out_specs=VMEM,
        compiler_params=params(16),
    )(*pieces)


def turn_back(out_ref, first, value, cos_table, sin_table):
    for at in range(0, value.shape[0], HDIM):
        low = value[at : at + HALF]
        high = value[at + HALF : at + HDIM]
        spot = first + at
        out_ref[spot : spot + HALF, :] = (low * cos_table + high * sin_table).astype(BF16)
        out_ref[spot + HALF : spot + HDIM, :] = (high * cos_table - low * sin_table).astype(BF16)


def unproject_kernel(count, n_tp, x_ref, w_ref, cos_ref, sin_ref, dq_ref, dq_back, *refs):
    dkv_refs = refs[:count]
    proj_out = refs[count]
    part_refs = refs[count + 1 : count + 1 + n_tp]
    grad, dkv = refs[count + 1 + n_tp :]
    rows, model = x_ref.shape
    part = rows // n_tp
    width = dq_ref.shape[0]
    tp = lax.axis_index("tp")
    cos_table = cos_ref[...]
    sin_table = sin_ref[...]
    turn_back(proj_out, 0, dq_ref[...] + dq_back[...].astype(F32), cos_table, sin_table)
    total = dkv_refs[0][...]
    for ref in dkv_refs[1:]:
        total = total + ref[...].astype(F32)
    dkv[...] = total
    turn_back(proj_out, width, dkv[:width, :], cos_table, sin_table)
    proj_out[2 * width :, :] = dkv[width:, :].astype(BF16)
    grad[...] = mm(proj_out[...], w_ref[...], TN)

    def gains(i, carry):
        at = pl.ds(i * STRIP, STRIP)
        unit, unused = normed(x_ref[at, :].astype(F32))
        product = grad[at, :] * unit
        return carry + jnp.sum(product.reshape(STRIP // 8, 8, -1), axis=0)

    gain = lax.fori_loop(0, rows // STRIP, gains, jnp.zeros((8, model), F32))
    first = lax.broadcasted_iota(jnp.int32, (16, model), 0) == 0
    gain = jnp.where(first, jnp.sum(gain, axis=0, keepdims=True), 0.0)
    for k in range(n_tp):
        at = pl.ds(pl.multiple_of((tp ^ k) * part, part), part)
        part_refs[k][:part, :] = grad[at, :].astype(part_refs[k].dtype)
        part_refs[k][part:, :] = gain.astype(part_refs[k].dtype)


def unproject(n_tp, tokens, qkv_t, cos_table, sin_table, dq, dq_back, dkvs):
    rows, model = tokens.shape
    part = rows // n_tp
    count = len(dkvs)
    return pl.pallas_call(
        functools.partial(unproject_kernel, count, n_tp),
        out_shape=(shaped((qkv_t.shape[0], rows), BF16), shaped((part + 16, model), F32))
        + (shaped((part + 16, model), BF16),) * (n_tp - 1),
        in_specs=[VMEM] * (6 + count),
        out_specs=(VMEM,) * (1 + n_tp),
        scratch_shapes=[pltpu.VMEM((rows, model), F32), pltpu.VMEM(dkvs[0].shape, F32)],
        compiler_params=params(40),
    )(tokens, qkv_t, cos_table, sin_table, dq, dq_back, *dkvs)


def input_kernel(n_tp, x_ref, gain_ref, grad_ref, gain_two_ref, *refs):
    arrived = refs[:n_tp]
    out_ref, gain_out = refs[n_tp:]
    part, model = grad_ref.shape
    tp = lax.axis_index("tp")
    at = pl.ds(pl.multiple_of(tp * part, part), part)
    total = arrived[0][...]
    for ref in arrived[1:]:
        total = total + ref[...].astype(F32)
    unit, scale = normed(x_ref[at, :].astype(F32))
    value = grad_ref[...] + norm_back(unit, scale, total[:part], gain_ref[...])
    out_ref[...] = value.astype(BF16)
    line = lax.broadcasted_iota(jnp.int32, (8, model), 0)
    gain_two = jnp.sum(gain_two_ref[...], axis=0, keepdims=True)
    gain_out[...] = jnp.where(
        line == 0, total[part : part + 8], jnp.where(line == 1, gain_two, 0.0)
    )


def input_side(tokens, gain, middle_grad, gain_two_part, arrived):
    part, model = middle_grad.shape
    return pl.pallas_call(
        functools.partial(input_kernel, len(arrived)),
        out_shape=(shaped((part, model), BF16), shaped((8, model), F32)),
        in_specs=[VMEM] * (4 + len(arrived)),
        out_specs=(VMEM, VMEM),
        compiler_params=params(16),
    )(tokens, gain, middle_grad, gain_two_part, *arrived)


def sum_over_seq(value, n_seq, me):
    rows, columns = value.shape
    count = n_seq // 2
    half = columns // 2
    core = me % 2
    chip = me // 2
    low = value.astype(BF16)
    pick = lambda x, c: lax.dynamic_slice_in_dim(x, c * half, half, 1)
    mine = pick(value, core) + swap(pick(low, 1 - core), "seq", 1, n_seq).astype(F32)
    if rows % count:
        total = mine
        for k in range(1, count):
            total = total + swap(mine.astype(BF16), "seq", 2 * k, n_seq).astype(F32)
        held = total.astype(BF16)
    else:
        piece = rows // count
        parts = mine.reshape(count, piece, half)
        low = mine.astype(BF16).reshape(count, piece, half)
        total = lax.dynamic_index_in_dim(parts, chip, 0, keepdims=False)
        for k in range(1, count):
            sent = lax.dynamic_index_in_dim(low, chip ^ k, 0, keepdims=False)
            total = total + swap(sent, "seq", 2 * k, n_seq).astype(F32)
        total = total.astype(BF16)
        held = jnp.zeros((count, piece, half), BF16)
        for k in range(count):
            sent = swap(total, "seq", 2 * k, n_seq) if k else total
            held = lax.dynamic_update_slice_in_dim(held, sent[None], chip ^ k, 0)
        held = held.reshape(rows, half)
    other = swap(held, "seq", 1, n_seq)
    left = jnp.where(core == 0, held, other)
    right = jnp.where(core == 0, other, held)
    return jnp.concatenate([left, right], axis=1).astype(F32)


def body(
    n_seq,
    n_tp,
    tokens,
    gain_one,
    w_qkv,
    w_out,
    gain_two,
    w_in,
    w_down,
    cotangent,
    doc_lengths,
    roster,
):
    rows, model = tokens.shape
    width = w_qkv.shape[2]
    units = w_in.shape[2]
    count = n_seq // 2
    me = lax.axis_index("seq")
    qkv_t = w_qkv.transpose(1, 2, 0).reshape(3 * width, model)
    in_t = w_in.transpose(1, 2, 0).reshape(2 * units, model)
    gain_one = gain_one[None]
    gain_two = gain_two[None]
    over_tp = lambda x, k: swap(x, "tp", k, n_tp)
    over_chips = lambda x, k: swap(x, "seq", 2 * k, n_seq)
    over_cores = lambda x: swap(x, "seq", 1, n_seq)

    queries, kv, h_one, cos_table, sin_table = project(
        doc_lengths, roster, tokens, gain_one, qkv_t
    )
    blocks = [kv] + [over_chips(kv, j) for j in range(1, count)]
    q_pair = over_cores(queries)
    w_outs = [w_out] + [over_tp(w_out, k) for k in range(1, n_tp)]

    state_own, state_pair = attention_forward(doc_lengths, roster, queries, q_pair, blocks)
    out_b, totals = join(state_own, over_cores(state_pair))
    outs = [out_b] + [over_tp(out_b, k) for k in range(1, n_tp)]
    out_pair = over_cores(out_b)
    totals_pair = over_cores(totals)

    middle, h_two, mixed, gate_grad, gain_two_part, *parts = feed(
        tokens, cotangent, gain_two, in_t, w_down, outs, w_outs
    )
    arrived = [parts[0]] + [over_tp(parts[k], k) for k in range(1, n_tp)]
    middle_grad, branch_grad, *pieces = branch(middle, cotangent, gain_two, arrived, w_outs)
    out_grad = lay_turned([pieces[0]] + [over_tp(pieces[k], k) for k in range(1, n_tp)])
    grad_pair = over_cores(out_grad)

    grad_down = mm(mixed, cotangent, NN).astype(BF16)
    grad_in = mm(gate_grad, h_two, NN).astype(BF16)
    branch_full = stack_parts([branch_grad] + [over_tp(branch_grad, k) for k in range(1, n_tp)])
    grad_out = mm(out_b, branch_full, NN).astype(BF16)
    early = lax.psum((grad_down, grad_in, grad_out), "seq")

    dq_own, dq_pair, *dkvs = attention_backward(
        doc_lengths,
        roster,
        (queries, q_pair),
        (out_grad, grad_pair),
        (out_b, out_pair),
        (totals, totals_pair),
        blocks,
    )
    dkvs = [dkvs[0]] + [over_chips(dkvs[j], j) for j in range(1, count)]

    mixed_late, unused = lax.optimization_barrier((mixed, dq_pair))
    branch_two = mm(mixed_late, w_down, TN)
    tp = lax.axis_index("tp")
    part = rows // n_tp
    own = lambda x, k: lax.dynamic_slice_in_dim(x, (tp ^ k) * part, part, 0)
    total = own(middle, 0) + own(branch_two, 0)
    low = branch_two.astype(BF16)
    for k in range(1, n_tp):
        total = total + over_tp(own(low, k), k).astype(F32)
    total = total.astype(BF16)
    layer_out = stack_parts([total] + [over_tp(total, k) for k in range(1, n_tp)])

    proj_grad, *parts = unproject(
        n_tp, tokens, qkv_t, cos_table, sin_table, dq_own, over_cores(dq_pair), dkvs
    )
    arrived = [parts[0]] + [over_tp(parts[k], k) for k in range(1, n_tp)]
    input_part, gains = input_side(tokens, gain_one, middle_grad, gain_two_part, arrived)
    input_grad = stack_parts([input_part] + [over_tp(input_part, k) for k in range(1, n_tp)])
    grad_qkv = sum_over_seq(mm(proj_grad, h_one, NN), n_seq, me)
    chip_gains = gains + over_cores(gains)
    gains = chip_gains
    for k in range(1, count):
        gains = gains + over_chips(chip_gains, k)
    gain_two_sum = gains[1]
    for k in range(1, n_tp):
        gain_two_sum = gain_two_sum + over_tp(gains[1], k)

    back = lambda x, n: x.reshape(-1, n, model).transpose(2, 0, 1)
    return (
        layer_out,
        input_grad,
        gains[0],
        back(grad_qkv, width),
        early[2].astype(F32),
        gain_two_sum,
        back(early[1].astype(F32), units),
        early[0].astype(F32),
    )


def solution(mesh):
    placed = (
        P("seq", None),
        P(),
        P(None, None, "tp"),
        P("tp", None),
        P(),
        P(None, None, "tp"),
        P("tp", None),
        P("seq", None),
        P(),
        P(),
    )
    return jax.shard_map(
        functools.partial(body, mesh.shape["seq"], mesh.shape["tp"]),
        mesh=mesh,
        in_specs=placed,
        out_specs=(
            P("seq", None),
            P("seq", None),
            P(),
            P(None, None, "tp"),
            P("tp", None),
            P(),
            P(None, None, "tp"),
            P("tp", None),
        ),
        check_vma=False,
    )
```

```python
import functools

import jax
import jax.numpy as jnp
from jax import lax
from jax.experimental import pallas as pl
from jax.experimental.pallas import tpu as pltpu
from jax.sharding import PartitionSpec as P

HDIM = 64
HALF = HDIM // 2
EPSILON = 1e-05
ROPE_THETA = 160000.0
MASKED = -1e30
AUG = 80
STRIP = 64
F32 = jnp.float32
BF16 = jnp.bfloat16
ANY = pl.BlockSpec(memory_space=pl.ANY)
VMEM = pl.BlockSpec(memory_space=pltpu.VMEM)
SMEM = pl.BlockSpec(memory_space=pltpu.SMEM)

NN = (((1,), (0,)), ((), ()))
NT = (((1,), (1,)), ((), ()))
TN = (((0,), (0,)), ((), ()))


def params(mib):
    return pltpu.CompilerParams(vmem_limit_bytes=mib * 2**20)


def shaped(shape, dtype):
    return jax.ShapeDtypeStruct(shape, dtype)


def mm(a, b, dims):
    return lax.dot_general(a, b, dims, preferred_element_type=F32)


def waiting(kernel, given, ready):
    def inner(*refs):
        kernel(*refs[:given], *refs[given + len(ready) :])

    return inner


def swap(x, axis, hop, count):
    return lax.ppermute(x, axis, [(i, i ^ hop) for i in range(count)])


def doc_scratch(doc_lengths, roster):
    return [pltpu.SMEM(doc_lengths.shape, jnp.int32), pltpu.SMEM(roster.shape, jnp.int32)]


def fetch_docs(len_any, roster_any, len_ref, roster_ref, len_sem, roster_sem):
    one = pltpu.make_async_copy(len_any, len_ref, len_sem)
    two = pltpu.make_async_copy(roster_any, roster_ref, roster_sem)
    one.start()
    two.start()
    one.wait()
    two.wait()


def doc_bounds(len_ref):
    ends, total = [], jnp.int32(0)
    for d in range(len_ref.shape[0]):
        total = total + len_ref[d]
        ends.append(total)
    return ends


def doc_of(ends, position):
    found = jnp.int32(0)
    for end in ends:
        found = found + (end <= position).astype(jnp.int32)
    return found


def meet(ends, base_a, base_b, rows):
    low = jnp.maximum(doc_of(ends, base_a), doc_of(ends, base_b))
    high = jnp.minimum(doc_of(ends, base_a + rows - 1), doc_of(ends, base_b + rows - 1))
    return low <= high


def doc_rows(ends, base, rows):
    spot = base + lax.broadcasted_iota(jnp.int32, (16, rows), 1)
    line = lax.broadcasted_iota(jnp.int32, (16, rows), 0)
    held = jnp.zeros((16, rows), F32)
    start = jnp.int32(0)
    for d, end in enumerate(ends):
        inside = (line == d) & (spot >= start) & (spot < end)
        held = jnp.where(inside, 1.0, held)
        start = end
    return held


def ban_rows(ends, base, rows):
    line = lax.broadcasted_iota(jnp.int32, (16, rows), 0)
    held = doc_rows(ends, base, rows)
    return jnp.where((held > 0.5) | (line >= len(ends)), 0.0, MASKED)


def key_row(block, seq_index):
    return seq_index ^ (2 * block)


def place_row(ends, base, rows):
    spot = base + lax.broadcasted_iota(jnp.int32, (1, rows), 1)
    start = jnp.zeros((1, rows), jnp.int32)
    for end in ends:
        start = jnp.where(spot >= end, end, start)
    return (spot - start).astype(F32)


def normed(values):
    centre = jnp.mean(values, axis=-1, keepdims=True)
    shifted = values - centre
    spread = jnp.mean(shifted * shifted, axis=-1, keepdims=True)
    scale = lax.rsqrt(spread + EPSILON)
    return shifted * scale, scale


def norm_back(unit, scale, grad, gain):
    u = grad * gain
    mean_u = jnp.mean(u, axis=-1, keepdims=True)
    mean_un = jnp.mean(u * unit, axis=-1, keepdims=True)
    return scale * (u - mean_u - unit * mean_un)


def project_kernel(width, len_any, roster_any, x_any, w_any, gain_ref, freq_ref, *refs):
    q_out, kv_out, h_out, cos_out, sin_out = refs[:5]
    x_ref, w_ref, proj, len_ref, roster_ref, sems = refs[5:]
    rows = x_ref.shape[0]
    x_copy = pltpu.make_async_copy(x_any, x_ref, sems.at[0])
    w_copy = pltpu.make_async_copy(w_any, w_ref, sems.at[1])
    x_copy.start()
    w_copy.start()
    fetch_docs(len_any, roster_any, len_ref, roster_ref, sems.at[2], sems.at[3])
    ends = doc_bounds(len_ref)
    place = place_row(ends, roster_ref[lax.axis_index("seq")] * rows, rows)
    angles = place * freq_ref[...]
    cos_table = jnp.cos(angles)
    sin_table = jnp.sin(angles)
    cos_out[...] = cos_table
    sin_out[...] = sin_table
    x_copy.wait()

    def strip(i, carry):
        at = pl.ds(i * STRIP, STRIP)
        unit, unused = normed(x_ref[at, :].astype(F32))
        h_out[at, :] = (unit * gain_ref[...]).astype(BF16)
        return carry

    lax.fori_loop(0, rows // STRIP, strip, 0)
    w_copy.wait()
    proj[...] = mm(w_ref[...], h_out[...], NT)
    for at in range(0, 2 * width, HDIM):
        low = proj[at : at + HALF, :]
        high = proj[at + HALF : at + HDIM, :]
        turned_low = (low * cos_out[...] - high * sin_out[...]).astype(BF16)
        turned_high = (high * cos_out[...] + low * sin_out[...]).astype(BF16)
        if at < width:
            q_out[at : at + HALF, :] = (turned_low.astype(F32) * HDIM**-0.5).astype(BF16)
            q_out[at + HALF : at + HDIM, :] = (turned_high.astype(F32) * HDIM**-0.5).astype(BF16)
        else:
            kv_out[at - width : at - width + HALF, :] = turned_low
            kv_out[at - width + HALF : at - width + HDIM, :] = turned_high
    kv_out[width:, :] = proj[2 * width :, :].astype(BF16)


def project(doc_lengths, roster, tokens, gain, qkv_t):
    rows, model = tokens.shape
    width = qkv_t.shape[0] // 3
    freq = ROPE_THETA ** (-(jnp.arange(HALF).astype(F32) * (2.0 / HDIM)))
    table = shaped((HALF, rows), F32)
    return pl.pallas_call(
        functools.partial(project_kernel, width),
        out_shape=(
            shaped((width, rows), BF16),
            shaped((2 * width, rows), BF16),
            shaped((rows, model), BF16),
            table,
            table,
        ),
        in_specs=[ANY] * 4 + [VMEM] * 2,
        out_specs=(VMEM,) * 5,
        scratch_shapes=[
            pltpu.VMEM((rows, model), BF16),
            pltpu.VMEM(qkv_t.shape, BF16),
            pltpu.VMEM((3 * width, rows), F32),
        ]
        + doc_scratch(doc_lengths, roster)
        + [pltpu.SemaphoreType.DMA((4,))],
        name="project",
        compiler_params=params(24),
    )(doc_lengths, roster, tokens, qkv_t, gain, freq[:, None])


def forward_kernel(first, count, heads, last, len_any, roster_any, q_own, q_pair, *refs):
    kv_refs = refs[:count]
    refs = refs[count:]
    if first:
        state_in, refs = refs[0], refs[1:]
    outs = refs[: 2 if last else 1]
    kv, q_aug, state, len_ref, roster_ref, sems = refs[len(outs) :]
    rows = q_own.shape[1]
    width = heads * HDIM
    me = lax.axis_index("seq")
    copies = [pltpu.make_async_copy(kv_refs[j], kv.at[j], sems.at[j]) for j in range(count)]
    for copy in copies:
        copy.start()
    fetch_docs(len_any, roster_any, len_ref, roster_ref, sems.at[count], sems.at[count + 1])
    ends = doc_bounds(len_ref)
    bases = (roster_ref[me] * rows, roster_ref[me ^ 1] * rows)
    for g, q_ref in enumerate((q_own, q_pair)):
        mark = doc_rows(ends, bases[g], rows).astype(BF16)
        for h in range(heads):
            q_aug[g * heads + h, :HDIM, :] = q_ref[h * HDIM : (h + 1) * HDIM, :]
            q_aug[g * heads + h, HDIM:, :] = mark
    if first:
        state[...] = state_in[...]
    else:
        line = lax.broadcasted_iota(jnp.int32, (2 * heads, AUG, rows), 1)
        state[...] = jnp.where(line >= 72, MASKED, 0.0)
    for copy in copies:
        copy.wait()

    top = lax.broadcasted_iota(jnp.int32, (16, rows), 0) == 0
    ones = jnp.where(top, 1.0, 0.0).astype(BF16)

    def block(j, carry):
        key_base = roster_ref[key_row(j + first, me)] * rows
        ban = ban_rows(ends, key_base, rows).astype(BF16)
        for g in range(2):

            @pl.when(meet(ends, bases[g], key_base, rows))
            def _():
                for h in range(heads):
                    at = g * heads + h
                    keys = jnp.concatenate([kv[j, h * HDIM : (h + 1) * HDIM, :], ban], axis=0)
                    vals = jnp.concatenate(
                        [kv[j, width + h * HDIM : width + (h + 1) * HDIM, :], ones], axis=0
                    )
                    scores = mm(keys, q_aug[at], TN)
                    old = state[at, 72:73, :]
                    new = jnp.maximum(old, jnp.max(scores, axis=0, keepdims=True))
                    probs = jnp.exp(scores - new).astype(BF16)
                    part = mm(vals, probs, NN)
                    fade = jnp.exp(old - new)
                    state[at, :72, :] = state[at, :72, :] * fade + part[:72]
                    state[at, 72:, :] = jnp.broadcast_to(new, (8, rows))

        return carry

    lax.fori_loop(0, count, block, 0)
    if last:
        outs[0][...] = state[:heads]
        outs[1][...] = state[heads:]
    else:
        outs[0][...] = state[...]


def attention_forward(first, last, doc_lengths, roster, q_own, q_pair, blocks, state=None):
    width, rows = q_own.shape
    heads = width // HDIM
    count = len(blocks)
    half = shaped((heads, AUG, rows), F32)
    whole = shaped((2 * heads, AUG, rows), F32)
    given = () if state is None else (state,)
    return pl.pallas_call(
        functools.partial(forward_kernel, first, count, heads, last),
        out_shape=(half, half) if last else (whole,),
        in_specs=[ANY, ANY, VMEM, VMEM] + [ANY] * count + [VMEM] * len(given),
        out_specs=(VMEM, VMEM) if last else (VMEM,),
        scratch_shapes=[
            pltpu.VMEM((count, 2 * width, rows), BF16),
            pltpu.VMEM((2 * heads, AUG, rows), BF16),
            pltpu.VMEM((2 * heads, AUG, rows), F32),
        ]
        + doc_scratch(doc_lengths, roster)
        + [pltpu.SemaphoreType.DMA((count + 2,))],
        name="attention_forward",
        compiler_params=params(24 if count < 8 else 48),
    )(doc_lengths, roster, q_own, q_pair, *blocks, *given)


def backward_kernel(index, heads, more, last, len_any, roster_any, *refs):
    q_own, q_pair, g_own, g_pair, o_own, o_pair, t_own, t_pair, kv_ref = refs[:9]
    refs = refs[9:]
    if more:
        dq_in, refs = refs[0], refs[1:]
    outs = refs[: 3 if last else 2]
    kv, q_aug, delta, dq, dkv, len_ref, roster_ref, sems = refs[len(outs) :]
    rows = q_own.shape[1]
    width = heads * HDIM
    me = lax.axis_index("seq")
    copy = pltpu.make_async_copy(kv_ref, kv, sems.at[0])
    copy.start()
    fetch_docs(len_any, roster_any, len_ref, roster_ref, sems.at[1], sems.at[2])
    ends = doc_bounds(len_ref)
    bases = (roster_ref[me] * rows, roster_ref[me ^ 1] * rows)
    for g, (q_ref, g_ref, o_ref) in enumerate(((q_own, g_own, o_own), (q_pair, g_pair, o_pair))):
        mark = doc_rows(ends, bases[g], rows).astype(BF16)
        for h in range(heads):
            part = slice(h * HDIM, (h + 1) * HDIM)
            q_aug[g * heads + h, :HDIM, :] = q_ref[part, :]
            q_aug[g * heads + h, HDIM:, :] = mark
            product = g_ref[part, :].astype(F32) * o_ref[part, :].astype(F32)
            delta[g * heads + h] = jnp.broadcast_to(
                jnp.sum(product, axis=0, keepdims=True), (8, rows)
            )
    if more:
        dq[...] = dq_in[...]
    else:
        dq[...] = jnp.zeros_like(dq)
    dkv[...] = jnp.zeros_like(dkv)
    key_base = roster_ref[key_row(index, me)] * rows
    ban = ban_rows(ends, key_base, rows).astype(BF16)
    copy.wait()

    for g, (g_ref, t_ref) in enumerate(((g_own, t_own), (g_pair, t_pair))):

        @pl.when(meet(ends, bases[g], key_base, rows))
        def _():
            for h in range(heads):
                at = g * heads + h
                part = slice(h * HDIM, (h + 1) * HDIM)
                late = slice(width + h * HDIM, width + (h + 1) * HDIM)
                keys = kv[part, :]
                scores = mm(jnp.concatenate([keys, ban], axis=0), q_aug[at], TN)
                probs = jnp.exp(scores - t_ref[h, 0:1, :])
                prob_grads = mm(kv[late, :], g_ref[part, :], TN)
                score_grad = (probs * (prob_grads - delta[at, 0:1, :])).astype(BF16)
                dkv[late, :] += mm(g_ref[part, :], probs.astype(BF16), NT)
                dkv[part, :] += mm(q_aug[at, :HDIM, :], score_grad, NT)
                dq[at] += mm(keys, score_grad, NN)

    outs[0][...] = dkv[...].astype(outs[0].dtype)
    if last:
        for h in range(heads):
            part = slice(h * HDIM, (h + 1) * HDIM)
            outs[1][part, :] = dq[h] * HDIM**-0.5
            outs[2][part, :] = (dq[heads + h] * HDIM**-0.5).astype(BF16)
    else:
        outs[1][...] = dq[...]


def attention_backward(index, last, doc_lengths, roster, held, block, dq=None, ready=()):
    width, rows = held[0].shape
    heads = width // HDIM
    given = () if dq is None else (dq,)
    total = shaped((2 * heads, HDIM, rows), F32)
    if last:
        queries = (shaped((width, rows), F32), shaped((width, rows), BF16))
    else:
        queries = (total,)
    return pl.pallas_call(
        waiting(
            functools.partial(backward_kernel, index, heads, bool(given), last),
            11 + len(given),
            ready,
        ),
        out_shape=(shaped((2 * width, rows), BF16 if index else F32),) + queries,
        in_specs=[ANY, ANY] + [VMEM] * 8 + [ANY] + [VMEM] * len(given) + [ANY] * len(ready),
        out_specs=(VMEM,) * (1 + len(queries)),
        scratch_shapes=[
            pltpu.VMEM((2 * width, rows), BF16),
            pltpu.VMEM((2 * heads, AUG, rows), BF16),
            pltpu.VMEM((2 * heads, 8, rows), F32),
            pltpu.VMEM((2 * heads, HDIM, rows), F32),
            pltpu.VMEM((2 * width, rows), F32),
        ]
        + doc_scratch(doc_lengths, roster)
        + [pltpu.SemaphoreType.DMA((3,))],
        name="attention_backward",
        compiler_params=params(24),
    )(doc_lengths, roster, *held, block, *given, *ready)


def join_kernel(heads, own_ref, back_ref, out_ref, total_ref):
    rows = own_ref.shape[2]
    for h in range(heads):
        top_own = own_ref[h, 72:73, :]
        top_back = back_ref[h, 72:73, :]
        top = jnp.maximum(top_own, top_back)
        fade_own = jnp.exp(top_own - top)
        fade_back = jnp.exp(top_back - top)
        total = own_ref[h, 64:65, :] * fade_own + back_ref[h, 64:65, :] * fade_back
        share_own = fade_own / total
        share_back = fade_back / total
        value = own_ref[h, :HDIM, :] * share_own + back_ref[h, :HDIM, :] * share_back
        out_ref[h * HDIM : (h + 1) * HDIM, :] = value.astype(BF16)
        total_ref[h] = jnp.broadcast_to(top + jnp.log(total), (8, rows))


def join(own, back):
    heads, unused, rows = own.shape
    return pl.pallas_call(
        functools.partial(join_kernel, heads),
        out_shape=(shaped((heads * HDIM, rows), BF16), shaped((heads, 8, rows), F32)),
        in_specs=[VMEM, VMEM],
        out_specs=(VMEM, VMEM),
        name="join",
        compiler_params=params(16),
    )(own, back)


def feed_kernel(n_tp, x_ref, cot_ref, gain_ref, in_ref, down_ref, w_ref, *refs):
    out_refs = refs[:n_tp]
    middle_out, h_out, mixed_out, gate_out, gain_out = refs[n_tp : n_tp + 5]
    part_refs = refs[n_tp + 5 : 2 * n_tp + 5]
    outs, unit, gate_up, mixed_grad, grad = refs[2 * n_tp + 5 :]
    rows = x_ref.shape[0]
    part = rows // n_tp
    units = down_ref.shape[0]
    width = out_refs[0].shape[0]
    tp = lax.axis_index("tp")
    for k in range(n_tp):
        at = pl.ds(pl.multiple_of((tp ^ k) * width, width), width)
        outs[at, :] = out_refs[k][...]
    middle_out[...] = mm(outs[...], w_ref[...], TN)
    mixed_grad[...] = mm(down_ref[...], cot_ref[...], NT)

    def strip(i, carry):
        at = pl.ds(i * STRIP, STRIP)
        middle = middle_out[at, :] + x_ref[at, :].astype(F32)
        middle_out[at, :] = middle
        held, unused = normed(middle)
        unit[at, :] = held
        h_out[at, :] = (held * gain_ref[...]).astype(BF16)
        return carry

    lax.fori_loop(0, rows // STRIP, strip, 0)
    gate_up[...] = mm(in_ref[...], h_out[...], NT)

    def wave(i, carry):
        at = pl.ds(i * 32, 32)
        late = pl.ds(units + i * 32, 32)
        gate = gate_up[at, :]
        up = gate_up[late, :]
        back = mixed_grad[at, :]
        bell = 0.5 * (1.0 + lax.erf(gate * (2.0**-0.5)))
        active = gate * bell
        slope = bell + gate * jnp.exp(-0.5 * gate * gate) * ((2.0 * jnp.pi) ** -0.5)
        mixed_out[at, :] = (active * up).astype(BF16)
        gate_out[at, :] = (back * up * slope).astype(BF16)
        gate_out[late, :] = (back * active).astype(BF16)
        return carry

    lax.fori_loop(0, units // 32, wave, 0)
    grad[...] = mm(gate_out[...], in_ref[...], TN)

    def gains(i, carry):
        at = pl.ds(i * STRIP, STRIP)
        product = grad[at, :] * unit[at, :]
        return carry + jnp.sum(product.reshape(STRIP // 8, 8, -1), axis=0)

    gain_out[...] = lax.fori_loop(0, rows // STRIP, gains, jnp.zeros(gain_out.shape, F32))
    for k in range(n_tp):
        at = pl.ds(pl.multiple_of((tp ^ k) * part, part), part)
        part_refs[k][...] = grad[at, :].astype(part_refs[k].dtype)


def feed(tokens, cotangent, gain, in_t, w_down, w_full, outs):
    rows, model = tokens.shape
    n_tp = len(outs)
    units = w_down.shape[0]
    part = rows // n_tp
    return pl.pallas_call(
        functools.partial(feed_kernel, n_tp),
        out_shape=(
            shaped((rows, model), F32),
            shaped((rows, model), BF16),
            shaped((units, rows), BF16),
            shaped((2 * units, rows), BF16),
            shaped((8, model), F32),
            shaped((part, model), F32),
        )
        + (shaped((part, model), BF16),) * (n_tp - 1),
        in_specs=[VMEM] * (6 + n_tp),
        out_specs=(VMEM,) * (5 + n_tp),
        scratch_shapes=[
            pltpu.VMEM((n_tp * outs[0].shape[0], rows), BF16),
            pltpu.VMEM((rows, model), F32),
            pltpu.VMEM((2 * units, rows), F32),
            pltpu.VMEM((units, rows), F32),
            pltpu.VMEM((rows, model), F32),
        ],
        name="feed",
        compiler_params=params(32),
    )(tokens, cotangent, gain, in_t, w_down, w_full, *outs)


def branch_kernel(n_tp, middle_ref, cot_ref, gain_ref, w_ref, *refs):
    arrived = refs[:n_tp]
    grad_out, branch_out = refs[n_tp : n_tp + 2]
    piece_refs = refs[n_tp + 2 :]
    width = piece_refs[0].shape[1]
    part = arrived[0].shape[0]
    tp = lax.axis_index("tp")
    at = pl.ds(pl.multiple_of(tp * part, part), part)
    total = arrived[0][...]
    for ref in arrived[1:]:
        total = total + ref[...].astype(F32)
    unit, scale = normed(middle_ref[at, :])
    value = cot_ref[at, :].astype(F32) + norm_back(unit, scale, total, gain_ref[...])
    grad_out[...] = value
    branch_out[...] = value.astype(BF16)
    for k in range(n_tp):
        at = pl.ds(pl.multiple_of((tp ^ k) * width, width), width)
        piece_refs[k][...] = mm(branch_out[...], w_ref[at, :], NT).astype(BF16)


def branch(middle, cotangent, gain, w_full, arrived, ready):
    part, model = arrived[0].shape
    n_tp = len(arrived)
    width = w_full.shape[0] // n_tp
    return pl.pallas_call(
        waiting(functools.partial(branch_kernel, n_tp), 4 + n_tp, ready),
        out_shape=(shaped((part, model), F32), shaped((part, model), BF16))
        + (shaped((part, width), BF16),) * n_tp,
        in_specs=[VMEM] * (4 + n_tp) + [ANY] * len(ready),
        out_specs=(VMEM,) * (2 + n_tp),
        name="branch",
        compiler_params=params(24),
    )(middle, cotangent, gain, w_full, *arrived, *ready)


def lay_kernel(n_tp, *refs):
    out_ref, held = refs[n_tp:]
    part = refs[0].shape[0]
    tp = lax.axis_index("tp")
    for k in range(n_tp):
        at = pl.ds(pl.multiple_of((tp ^ k) * part, part), part)
        held[at, :] = refs[k][...].astype(F32)
    out_ref[...] = held[...].T.astype(BF16)


def lay_turned(pieces):
    part, width = pieces[0].shape
    rows = part * len(pieces)
    return pl.pallas_call(
        functools.partial(lay_kernel, len(pieces)),
        out_shape=shaped((width, rows), BF16),
        in_specs=[VMEM] * len(pieces),
        out_specs=VMEM,
        scratch_shapes=[pltpu.VMEM((rows, width), F32)],
        name="lay_turned",
        compiler_params=params(16),
    )(*pieces)


def stack_kernel(n_tp, *refs):
    out_ref = refs[n_tp]
    part = refs[0].shape[0]
    tp = lax.axis_index("tp")
    for k in range(n_tp):
        at = pl.ds(pl.multiple_of((tp ^ k) * part, part), part)
        out_ref[at, :] = refs[k][...]


def stack_parts(pieces):
    part, model = pieces[0].shape
    return pl.pallas_call(
        functools.partial(stack_kernel, len(pieces)),
        out_shape=shaped((part * len(pieces), model), pieces[0].dtype),
        in_specs=[VMEM] * len(pieces),
        out_specs=VMEM,
        name="stack_parts",
        compiler_params=params(16),
    )(*pieces)


def turn_back(out_ref, first, value, cos_table, sin_table):
    for at in range(0, value.shape[0], HDIM):
        low = value[at : at + HALF]
        high = value[at + HALF : at + HDIM]
        spot = first + at
        out_ref[spot : spot + HALF, :] = (low * cos_table + high * sin_table).astype(BF16)
        out_ref[spot + HALF : spot + HDIM, :] = (high * cos_table - low * sin_table).astype(BF16)


def unproject_kernel(count, n_tp, x_ref, w_ref, cos_ref, sin_ref, two_ref, dq_ref, dq_back, *refs):
    dkv_refs = refs[:count]
    proj_out = refs[count]
    part_refs = refs[count + 1 : count + 1 + n_tp]
    grad, dkv = refs[count + 1 + n_tp :]
    rows, model = x_ref.shape
    part = rows // n_tp
    width = dq_ref.shape[0]
    tp = lax.axis_index("tp")
    cos_table = cos_ref[...]
    sin_table = sin_ref[...]
    turn_back(proj_out, 0, dq_ref[...] + dq_back[...].astype(F32), cos_table, sin_table)
    total = dkv_refs[0][...]
    for ref in dkv_refs[1:]:
        total = total + ref[...].astype(F32)
    dkv[...] = total
    turn_back(proj_out, width, dkv[:width, :], cos_table, sin_table)
    proj_out[2 * width :, :] = dkv[width:, :].astype(BF16)
    grad[...] = mm(proj_out[...], w_ref[...], TN)

    def gains(i, carry):
        at = pl.ds(i * STRIP, STRIP)
        unit, unused = normed(x_ref[at, :].astype(F32))
        product = grad[at, :] * unit
        return carry + jnp.sum(product.reshape(STRIP // 8, 8, -1), axis=0)

    gain = lax.fori_loop(0, rows // STRIP, gains, jnp.zeros((8, model), F32))
    line = lax.broadcasted_iota(jnp.int32, (16, model), 0)
    gain_two = jnp.sum(two_ref[...], axis=0, keepdims=True)
    gain = jnp.sum(gain, axis=0, keepdims=True)
    gain = jnp.where(line == 0, gain, jnp.where(line == 1, gain_two, 0.0))
    for k in range(n_tp):
        at = pl.ds(pl.multiple_of((tp ^ k) * part, part), part)
        part_refs[k][:part, :] = grad[at, :].astype(part_refs[k].dtype)
        part_refs[k][part:, :] = gain.astype(part_refs[k].dtype)


def unproject(
    n_tp, tokens, qkv_t, cos_table, sin_table, gain_two_part, dq, dq_back, dkvs, ready
):
    rows, model = tokens.shape
    part = rows // n_tp
    count = len(dkvs)
    return pl.pallas_call(
        waiting(functools.partial(unproject_kernel, count, n_tp), 7 + count, ready),
        out_shape=(shaped((qkv_t.shape[0], rows), BF16), shaped((part + 16, model), F32))
        + (shaped((part + 16, model), BF16),) * (n_tp - 1),
        in_specs=[VMEM] * (7 + count) + [ANY] * len(ready),
        out_specs=(VMEM,) * (1 + n_tp),
        scratch_shapes=[pltpu.VMEM((rows, model), F32), pltpu.VMEM(dkvs[0].shape, F32)],
        name="unproject",
        compiler_params=params(40),
    )(tokens, qkv_t, cos_table, sin_table, gain_two_part, dq, dq_back, *dkvs, *ready)


def input_kernel(n_tp, x_ref, gain_ref, grad_ref, *refs):
    arrived = refs[:n_tp]
    out_ref, gain_out = refs[n_tp:]
    part, model = grad_ref.shape
    tp = lax.axis_index("tp")
    at = pl.ds(pl.multiple_of(tp * part, part), part)
    total = arrived[0][...]
    for ref in arrived[1:]:
        total = total + ref[...].astype(F32)
    unit, scale = normed(x_ref[at, :].astype(F32))
    value = grad_ref[...] + norm_back(unit, scale, total[:part], gain_ref[...])
    out_ref[...] = value.astype(BF16)
    gain_out[...] = total[part : part + 8]


def input_side(tokens, gain, middle_grad, arrived, ready):
    part, model = middle_grad.shape
    return pl.pallas_call(
        waiting(functools.partial(input_kernel, len(arrived)), 3 + len(arrived), ready),
        out_shape=(shaped((part, model), BF16), shaped((8, model), F32)),
        in_specs=[VMEM] * (3 + len(arrived)) + [ANY] * len(ready),
        out_specs=(VMEM, VMEM),
        name="input_side",
        compiler_params=params(16),
    )(tokens, gain, middle_grad, *arrived, *ready)


def early_kernel(mixed_ref, gate_ref, cot_ref, h_ref, out_ref):
    units = mixed_ref.shape[0]
    out_ref[:units, :] = mm(mixed_ref[...], cot_ref[...], NN)
    out_ref[units : 3 * units, :] = mm(gate_ref[...], h_ref[...], NN)
    out_ref[3 * units :, :] = jnp.zeros((out_ref.shape[0] - 3 * units, out_ref.shape[1]), F32)


def early_grads(mixed, gate_grad, cotangent, h_two):
    model = cotangent.shape[1]
    return pl.pallas_call(
        early_kernel,
        out_shape=shaped((4 * mixed.shape[0], model), F32),
        in_specs=[VMEM] * 4,
        out_specs=VMEM,
        name="early_grads",
        compiler_params=params(24),
    )(mixed, gate_grad, cotangent, h_two)


def widen_kernel(in_ref, *out_refs):
    at = 0
    for ref in out_refs:
        ref[...] = in_ref[at : at + ref.shape[0], :].astype(F32)
        at += ref.shape[0]


def widen(value, sizes):
    return pl.pallas_call(
        widen_kernel,
        out_shape=tuple(shaped((size, value.shape[1]), F32) for size in sizes),
        in_specs=[VMEM],
        out_specs=(VMEM,) * len(sizes),
        name="widen",
        compiler_params=params(24),
    )(value)


def late_kernel(n_tp, proj_ref, h_ref, out_ref, *refs):
    branch_refs = refs[:n_tp]
    keep_ref, send_ref, branch_full = refs[n_tp:]
    part = branch_refs[0].shape[0]
    half = keep_ref.shape[1]
    wide = proj_ref.shape[0]
    tp = lax.axis_index("tp")
    core = lax.axis_index("seq") % 2
    for k in range(n_tp):
        at = pl.ds(pl.multiple_of((tp ^ k) * part, part), part)
        branch_full[at, :] = branch_refs[k][...]
    for ref, side in ((send_ref, 1 - core), (keep_ref, core)):
        columns = pl.ds(pl.multiple_of(side * half, half), half)
        ref[:wide, :] = mm(proj_ref[...], h_ref[:, columns], NN).astype(ref.dtype)
        ref[wide:, :] = mm(out_ref[...], branch_full[:, columns], NN).astype(ref.dtype)


def late_grads(proj_grad, h_one, out_b, branches, ready):
    rows, model = h_one.shape
    wide = proj_grad.shape[0] + out_b.shape[0]
    return pl.pallas_call(
        waiting(functools.partial(late_kernel, len(branches)), 3 + len(branches), ready),
        out_shape=(shaped((wide, model // 2), F32), shaped((wide, model // 2), BF16)),
        in_specs=[VMEM] * (3 + len(branches)) + [ANY] * len(ready),
        out_specs=(VMEM, VMEM),
        scratch_shapes=[pltpu.VMEM((rows, model), BF16)],
        name="late_grads",
        compiler_params=params(24),
    )(proj_grad, h_one, out_b, *branches, *ready)


def spread_kernel(count, keep_ref, back_ref, *refs):
    held = refs[count]
    piece = refs[0].shape[0]
    chip = lax.axis_index("seq") // 2
    held[...] = keep_ref[...] + back_ref[...].astype(F32)
    for k in range(count):
        at = pl.ds(pl.multiple_of((chip ^ k) * piece, piece), piece)
        refs[k][...] = held[at, :].astype(refs[k].dtype)


def spread(count, keep, back):
    wide, half = keep.shape
    piece = wide // count
    return pl.pallas_call(
        functools.partial(spread_kernel, count),
        out_shape=(shaped((piece, half), F32),) + (shaped((piece, half), BF16),) * (count - 1),
        in_specs=[VMEM, VMEM],
        out_specs=(VMEM,) * count,
        scratch_shapes=[pltpu.VMEM((wide, half), F32)],
        name="spread",
        compiler_params=params(16),
    )(keep, back)


def piece_kernel(count, gain_ref, *refs):
    out_ref = refs[count]
    half = out_ref.shape[1]
    total = refs[0][...]
    for ref in refs[1:count]:
        total = total + ref[...].astype(F32)
    line = lax.broadcasted_iota(jnp.int32, (16, half), 0)
    gains = jnp.zeros((16, half), F32)
    for at in range(4):
        row = gain_ref[at // 2 : at // 2 + 1, at % 2 * half : (at % 2 + 1) * half]
        gains = jnp.where(line == at, row, gains)
    out_ref[...] = jnp.concatenate([total, gains], axis=0).astype(BF16)


def sum_piece(gains, pieces, ready):
    piece, half = pieces[0].shape
    return pl.pallas_call(
        waiting(functools.partial(piece_kernel, len(pieces)), 1 + len(pieces), ready),
        out_shape=shaped((piece + 16, half), BF16),
        in_specs=[VMEM] * (1 + len(pieces)) + [ANY] * len(ready),
        out_specs=VMEM,
        name="sum_piece",
        compiler_params=params(16),
    )(gains, *pieces, *ready)


def collect_kernel(count, *refs):
    out_ref, held = refs[count:]
    piece = refs[0].shape[0] - 16
    wide = count * piece
    chip = lax.axis_index("seq") // 2
    gains = jnp.zeros((16, out_ref.shape[1]), F32)
    for k in range(count):
        at = pl.ds(pl.multiple_of((chip ^ k) * piece, piece), piece)
        whole = refs[k][...].astype(F32)
        held[at, :] = whole[:piece]
        gains = gains + whole[piece:]
    held[wide:, :] = gains
    out_ref[...] = held[...].astype(BF16)


def collect(pieces, ready=()):
    piece, half = pieces[0].shape
    wide = (piece - 16) * len(pieces) + 16
    return pl.pallas_call(
        waiting(functools.partial(collect_kernel, len(pieces)), len(pieces), ready),
        out_shape=shaped((wide, half), BF16),
        in_specs=[VMEM] * len(pieces) + [ANY] * len(ready),
        out_specs=VMEM,
        scratch_shapes=[pltpu.VMEM((wide, half), F32)],
        name="collect",
        compiler_params=params(16),
    )(*pieces, *ready)


def finish_kernel(own_ref, pair_ref, qkv_ref, out_ref, one_ref, two_ref):
    half = own_ref.shape[1]
    wide, tall = qkv_ref.shape[0], out_ref.shape[0]
    core = lax.axis_index("seq") % 2
    for ref, side in ((own_ref, core), (pair_ref, 1 - core)):
        columns = pl.ds(pl.multiple_of(side * half, half), half)
        qkv_ref[:, columns] = ref[:wide, :].astype(F32)
        out_ref[:, columns] = ref[wide : wide + tall, :].astype(F32)
    gains = own_ref[wide + tall :, :].astype(F32) + pair_ref[wide + tall :, :].astype(F32)
    for at, ref in ((0, one_ref), (2, two_ref)):
        ref[:, :half] = gains[at : at + 1]
        ref[:, half:] = gains[at + 1 : at + 2]


def finish(own, pair, wide):
    half = own.shape[1]
    tall = own.shape[0] - 16 - wide
    model = 2 * half
    return pl.pallas_call(
        finish_kernel,
        out_shape=(
            shaped((wide, model), F32),
            shaped((tall, model), F32),
            shaped((1, model), F32),
            shaped((1, model), F32),
        ),
        in_specs=[VMEM, VMEM],
        out_specs=(VMEM,) * 4,
        name="finish",
        compiler_params=params(16),
    )(own, pair)


def down_kernel(n_tp, mixed_ref, w_ref, middle_ref, keep_ref, send_ref, total):
    part = keep_ref.shape[0] * 2 // n_tp
    tp = lax.axis_index("tp")
    total[...] = mm(mixed_ref[...], w_ref[...], TN)
    for k in range(n_tp):
        at = pl.ds(pl.multiple_of((tp ^ k) * part, part), part)
        spot = k // 2 * part
        if k % 2:
            send_ref[spot : spot + part, :] = total[at, :].astype(BF16)
        else:
            value = total[at, :] + middle_ref[at, :] if k == 0 else total[at, :]
            keep_ref[spot : spot + part, :] = value


def down(n_tp, mixed, w_down, middle, ready):
    rows, model = middle.shape
    return pl.pallas_call(
        waiting(functools.partial(down_kernel, n_tp), 3, ready),
        out_shape=(shaped((rows // 2, model), F32), shaped((rows // 2, model), BF16)),
        in_specs=[VMEM] * 3 + [ANY] * len(ready),
        out_specs=(VMEM, VMEM),
        scratch_shapes=[pltpu.VMEM((rows, model), F32)],
        name="down",
        compiler_params=params(16),
    )(mixed, w_down, middle, *ready)


def pair_kernel(keep_ref, back_ref, own_ref, *send_refs):
    part = own_ref.shape[0]
    own_ref[...] = keep_ref[:part, :] + back_ref[:part, :].astype(F32)
    for k, ref in enumerate(send_refs):
        at = (k + 1) * part
        total = keep_ref[at : at + part, :] + back_ref[at : at + part, :].astype(F32)
        ref[...] = total.astype(BF16)


def pair_sum(n_tp, keep, back):
    part = keep.shape[0] * 2 // n_tp
    model = keep.shape[1]
    return pl.pallas_call(
        pair_kernel,
        out_shape=(shaped((part, model), F32),)
        + (shaped((part, model), BF16),) * (n_tp // 2 - 1),
        in_specs=[VMEM, VMEM],
        out_specs=(VMEM,) * (n_tp // 2),
        name="pair_sum",
        compiler_params=params(16),
    )(keep, back)


def total_kernel(count, *refs):
    total = refs[0][...]
    for ref in refs[1:count]:
        total = total + ref[...].astype(F32)
    refs[count][...] = total.astype(refs[count].dtype)


def total_of(parts, dtype=BF16):
    return pl.pallas_call(
        functools.partial(total_kernel, len(parts)),
        out_shape=shaped(parts[0].shape, dtype),
        in_specs=[VMEM] * len(parts),
        out_specs=VMEM,
        name="total_of",
        compiler_params=params(16),
    )(*parts)


def body(
    n_seq,
    n_tp,
    tokens,
    gain_one,
    w_qkv,
    w_out,
    gain_two,
    w_in,
    w_down,
    cotangent,
    doc_lengths,
    roster,
):
    rows, model = tokens.shape
    width = w_qkv.shape[2]
    units = w_in.shape[2]
    count = n_seq // 2
    qkv_t = w_qkv.transpose(1, 2, 0).reshape(3 * width, model)
    in_t = w_in.transpose(1, 2, 0).reshape(2 * units, model)
    gain_one = gain_one[None]
    gain_two = gain_two[None]
    over_tp = lambda x, k: swap(x, "tp", k, n_tp)
    over_chips = lambda x, k: swap(x, "seq", 2 * k, n_seq)
    over_cores = lambda x: swap(x, "seq", 1, n_seq)
    everywhere = lambda xs: [xs[0]] + [over_tp(xs[k], k) for k in range(1, n_tp)]

    def by_steps(part):
        parts = {0: part}
        hop = n_tp // 2
        while hop:
            parts.update({k ^ hop: over_tp(x, hop) for k, x in parts.items()})
            hop //= 2
        return [parts[k] for k in range(n_tp)]

    docs = (doc_lengths, roster)

    queries, kv, h_one, cos_table, sin_table = project(*docs, tokens, gain_one, qkv_t)
    blocks = [kv] + [over_chips(kv, j) for j in range(1, count)]
    q_pair = over_cores(queries)
    w_full = lax.all_gather(w_out, "tp", axis=0, tiled=True)

    (state,) = attention_forward(0, False, *docs, queries, q_pair, blocks[:-1])
    state_own, state_pair = attention_forward(
        count - 1, True, *docs, queries, q_pair, blocks[-1:], state
    )
    out_b, totals = join(state_own, over_cores(state_pair))
    outs = everywhere([out_b] * n_tp)
    out_pair = over_cores(out_b)
    totals_pair = over_cores(totals)

    middle, h_two, mixed, gate_grad, gain_two_part, *parts = feed(
        tokens, cotangent, gain_two, in_t, w_down, w_full, outs
    )
    early = early_grads(mixed, gate_grad, cotangent, h_two)
    keep, send = down(n_tp, mixed, w_down, middle, (early,))
    middle_grad, branch_grad, *pieces = branch(
        middle, cotangent, gain_two, w_full, everywhere(parts), (keep,)
    )
    early = lax.psum(early, "seq")
    out_grad = lay_turned(everywhere(pieces))
    grad_pair = over_cores(out_grad)
    branches = by_steps(branch_grad)

    own, *others = pair_sum(n_tp, keep, over_tp(send, 1))
    total = total_of([own] + [over_tp(others[k], 2 * k + 2) for k in range(n_tp // 2 - 1)])
    totals_all = by_steps(total)

    held = (queries, q_pair, out_grad, grad_pair, out_b, out_pair, totals, totals_pair)
    dkvs = [None] * count
    dq = None
    for j in range(count - 1, 0, -1):
        ready = (own,) if dq is None else ()
        terms, dq = attention_backward(j, False, *docs, held, blocks[j], dq, ready)
        dkvs[j] = over_chips(terms, j)
    dkv, dq_own, dq_pair = attention_backward(0, True, *docs, held, blocks[0], dq, (total,))
    for j in range(count - 1, 1, -1):
        dkv = total_of([dkv, dkvs[j]], F32)

    proj_grad, *parts = unproject(
        n_tp,
        tokens,
        qkv_t,
        cos_table,
        sin_table,
        gain_two_part,
        dq_own,
        over_cores(dq_pair),
        [dkv, dkvs[1]],
        branches[1:],
    )
    arrived = everywhere(parts)
    input_part, gains = input_side(tokens, gain_one, middle_grad, arrived, ())
    inputs_all = everywhere([input_part] * n_tp)

    keep, send = late_grads(proj_grad, h_one, out_b, branches, ())
    own, *others = spread(count, keep, over_cores(send))
    arrived = [own] + [over_chips(others[k - 1], k) for k in range(1, count)]
    grad_down, grad_in = widen(early, (units, 2 * units))
    layer_out = stack_parts(totals_all)
    piece = sum_piece(gains, arrived, (layer_out, grad_down))
    input_grad = stack_parts(inputs_all)
    collected = collect([piece] + [over_chips(piece, k) for k in range(1, count)], (input_grad,))
    grad_qkv, grad_out, grad_one, grad_two = finish(collected, over_cores(collected), 3 * width)

    back = lambda x, n: x.reshape(-1, n, model).transpose(2, 0, 1)
    return (
        layer_out,
        input_grad,
        grad_one[0],
        back(grad_qkv, width),
        grad_out,
        grad_two[0],
        back(grad_in, units),
        grad_down,
    )


def solution(mesh):
    placed = (
        P("seq", None),
        P(),
        P(None, None, "tp"),
        P("tp", None),
        P(),
        P(None, None, "tp"),
        P("tp", None),
        P("seq", None),
        P(),
        P(),
    )
    return jax.shard_map(
        functools.partial(body, mesh.shape["seq"], mesh.shape["tp"]),
        mesh=mesh,
        in_specs=placed,
        out_specs=(
            P("seq", None),
            P("seq", None),
            P(),
            P(None, None, "tp"),
            P("tp", None),
            P(),
            P(None, None, "tp"),
            P("tp", None),
        ),
        check_vma=False,
    )
```

```python
import functools

import jax
import jax.numpy as jnp
from jax import lax
from jax.experimental import pallas as pl
from jax.experimental.pallas import tpu as pltpu
from jax.sharding import PartitionSpec as P

HDIM = 64
HALF = HDIM // 2
EPSILON = 1e-05
ROPE_THETA = 160000.0
MASKED = -1e30
AUG = 80
STRIP = 64
F32 = jnp.float32
BF16 = jnp.bfloat16
HBM = pl.BlockSpec(memory_space=pltpu.HBM)
VMEM = pl.BlockSpec(memory_space=pltpu.VMEM)

NN = (((1,), (0,)), ((), ()))
NT = (((1,), (1,)), ((), ()))
TN = (((0,), (0,)), ((), ()))


def params(mib):
    return pltpu.CompilerParams(vmem_limit_bytes=mib * 2**20)


def mm(a, b, dims):
    return lax.dot_general(a, b, dims, preferred_element_type=F32)


def shaped(shape, dtype):
    return jax.ShapeDtypeStruct(shape, dtype)


def kinds(arrays, kind):
    return [(array, kind) for array in arrays]


def pin(array, kind):
    return array if kind in ("v", "free") else pltpu.with_memory_space_constraint(array, pltpu.HBM)


def call(name, kernel, ins, outs, scratch=(), mib=16, after=()):
    fetched = [i for i, given in enumerate(ins) if given[1] not in ("v", "raw", "free")]
    left = [i for i, out in enumerate(outs) if out[2] == "h"]

    def held(array, kind):
        rows = array.shape[0] if kind == "h" else kind
        return pltpu.VMEM((rows,) + array.shape[1:], array.dtype)

    def run(*refs):
        in_refs = list(refs[: len(ins)])
        at = len(ins) + len(after)
        out_refs = list(refs[at : at + len(outs)])
        at += len(outs)
        own = refs[at : at + len(scratch)]
        at += len(scratch)
        buffers = refs[at : at + len(fetched) + len(left)]
        sems = refs[-1]
        copies = []
        for n, i in enumerate(fetched):
            source = in_refs[i]
            if ins[i][1] != "h":
                rows = ins[i][1]
                at = pl.multiple_of(lax.axis_index("tp") * rows, rows)
                source = source.at[pl.ds(at, rows)]
            copies.append(pltpu.make_async_copy(source, buffers[n], sems.at[n]))
            in_refs[i] = buffers[n]
        for copy in copies:
            copy.start()
        for copy in copies:
            copy.wait()
        copies = []
        for n, i in enumerate(left):
            spot = len(fetched) + n
            copies.append(pltpu.make_async_copy(buffers[spot], out_refs[i], sems.at[spot]))
            out_refs[i] = buffers[spot]
        kernel(*in_refs, *out_refs, *own)
        for copy in copies:
            copy.start()
        for copy in copies:
            copy.wait()

    spec = lambda kind: VMEM if kind == "v" else HBM
    count = len(fetched) + len(left)
    return pl.pallas_call(
        run,
        out_shape=tuple(
            shaped(shape, dtype) if kind == "v" else pltpu.HBM(shape, dtype)
            for shape, dtype, kind in outs
        ),
        in_specs=[spec(kind) for unused, kind in ins] + [spec(kind) for unused, kind in after],
        out_specs=tuple(spec(kind) for unused, unused, kind in outs),
        scratch_shapes=list(scratch)
        + [held(*ins[i]) for i in fetched]
        + [pltpu.VMEM(outs[i][0], outs[i][1]) for i in left]
        + [pltpu.SemaphoreType.DMA((max(count, 1),))],
        name=name,
        compiler_params=params(mib),
    )(*[pin(*given) for given in ins], *[pin(*given) for given in after])


def swap(x, axis, hop, count):
    return lax.ppermute(x, axis, [(i, i ^ hop) for i in range(count)])


def doc_scratch(doc_lengths, roster):
    return [pltpu.SMEM(doc_lengths.shape, jnp.int32), pltpu.SMEM(roster.shape, jnp.int32)]


def fetch_docs(len_any, roster_any, len_ref, roster_ref, len_sem, roster_sem):
    one = pltpu.make_async_copy(len_any, len_ref, len_sem)
    two = pltpu.make_async_copy(roster_any, roster_ref, roster_sem)
    one.start()
    two.start()
    one.wait()
    two.wait()


def doc_bounds(len_ref):
    ends, total = [], jnp.int32(0)
    for d in range(len_ref.shape[0]):
        total = total + len_ref[d]
        ends.append(total)
    return ends


def doc_of(ends, position):
    found = jnp.int32(0)
    for end in ends:
        found = found + (end <= position).astype(jnp.int32)
    return found


def meet(ends, base_a, base_b, rows):
    low = jnp.maximum(doc_of(ends, base_a), doc_of(ends, base_b))
    high = jnp.minimum(doc_of(ends, base_a + rows - 1), doc_of(ends, base_b + rows - 1))
    return low <= high


def doc_rows(ends, base, rows):
    spot = base + lax.broadcasted_iota(jnp.int32, (16, rows), 1)
    line = lax.broadcasted_iota(jnp.int32, (16, rows), 0)
    held = jnp.zeros((16, rows), F32)
    start = jnp.int32(0)
    for d, end in enumerate(ends):
        inside = (line == d) & (spot >= start) & (spot < end)
        held = jnp.where(inside, 1.0, held)
        start = end
    return held


def ban_rows(ends, base, rows):
    line = lax.broadcasted_iota(jnp.int32, (16, rows), 0)
    held = doc_rows(ends, base, rows)
    return jnp.where((held > 0.5) | (line >= len(ends)), 0.0, MASKED)


def key_row(block, seq_index):
    return seq_index ^ (2 * block)


def place_row(ends, base, rows):
    spot = base + lax.broadcasted_iota(jnp.int32, (1, rows), 1)
    start = jnp.zeros((1, rows), jnp.int32)
    for end in ends:
        start = jnp.where(spot >= end, end, start)
    return (spot - start).astype(F32)


def normed(values):
    centre = jnp.mean(values, axis=-1, keepdims=True)
    shifted = values - centre
    spread = jnp.mean(shifted * shifted, axis=-1, keepdims=True)
    scale = lax.rsqrt(spread + EPSILON)
    return shifted * scale, scale


def norm_back(unit, scale, grad, gain):
    u = grad * gain
    mean_u = jnp.mean(u, axis=-1, keepdims=True)
    mean_un = jnp.mean(u * unit, axis=-1, keepdims=True)
    return scale * (u - mean_u - unit * mean_un)


def project_kernel(width, len_any, roster_any, x_any, w_any, gain_ref, freq_ref, *refs):
    q_out, kv_out, h_out, cos_out, sin_out = refs[:5]
    x_ref, w_ref, proj, len_ref, roster_ref, sems = refs[5:]
    rows = x_ref.shape[0]
    x_copy = pltpu.make_async_copy(x_any, x_ref, sems.at[0])
    w_copy = pltpu.make_async_copy(w_any, w_ref, sems.at[1])
    x_copy.start()
    w_copy.start()
    fetch_docs(len_any, roster_any, len_ref, roster_ref, sems.at[2], sems.at[3])
    ends = doc_bounds(len_ref)
    place = place_row(ends, roster_ref[lax.axis_index("seq")] * rows, rows)
    angles = place * freq_ref[...]
    cos_table = jnp.cos(angles)
    sin_table = jnp.sin(angles)
    cos_out[...] = cos_table
    sin_out[...] = sin_table
    x_copy.wait()

    def strip(i, carry):
        at = pl.ds(i * STRIP, STRIP)
        unit, unused = normed(x_ref[at, :].astype(F32))
        h_out[at, :] = (unit * gain_ref[...]).astype(BF16)
        return carry

    lax.fori_loop(0, rows // STRIP, strip, 0)
    w_copy.wait()
    proj[...] = mm(w_ref[...], h_out[...], NT)
    for at in range(0, 2 * width, HDIM):
        low = proj[at : at + HALF, :]
        high = proj[at + HALF : at + HDIM, :]
        turned_low = (low * cos_out[...] - high * sin_out[...]).astype(BF16)
        turned_high = (high * cos_out[...] + low * sin_out[...]).astype(BF16)
        if at < width:
            q_out[at : at + HALF, :] = (turned_low.astype(F32) * HDIM**-0.5).astype(BF16)
            q_out[at + HALF : at + HDIM, :] = (turned_high.astype(F32) * HDIM**-0.5).astype(BF16)
        else:
            kv_out[at - width : at - width + HALF, :] = turned_low
            kv_out[at - width + HALF : at - width + HDIM, :] = turned_high
    kv_out[width:, :] = proj[2 * width :, :].astype(BF16)


def project(doc_lengths, roster, tokens, gain, qkv_t):
    rows, model = tokens.shape
    width = qkv_t.shape[0] // 3
    freq = ROPE_THETA ** (-(jnp.arange(HALF).astype(F32) * (2.0 / HDIM)))
    return call(
        "project",
        functools.partial(project_kernel, width),
        [(x, "raw") for x in (doc_lengths, roster, tokens, qkv_t)]
        + [(gain, "h"), (freq[:, None], "h")],
        [
            ((width, rows), BF16, "v"),
            ((2 * width, rows), BF16, "v"),
            ((rows, model), BF16, "h"),
            ((HALF, rows), F32, "h"),
            ((HALF, rows), F32, "h"),
        ],
        [
            pltpu.VMEM((rows, model), BF16),
            pltpu.VMEM(qkv_t.shape, BF16),
            pltpu.VMEM((3 * width, rows), F32),
        ]
        + doc_scratch(doc_lengths, roster)
        + [pltpu.SemaphoreType.DMA((4,))],
    )


def forward_kernel(first, count, heads, last, len_any, roster_any, q_own, q_pair, *refs):
    kv_refs = refs[:count]
    refs = refs[count:]
    if first:
        state_in, refs = refs[0], refs[1:]
    outs = refs[: 2 if last else 1]
    kv, q_aug, state, len_ref, roster_ref, sems = refs[len(outs) :]
    rows = q_own.shape[1]
    width = heads * HDIM
    me = lax.axis_index("seq")
    copies = [pltpu.make_async_copy(kv_refs[j], kv.at[j], sems.at[j]) for j in range(count)]
    for copy in copies:
        copy.start()
    fetch_docs(len_any, roster_any, len_ref, roster_ref, sems.at[count], sems.at[count + 1])
    ends = doc_bounds(len_ref)
    bases = (roster_ref[me] * rows, roster_ref[me ^ 1] * rows)
    for g, q_ref in enumerate((q_own, q_pair)):
        mark = doc_rows(ends, bases[g], rows).astype(BF16)
        for h in range(heads):
            q_aug[g * heads + h, :HDIM, :] = q_ref[h * HDIM : (h + 1) * HDIM, :]
            q_aug[g * heads + h, HDIM:, :] = mark
    if first:
        state[...] = state_in[...]
    else:
        line = lax.broadcasted_iota(jnp.int32, (2 * heads, AUG, rows), 1)
        state[...] = jnp.where(line >= 72, MASKED, 0.0)
    for copy in copies:
        copy.wait()

    top = lax.broadcasted_iota(jnp.int32, (16, rows), 0) == 0
    ones = jnp.where(top, 1.0, 0.0).astype(BF16)

    def block(j, carry):
        key_base = roster_ref[key_row(j + first, me)] * rows
        ban = ban_rows(ends, key_base, rows).astype(BF16)
        for g in range(2):

            @pl.when(meet(ends, bases[g], key_base, rows))
            def _():
                for h in range(heads):
                    at = g * heads + h
                    keys = jnp.concatenate([kv[j, h * HDIM : (h + 1) * HDIM, :], ban], axis=0)
                    vals = jnp.concatenate(
                        [kv[j, width + h * HDIM : width + (h + 1) * HDIM, :], ones], axis=0
                    )
                    scores = mm(keys, q_aug[at], TN)
                    old = state[at, 72:73, :]
                    new = jnp.maximum(old, jnp.max(scores, axis=0, keepdims=True))
                    probs = jnp.exp(scores - new).astype(BF16)
                    part = mm(vals, probs, NN)
                    fade = jnp.exp(old - new)
                    state[at, :72, :] = state[at, :72, :] * fade + part[:72]
                    state[at, 72:, :] = jnp.broadcast_to(new, (8, rows))

        return carry

    lax.fori_loop(0, count, block, 0)
    if last:
        outs[0][...] = state[:heads]
        outs[1][...] = state[heads:]
    else:
        outs[0][...] = state[...]


def attention_forward(first, last, doc_lengths, roster, q_own, q_pair, blocks, state=None):
    width, rows = q_own.shape
    heads = width // HDIM
    count = len(blocks)
    half = ((heads, AUG, rows), F32, "v")
    whole = ((2 * heads, AUG, rows), F32, "v")
    given = [] if state is None else [(state, "v")]
    return call(
        "attention_forward",
        functools.partial(forward_kernel, first, count, heads, last),
        [(doc_lengths, "raw"), (roster, "raw"), (q_own, "v"), (q_pair, "v")]
        + kinds(blocks, "free")
        + given,
        [half, half] if last else [whole],
        [
            pltpu.VMEM((count, 2 * width, rows), BF16),
            pltpu.VMEM((2 * heads, AUG, rows), BF16),
            pltpu.VMEM((2 * heads, AUG, rows), F32),
        ]
        + doc_scratch(doc_lengths, roster)
        + [pltpu.SemaphoreType.DMA((count + 2,))],
        16 if count < 8 else 40,
    )


def backward_kernel(index, heads, more, last, len_any, roster_any, *refs):
    q_own, q_pair, g_own, g_pair, o_own, o_pair, t_own, t_pair, kv_ref = refs[:9]
    refs = refs[9:]
    if more:
        dq_in, refs = refs[0], refs[1:]
    outs = refs[: 3 if last else 2]
    kv, q_aug, delta, dq, dkv, len_ref, roster_ref, sems = refs[len(outs) :]
    rows = q_own.shape[1]
    width = heads * HDIM
    me = lax.axis_index("seq")
    copy = pltpu.make_async_copy(kv_ref, kv, sems.at[0])
    copy.start()
    fetch_docs(len_any, roster_any, len_ref, roster_ref, sems.at[1], sems.at[2])
    ends = doc_bounds(len_ref)
    bases = (roster_ref[me] * rows, roster_ref[me ^ 1] * rows)
    for g, (q_ref, g_ref, o_ref) in enumerate(((q_own, g_own, o_own), (q_pair, g_pair, o_pair))):
        mark = doc_rows(ends, bases[g], rows).astype(BF16)
        for h in range(heads):
            part = slice(h * HDIM, (h + 1) * HDIM)
            q_aug[g * heads + h, :HDIM, :] = q_ref[part, :]
            q_aug[g * heads + h, HDIM:, :] = mark
            product = g_ref[part, :].astype(F32) * o_ref[part, :].astype(F32)
            delta[g * heads + h] = jnp.broadcast_to(
                jnp.sum(product, axis=0, keepdims=True), (8, rows)
            )
    if more:
        dq[...] = dq_in[...]
    else:
        dq[...] = jnp.zeros_like(dq)
    dkv[...] = jnp.zeros_like(dkv)
    key_base = roster_ref[key_row(index, me)] * rows
    ban = ban_rows(ends, key_base, rows).astype(BF16)
    copy.wait()

    for g, (g_ref, t_ref) in enumerate(((g_own, t_own), (g_pair, t_pair))):

        @pl.when(meet(ends, bases[g], key_base, rows))
        def _():
            for h in range(heads):
                at = g * heads + h
                part = slice(h * HDIM, (h + 1) * HDIM)
                late = slice(width + h * HDIM, width + (h + 1) * HDIM)
                keys = kv[part, :]
                scores = mm(jnp.concatenate([keys, ban], axis=0), q_aug[at], TN)
                probs = jnp.exp(scores - t_ref[h, 0:1, :])
                prob_grads = mm(kv[late, :], g_ref[part, :], TN)
                score_grad = (probs * (prob_grads - delta[at, 0:1, :])).astype(BF16)
                dkv[late, :] += mm(g_ref[part, :], probs.astype(BF16), NT)
                dkv[part, :] += mm(q_aug[at, :HDIM, :], score_grad, NT)
                dq[at] += mm(keys, score_grad, NN)

    outs[0][...] = dkv[...].astype(outs[0].dtype)
    if last:
        for h in range(heads):
            part = slice(h * HDIM, (h + 1) * HDIM)
            outs[1][part, :] = dq[h] * HDIM**-0.5
            outs[2][part, :] = (dq[heads + h] * HDIM**-0.5).astype(BF16)
    else:
        outs[1][...] = dq[...]


def attention_backward(index, last, doc_lengths, roster, held, block, dq=None, after=()):
    width, rows = held[0].shape
    heads = width // HDIM
    given = [] if dq is None else [(dq, "v")]
    if last:
        queries = [((width, rows), F32, "v"), ((width, rows), BF16, "v")]
    else:
        queries = [((2 * heads, HDIM, rows), F32, "v")]
    return call(
        "attention_backward",
        functools.partial(backward_kernel, index, heads, bool(given), last),
        [(doc_lengths, "raw"), (roster, "raw")] + kinds(held, "v") + [(block, "free")] + given,
        [((2 * width, rows), BF16 if index else F32, "v")] + queries,
        [
            pltpu.VMEM((2 * width, rows), BF16),
            pltpu.VMEM((2 * heads, AUG, rows), BF16),
            pltpu.VMEM((2 * heads, 8, rows), F32),
            pltpu.VMEM((2 * heads, HDIM, rows), F32),
            pltpu.VMEM((2 * width, rows), F32),
        ]
        + doc_scratch(doc_lengths, roster)
        + [pltpu.SemaphoreType.DMA((3,))],
        16,
        after,
    )


def join_kernel(heads, own_ref, back_ref, out_ref, total_ref):
    rows = own_ref.shape[2]
    for h in range(heads):
        top_own = own_ref[h, 72:73, :]
        top_back = back_ref[h, 72:73, :]
        top = jnp.maximum(top_own, top_back)
        fade_own = jnp.exp(top_own - top)
        fade_back = jnp.exp(top_back - top)
        total = own_ref[h, 64:65, :] * fade_own + back_ref[h, 64:65, :] * fade_back
        share_own = fade_own / total
        share_back = fade_back / total
        value = own_ref[h, :HDIM, :] * share_own + back_ref[h, :HDIM, :] * share_back
        out_ref[h * HDIM : (h + 1) * HDIM, :] = value.astype(BF16)
        total_ref[h] = jnp.broadcast_to(top + jnp.log(total), (8, rows))


def join(own, back):
    heads, unused, rows = own.shape
    return call(
        "join",
        functools.partial(join_kernel, heads),
        [(own, "v"), (back, "v")],
        [((heads * HDIM, rows), BF16, "v"), ((heads, 8, rows), F32, "v")],
    )


def feed_kernel(n_tp, x_ref, cot_ref, gain_ref, in_ref, down_ref, w_ref, *refs):
    out_refs = refs[:n_tp]
    middle_out, h_out, mixed_out, gate_out, gain_out = refs[n_tp : n_tp + 5]
    part_refs = refs[n_tp + 5 : 2 * n_tp + 5]
    outs, unit, gate_up, mixed_grad, grad = refs[2 * n_tp + 5 :]
    rows = x_ref.shape[0]
    part = rows // n_tp
    units = down_ref.shape[0]
    width = out_refs[0].shape[0]
    tp = lax.axis_index("tp")
    for k in range(n_tp):
        at = pl.ds(pl.multiple_of((tp ^ k) * width, width), width)
        outs[at, :] = out_refs[k][...]
    middle_out[...] = mm(outs[...], w_ref[...], TN)
    mixed_grad[...] = mm(down_ref[...], cot_ref[...], NT)

    def strip(i, carry):
        at = pl.ds(i * STRIP, STRIP)
        middle = middle_out[at, :] + x_ref[at, :].astype(F32)
        middle_out[at, :] = middle
        held, unused = normed(middle)
        unit[at, :] = held
        h_out[at, :] = (held * gain_ref[...]).astype(BF16)
        return carry

    lax.fori_loop(0, rows // STRIP, strip, 0)
    gate_up[...] = mm(in_ref[...], h_out[...], NT)

    def wave(i, carry):
        at = pl.ds(i * 32, 32)
        late = pl.ds(units + i * 32, 32)
        gate = gate_up[at, :]
        up = gate_up[late, :]
        back = mixed_grad[at, :]
        bell = 0.5 * (1.0 + lax.erf(gate * (2.0**-0.5)))
        active = gate * bell
        slope = bell + gate * jnp.exp(-0.5 * gate * gate) * ((2.0 * jnp.pi) ** -0.5)
        mixed_out[at, :] = (active * up).astype(BF16)
        gate_out[at, :] = (back * up * slope).astype(BF16)
        gate_out[late, :] = (back * active).astype(BF16)
        return carry

    lax.fori_loop(0, units // 32, wave, 0)
    grad[...] = mm(gate_out[...], in_ref[...], TN)

    def gains(i, carry):
        at = pl.ds(i * STRIP, STRIP)
        product = grad[at, :] * unit[at, :]
        return carry + jnp.sum(product.reshape(STRIP // 8, 8, -1), axis=0)

    gain_out[...] = lax.fori_loop(0, rows // STRIP, gains, jnp.zeros(gain_out.shape, F32))
    for k in range(n_tp):
        at = pl.ds(pl.multiple_of((tp ^ k) * part, part), part)
        part_refs[k][...] = grad[at, :].astype(part_refs[k].dtype)


def feed(tokens, cotangent, gain, in_t, w_down, w_full, outs):
    rows, model = tokens.shape
    n_tp = len(outs)
    units = w_down.shape[0]
    part = rows // n_tp
    return call(
        "feed",
        functools.partial(feed_kernel, n_tp),
        kinds((tokens, cotangent, gain, in_t, w_down, w_full), "h") + kinds(outs, "v"),
        [
            ((rows, model), F32, "h"),
            ((rows, model), BF16, "h"),
            ((units, rows), BF16, "h"),
            ((2 * units, rows), BF16, "h"),
            ((8, model), F32, "h"),
            ((part, model), F32, "h"),
        ]
        + [((part, model), BF16, "h")] * (n_tp - 1),
        [
            pltpu.VMEM((n_tp * outs[0].shape[0], rows), BF16),
            pltpu.VMEM((rows, model), F32),
            pltpu.VMEM((2 * units, rows), F32),
            pltpu.VMEM((units, rows), F32),
            pltpu.VMEM((rows, model), F32),
        ],
        32,
    )


def branch_kernel(n_tp, middle_ref, cot_ref, gain_ref, w_ref, *refs):
    arrived = refs[:n_tp]
    grad_out, branch_out = refs[n_tp : n_tp + 2]
    piece_refs = refs[n_tp + 2 :]
    width = piece_refs[0].shape[1]
    tp = lax.axis_index("tp")
    total = arrived[0][...]
    for ref in arrived[1:]:
        total = total + ref[...].astype(F32)
    unit, scale = normed(middle_ref[...])
    value = cot_ref[...].astype(F32) + norm_back(unit, scale, total, gain_ref[...])
    grad_out[...] = value
    branch_out[...] = value.astype(BF16)
    for k in range(n_tp):
        at = pl.ds(pl.multiple_of((tp ^ k) * width, width), width)
        piece_refs[k][...] = mm(branch_out[...], w_ref[at, :], NT).astype(BF16)


def branch(middle, cotangent, gain, w_full, arrived, after):
    part, model = arrived[0].shape
    n_tp = len(arrived)
    width = w_full.shape[0] // n_tp
    return call(
        "branch",
        functools.partial(branch_kernel, n_tp),
        [(middle, part), (cotangent, part)] + kinds((gain, w_full, arrived[0]), "h") + kinds(arrived[1:], "v"),
        [((part, model), F32, "h"), ((part, model), BF16, "h")]
        + [((part, width), BF16, "v")] * n_tp,
        (),
        16,
        after,
    )


def lay_kernel(n_tp, *refs):
    out_ref, held = refs[n_tp:]
    part = refs[0].shape[0]
    tp = lax.axis_index("tp")
    for k in range(n_tp):
        at = pl.ds(pl.multiple_of((tp ^ k) * part, part), part)
        held[at, :] = refs[k][...].astype(F32)
    out_ref[...] = held[...].T.astype(BF16)


def lay_turned(pieces):
    part, width = pieces[0].shape
    rows = part * len(pieces)
    (out,) = call(
        "lay_turned",
        functools.partial(lay_kernel, len(pieces)),
        kinds(pieces, "v"),
        [((width, rows), BF16, "v")],
        [pltpu.VMEM((rows, width), F32)],
    )
    return out


def stack_kernel(n_tp, *refs):
    out_ref = refs[n_tp]
    part = refs[0].shape[0]
    tp = lax.axis_index("tp")
    for k in range(n_tp):
        at = pl.ds(pl.multiple_of((tp ^ k) * part, part), part)
        out_ref[at, :] = refs[k][...]


def stack_parts(pieces, after=()):
    part, model = pieces[0].shape
    (out,) = call(
        "stack_parts",
        functools.partial(stack_kernel, len(pieces)),
        kinds(pieces, "v"),
        [((part * len(pieces), model), pieces[0].dtype, "h")],
        (),
        16,
        after,
    )
    return out


def turn_back(out_ref, first, value, cos_table, sin_table):
    for at in range(0, value.shape[0], HDIM):
        low = value[at : at + HALF]
        high = value[at + HALF : at + HDIM]
        spot = first + at
        out_ref[spot : spot + HALF, :] = (low * cos_table + high * sin_table).astype(BF16)
        out_ref[spot + HALF : spot + HDIM, :] = (high * cos_table - low * sin_table).astype(BF16)


def unproject_kernel(count, n_tp, x_ref, w_ref, cos_ref, sin_ref, two_ref, dq_ref, dq_back, *refs):
    dkv_refs = refs[:count]
    proj_out = refs[count]
    part_refs = refs[count + 1 : count + 1 + n_tp]
    grad, dkv = refs[count + 1 + n_tp :]
    rows, model = x_ref.shape
    part = rows // n_tp
    width = dq_ref.shape[0]
    tp = lax.axis_index("tp")
    cos_table = cos_ref[...]
    sin_table = sin_ref[...]
    turn_back(proj_out, 0, dq_ref[...] + dq_back[...].astype(F32), cos_table, sin_table)
    total = dkv_refs[0][...]
    for ref in dkv_refs[1:]:
        total = total + ref[...].astype(F32)
    dkv[...] = total
    turn_back(proj_out, width, dkv[:width, :], cos_table, sin_table)
    proj_out[2 * width :, :] = dkv[width:, :].astype(BF16)
    grad[...] = mm(proj_out[...], w_ref[...], TN)

    def gains(i, carry):
        at = pl.ds(i * STRIP, STRIP)
        unit, unused = normed(x_ref[at, :].astype(F32))
        product = grad[at, :] * unit
        return carry + jnp.sum(product.reshape(STRIP // 8, 8, -1), axis=0)

    gain = lax.fori_loop(0, rows // STRIP, gains, jnp.zeros((8, model), F32))
    line = lax.broadcasted_iota(jnp.int32, (16, model), 0)
    gain_two = jnp.sum(two_ref[...], axis=0, keepdims=True)
    gain = jnp.sum(gain, axis=0, keepdims=True)
    gain = jnp.where(line == 0, gain, jnp.where(line == 1, gain_two, 0.0))
    for k in range(n_tp):
        at = pl.ds(pl.multiple_of((tp ^ k) * part, part), part)
        part_refs[k][:part, :] = grad[at, :].astype(part_refs[k].dtype)
        part_refs[k][part:, :] = gain.astype(part_refs[k].dtype)


def unproject(n_tp, tokens, qkv_t, cos_table, sin_table, gain_two_part, dq, dq_back, dkvs, after):
    rows, model = tokens.shape
    part = rows // n_tp
    return call(
        "unproject",
        functools.partial(unproject_kernel, len(dkvs), n_tp),
        kinds((tokens, qkv_t, cos_table, sin_table, gain_two_part), "h")
        + kinds((dq, dq_back, *dkvs), "v"),
        [((qkv_t.shape[0], rows), BF16, "v"), ((part + 16, model), F32, "v")]
        + [((part + 16, model), BF16, "v")] * (n_tp - 1),
        [pltpu.VMEM((rows, model), F32), pltpu.VMEM(dkvs[0].shape, F32)],
        16,
        after,
    )


def input_kernel(n_tp, x_ref, gain_ref, grad_ref, *refs):
    arrived = refs[:n_tp]
    out_ref, gain_out = refs[n_tp:]
    part, model = grad_ref.shape
    total = arrived[0][...]
    for ref in arrived[1:]:
        total = total + ref[...].astype(F32)
    unit, scale = normed(x_ref[...].astype(F32))
    value = grad_ref[...] + norm_back(unit, scale, total[:part], gain_ref[...])
    out_ref[...] = value.astype(BF16)
    gain_out[...] = total[part : part + 8]


def input_side(tokens, gain, middle_grad, arrived, after):
    part, model = middle_grad.shape
    return call(
        "input_side",
        functools.partial(input_kernel, len(arrived)),
        [(tokens, part), (gain, "h"), (middle_grad, "h")] + kinds(arrived, "v"),
        [((part, model), BF16, "v"), ((8, model), F32, "v")],
        (),
        16,
        after,
    )


def early_kernel(mixed_ref, gate_ref, cot_ref, h_ref, out_ref):
    units = mixed_ref.shape[0]
    out_ref[:units, :] = mm(mixed_ref[...], cot_ref[...], NN)
    out_ref[units : 3 * units, :] = mm(gate_ref[...], h_ref[...], NN)
    if out_ref.shape[0] > 3 * units:
        out_ref[3 * units :, :] = jnp.zeros((out_ref.shape[0] - 3 * units, out_ref.shape[1]), F32)


def early_grads(mixed, gate_grad, cotangent, h_two):
    model = cotangent.shape[1]
    (out,) = call(
        "early_grads",
        early_kernel,
        kinds((mixed, gate_grad, cotangent, h_two), "h"),
        [((4 * mixed.shape[0], model), F32, "h")],
    )
    return out


def part_kernel(in_ref, *refs):
    out_refs, sems = refs[:-1], refs[-1]
    copies = []
    at = 0
    for n, ref in enumerate(out_refs):
        source = in_ref.at[pl.ds(at, ref.shape[0])]
        copies.append(pltpu.make_async_copy(source, ref, sems.at[n]))
        at += ref.shape[0]
    for copy in copies:
        copy.start()
    for copy in copies:
        copy.wait()


def parted(value, sizes):
    return pl.pallas_call(
        part_kernel,
        out_shape=tuple(shaped((size, value.shape[1]), value.dtype) for size in sizes),
        in_specs=[HBM],
        out_specs=(HBM,) * len(sizes),
        scratch_shapes=[pltpu.SemaphoreType.DMA((len(sizes),))],
        name="parted",
    )(pin(value, "h"))


def late_kernel(n_tp, proj_ref, h_ref, out_ref, *refs):
    branch_refs = refs[:n_tp]
    keep_ref, send_ref, branch_full = refs[n_tp:]
    part = branch_refs[0].shape[0]
    half = keep_ref.shape[1]
    wide = proj_ref.shape[0]
    tp = lax.axis_index("tp")
    core = lax.axis_index("seq") % 2
    for k in range(n_tp):
        at = pl.ds(pl.multiple_of((tp ^ k) * part, part), part)
        branch_full[at, :] = branch_refs[k][...]
    for ref, side in ((send_ref, 1 - core), (keep_ref, core)):
        columns = pl.ds(pl.multiple_of(side * half, half), half)
        ref[:wide, :] = mm(proj_ref[...], h_ref[:, columns], NN).astype(ref.dtype)
        ref[wide:, :] = mm(out_ref[...], branch_full[:, columns], NN).astype(ref.dtype)


def late_grads(proj_grad, h_one, out_b, branches):
    rows, model = h_one.shape
    wide = proj_grad.shape[0] + out_b.shape[0]
    return call(
        "late_grads",
        functools.partial(late_kernel, len(branches)),
        [(proj_grad, "v"), (h_one, "h"), (out_b, "v"), (branches[0], "h")]
        + kinds(branches[1:], "v"),
        [((wide, model // 2), F32, "v"), ((wide, model // 2), BF16, "v")],
        [pltpu.VMEM((rows, model), BF16)],
    )


def spread_kernel(count, keep_ref, back_ref, *refs):
    held = refs[count]
    piece = refs[0].shape[0]
    chip = lax.axis_index("seq") // 2
    held[...] = keep_ref[...] + back_ref[...].astype(F32)
    for k in range(count):
        at = pl.ds(pl.multiple_of((chip ^ k) * piece, piece), piece)
        refs[k][...] = held[at, :].astype(refs[k].dtype)


def spread(count, keep, back):
    wide, half = keep.shape
    piece = wide // count
    return call(
        "spread",
        functools.partial(spread_kernel, count),
        [(keep, "v"), (back, "v")],
        [((piece, half), F32, "v")] + [((piece, half), BF16, "v")] * (count - 1),
        [pltpu.VMEM((wide, half), F32)],
    )


def piece_kernel(count, gain_ref, *refs):
    out_ref = refs[count]
    half = out_ref.shape[1]
    total = refs[0][...]
    for ref in refs[1:count]:
        total = total + ref[...].astype(F32)
    line = lax.broadcasted_iota(jnp.int32, (16, half), 0)
    gains = jnp.zeros((16, half), F32)
    for at in range(4):
        row = gain_ref[at // 2 : at // 2 + 1, at % 2 * half : (at % 2 + 1) * half]
        gains = jnp.where(line == at, row, gains)
    out_ref[...] = jnp.concatenate([total, gains], axis=0).astype(BF16)


def sum_piece(gains, pieces, after=()):
    piece, half = pieces[0].shape
    (out,) = call(
        "sum_piece",
        functools.partial(piece_kernel, len(pieces)),
        [(gains, "v")] + kinds(pieces, "v"),
        [((piece + 16, half), BF16, "v")],
        (),
        16,
        after,
    )
    return out


def collect_kernel(count, *refs):
    out_ref, held = refs[count:]
    piece = refs[0].shape[0] - 16
    wide = count * piece
    chip = lax.axis_index("seq") // 2
    gains = jnp.zeros((16, out_ref.shape[1]), F32)
    for k in range(count):
        at = pl.ds(pl.multiple_of((chip ^ k) * piece, piece), piece)
        whole = refs[k][...].astype(F32)
        held[at, :] = whole[:piece]
        gains = gains + whole[piece:]
    held[wide:, :] = gains
    out_ref[...] = held[...].astype(BF16)


def collect(pieces, after=()):
    piece, half = pieces[0].shape
    wide = (piece - 16) * len(pieces) + 16
    (out,) = call(
        "collect",
        functools.partial(collect_kernel, len(pieces)),
        kinds(pieces, "v"),
        [((wide, half), BF16, "v")],
        [pltpu.VMEM((wide, half), F32)],
        16,
        after,
    )
    return out


def finish_kernel(own_ref, pair_ref, qkv_ref, out_ref, one_ref, two_ref):
    half = own_ref.shape[1]
    wide, tall = qkv_ref.shape[0], out_ref.shape[0]
    core = lax.axis_index("seq") % 2
    for ref, side in ((own_ref, core), (pair_ref, 1 - core)):
        columns = pl.ds(pl.multiple_of(side * half, half), half)
        qkv_ref[:, columns] = ref[:wide, :].astype(F32)
        out_ref[:, columns] = ref[wide : wide + tall, :].astype(F32)
    gains = own_ref[wide + tall :, :].astype(F32) + pair_ref[wide + tall :, :].astype(F32)
    for at, ref in ((0, one_ref), (2, two_ref)):
        ref[:, :half] = gains[at : at + 1]
        ref[:, half:] = gains[at + 1 : at + 2]


def finish(own, pair, wide, after=()):
    half = own.shape[1]
    tall = own.shape[0] - 16 - wide
    model = 2 * half
    return call(
        "finish",
        finish_kernel,
        [(own, "v"), (pair, "v")],
        [
            ((wide, model), F32, "h"),
            ((tall, model), F32, "h"),
            ((1, model), F32, "h"),
            ((1, model), F32, "h"),
        ],
        (),
        16,
        after,
    )


def down_kernel(n_tp, mixed_ref, w_ref, middle_ref, keep_ref, send_ref, total):
    part = keep_ref.shape[0] * 2 // n_tp
    tp = lax.axis_index("tp")
    total[...] = mm(mixed_ref[...], w_ref[...], TN)
    for k in range(n_tp):
        at = pl.ds(pl.multiple_of((tp ^ k) * part, part), part)
        spot = k // 2 * part
        if k % 2:
            send_ref[spot : spot + part, :] = total[at, :].astype(BF16)
        else:
            value = total[at, :] + middle_ref[at, :] if k == 0 else total[at, :]
            keep_ref[spot : spot + part, :] = value


def down(n_tp, mixed, w_down, middle, after):
    rows, model = middle.shape
    return call(
        "down",
        functools.partial(down_kernel, n_tp),
        kinds((mixed, w_down, middle), "h"),
        [((rows // 2, model), F32, "h"), ((rows // 2, model), BF16, "h")],
        [pltpu.VMEM((rows, model), F32)],
        16,
        after,
    )


def pair_kernel(keep_ref, back_ref, own_ref, *send_refs):
    part = own_ref.shape[0]
    own_ref[...] = keep_ref[:part, :] + back_ref[:part, :].astype(F32)
    for k, ref in enumerate(send_refs):
        at = (k + 1) * part
        total = keep_ref[at : at + part, :] + back_ref[at : at + part, :].astype(F32)
        ref[...] = total.astype(BF16)


def pair_sum(n_tp, keep, back, after=()):
    part = keep.shape[0] * 2 // n_tp
    model = keep.shape[1]
    return call(
        "pair_sum",
        pair_kernel,
        [(keep, "h"), (back, "v")],
        [((part, model), F32, "v")] + [((part, model), BF16, "v")] * (n_tp // 2 - 1),
        (),
        16,
        after,
    )


def total_kernel(count, *refs):
    total = refs[0][...]
    for ref in refs[1:count]:
        total = total + ref[...].astype(F32)
    refs[count][...] = total.astype(refs[count].dtype)


def total_of(parts, dtype=BF16, kind="v", after=()):
    (out,) = call(
        "total_of",
        functools.partial(total_kernel, len(parts)),
        kinds(parts, kind),
        [(parts[0].shape, dtype, kind)],
        (),
        16,
        after,
    )
    return out


def body(
    n_seq,
    n_tp,
    tokens,
    gain_one,
    w_qkv,
    w_out,
    gain_two,
    w_in,
    w_down,
    cotangent,
    doc_lengths,
    roster,
):
    rows, model = tokens.shape
    width = w_qkv.shape[2]
    units = w_in.shape[2]
    count = n_seq // 2
    qkv_t = w_qkv.transpose(1, 2, 0).reshape(3 * width, model)
    in_t = w_in.transpose(1, 2, 0).reshape(2 * units, model)
    gain_one = gain_one[None]
    gain_two = gain_two[None]
    over_tp = lambda x, k: swap(x, "tp", k, n_tp)
    over_chips = lambda x, k: swap(x, "seq", 2 * k, n_seq)
    over_cores = lambda x: swap(x, "seq", 1, n_seq)
    everywhere = lambda xs: [xs[0]] + [over_tp(xs[k], k) for k in range(1, n_tp)]

    def by_steps(part):
        parts = {0: part}
        hop = n_tp // 2
        while hop:
            parts.update({k ^ hop: over_tp(x, hop) for k, x in parts.items()})
            hop //= 2
        return [parts[k] for k in range(n_tp)]

    docs = (doc_lengths, roster)

    queries, kv, h_one, cos_table, sin_table = project(*docs, tokens, gain_one, qkv_t)
    blocks = [kv] + [over_chips(kv, j) for j in range(1, count)]
    q_pair = over_cores(queries)
    w_full = lax.all_gather(w_out, "tp", axis=0, tiled=True)

    split = (count + 1) // 2
    (state,) = attention_forward(0, False, *docs, queries, q_pair, blocks[:split])
    state_own, state_pair = attention_forward(
        split, True, *docs, queries, q_pair, blocks[split:], state
    )
    out_b, totals = join(state_own, over_cores(state_pair))
    outs = everywhere([out_b] * n_tp)
    out_pair = over_cores(out_b)
    totals_pair = over_cores(totals)

    middle, h_two, mixed, gate_grad, gain_two_part, *parts = feed(
        tokens, cotangent, gain_two, in_t, w_down, w_full, outs
    )
    early = early_grads(mixed, gate_grad, cotangent, h_two)
    keep, send = down(n_tp, mixed, w_down, middle, [(early, "h")])
    middle_grad, branch_grad, *pieces = branch(
        middle, cotangent, gain_two, w_full, everywhere(parts), [(keep, "h")]
    )
    early = lax.psum(early, "seq")
    grad_down, grad_in = parted(early, (units, 2 * units))
    out_grad = lay_turned(everywhere(pieces))
    grad_pair = over_cores(out_grad)
    branches = by_steps(branch_grad)

    own, *others = pair_sum(n_tp, keep, over_tp(send, 1), [(out_grad, "v")])
    total = total_of(
        [own] + [over_tp(others[k], 2 * k + 2) for k in range(n_tp // 2 - 1)], BF16
    )
    totals_all = by_steps(total)

    held = (queries, q_pair, out_grad, grad_pair, out_b, out_pair, totals, totals_pair)
    dkvs = [None] * count
    dq = None
    after = [(own, "v")]
    for j in range(count - 1, 0, -1):
        terms, dq = attention_backward(j, False, *docs, held, blocks[j], dq, after)
        after = ()
        dkvs[j] = over_chips(terms, j)
    dkv, dq_own, dq_pair = attention_backward(0, True, *docs, held, blocks[0], dq)
    for j in range(count - 1, 1, -1):
        dkv = total_of([dkv, dkvs[j]], F32)

    proj_grad, *parts = unproject(
        n_tp,
        tokens,
        qkv_t,
        cos_table,
        sin_table,
        gain_two_part,
        dq_own,
        over_cores(dq_pair),
        [dkv, dkvs[1]],
        kinds([*branches[1:], totals_all[n_tp // 2]], "v"),
    )
    keep, send = late_grads(proj_grad, h_one, out_b, branches)
    own, *others = spread(count, keep, over_cores(send))
    chip_sum = total_of([own] + [over_chips(others[k - 1], k) for k in range(1, count)], F32)
    input_part, gains = input_side(
        tokens, gain_one, middle_grad, everywhere(parts), [(own, "v")]
    )
    inputs_all = everywhere([input_part] * n_tp)
    piece = sum_piece(gains, [chip_sum], ())
    input_grad = stack_parts(inputs_all)
    collected = collect(
        [piece] + [over_chips(piece, k) for k in range(1, count)], [(input_grad, "h"), (grad_down, "h")]
    )
    layer_out = stack_parts(totals_all, [(input_part, "v")])
    grad_qkv, grad_out, grad_one, grad_two = finish(
        collected, over_cores(collected), 3 * width, [(layer_out, "h")]
    )

    back = lambda x, n: x.reshape(-1, n, model).transpose(2, 0, 1)
    return (
        layer_out,
        input_grad,
        grad_one[0],
        back(grad_qkv, width),
        grad_out,
        grad_two[0],
        back(grad_in, units),
        grad_down,
    )


def solution(mesh):
    placed = (
        P("seq", None),
        P(),
        P(None, None, "tp"),
        P("tp", None),
        P(),
        P(None, None, "tp"),
        P("tp", None),
        P("seq", None),
        P(),
        P(),
    )
    return jax.shard_map(
        functools.partial(body, mesh.shape["seq"], mesh.shape["tp"]),
        mesh=mesh,
        in_specs=placed,
        out_specs=(
            P("seq", None),
            P("seq", None),
            P(),
            P(None, None, "tp"),
            P("tp", None),
            P(),
            P(None, None, "tp"),
            P("tp", None),
        ),
        check_vma=False,
    )
```

```python
import functools

import jax
import jax.numpy as jnp
import numpy as np
from jax import lax
from jax.experimental import pallas as pl
from jax.experimental.pallas import tpu as pltpu
from jax.sharding import PartitionSpec as P

HDIM = 64
HALF = HDIM // 2
EPSILON = 1e-05
ROPE_THETA = 160000.0
MASKED = -1e30
AUG = 80
STRIP = 64
F32 = jnp.float32
BF16 = jnp.bfloat16
HBM = pl.BlockSpec(memory_space=pltpu.HBM)
VMEM = pl.BlockSpec(memory_space=pltpu.VMEM)

NN = (((1,), (0,)), ((), ()))
NT = (((1,), (1,)), ((), ()))
TN = (((0,), (0,)), ((), ()))


def params(mib):
    return pltpu.CompilerParams(vmem_limit_bytes=mib * 2**20)


def mm(a, b, dims):
    return lax.dot_general(a, b, dims, preferred_element_type=F32)


def shaped(shape, dtype):
    return jax.ShapeDtypeStruct(shape, dtype)


def kinds(arrays, kind):
    return [(array, kind) for array in arrays]


def pin(array, kind):
    return array if kind in ("v", "free") else pltpu.with_memory_space_constraint(array, pltpu.HBM)


def call(name, kernel, ins, outs, scratch=(), mib=16, after=(), lazy=False):
    fetched = [i for i, given in enumerate(ins) if given[1] not in ("v", "raw", "free")]
    left = [i for i, out in enumerate(outs) if out[2] == "h"]

    def held(array, kind):
        rows = array.shape[0] if kind == "h" else kind
        return pltpu.VMEM((rows,) + array.shape[1:], array.dtype)

    def run(*refs):
        in_refs = list(refs[: len(ins)])
        at = len(ins) + len(after)
        out_refs = list(refs[at : at + len(outs)])
        at += len(outs)
        own = refs[at : at + len(scratch)]
        at += len(scratch)
        buffers = refs[at : at + len(fetched) + len(left)]
        sems = refs[-1]
        copies = []
        for n, i in enumerate(fetched):
            source = in_refs[i]
            if ins[i][1] != "h":
                rows = ins[i][1]
                at = pl.multiple_of(lax.axis_index("tp") * rows, rows)
                source = source.at[pl.ds(at, rows)]
            copies.append(pltpu.make_async_copy(source, buffers[n], sems.at[n]))
            in_refs[i] = buffers[n]
        for copy in copies:
            copy.start()
        coming = dict(zip(fetched, copies))
        going = {}
        for n, i in enumerate(left):
            spot = len(fetched) + n
            going[i] = pltpu.make_async_copy(buffers[spot], out_refs[i], sems.at[spot])
            out_refs[i] = buffers[spot]
        gone = []

        def need(*which):
            for i in which:
                if i in coming:
                    coming.pop(i).wait()

        def give(*which):
            for i in which:
                if i in going:
                    gone.append(going.pop(i))
                    gone[-1].start()

        if lazy:
            kernel(need, give, *in_refs, *out_refs, *own)
        else:
            need(*fetched)
            kernel(*in_refs, *out_refs, *own)
        need(*fetched)
        give(*left)
        for copy in gone:
            copy.wait()

    spec = lambda kind: VMEM if kind == "v" else HBM
    count = len(fetched) + len(left)
    return pl.pallas_call(
        run,
        out_shape=tuple(
            shaped(shape, dtype) if kind == "v" else pltpu.HBM(shape, dtype)
            for shape, dtype, kind in outs
        ),
        in_specs=[spec(kind) for unused, kind in ins] + [spec(kind) for unused, kind in after],
        out_specs=tuple(spec(kind) for unused, unused, kind in outs),
        scratch_shapes=list(scratch)
        + [held(*ins[i]) for i in fetched]
        + [pltpu.VMEM(outs[i][0], outs[i][1]) for i in left]
        + [pltpu.SemaphoreType.DMA((max(count, 1),))],
        name=name,
        compiler_params=params(mib),
    )(*[pin(*given) for given in ins], *[pin(*given) for given in after])


def swap(x, axis, hop, count):
    return lax.ppermute(x, axis, [(i, i ^ hop) for i in range(count)])


def doc_scratch(doc_lengths, roster):
    return [pltpu.SMEM(doc_lengths.shape, jnp.int32), pltpu.SMEM(roster.shape, jnp.int32)]


def fetch_docs(len_any, roster_any, len_ref, roster_ref, len_sem, roster_sem):
    one = pltpu.make_async_copy(len_any, len_ref, len_sem)
    two = pltpu.make_async_copy(roster_any, roster_ref, roster_sem)
    one.start()
    two.start()
    one.wait()
    two.wait()


def doc_bounds(len_ref):
    ends, total = [], jnp.int32(0)
    for d in range(len_ref.shape[0]):
        total = total + len_ref[d]
        ends.append(total)
    return ends


def doc_of(ends, position):
    found = jnp.int32(0)
    for end in ends:
        found = found + (end <= position).astype(jnp.int32)
    return found


def meet(ends, base_a, base_b, rows):
    low = jnp.maximum(doc_of(ends, base_a), doc_of(ends, base_b))
    high = jnp.minimum(doc_of(ends, base_a + rows - 1), doc_of(ends, base_b + rows - 1))
    return low <= high


def doc_rows(ends, base, rows):
    spot = base + lax.broadcasted_iota(jnp.int32, (16, rows), 1)
    line = lax.broadcasted_iota(jnp.int32, (16, rows), 0)
    held = jnp.zeros((16, rows), F32)
    start = jnp.int32(0)
    for d, end in enumerate(ends):
        inside = (line == d) & (spot >= start) & (spot < end)
        held = jnp.where(inside, 1.0, held)
        start = end
    return held


def ban_rows(ends, base, rows):
    line = lax.broadcasted_iota(jnp.int32, (16, rows), 0)
    held = doc_rows(ends, base, rows)
    return jnp.where((held > 0.5) | (line >= len(ends)), 0.0, MASKED)


def key_row(block, seq_index):
    return seq_index ^ (2 * block)


def place_row(ends, base, rows):
    spot = base + lax.broadcasted_iota(jnp.int32, (1, rows), 1)
    start = jnp.zeros((1, rows), jnp.int32)
    for end in ends:
        start = jnp.where(spot >= end, end, start)
    return (spot - start).astype(F32)


def normed(values):
    centre = jnp.mean(values, axis=-1, keepdims=True)
    shifted = values - centre
    spread = jnp.mean(shifted * shifted, axis=-1, keepdims=True)
    scale = lax.rsqrt(spread + EPSILON)
    return shifted * scale, scale


def norm_back(unit, scale, grad, gain):
    u = grad * gain
    mean_u = jnp.mean(u, axis=-1, keepdims=True)
    mean_un = jnp.mean(u * unit, axis=-1, keepdims=True)
    return scale * (u - mean_u - unit * mean_un)


def project_kernel(
    width, need, give, len_any, roster_any, x_ref, w_ref, gain_ref, freq_ref, *refs
):
    q_out, kv_out, h_out, cos_out, sin_out = refs[:5]
    proj, len_ref, roster_ref, sems = refs[5:]
    rows = x_ref.shape[0]
    fetch_docs(len_any, roster_any, len_ref, roster_ref, sems.at[0], sems.at[1])
    need(5)
    ends = doc_bounds(len_ref)
    place = place_row(ends, roster_ref[lax.axis_index("seq")] * rows, rows)
    angles = place * freq_ref[...]
    cos_table = jnp.cos(angles)
    sin_table = jnp.sin(angles)
    cos_out[...] = cos_table
    sin_out[...] = sin_table
    give(3, 4)
    need(2, 4)
    gain = gain_ref[...].reshape(1, -1)

    def strip(i, carry):
        at = pl.ds(i * STRIP, STRIP)
        unit, unused = normed(x_ref[at, :].astype(F32))
        h_out[at, :] = (unit * gain).astype(BF16)
        return carry

    lax.fori_loop(0, rows // STRIP, strip, 0)
    give(2)
    need(3)
    proj[...] = mm(w_ref[...], h_out[...], NT)
    for at in range(0, 2 * width, HDIM):
        low = proj[at : at + HALF, :]
        high = proj[at + HALF : at + HDIM, :]
        turned_low = (low * cos_out[...] - high * sin_out[...]).astype(BF16)
        turned_high = (high * cos_out[...] + low * sin_out[...]).astype(BF16)
        if at < width:
            q_out[at : at + HALF, :] = (turned_low.astype(F32) * HDIM**-0.5).astype(BF16)
            q_out[at + HALF : at + HDIM, :] = (turned_high.astype(F32) * HDIM**-0.5).astype(BF16)
        else:
            kv_out[at - width : at - width + HALF, :] = turned_low
            kv_out[at - width + HALF : at - width + HDIM, :] = turned_high
    kv_out[width:, :] = proj[2 * width :, :].astype(BF16)


def project(doc_lengths, roster, tokens, gain, qkv_t):
    rows, model = tokens.shape
    width = qkv_t.shape[0] // 3
    freq = (ROPE_THETA ** -(np.arange(HALF) * (2.0 / HDIM))).astype(np.float32)[:, None]
    return call(
        "project",
        functools.partial(project_kernel, width),
        kinds((doc_lengths, roster), "raw") + kinds((tokens, qkv_t, gain, jnp.asarray(freq)), "h"),
        [
            ((width, rows), BF16, "v"),
            ((2 * width, rows), BF16, "v"),
            ((rows, model), BF16, "h"),
            ((HALF, rows), F32, "h"),
            ((HALF, rows), F32, "h"),
        ],
        [pltpu.VMEM((3 * width, rows), F32)]
        + doc_scratch(doc_lengths, roster)
        + [pltpu.SemaphoreType.DMA((2,))],
        lazy=True,
    )


def forward_kernel(first, count, heads, last, len_any, roster_any, q_own, q_pair, *refs):
    kv_refs = refs[:count]
    refs = refs[count:]
    if first:
        state_in, refs = refs[0], refs[1:]
    outs = refs[: 2 if last else 1]
    kv, q_aug, state, len_ref, roster_ref, sems = refs[len(outs) :]
    rows = q_own.shape[1]
    width = heads * HDIM
    me = lax.axis_index("seq")
    copies = [pltpu.make_async_copy(kv_refs[j], kv.at[j], sems.at[j]) for j in range(count)]
    for copy in copies:
        copy.start()
    fetch_docs(len_any, roster_any, len_ref, roster_ref, sems.at[count], sems.at[count + 1])
    ends = doc_bounds(len_ref)
    bases = (roster_ref[me] * rows, roster_ref[me ^ 1] * rows)
    for g, q_ref in enumerate((q_own, q_pair)):
        mark = doc_rows(ends, bases[g], rows).astype(BF16)
        for h in range(heads):
            q_aug[g * heads + h, :HDIM, :] = q_ref[h * HDIM : (h + 1) * HDIM, :]
            q_aug[g * heads + h, HDIM:, :] = mark
    if first:
        state[...] = state_in[...]
    else:
        line = lax.broadcasted_iota(jnp.int32, (2 * heads, AUG, rows), 1)
        state[...] = jnp.where(line >= 72, MASKED, 0.0)
    for copy in copies:
        copy.wait()

    top = lax.broadcasted_iota(jnp.int32, (16, rows), 0) == 0
    ones = jnp.where(top, 1.0, 0.0).astype(BF16)

    def block(j, carry):
        key_base = roster_ref[key_row(j + first, me)] * rows
        ban = ban_rows(ends, key_base, rows).astype(BF16)
        for g in range(2):

            @pl.when(meet(ends, bases[g], key_base, rows))
            def _():
                for h in range(heads):
                    at = g * heads + h
                    keys = jnp.concatenate([kv[j, h * HDIM : (h + 1) * HDIM, :], ban], axis=0)
                    vals = jnp.concatenate(
                        [kv[j, width + h * HDIM : width + (h + 1) * HDIM, :], ones], axis=0
                    )
                    scores = mm(keys, q_aug[at], TN)
                    old = state[at, 72:73, :]
                    new = jnp.maximum(old, jnp.max(scores, axis=0, keepdims=True))
                    probs = jnp.exp(scores - new).astype(BF16)
                    part = mm(vals, probs, NN)
                    fade = jnp.exp(old - new)
                    state[at, :72, :] = state[at, :72, :] * fade + part[:72]
                    state[at, 72:, :] = jnp.broadcast_to(new, (8, rows))

        return carry

    lax.fori_loop(0, count, block, 0)
    if last:
        outs[0][...] = state[:heads]
        outs[1][...] = state[heads:]
    else:
        outs[0][...] = state[...]


def attention_forward(first, last, doc_lengths, roster, q_own, q_pair, blocks, state=None):
    width, rows = q_own.shape
    heads = width // HDIM
    count = len(blocks)
    half = ((heads, AUG, rows), F32, "v")
    whole = ((2 * heads, AUG, rows), F32, "v")
    given = [] if state is None else [(state, "v")]
    return call(
        "attention_forward",
        functools.partial(forward_kernel, first, count, heads, last),
        [(doc_lengths, "raw"), (roster, "raw"), (q_own, "v"), (q_pair, "v")]
        + kinds(blocks, "free")
        + given,
        [half, half] if last else [whole],
        [
            pltpu.VMEM((count, 2 * width, rows), BF16),
            pltpu.VMEM((2 * heads, AUG, rows), BF16),
            pltpu.VMEM((2 * heads, AUG, rows), F32),
        ]
        + doc_scratch(doc_lengths, roster)
        + [pltpu.SemaphoreType.DMA((count + 2,))],
        16 if count < 8 else 40,
    )


def backward_kernel(first, count, heads, more, last, len_any, roster_any, *refs):
    q_own, q_pair, g_own, g_pair, o_own, o_pair, t_own, t_pair = refs[:8]
    kv_refs, refs = refs[8 : 8 + count], refs[8 + count :]
    if more:
        dq_in, refs = refs[0], refs[1:]
    outs, refs = refs[:count], refs[count:]
    dq_outs, refs = (refs[:2], refs[2:]) if last else (refs[:1], refs[1:])
    kv, q_aug, delta, dq, dkv, len_ref, roster_ref, sems = refs
    rows = q_own.shape[1]
    width = heads * HDIM
    me = lax.axis_index("seq")
    copies = [pltpu.make_async_copy(kv_refs[j], kv.at[j], sems.at[j]) for j in range(count)]
    for copy in copies:
        copy.start()
    fetch_docs(len_any, roster_any, len_ref, roster_ref, sems.at[count], sems.at[count + 1])
    ends = doc_bounds(len_ref)
    bases = (roster_ref[me] * rows, roster_ref[me ^ 1] * rows)
    for g, (q_ref, g_ref, o_ref) in enumerate(((q_own, g_own, o_own), (q_pair, g_pair, o_pair))):
        mark = doc_rows(ends, bases[g], rows).astype(BF16)
        for h in range(heads):
            part = slice(h * HDIM, (h + 1) * HDIM)
            q_aug[g * heads + h, :HDIM, :] = q_ref[part, :]
            q_aug[g * heads + h, HDIM:, :] = mark
            product = g_ref[part, :].astype(F32) * o_ref[part, :].astype(F32)
            delta[g * heads + h] = jnp.broadcast_to(
                jnp.sum(product, axis=0, keepdims=True), (8, rows)
            )
    if more:
        dq[...] = dq_in[...]
    else:
        dq[...] = jnp.zeros_like(dq)
    for copy in copies:
        copy.wait()

    def block(j, carry):
        key_base = roster_ref[key_row(j + first, me)] * rows
        ban = ban_rows(ends, key_base, rows).astype(BF16)
        dkv[j] = jnp.zeros((2 * width, rows), F32)
        for g, (g_ref, t_ref) in enumerate(((g_own, t_own), (g_pair, t_pair))):

            @pl.when(meet(ends, bases[g], key_base, rows))
            def _():
                for h in range(heads):
                    at = g * heads + h
                    part = slice(h * HDIM, (h + 1) * HDIM)
                    late = slice(width + h * HDIM, width + (h + 1) * HDIM)
                    keys = kv[j, part, :]
                    scores = mm(jnp.concatenate([keys, ban], axis=0), q_aug[at], TN)
                    probs = jnp.exp(scores - t_ref[h, 0:1, :])
                    prob_grads = mm(kv[j, late, :], g_ref[part, :], TN)
                    score_grad = (probs * (prob_grads - delta[at, 0:1, :])).astype(BF16)
                    dkv[j, late, :] += mm(g_ref[part, :], probs.astype(BF16), NT)
                    dkv[j, part, :] += mm(q_aug[at, :HDIM, :], score_grad, NT)
                    dq[at] += mm(keys, score_grad, NN)

        return carry

    lax.fori_loop(0, count, block, 0)
    for j in range(count):
        outs[j][...] = dkv[j].astype(outs[j].dtype)
    if last:
        for h in range(heads):
            part = slice(h * HDIM, (h + 1) * HDIM)
            dq_outs[0][part, :] = dq[h] * HDIM**-0.5
            dq_outs[1][part, :] = (dq[heads + h] * HDIM**-0.5).astype(BF16)
    else:
        dq_outs[0][...] = dq[...]


def attention_backward(first, last, doc_lengths, roster, held, blocks, dq=None, after=()):
    width, rows = held[0].shape
    heads = width // HDIM
    count = len(blocks)
    given = [] if dq is None else [(dq, "v")]
    if last:
        queries = [((width, rows), F32, "v"), ((width, rows), BF16, "v")]
    else:
        queries = [((2 * heads, HDIM, rows), F32, "v")]
    return call(
        "attention_backward",
        functools.partial(backward_kernel, first, count, heads, bool(given), last),
        kinds((doc_lengths, roster), "raw") + kinds(held, "v") + kinds(blocks, "free") + given,
        [((2 * width, rows), BF16 if first else F32, "v")] * count + queries,
        [
            pltpu.VMEM((count, 2 * width, rows), BF16),
            pltpu.VMEM((2 * heads, AUG, rows), BF16),
            pltpu.VMEM((2 * heads, 8, rows), F32),
            pltpu.VMEM((2 * heads, HDIM, rows), F32),
            pltpu.VMEM((count, 2 * width, rows), F32),
        ]
        + doc_scratch(doc_lengths, roster)
        + [pltpu.SemaphoreType.DMA((count + 2,))],
        16 if count < 8 else 40,
        after,
    )


def join_kernel(heads, own_ref, back_ref, out_ref, total_ref):
    rows = own_ref.shape[2]
    for h in range(heads):
        top_own = own_ref[h, 72:73, :]
        top_back = back_ref[h, 72:73, :]
        top = jnp.maximum(top_own, top_back)
        fade_own = jnp.exp(top_own - top)
        fade_back = jnp.exp(top_back - top)
        total = own_ref[h, 64:65, :] * fade_own + back_ref[h, 64:65, :] * fade_back
        share_own = fade_own / total
        share_back = fade_back / total
        value = own_ref[h, :HDIM, :] * share_own + back_ref[h, :HDIM, :] * share_back
        out_ref[h * HDIM : (h + 1) * HDIM, :] = value.astype(BF16)
        total_ref[h] = jnp.broadcast_to(top + jnp.log(total), (8, rows))


def join(own, back):
    heads, unused, rows = own.shape
    return call(
        "join",
        functools.partial(join_kernel, heads),
        [(own, "v"), (back, "v")],
        [((heads * HDIM, rows), BF16, "v"), ((heads, 8, rows), F32, "v")],
    )


def feed_kernel(n_tp, need, give, x_ref, cot_ref, gain_ref, in_ref, down_ref, w_ref, *refs):
    out_refs = refs[:n_tp]
    middle_out, h_out, mixed_out, gate_out, gain_out = refs[n_tp : n_tp + 5]
    part_refs = refs[n_tp + 5 : 2 * n_tp + 5]
    outs, unit, gate_up, mixed_grad, grad = refs[2 * n_tp + 5 :]
    rows = x_ref.shape[0]
    part = rows // n_tp
    units = down_ref.shape[0]
    width = out_refs[0].shape[0]
    tp = lax.axis_index("tp")
    for k in range(n_tp):
        at = pl.ds(pl.multiple_of((tp ^ k) * width, width), width)
        outs[at, :] = out_refs[k][...]
    need(5)
    middle_out[...] = mm(outs[...], w_ref[...], TN)
    need(0, 2)
    gain = gain_ref[...].reshape(1, -1)

    def strip(i, carry):
        at = pl.ds(i * STRIP, STRIP)
        middle = middle_out[at, :] + x_ref[at, :].astype(F32)
        middle_out[at, :] = middle
        held, unused = normed(middle)
        unit[at, :] = held
        h_out[at, :] = (held * gain).astype(BF16)
        return carry

    lax.fori_loop(0, rows // STRIP, strip, 0)
    give(0, 1)
    need(1, 4)
    mixed_grad[...] = mm(down_ref[...], cot_ref[...], NT)
    need(3)
    gate_up[...] = mm(in_ref[...], h_out[...], NT)

    def wave(i, carry):
        at = pl.ds(i * 32, 32)
        late = pl.ds(units + i * 32, 32)
        gate = gate_up[at, :]
        up = gate_up[late, :]
        back = mixed_grad[at, :]
        bell = 0.5 * (1.0 + lax.erf(gate * (2.0**-0.5)))
        active = gate * bell
        slope = bell + gate * jnp.exp(-0.5 * gate * gate) * ((2.0 * jnp.pi) ** -0.5)
        mixed_out[at, :] = (active * up).astype(BF16)
        gate_out[at, :] = (back * up * slope).astype(BF16)
        gate_out[late, :] = (back * active).astype(BF16)
        return carry

    lax.fori_loop(0, units // 32, wave, 0)
    give(2, 3)
    grad[...] = mm(gate_out[...], in_ref[...], TN)
    for k in range(n_tp):
        at = pl.ds(pl.multiple_of((tp ^ k) * part, part), part)
        part_refs[k][...] = grad[at, :].astype(part_refs[k].dtype)
        give(5 + k)

    def gains(i, carry):
        at = pl.ds(i * STRIP, STRIP)
        product = grad[at, :] * unit[at, :]
        return carry + jnp.sum(product.reshape(STRIP // 8, 8, -1), axis=0)

    gain_out[...] = lax.fori_loop(0, rows // STRIP, gains, jnp.zeros(gain_out.shape, F32))


def feed(tokens, cotangent, gain, in_t, w_down, w_full, outs):
    rows, model = tokens.shape
    n_tp = len(outs)
    units = w_down.shape[0]
    part = rows // n_tp
    return call(
        "feed",
        functools.partial(feed_kernel, n_tp),
        kinds((tokens, cotangent, gain, in_t, w_down, w_full), "h") + kinds(outs, "v"),
        [
            ((rows, model), F32, "h"),
            ((rows, model), BF16, "h"),
            ((units, rows), BF16, "h"),
            ((2 * units, rows), BF16, "h"),
            ((8, model), F32, "h"),
            ((part, model), F32, "h"),
        ]
        + [((part, model), BF16, "h")] * (n_tp - 1),
        [
            pltpu.VMEM((n_tp * outs[0].shape[0], rows), BF16),
            pltpu.VMEM((rows, model), F32),
            pltpu.VMEM((2 * units, rows), F32),
            pltpu.VMEM((units, rows), F32),
            pltpu.VMEM((rows, model), F32),
        ],
        32,
        lazy=True,
    )


def branch_kernel(n_tp, need, give, middle_ref, cot_ref, gain_ref, w_ref, *refs):
    arrived = refs[:n_tp]
    grad_out, branch_out = refs[n_tp : n_tp + 2]
    piece_refs = refs[n_tp + 2 :]
    width = piece_refs[0].shape[1]
    tp = lax.axis_index("tp")
    need(0, 1, 2, 4)
    total = arrived[0][...]
    for ref in arrived[1:]:
        total = total + ref[...].astype(F32)
    unit, scale = normed(middle_ref[...])
    gain = gain_ref[...].reshape(1, -1)
    value = cot_ref[...].astype(F32) + norm_back(unit, scale, total, gain)
    grad_out[...] = value
    branch_out[...] = value.astype(BF16)
    give(0, 1)
    need(3)
    for k in range(n_tp):
        at = pl.ds(pl.multiple_of((tp ^ k) * width, width), width)
        piece_refs[k][...] = mm(branch_out[...], w_ref[at, :], NT).astype(BF16)


def branch(middle, cotangent, gain, w_full, arrived, after):
    part, model = arrived[0].shape
    n_tp = len(arrived)
    width = w_full.shape[0] // n_tp
    return call(
        "branch",
        functools.partial(branch_kernel, n_tp),
        [(middle, part), (cotangent, part)] + kinds((gain, w_full, arrived[0]), "h") + kinds(arrived[1:], "v"),
        [((part, model), F32, "h"), ((part, model), BF16, "h")]
        + [((part, width), BF16, "v")] * n_tp,
        (),
        16,
        after,
        True,
    )


def lay_kernel(n_tp, *refs):
    out_ref, held = refs[n_tp:]
    part = refs[0].shape[0]
    tp = lax.axis_index("tp")
    for k in range(n_tp):
        at = pl.ds(pl.multiple_of((tp ^ k) * part, part), part)
        held[at, :] = refs[k][...].astype(F32)
    out_ref[...] = held[...].T.astype(BF16)


def lay_turned(pieces):
    part, width = pieces[0].shape
    rows = part * len(pieces)
    (out,) = call(
        "lay_turned",
        functools.partial(lay_kernel, len(pieces)),
        kinds(pieces, "v"),
        [((width, rows), BF16, "v")],
        [pltpu.VMEM((rows, width), F32)],
    )
    return out


def stack_kernel(n_tp, *refs):
    out_ref = refs[n_tp]
    part = refs[0].shape[0]
    tp = lax.axis_index("tp")
    for k in range(n_tp):
        at = pl.ds(pl.multiple_of((tp ^ k) * part, part), part)
        out_ref[at, :] = refs[k][...]


def stack_parts(pieces, after=()):
    part, model = pieces[0].shape
    (out,) = call(
        "stack_parts",
        functools.partial(stack_kernel, len(pieces)),
        kinds(pieces, "v"),
        [((part * len(pieces), model), pieces[0].dtype, "h")],
        (),
        16,
        after,
    )
    return out


def turn_back(out_ref, first, value, cos_table, sin_table):
    for at in range(0, value.shape[0], HDIM):
        low = value[at : at + HALF]
        high = value[at + HALF : at + HDIM]
        spot = first + at
        out_ref[spot : spot + HALF, :] = (low * cos_table + high * sin_table).astype(BF16)
        out_ref[spot + HALF : spot + HDIM, :] = (high * cos_table - low * sin_table).astype(BF16)


def unproject_kernel(
    count, n_tp, need, give, x_ref, w_ref, cos_ref, sin_ref, two_ref, dq_ref, dq_back, *refs
):
    dkv_refs = refs[:count]
    proj_out = refs[count]
    part_refs = refs[count + 1 : count + 1 + n_tp]
    grad, dkv = refs[count + 1 + n_tp :]
    rows, model = x_ref.shape
    part = rows // n_tp
    width = dq_ref.shape[0]
    tp = lax.axis_index("tp")
    need(2, 3)
    cos_table = cos_ref[...]
    sin_table = sin_ref[...]
    turn_back(proj_out, 0, dq_ref[...] + dq_back[...].astype(F32), cos_table, sin_table)
    total = dkv_refs[0][...]
    for ref in dkv_refs[1:]:
        total = total + ref[...].astype(F32)
    dkv[...] = total
    turn_back(proj_out, width, dkv[:width, :], cos_table, sin_table)
    proj_out[2 * width :, :] = dkv[width:, :].astype(BF16)
    need(1)
    grad[...] = mm(proj_out[...], w_ref[...], TN)
    need(0, 4)

    def gains(i, carry):
        at = pl.ds(i * STRIP, STRIP)
        unit, unused = normed(x_ref[at, :].astype(F32))
        product = grad[at, :] * unit
        return carry + jnp.sum(product.reshape(STRIP // 8, 8, -1), axis=0)

    gain = lax.fori_loop(0, rows // STRIP, gains, jnp.zeros((8, model), F32))
    line = lax.broadcasted_iota(jnp.int32, (16, model), 0)
    gain_two = jnp.sum(two_ref[...], axis=0, keepdims=True)
    gain = jnp.sum(gain, axis=0, keepdims=True)
    gain = jnp.where(line == 0, gain, jnp.where(line == 1, gain_two, 0.0))
    for k in range(n_tp):
        at = pl.ds(pl.multiple_of((tp ^ k) * part, part), part)
        part_refs[k][:part, :] = grad[at, :].astype(part_refs[k].dtype)
        part_refs[k][part:, :] = gain.astype(part_refs[k].dtype)


def unproject(n_tp, tokens, qkv_t, cos_table, sin_table, gain_two_part, dq, dq_back, dkvs, after):
    rows, model = tokens.shape
    part = rows // n_tp
    return call(
        "unproject",
        functools.partial(unproject_kernel, len(dkvs), n_tp),
        kinds((tokens, qkv_t, cos_table, sin_table, gain_two_part), "h")
        + kinds((dq, dq_back, *dkvs), "v"),
        [((qkv_t.shape[0], rows), BF16, "v"), ((part + 16, model), F32, "v")]
        + [((part + 16, model), BF16, "v")] * (n_tp - 1),
        [pltpu.VMEM((rows, model), F32), pltpu.VMEM(dkvs[0].shape, F32)],
        16,
        after,
        True,
    )


def input_kernel(n_tp, x_ref, gain_ref, grad_ref, *refs):
    arrived = refs[:n_tp]
    out_ref, gain_out = refs[n_tp:]
    part, model = grad_ref.shape
    total = arrived[0][...]
    for ref in arrived[1:]:
        total = total + ref[...].astype(F32)
    unit, scale = normed(x_ref[...].astype(F32))
    gain = gain_ref[...].reshape(1, -1)
    value = grad_ref[...] + norm_back(unit, scale, total[:part], gain)
    out_ref[...] = value.astype(BF16)
    gain_out[...] = total[part : part + 8]


def input_side(tokens, gain, middle_grad, arrived, after):
    part, model = middle_grad.shape
    return call(
        "input_side",
        functools.partial(input_kernel, len(arrived)),
        [(tokens, part), (gain, "h"), (middle_grad, "h")] + kinds(arrived, "v"),
        [((part, model), BF16, "v"), ((8, model), F32, "v")],
        (),
        16,
        after,
    )


def early_kernel(mixed_ref, gate_ref, cot_ref, h_ref, out_ref):
    units = mixed_ref.shape[0]
    out_ref[:units, :] = mm(mixed_ref[...], cot_ref[...], NN)
    out_ref[units : 3 * units, :] = mm(gate_ref[...], h_ref[...], NN)
    if out_ref.shape[0] > 3 * units:
        out_ref[3 * units :, :] = jnp.zeros((out_ref.shape[0] - 3 * units, out_ref.shape[1]), F32)


def early_grads(mixed, gate_grad, cotangent, h_two):
    model = cotangent.shape[1]
    (out,) = call(
        "early_grads",
        early_kernel,
        kinds((mixed, gate_grad, cotangent, h_two), "h"),
        [((1104, model), F32, "h")],
    )
    return out


def part_kernel(in_any, *refs):
    out_refs, held, sem = refs[:-2], refs[-2], refs[-1]
    rows = held.shape[0]
    copy = pltpu.make_async_copy(in_any.at[pl.ds(0, rows)], held, sem)
    copy.start()
    copy.wait()
    at = 0
    for ref in out_refs:
        ref[...] = held[at : at + ref.shape[0], :]
        at += ref.shape[0]


def parted(value, sizes):
    model = value.shape[1]
    return call(
        "parted",
        part_kernel,
        [(value, "raw")],
        [((size, model), F32, "h") for size in sizes],
        [pltpu.VMEM((sum(sizes), model), F32), pltpu.SemaphoreType.DMA],
    )


def late_kernel(n_tp, proj_ref, h_ref, out_ref, *refs):
    branch_refs = refs[:n_tp]
    keep_ref, send_ref, branch_full = refs[n_tp:]
    part = branch_refs[0].shape[0]
    half = keep_ref.shape[1]
    wide = proj_ref.shape[0]
    tp = lax.axis_index("tp")
    core = lax.axis_index("seq") % 2
    for k in range(n_tp):
        at = pl.ds(pl.multiple_of((tp ^ k) * part, part), part)
        branch_full[at, :] = branch_refs[k][...]
    for ref, side in ((send_ref, 1 - core), (keep_ref, core)):
        columns = pl.ds(pl.multiple_of(side * half, half), half)
        ref[:wide, :] = mm(proj_ref[...], h_ref[:, columns], NN).astype(ref.dtype)
        ref[wide:, :] = mm(out_ref[...], branch_full[:, columns], NN).astype(ref.dtype)


def late_grads(proj_grad, h_one, out_b, branches, after):
    rows, model = h_one.shape
    wide = proj_grad.shape[0] + out_b.shape[0]
    return call(
        "late_grads",
        functools.partial(late_kernel, len(branches)),
        [(proj_grad, "v"), (h_one, "h"), (out_b, "v"), (branches[0], "h")]
        + kinds(branches[1:], "v"),
        [((wide, model // 2), F32, "v"), ((wide, model // 2), BF16, "v")],
        [pltpu.VMEM((rows, model), BF16)],
        16,
        after,
    )


def spread_kernel(count, keep_ref, back_ref, *refs):
    held = refs[count]
    piece = refs[0].shape[0]
    chip = lax.axis_index("seq") // 2
    held[...] = keep_ref[...] + back_ref[...].astype(F32)
    for k in range(count):
        at = pl.ds(pl.multiple_of((chip ^ k) * piece, piece), piece)
        refs[k][...] = held[at, :].astype(refs[k].dtype)


def spread(count, keep, back):
    wide, half = keep.shape
    piece = wide // count
    return call(
        "spread",
        functools.partial(spread_kernel, count),
        [(keep, "v"), (back, "v")],
        [((piece, half), F32, "v")] + [((piece, half), BF16, "v")] * (count - 1),
        [pltpu.VMEM((wide, half), F32)],
    )


def piece_kernel(count, gain_ref, *refs):
    out_ref = refs[count]
    half = out_ref.shape[1]
    total = refs[0][...]
    for ref in refs[1:count]:
        total = total + ref[...].astype(F32)
    line = lax.broadcasted_iota(jnp.int32, (16, half), 0)
    gains = jnp.zeros((16, half), F32)
    for at in range(4):
        row = gain_ref[at // 2 : at // 2 + 1, at % 2 * half : (at % 2 + 1) * half]
        gains = jnp.where(line == at, row, gains)
    out_ref[...] = jnp.concatenate([total, gains], axis=0).astype(BF16)


def sum_piece(gains, pieces, after=()):
    piece, half = pieces[0].shape
    (out,) = call(
        "sum_piece",
        functools.partial(piece_kernel, len(pieces)),
        [(gains, "v")] + kinds(pieces, "v"),
        [((piece + 16, half), BF16, "v")],
        (),
        16,
        after,
    )
    return out


def collect_kernel(count, *refs):
    out_ref, held = refs[count:]
    piece = refs[0].shape[0] - 16
    wide = count * piece
    chip = lax.axis_index("seq") // 2
    gains = jnp.zeros((16, out_ref.shape[1]), F32)
    for k in range(count):
        at = pl.ds(pl.multiple_of((chip ^ k) * piece, piece), piece)
        whole = refs[k][...].astype(F32)
        held[at, :] = whole[:piece]
        gains = gains + whole[piece:]
    held[wide:, :] = gains
    out_ref[...] = held[...].astype(BF16)


def collect(pieces, after=()):
    piece, half = pieces[0].shape
    wide = (piece - 16) * len(pieces) + 16
    (out,) = call(
        "collect",
        functools.partial(collect_kernel, len(pieces)),
        kinds(pieces, "v"),
        [((wide, half), BF16, "v")],
        [pltpu.VMEM((wide, half), F32)],
        16,
        after,
    )
    return out


def finish_kernel(own_ref, pair_ref, qkv_ref, out_ref, one_ref, two_ref):
    half = own_ref.shape[1]
    wide, tall = qkv_ref.shape[0], out_ref.shape[0]
    core = lax.axis_index("seq") % 2
    for ref, side in ((own_ref, core), (pair_ref, 1 - core)):
        columns = pl.ds(pl.multiple_of(side * half, half), half)
        qkv_ref[:, columns] = ref[:wide, :].astype(F32)
        out_ref[:, columns] = ref[wide : wide + tall, :].astype(F32)
    gains = own_ref[wide + tall :, :].astype(F32) + pair_ref[wide + tall :, :].astype(F32)
    for at, ref in ((0, one_ref), (2, two_ref)):
        ref[pl.ds(0, half)] = gains[at]
        ref[pl.ds(half, half)] = gains[at + 1]


def finish(own, pair, wide, after=()):
    half = own.shape[1]
    tall = own.shape[0] - 16 - wide
    model = 2 * half
    return call(
        "finish",
        finish_kernel,
        [(own, "v"), (pair, "v")],
        [
            ((wide, model), F32, "h"),
            ((tall, model), F32, "h"),
            ((model,), F32, "h"),
            ((model,), F32, "h"),
        ],
        (),
        16,
        after,
    )


def down_kernel(n_tp, mixed_ref, w_ref, middle_ref, keep_ref, send_ref, total):
    part = keep_ref.shape[0] * 2 // n_tp
    tp = lax.axis_index("tp")
    total[...] = mm(mixed_ref[...], w_ref[...], TN)
    for k in range(n_tp):
        at = pl.ds(pl.multiple_of((tp ^ k) * part, part), part)
        spot = k // 2 * part
        if k % 2:
            send_ref[spot : spot + part, :] = total[at, :].astype(BF16)
        else:
            value = total[at, :] + middle_ref[at, :] if k == 0 else total[at, :]
            keep_ref[spot : spot + part, :] = value


def down(n_tp, mixed, w_down, middle, after):
    rows, model = middle.shape
    return call(
        "down",
        functools.partial(down_kernel, n_tp),
        kinds((mixed, w_down, middle), "h"),
        [((rows // 2, model), F32, "h"), ((rows // 2, model), BF16, "h")],
        [pltpu.VMEM((rows, model), F32)],
        16,
        after,
    )


def pair_kernel(keep_ref, back_ref, own_ref, *send_refs):
    part = own_ref.shape[0]
    own_ref[...] = keep_ref[:part, :] + back_ref[:part, :].astype(F32)
    for k, ref in enumerate(send_refs):
        at = (k + 1) * part
        total = keep_ref[at : at + part, :] + back_ref[at : at + part, :].astype(F32)
        ref[...] = total.astype(BF16)


def pair_sum(n_tp, keep, back, after=()):
    part = keep.shape[0] * 2 // n_tp
    model = keep.shape[1]
    return call(
        "pair_sum",
        pair_kernel,
        [(keep, "h"), (back, "v")],
        [((part, model), F32, "v")] + [((part, model), BF16, "v")] * (n_tp // 2 - 1),
        (),
        16,
        after,
    )


def total_kernel(count, *refs):
    total = refs[0][...]
    for ref in refs[1:count]:
        total = total + ref[...].astype(F32)
    refs[count][...] = total.astype(refs[count].dtype)


def total_of(parts, dtype=BF16, kind="v", after=()):
    (out,) = call(
        "total_of",
        functools.partial(total_kernel, len(parts)),
        kinds(parts, kind),
        [(parts[0].shape, dtype, kind)],
        (),
        16,
        after,
    )
    return out


def body(
    n_seq,
    n_tp,
    tokens,
    gain_one,
    w_qkv,
    w_out,
    gain_two,
    w_in,
    w_down,
    cotangent,
    doc_lengths,
    roster,
):
    rows, model = tokens.shape
    width = w_qkv.shape[2]
    units = w_in.shape[2]
    count = n_seq // 2
    qkv_t = w_qkv.transpose(1, 2, 0).reshape(3 * width, model)
    in_t = w_in.transpose(1, 2, 0).reshape(2 * units, model)
    over_tp = lambda x, k: swap(x, "tp", k, n_tp)
    over_chips = lambda x, k: swap(x, "seq", 2 * k, n_seq)
    over_cores = lambda x: swap(x, "seq", 1, n_seq)
    everywhere = lambda xs: [xs[0]] + [over_tp(xs[k], k) for k in range(1, n_tp)]

    def by_steps(part):
        parts = {0: part}
        hop = n_tp // 2
        while hop:
            parts.update({k ^ hop: over_tp(x, hop) for k, x in parts.items()})
            hop //= 2
        return [parts[k] for k in range(n_tp)]

    docs = (doc_lengths, roster)

    queries, kv, h_one, cos_table, sin_table = project(*docs, tokens, gain_one, qkv_t)
    blocks = [kv] + [over_chips(kv, j) for j in range(1, count)]
    q_pair = over_cores(queries)
    w_full = lax.all_gather(w_out, "tp", axis=0, tiled=True)

    split = (count + 1) // 2
    (state,) = attention_forward(0, False, *docs, queries, q_pair, blocks[:split])
    state_own, state_pair = attention_forward(
        split, True, *docs, queries, q_pair, blocks[split:], state
    )
    out_b, totals = join(state_own, over_cores(state_pair))
    outs = everywhere([out_b] * n_tp)
    out_pair = over_cores(out_b)
    totals_pair = over_cores(totals)

    middle, h_two, mixed, gate_grad, gain_two_part, *parts = feed(
        tokens, cotangent, gain_two, in_t, w_down, w_full, outs
    )
    early = early_grads(mixed, gate_grad, cotangent, h_two)
    keep, send = down(n_tp, mixed, w_down, middle, [(early, "h")])
    middle_grad, branch_grad, *pieces = branch(
        middle, cotangent, gain_two, w_full, everywhere(parts), [(keep, "h")]
    )
    early = lax.psum(early, "seq")
    grad_down, grad_in = parted(early, (units, 2 * units))
    out_grad = lay_turned(everywhere(pieces))
    grad_pair = over_cores(out_grad)
    branches = by_steps(branch_grad)

    own, *others = pair_sum(n_tp, keep, over_tp(send, 1), [(out_grad, "v")])
    total = total_of(
        [own] + [over_tp(others[k], 2 * k + 2) for k in range(n_tp // 2 - 1)], BF16
    )
    totals_all = by_steps(total)

    held = (queries, q_pair, out_grad, grad_pair, out_b, out_pair, totals, totals_pair)
    *terms, dq = attention_backward(1, False, *docs, held, blocks[1:], None, [(own, "v")])
    dkv, dq_own, dq_pair = attention_backward(0, True, *docs, held, blocks[:1], dq)
    dkvs = [dkv] + [over_chips(terms[j - 1], j) for j in range(1, count)]

    proj_grad, *parts = unproject(
        n_tp,
        tokens,
        qkv_t,
        cos_table,
        sin_table,
        gain_two_part,
        dq_own,
        over_cores(dq_pair),
        dkvs,
        [(total, "v")],
    )
    layer_out = stack_parts(totals_all)
    keep, send = late_grads(proj_grad, h_one, out_b, branches, [(totals_all[n_tp // 2], "v")])
    own, *others = spread(count, keep, over_cores(send))
    chip_sum = total_of([own] + [over_chips(others[k - 1], k) for k in range(1, count)], F32)
    input_part, gains = input_side(
        tokens, gain_one, middle_grad, everywhere(parts), [(own, "v")]
    )
    inputs_all = everywhere([input_part] * n_tp)
    piece = sum_piece(gains, [chip_sum], [(layer_out, "h")])
    input_grad = stack_parts(inputs_all)
    collected = collect(
        [piece] + [over_chips(piece, k) for k in range(1, count)], [(input_grad, "h"), (grad_down, "h")]
    )
    grad_qkv, grad_out, grad_one, grad_two = finish(
        collected, over_cores(collected), 3 * width
    )

    back = lambda x, n: x.reshape(-1, n, model).transpose(2, 0, 1)
    return (
        layer_out,
        input_grad,
        grad_one,
        back(grad_qkv, width),
        grad_out,
        grad_two,
        back(grad_in, units),
        grad_down,
    )


def solution(mesh):
    placed = (
        P("seq", None),
        P(),
        P(None, None, "tp"),
        P("tp", None),
        P(),
        P(None, None, "tp"),
        P("tp", None),
        P("seq", None),
        P(),
        P(),
    )
    return jax.shard_map(
        functools.partial(body, mesh.shape["seq"], mesh.shape["tp"]),
        mesh=mesh,
        in_specs=placed,
        out_specs=(
            P("seq", None),
            P("seq", None),
            P(),
            P(None, None, "tp"),
            P("tp", None),
            P(),
            P(None, None, "tp"),
            P("tp", None),
        ),
        check_vma=False,
    )
```

```python
import functools

import jax
import jax.numpy as jnp
import numpy as np
from jax import lax
from jax.experimental import pallas as pl
from jax.experimental.pallas import tpu as pltpu
from jax.sharding import PartitionSpec as P

HDIM = 64
HALF = HDIM // 2
EPSILON = 1e-05
ROPE_THETA = 160000.0
MASKED = -1e30
AUG = 80
STRIP = 64
F32 = jnp.float32
BF16 = jnp.bfloat16
HBM = pl.BlockSpec(memory_space=pltpu.HBM)
VMEM = pl.BlockSpec(memory_space=pltpu.VMEM)

NN = (((1,), (0,)), ((), ()))
NT = (((1,), (1,)), ((), ()))
TN = (((0,), (0,)), ((), ()))


def params(mib):
    return pltpu.CompilerParams(vmem_limit_bytes=mib * 2**20)


def slot(tp, n_tp):
    return tp % 2 * (n_tp // 2) + tp // 2


def mm(a, b, dims):
    return lax.dot_general(a, b, dims, preferred_element_type=F32)


def shaped(shape, dtype):
    return jax.ShapeDtypeStruct(shape, dtype)


def kinds(arrays, kind):
    return [(array, kind) for array in arrays]


def pin(array, kind):
    return array if kind in ("v", "free") else pltpu.with_memory_space_constraint(array, pltpu.HBM)


def call(name, kernel, ins, outs, scratch=(), mib=16, after=(), lazy=False):
    fetched = [i for i, given in enumerate(ins) if given[1] not in ("v", "raw", "free")]
    left = [i for i, out in enumerate(outs) if out[2] == "h"]

    def held(array, kind):
        rows = array.shape[0] if kind == "h" else kind
        return pltpu.VMEM((rows,) + array.shape[1:], array.dtype)

    def run(*refs):
        in_refs = list(refs[: len(ins)])
        at = len(ins) + len(after)
        out_refs = list(refs[at : at + len(outs)])
        at += len(outs)
        own = refs[at : at + len(scratch)]
        at += len(scratch)
        buffers = refs[at : at + len(fetched) + len(left)]
        sems = refs[-1]
        copies = []
        for n, i in enumerate(fetched):
            source = in_refs[i]
            if ins[i][1] != "h":
                rows = ins[i][1]
                n_tp = ins[i][0].shape[0] // rows
                at = pl.multiple_of(slot(lax.axis_index("tp"), n_tp) * rows, rows)
                source = source.at[pl.ds(at, rows)]
            copies.append(pltpu.make_async_copy(source, buffers[n], sems.at[n]))
            in_refs[i] = buffers[n]
        for copy in copies:
            copy.start()
        coming = dict(zip(fetched, copies))
        going = {}
        for n, i in enumerate(left):
            spot = len(fetched) + n
            going[i] = pltpu.make_async_copy(buffers[spot], out_refs[i], sems.at[spot])
            out_refs[i] = buffers[spot]
        gone = []

        def need(*which):
            for i in which:
                if i in coming:
                    coming.pop(i).wait()

        def give(*which):
            for i in which:
                if i in going:
                    gone.append(going.pop(i))
                    gone[-1].start()

        if lazy:
            kernel(need, give, *in_refs, *out_refs, *own)
        else:
            need(*fetched)
            kernel(*in_refs, *out_refs, *own)
        need(*fetched)
        give(*left)
        for copy in gone:
            copy.wait()

    spec = lambda kind: VMEM if kind == "v" else HBM
    count = len(fetched) + len(left)
    return pl.pallas_call(
        run,
        out_shape=tuple(
            shaped(shape, dtype) if kind == "v" else pltpu.HBM(shape, dtype)
            for shape, dtype, kind in outs
        ),
        in_specs=[spec(kind) for unused, kind in ins] + [spec(kind) for unused, kind in after],
        out_specs=tuple(spec(kind) for unused, unused, kind in outs),
        scratch_shapes=list(scratch)
        + [held(*ins[i]) for i in fetched]
        + [pltpu.VMEM(outs[i][0], outs[i][1]) for i in left]
        + [pltpu.SemaphoreType.DMA((max(count, 1),))],
        name=name,
        compiler_params=params(mib),
    )(*[pin(*given) for given in ins], *[pin(*given) for given in after])


def swap(x, axis, hop, count):
    return lax.ppermute(x, axis, [(i, i ^ hop) for i in range(count)])


def doc_scratch(doc_lengths, roster):
    return [pltpu.SMEM(doc_lengths.shape, jnp.int32), pltpu.SMEM(roster.shape, jnp.int32)]


def fetch_docs(len_any, roster_any, len_ref, roster_ref, len_sem, roster_sem):
    one = pltpu.make_async_copy(len_any, len_ref, len_sem)
    two = pltpu.make_async_copy(roster_any, roster_ref, roster_sem)
    one.start()
    two.start()
    one.wait()
    two.wait()


def doc_bounds(len_ref):
    ends, total = [], jnp.int32(0)
    for d in range(len_ref.shape[0]):
        total = total + len_ref[d]
        ends.append(total)
    return ends


def doc_of(ends, position):
    found = jnp.int32(0)
    for end in ends:
        found = found + (end <= position).astype(jnp.int32)
    return found


def meet(ends, base_a, base_b, rows):
    low = jnp.maximum(doc_of(ends, base_a), doc_of(ends, base_b))
    high = jnp.minimum(doc_of(ends, base_a + rows - 1), doc_of(ends, base_b + rows - 1))
    return low <= high


def doc_rows(ends, base, rows):
    spot = base + lax.broadcasted_iota(jnp.int32, (16, rows), 1)
    line = lax.broadcasted_iota(jnp.int32, (16, rows), 0)
    held = jnp.zeros((16, rows), F32)
    start = jnp.int32(0)
    for d, end in enumerate(ends):
        inside = (line == d) & (spot >= start) & (spot < end)
        held = jnp.where(inside, 1.0, held)
        start = end
    return held


def ban_rows(ends, base, rows):
    line = lax.broadcasted_iota(jnp.int32, (16, rows), 0)
    held = doc_rows(ends, base, rows)
    return jnp.where((held > 0.5) | (line >= len(ends)), 0.0, MASKED)


def key_row(block, seq_index):
    return seq_index ^ (2 * block)


def place_row(ends, base, rows):
    spot = base + lax.broadcasted_iota(jnp.int32, (1, rows), 1)
    start = jnp.zeros((1, rows), jnp.int32)
    for end in ends:
        start = jnp.where(spot >= end, end, start)
    return (spot - start).astype(F32)


def normed(values):
    centre = jnp.mean(values, axis=-1, keepdims=True)
    shifted = values - centre
    spread = jnp.mean(shifted * shifted, axis=-1, keepdims=True)
    scale = lax.rsqrt(spread + EPSILON)
    return shifted * scale, scale


def norm_back(unit, scale, grad, gain):
    u = grad * gain
    mean_u = jnp.mean(u, axis=-1, keepdims=True)
    mean_un = jnp.mean(u * unit, axis=-1, keepdims=True)
    return scale * (u - mean_u - unit * mean_un)


def project_kernel(
    width, need, give, len_any, roster_any, x_ref, w_ref, gain_ref, freq_ref, *refs
):
    q_out, kv_out, h_out, cos_out, sin_out = refs[:5]
    proj, len_ref, roster_ref, sems = refs[5:]
    rows = x_ref.shape[0]
    fetch_docs(len_any, roster_any, len_ref, roster_ref, sems.at[0], sems.at[1])
    need(5)
    ends = doc_bounds(len_ref)
    place = place_row(ends, roster_ref[lax.axis_index("seq")] * rows, rows)
    angles = place * freq_ref[...]
    cos_table = jnp.cos(angles)
    sin_table = jnp.sin(angles)
    cos_out[...] = cos_table
    sin_out[...] = sin_table
    give(3, 4)
    need(2, 4)
    gain = gain_ref[...].reshape(1, -1)

    def strip(i, carry):
        at = pl.ds(i * STRIP, STRIP)
        unit, unused = normed(x_ref[at, :].astype(F32))
        h_out[at, :] = (unit * gain).astype(BF16)
        return carry

    lax.fori_loop(0, rows // STRIP, strip, 0)
    give(2)
    need(3)
    proj[...] = mm(w_ref[...], h_out[...], NT)
    for at in range(0, 2 * width, HDIM):
        low = proj[at : at + HALF, :]
        high = proj[at + HALF : at + HDIM, :]
        turned_low = (low * cos_out[...] - high * sin_out[...]).astype(BF16)
        turned_high = (high * cos_out[...] + low * sin_out[...]).astype(BF16)
        if at < width:
            q_out[at : at + HALF, :] = (turned_low.astype(F32) * HDIM**-0.5).astype(BF16)
            q_out[at + HALF : at + HDIM, :] = (turned_high.astype(F32) * HDIM**-0.5).astype(BF16)
        else:
            kv_out[at - width : at - width + HALF, :] = turned_low
            kv_out[at - width + HALF : at - width + HDIM, :] = turned_high
    kv_out[width:, :] = proj[2 * width :, :].astype(BF16)


def project(doc_lengths, roster, tokens, gain, qkv_t):
    rows, model = tokens.shape
    width = qkv_t.shape[0] // 3
    freq = (ROPE_THETA ** -(np.arange(HALF) * (2.0 / HDIM))).astype(np.float32)[:, None]
    return call(
        "project",
        functools.partial(project_kernel, width),
        kinds((doc_lengths, roster), "raw") + kinds((tokens, qkv_t, gain, jnp.asarray(freq)), "h"),
        [
            ((width, rows), BF16, "v"),
            ((2 * width, rows), BF16, "v"),
            ((rows, model), BF16, "h"),
            ((HALF, rows), F32, "h"),
            ((HALF, rows), F32, "h"),
        ],
        [pltpu.VMEM((3 * width, rows), F32)]
        + doc_scratch(doc_lengths, roster)
        + [pltpu.SemaphoreType.DMA((2,))],
        lazy=True,
    )


def forward_kernel(first, count, heads, last, len_any, roster_any, q_own, q_pair, *refs):
    kv_refs = refs[:count]
    refs = refs[count:]
    if first:
        state_in, refs = refs[0], refs[1:]
    outs = refs[: 2 if last else 1]
    kv, q_aug, state, len_ref, roster_ref, sems = refs[len(outs) :]
    rows = q_own.shape[1]
    width = heads * HDIM
    me = lax.axis_index("seq")
    copies = [pltpu.make_async_copy(kv_refs[j], kv.at[j], sems.at[j]) for j in range(count)]
    for copy in copies:
        copy.start()
    fetch_docs(len_any, roster_any, len_ref, roster_ref, sems.at[count], sems.at[count + 1])
    ends = doc_bounds(len_ref)
    bases = (roster_ref[me] * rows, roster_ref[me ^ 1] * rows)
    for g, q_ref in enumerate((q_own, q_pair)):
        mark = doc_rows(ends, bases[g], rows).astype(BF16)
        for h in range(heads):
            q_aug[g * heads + h, :HDIM, :] = q_ref[h * HDIM : (h + 1) * HDIM, :]
            q_aug[g * heads + h, HDIM:, :] = mark
    if first:
        state[...] = state_in[...]
    else:
        line = lax.broadcasted_iota(jnp.int32, (2 * heads, AUG, rows), 1)
        state[...] = jnp.where(line >= 72, MASKED, 0.0)
    for copy in copies:
        copy.wait()

    top = lax.broadcasted_iota(jnp.int32, (16, rows), 0) == 0
    ones = jnp.where(top, 1.0, 0.0).astype(BF16)

    def block(j, carry):
        key_base = roster_ref[key_row(j + first, me)] * rows
        ban = ban_rows(ends, key_base, rows).astype(BF16)
        for g in range(2):

            @pl.when(meet(ends, bases[g], key_base, rows))
            def _():
                for h in range(heads):
                    at = g * heads + h
                    keys = jnp.concatenate([kv[j, h * HDIM : (h + 1) * HDIM, :], ban], axis=0)
                    vals = jnp.concatenate(
                        [kv[j, width + h * HDIM : width + (h + 1) * HDIM, :], ones], axis=0
                    )
                    scores = mm(keys, q_aug[at], TN)
                    old = state[at, 72:73, :]
                    new = jnp.maximum(old, jnp.max(scores, axis=0, keepdims=True))
                    probs = jnp.exp(scores - new).astype(BF16)
                    part = mm(vals, probs, NN)
                    fade = jnp.exp(old - new)
                    state[at, :72, :] = state[at, :72, :] * fade + part[:72]
                    state[at, 72:, :] = jnp.broadcast_to(new, (8, rows))

        return carry

    lax.fori_loop(0, count, block, 0)
    if last:
        outs[0][...] = state[:heads]
        outs[1][...] = state[heads:]
    else:
        outs[0][...] = state[...]


def attention_forward(first, last, doc_lengths, roster, q_own, q_pair, blocks, state=None, after=()):
    width, rows = q_own.shape
    heads = width // HDIM
    count = len(blocks)
    half = ((heads, AUG, rows), F32, "v")
    whole = ((2 * heads, AUG, rows), F32, "v")
    given = [] if state is None else [(state, "v")]
    return call(
        "attention_forward",
        functools.partial(forward_kernel, first, count, heads, last),
        [(doc_lengths, "raw"), (roster, "raw"), (q_own, "v"), (q_pair, "v")]
        + kinds(blocks, "free")
        + given,
        [half, half] if last else [whole],
        [
            pltpu.VMEM((count, 2 * width, rows), BF16),
            pltpu.VMEM((2 * heads, AUG, rows), BF16),
            pltpu.VMEM((2 * heads, AUG, rows), F32),
        ]
        + doc_scratch(doc_lengths, roster)
        + [pltpu.SemaphoreType.DMA((count + 2,))],
        16 if count < 8 else 40,
        after,
    )


def backward_kernel(first, count, heads, more, last, len_any, roster_any, *refs):
    q_own, q_pair, g_own, g_pair, o_own, o_pair, t_own, t_pair = refs[:8]
    kv_refs, refs = refs[8 : 8 + count], refs[8 + count :]
    if more:
        dq_in, refs = refs[0], refs[1:]
    outs, refs = refs[:count], refs[count:]
    dq_outs, refs = (refs[:2], refs[2:]) if last else (refs[:1], refs[1:])
    kv, q_aug, delta, dq, dkv, len_ref, roster_ref, sems = refs
    rows = q_own.shape[1]
    width = heads * HDIM
    me = lax.axis_index("seq")
    copies = [pltpu.make_async_copy(kv_refs[j], kv.at[j], sems.at[j]) for j in range(count)]
    for copy in copies:
        copy.start()
    fetch_docs(len_any, roster_any, len_ref, roster_ref, sems.at[count], sems.at[count + 1])
    ends = doc_bounds(len_ref)
    bases = (roster_ref[me] * rows, roster_ref[me ^ 1] * rows)
    for g, (q_ref, g_ref, o_ref) in enumerate(((q_own, g_own, o_own), (q_pair, g_pair, o_pair))):
        mark = doc_rows(ends, bases[g], rows).astype(BF16)
        for h in range(heads):
            part = slice(h * HDIM, (h + 1) * HDIM)
            q_aug[g * heads + h, :HDIM, :] = q_ref[part, :]
            q_aug[g * heads + h, HDIM:, :] = mark
            product = g_ref[part, :].astype(F32) * o_ref[part, :].astype(F32)
            delta[g * heads + h] = jnp.broadcast_to(
                jnp.sum(product, axis=0, keepdims=True), (8, rows)
            )
    if more:
        dq[...] = dq_in[...]
    else:
        dq[...] = jnp.zeros_like(dq)
    for copy in copies:
        copy.wait()

    def block(j, carry):
        key_base = roster_ref[key_row(j + first, me)] * rows
        ban = ban_rows(ends, key_base, rows).astype(BF16)
        dkv[j] = jnp.zeros((2 * width, rows), F32)
        for g, (g_ref, t_ref) in enumerate(((g_own, t_own), (g_pair, t_pair))):

            @pl.when(meet(ends, bases[g], key_base, rows))
            def _():
                for h in range(heads):
                    at = g * heads + h
                    part = slice(h * HDIM, (h + 1) * HDIM)
                    late = slice(width + h * HDIM, width + (h + 1) * HDIM)
                    keys = kv[j, part, :]
                    scores = mm(jnp.concatenate([keys, ban], axis=0), q_aug[at], TN)
                    probs = jnp.exp(scores - t_ref[h, 0:1, :])
                    prob_grads = mm(kv[j, late, :], g_ref[part, :], TN)
                    score_grad = (probs * (prob_grads - delta[at, 0:1, :])).astype(BF16)
                    dkv[j, late, :] += mm(g_ref[part, :], probs.astype(BF16), NT)
                    dkv[j, part, :] += mm(q_aug[at, :HDIM, :], score_grad, NT)
                    dq[at] += mm(keys, score_grad, NN)

        return carry

    lax.fori_loop(0, count, block, 0)
    for j in range(count):
        outs[j][...] = dkv[j].astype(outs[j].dtype)
    if last:
        for h in range(heads):
            part = slice(h * HDIM, (h + 1) * HDIM)
            dq_outs[0][part, :] = dq[h] * HDIM**-0.5
            dq_outs[1][part, :] = (dq[heads + h] * HDIM**-0.5).astype(BF16)
    else:
        dq_outs[0][...] = dq[...]


def attention_backward(first, last, doc_lengths, roster, held, blocks, dq=None, after=()):
    width, rows = held[0].shape
    heads = width // HDIM
    count = len(blocks)
    given = [] if dq is None else [(dq, "v")]
    if last:
        queries = [((width, rows), F32, "v"), ((width, rows), BF16, "v")]
    else:
        queries = [((2 * heads, HDIM, rows), F32, "v")]
    return call(
        "attention_backward",
        functools.partial(backward_kernel, first, count, heads, bool(given), last),
        kinds((doc_lengths, roster), "raw") + kinds(held, "v") + kinds(blocks, "free") + given,
        [((2 * width, rows), BF16 if first else F32, "v")] * count + queries,
        [
            pltpu.VMEM((count, 2 * width, rows), BF16),
            pltpu.VMEM((2 * heads, AUG, rows), BF16),
            pltpu.VMEM((2 * heads, 8, rows), F32),
            pltpu.VMEM((2 * heads, HDIM, rows), F32),
            pltpu.VMEM((count, 2 * width, rows), F32),
        ]
        + doc_scratch(doc_lengths, roster)
        + [pltpu.SemaphoreType.DMA((count + 2,))],
        16 if count < 8 else 40,
        after,
    )


def join_kernel(heads, own_ref, back_ref, out_ref, total_ref, mine_ref, other_ref):
    rows = own_ref.shape[2]
    for h in range(heads):
        top_own = own_ref[h, 72:73, :]
        top_back = back_ref[h, 72:73, :]
        top = jnp.maximum(top_own, top_back)
        fade_own = jnp.exp(top_own - top)
        fade_back = jnp.exp(top_back - top)
        total = own_ref[h, 64:65, :] * fade_own + back_ref[h, 64:65, :] * fade_back
        share_own = fade_own / total
        share_back = fade_back / total
        value = own_ref[h, :HDIM, :] * share_own + back_ref[h, :HDIM, :] * share_back
        out_ref[h * HDIM : (h + 1) * HDIM, :] = value.astype(BF16)
        total_ref[h] = jnp.broadcast_to(top + jnp.log(total), (8, rows))
    half = rows // 2
    for bit in range(2):

        @pl.when(lax.axis_index("tp") % 2 == bit)
        def _():
            mine_ref[...] = out_ref[:, bit * half : (bit + 1) * half]
            other_ref[...] = out_ref[:, (1 - bit) * half : (2 - bit) * half]


def join(own, back):
    heads, unused, rows = own.shape
    return call(
        "join",
        functools.partial(join_kernel, heads),
        [(own, "v"), (back, "v")],
        [
            ((heads * HDIM, rows), BF16, "v"),
            ((heads, 8, rows), F32, "v"),
            ((heads * HDIM, rows // 2), BF16, "v"),
            ((heads * HDIM, rows // 2), BF16, "v"),
        ],
    )


def stage_kernel(x_any, cot_any, w_any, in_any, in_pair, down_any, down_pair, *refs):
    x_ref, cot_ref, w_ref, in_ref, down_ref, sems = refs
    half = x_ref.shape[0]
    mine = pl.ds(pl.multiple_of(lax.axis_index("tp") % 2 * half, half), half)
    moves = [(w_any, w_ref), (x_any.at[mine], x_ref), (cot_any.at[mine], cot_ref)]
    for (own, pair), ref in (((down_any, down_pair), down_ref), ((in_any, in_pair), in_ref)):
        rows = own.shape[0]
        moves.append((own, ref.at[pl.ds(0, rows)]))
        moves.append((pair, ref.at[pl.ds(rows, rows)]))
    copies = [pltpu.make_async_copy(*move, sems.at[n]) for n, move in enumerate(moves)]
    for copy in copies:
        copy.start()
    for copy in copies:
        copy.wait()


def stage(tokens, cotangent, w_full, in_t, in_pair, w_down, down_pair):
    rows, model = tokens.shape
    return call(
        "stage",
        stage_kernel,
        kinds((tokens, cotangent, w_full, in_t, in_pair, w_down, down_pair), "raw"),
        [
            ((rows // 2, model), BF16, "v"),
            ((rows // 2, model), BF16, "v"),
            (w_full.shape, BF16, "v"),
            ((2 * in_t.shape[0], model), BF16, "v"),
            ((2 * w_down.shape[0], model), BF16, "v"),
        ],
        [pltpu.SemaphoreType.DMA((7,))],
    )


def gated(units, first, gate_up, mixed_grad, mixed_out, gate_out):
    def wave(i, carry):
        spot = pl.ds(first + i * 32, 32)
        at = pl.ds(2 * first + i * 32, 32)
        late = pl.ds(2 * first + units + i * 32, 32)
        gate = gate_up[at, :]
        up = gate_up[late, :]
        back = mixed_grad[spot, :]
        bell = 0.5 * (1.0 + lax.erf(gate * (2.0**-0.5)))
        active = gate * bell
        slope = bell + gate * jnp.exp(-0.5 * gate * gate) * ((2.0 * jnp.pi) ** -0.5)
        mixed_out[spot, :] = (active * up).astype(BF16)
        gate_out[at, :] = (back * up * slope).astype(BF16)
        gate_out[late, :] = (back * active).astype(BF16)
        return carry

    lax.fori_loop(0, units // 32, wave, 0)


def feed_kernel(n_tp, need, give, x_ref, cot_ref, w_ref, in_ref, down_ref, gain_ref, *refs):
    out_refs = refs[:n_tp]
    middle_out, part_out, h_out, mixed_out, gate_out, gain_out = refs[n_tp : n_tp + 6]
    keep_ref, *send_refs = refs[n_tp + 6 : n_tp + 6 + n_tp // 2]
    outs, unit, gate_up, mixed_grad, grad = refs[n_tp + 6 + n_tp // 2 :]
    rows = x_ref.shape[0]
    part = keep_ref.shape[0]
    units = down_ref.shape[0] // 2
    width = out_refs[0].shape[0]
    tp = lax.axis_index("tp")
    for k in range(n_tp):
        at = pl.ds(pl.multiple_of((tp ^ k) * width, width), width)
        outs[at, :] = out_refs[k][...]
    mixed_grad[...] = mm(down_ref[...], cot_ref[...], NT)
    middle_out[...] = mm(outs[...], w_ref[...], TN)
    need(5)
    gain = gain_ref[...].reshape(1, -1)

    def strip(i, carry):
        at = pl.ds(i * 32, 32)
        middle = middle_out[at, :] + x_ref[at, :].astype(F32)
        middle_out[at, :] = middle
        held, unused = normed(middle)
        unit[at, :] = held
        h_out[at, :] = (held * gain).astype(BF16)
        return carry

    lax.fori_loop(0, rows // 32, strip, 0)
    give(0, 2)
    gate_up[...] = mm(in_ref[...], h_out[...], NT)
    for first in (0, units):
        gated(units, first, gate_up, mixed_grad, mixed_out, gate_out)
    give(3, 4)
    grad[...] = mm(gate_out[...], in_ref[...], TN)
    for n, ref in enumerate((keep_ref, *send_refs)):
        at = pl.ds(pl.multiple_of((tp ^ (2 * n)) // 2 * part, part), part)
        ref[...] = grad[at, :].astype(ref.dtype)
        give(6 + n)
    own = pl.ds(pl.multiple_of(tp // 2 * part, part), part)
    part_out[...] = middle_out[own, :]
    give(1)

    def gains(i, carry):
        at = pl.ds(i * 32, 32)
        product = grad[at, :] * unit[at, :]
        return carry + jnp.sum(product.reshape(4, 8, -1), axis=0)

    gain_out[...] = lax.fori_loop(0, rows // 32, gains, jnp.zeros(gain_out.shape, F32))


def feed(gain, staged, outs):
    rows, model = staged[0].shape
    n_tp = len(outs)
    units = staged[4].shape[0]
    part = 2 * rows // n_tp
    return call(
        "feed",
        functools.partial(feed_kernel, n_tp),
        kinds(staged, "v") + [(gain, "h")] + kinds(outs, "v"),
        [
            ((rows, model), F32, "h"),
            ((part, model), F32, "h"),
            ((rows, model), BF16, "h"),
            ((units, rows), BF16, "h"),
            ((2 * units, rows), BF16, "h"),
            ((8, model), F32, "h"),
            ((part, model), F32, "h"),
        ]
        + [((part, model), BF16, "h")] * (n_tp // 2 - 1),
        [
            pltpu.VMEM((n_tp * outs[0].shape[0], rows), BF16),
            pltpu.VMEM((rows, model), F32),
            pltpu.VMEM((2 * units, rows), F32),
            pltpu.VMEM((units, rows), F32),
            pltpu.VMEM((rows, model), F32),
        ],
        24,
        lazy=True,
    )


def branch_kernel(n_tp, count, need, give, middle_ref, cot_ref, gain_ref, w_ref, *refs):
    arrived = refs[:count]
    grad_out, branch_out = refs[count : count + 2]
    piece_refs = refs[count + 2 :]
    width = piece_refs[0].shape[1]
    tp = lax.axis_index("tp")
    need(0, 1, 2, 4)
    total = arrived[0][...]
    for ref in arrived[1:]:
        total = total + ref[...].astype(F32)
    unit, scale = normed(middle_ref[...])
    gain = gain_ref[...].reshape(1, -1)
    value = cot_ref[...].astype(F32) + norm_back(unit, scale, total, gain)
    grad_out[...] = value
    branch_out[...] = value.astype(BF16)
    give(0, 1)
    need(3)
    for k in range(n_tp):
        at = pl.ds(pl.multiple_of((tp ^ k) * width, width), width)
        piece_refs[k][...] = mm(branch_out[...], w_ref[at, :], NT).astype(BF16)


def branch(n_tp, middle_part, cotangent, gain, w_full, arrived, after):
    part, model = arrived[0].shape
    width = w_full.shape[0] // n_tp
    return call(
        "branch",
        functools.partial(branch_kernel, n_tp, len(arrived)),
        [(middle_part, "h"), (cotangent, part)]
        + kinds((gain, w_full, arrived[0]), "h")
        + kinds(arrived[1:], "v"),
        [((part, model), F32, "h"), ((part, model), BF16, "h")]
        + [((part, width), BF16, "v")] * n_tp,
        (),
        16,
        after,
        True,
    )


def lay_kernel(n_tp, *refs):
    out_ref, held = refs[n_tp:]
    part = refs[0].shape[0]
    tp = lax.axis_index("tp")
    for k in range(n_tp):
        at = pl.ds(pl.multiple_of(slot(tp ^ k, n_tp) * part, part), part)
        held[at, :] = refs[k][...].astype(F32)
    out_ref[...] = held[...].T.astype(BF16)


def lay_turned(pieces, after):
    part, width = pieces[0].shape
    rows = part * len(pieces)
    (out,) = call(
        "lay_turned",
        functools.partial(lay_kernel, len(pieces)),
        kinds(pieces, "v"),
        [((width, rows), BF16, "v")],
        [pltpu.VMEM((rows, width), F32)],
        16,
        after,
    )
    return out


def stack_kernel(n_tp, *refs):
    out_ref = refs[n_tp]
    part = refs[0].shape[0]
    tp = lax.axis_index("tp")
    for k in range(n_tp):
        at = pl.ds(pl.multiple_of(slot(tp ^ k, n_tp) * part, part), part)
        out_ref[at, :] = refs[k][...]


def stack_parts(pieces, after=()):
    part, model = pieces[0].shape
    (out,) = call(
        "stack_parts",
        functools.partial(stack_kernel, len(pieces)),
        kinds(pieces, "v"),
        [((part * len(pieces), model), pieces[0].dtype, "h")],
        (),
        16,
        after,
    )
    return out


def turn_back(out_ref, first, value, cos_table, sin_table):
    for at in range(0, value.shape[0], HDIM):
        low = value[at : at + HALF]
        high = value[at + HALF : at + HDIM]
        spot = first + at
        out_ref[spot : spot + HALF, :] = (low * cos_table + high * sin_table).astype(BF16)
        out_ref[spot + HALF : spot + HDIM, :] = (high * cos_table - low * sin_table).astype(BF16)


def unproject_kernel(
    count, n_tp, need, give, x_ref, w_ref, cos_ref, sin_ref, two_ref, dq_ref, dq_back, *refs
):
    dkv_refs = refs[:count]
    proj_out = refs[count]
    part_refs = refs[count + 1 : count + 1 + n_tp]
    grad, dkv = refs[count + 1 + n_tp :]
    rows, model = x_ref.shape
    part = rows // n_tp
    width = dq_ref.shape[0]
    tp = lax.axis_index("tp")
    need(2, 3)
    cos_table = cos_ref[...]
    sin_table = sin_ref[...]
    turn_back(proj_out, 0, dq_ref[...] + dq_back[...].astype(F32), cos_table, sin_table)
    total = dkv_refs[0][...]
    for ref in dkv_refs[1:]:
        total = total + ref[...].astype(F32)
    dkv[...] = total
    turn_back(proj_out, width, dkv[:width, :], cos_table, sin_table)
    proj_out[2 * width :, :] = dkv[width:, :].astype(BF16)
    need(1)
    grad[...] = mm(proj_out[...], w_ref[...], TN)
    need(0, 4)

    def gains(i, carry):
        at = pl.ds(i * STRIP, STRIP)
        unit, unused = normed(x_ref[at, :].astype(F32))
        product = grad[at, :] * unit
        return carry + jnp.sum(product.reshape(STRIP // 8, 8, -1), axis=0)

    gain = lax.fori_loop(0, rows // STRIP, gains, jnp.zeros((8, model), F32))
    line = lax.broadcasted_iota(jnp.int32, (16, model), 0)
    gain_two = jnp.sum(two_ref[...], axis=0, keepdims=True)
    gain = jnp.sum(gain, axis=0, keepdims=True)
    gain = jnp.where(line == 0, gain, jnp.where(line == 1, gain_two, 0.0))
    for k in range(n_tp):
        at = pl.ds(pl.multiple_of(slot(tp ^ k, n_tp) * part, part), part)
        part_refs[k][:part, :] = grad[at, :].astype(part_refs[k].dtype)
        part_refs[k][part:, :] = gain.astype(part_refs[k].dtype)


def unproject(n_tp, tokens, qkv_t, cos_table, sin_table, gain_two_part, dq, dq_back, dkvs, after):
    rows, model = tokens.shape
    part = rows // n_tp
    return call(
        "unproject",
        functools.partial(unproject_kernel, len(dkvs), n_tp),
        kinds((tokens, qkv_t, cos_table, sin_table, gain_two_part), "v")
        + kinds((dq, dq_back, *dkvs), "v"),
        [((qkv_t.shape[0], rows), BF16, "v"), ((part + 16, model), F32, "v")]
        + [((part + 16, model), BF16, "v")] * (n_tp - 1),
        [pltpu.VMEM((rows, model), F32), pltpu.VMEM(dkvs[0].shape, F32)],
        16,
        after,
        True,
    )


def input_kernel(n_tp, x_ref, gain_ref, grad_ref, *refs):
    arrived = refs[:n_tp]
    out_ref, gain_out = refs[n_tp:]
    part, model = grad_ref.shape
    total = arrived[0][...]
    for ref in arrived[1:]:
        total = total + ref[...].astype(F32)
    unit, scale = normed(x_ref[...].astype(F32))
    gain = gain_ref[...].reshape(1, -1)
    value = grad_ref[...] + norm_back(unit, scale, total[:part], gain)
    out_ref[...] = value.astype(BF16)
    gain_out[...] = total[part : part + 8]


def input_side(tokens, gain, middle_grad, arrived, after):
    part, model = middle_grad.shape
    return call(
        "input_side",
        functools.partial(input_kernel, len(arrived)),
        [(tokens, part), (gain, "h"), (middle_grad, "v")] + kinds(arrived, "v"),
        [((part, model), BF16, "v"), ((8, model), F32, "v")],
        (),
        16,
        after,
    )


def early_kernel(mixed_ref, gate_ref, cot_ref, h_ref, in_ref, down_ref, h_pair, out_ref, *refs):
    gate_up, mixed_grad, mixed, gate = refs
    units = down_ref.shape[0]
    half = h_ref.shape[0]
    bit = lax.axis_index("tp") % 2
    mine = pl.ds(pl.multiple_of(bit * half, half), half)
    other = pl.ds(pl.multiple_of((1 - bit) * half, half), half)
    gate_up[...] = mm(in_ref[...], h_pair[...], NT)
    mixed_grad[...] = mm(down_ref[...], cot_ref[other, :], NT)
    gated(units, 0, gate_up, mixed_grad, mixed, gate)
    out_ref[:units, :] = mm(mixed_ref[:units, :], cot_ref[mine, :], NN)
    out_ref[:units, :] += mm(mixed[...], cot_ref[other, :], NN)
    out_ref[units : 3 * units, :] = mm(gate_ref[: 2 * units, :], h_ref[...], NN)
    out_ref[units : 3 * units, :] += mm(gate[...], h_pair[...], NN)
    if out_ref.shape[0] > 3 * units:
        out_ref[3 * units :, :] = jnp.zeros((out_ref.shape[0] - 3 * units, out_ref.shape[1]), F32)


def early_grads(mixed, gate_grad, cotangent, h_two, in_t, w_down, h_pair, after):
    units, model = w_down.shape
    half = h_two.shape[0]
    (out,) = call(
        "early_grads",
        early_kernel,
        kinds((mixed, gate_grad, cotangent, h_two, in_t, w_down), "h") + [(h_pair, "v")],
        [((7 * units // 2, model), F32, "h")],
        [
            pltpu.VMEM((2 * units, half), F32),
            pltpu.VMEM((units, half), F32),
            pltpu.VMEM((units, half), BF16),
            pltpu.VMEM((2 * units, half), BF16),
        ],
        24,
        after,
    )
    return out


def part_kernel(in_any, *refs):
    out_refs, held, sem = refs[:-2], refs[-2], refs[-1]
    rows = held.shape[0]
    copy = pltpu.make_async_copy(in_any.at[pl.ds(0, rows)], held, sem)
    copy.start()
    copy.wait()
    at = 0
    for ref in out_refs:
        ref[...] = held[at : at + ref.shape[0], :]
        at += ref.shape[0]


def parted(value, sizes):
    model = value.shape[1]
    return call(
        "parted",
        part_kernel,
        [(value, "raw")],
        [((size, model), F32, "h") for size in sizes],
        [pltpu.VMEM((sum(sizes), model), F32), pltpu.SemaphoreType.DMA],
    )


def late_kernel(n_tp, proj_ref, h_ref, out_ref, *refs):
    branch_refs = refs[:n_tp]
    keep_ref, send_ref, branch_full = refs[n_tp:]
    part = branch_refs[0].shape[0]
    half = keep_ref.shape[1]
    wide = proj_ref.shape[0]
    tp = lax.axis_index("tp")
    core = lax.axis_index("seq") % 2
    for k in range(n_tp):
        at = pl.ds(pl.multiple_of(slot(tp ^ k, n_tp) * part, part), part)
        branch_full[at, :] = branch_refs[k][...]
    for ref, side in ((send_ref, 1 - core), (keep_ref, core)):
        columns = pl.ds(pl.multiple_of(side * half, half), half)
        ref[:wide, :] = mm(proj_ref[...], h_ref[:, columns], NN).astype(ref.dtype)
        ref[wide:, :] = mm(out_ref[...], branch_full[:, columns], NN).astype(ref.dtype)


def late_grads(proj_grad, h_one, out_b, branches, after):
    rows, model = h_one.shape
    wide = proj_grad.shape[0] + out_b.shape[0]
    return call(
        "late_grads",
        functools.partial(late_kernel, len(branches)),
        [(proj_grad, "v"), (h_one, "v"), (out_b, "v"), (branches[0], "v")]
        + kinds(branches[1:], "v"),
        [((wide, model // 2), F32, "v"), ((wide, model // 2), BF16, "v")],
        [pltpu.VMEM((rows, model), BF16)],
        16,
        after,
    )


def spread_kernel(count, keep_ref, back_ref, *refs):
    held = refs[count]
    piece = refs[0].shape[0]
    chip = lax.axis_index("seq") // 2
    held[...] = keep_ref[...] + back_ref[...].astype(F32)
    for k in range(count):
        at = pl.ds(pl.multiple_of((chip ^ k) * piece, piece), piece)
        refs[k][...] = held[at, :].astype(refs[k].dtype)


def spread(count, keep, back):
    wide, half = keep.shape
    piece = wide // count
    return call(
        "spread",
        functools.partial(spread_kernel, count),
        [(keep, "v"), (back, "v")],
        [((piece, half), F32, "v")] + [((piece, half), BF16, "v")] * (count - 1),
        [pltpu.VMEM((wide, half), F32)],
    )


def piece_kernel(count, gain_ref, *refs):
    out_ref = refs[count]
    half = out_ref.shape[1]
    total = refs[0][...]
    for ref in refs[1:count]:
        total = total + ref[...].astype(F32)
    line = lax.broadcasted_iota(jnp.int32, (16, half), 0)
    gains = jnp.zeros((16, half), F32)
    for at in range(4):
        row = gain_ref[at // 2 : at // 2 + 1, at % 2 * half : (at % 2 + 1) * half]
        gains = jnp.where(line == at, row, gains)
    out_ref[...] = jnp.concatenate([total, gains], axis=0).astype(BF16)


def sum_piece(gains, pieces, after=()):
    piece, half = pieces[0].shape
    (out,) = call(
        "sum_piece",
        functools.partial(piece_kernel, len(pieces)),
        [(gains, "v")] + kinds(pieces, "v"),
        [((piece + 16, half), BF16, "v")],
        (),
        16,
        after,
    )
    return out


def collect_kernel(count, *refs):
    out_ref, held = refs[count:]
    piece = refs[0].shape[0] - 16
    wide = count * piece
    chip = lax.axis_index("seq") // 2
    gains = jnp.zeros((16, out_ref.shape[1]), F32)
    for k in range(count):
        at = pl.ds(pl.multiple_of((chip ^ k) * piece, piece), piece)
        whole = refs[k][...].astype(F32)
        held[at, :] = whole[:piece]
        gains = gains + whole[piece:]
    held[wide:, :] = gains
    out_ref[...] = held[...].astype(BF16)


def collect(pieces, after=()):
    piece, half = pieces[0].shape
    wide = (piece - 16) * len(pieces) + 16
    (out,) = call(
        "collect",
        functools.partial(collect_kernel, len(pieces)),
        kinds(pieces, "v"),
        [((wide, half), BF16, "v")],
        [pltpu.VMEM((wide, half), F32)],
        16,
        after,
    )
    return out


def finish_kernel(own_ref, pair_ref, qkv_ref, out_ref, one_ref, two_ref):
    half = own_ref.shape[1]
    wide, tall = qkv_ref.shape[0], out_ref.shape[0]
    core = lax.axis_index("seq") % 2
    for ref, side in ((own_ref, core), (pair_ref, 1 - core)):
        columns = pl.ds(pl.multiple_of(side * half, half), half)
        qkv_ref[:, columns] = ref[:wide, :].astype(F32)
        out_ref[:, columns] = ref[wide : wide + tall, :].astype(F32)
    gains = own_ref[wide + tall :, :].astype(F32) + pair_ref[wide + tall :, :].astype(F32)
    for at, ref in ((0, one_ref), (2, two_ref)):
        ref[pl.ds(0, half)] = gains[at]
        ref[pl.ds(half, half)] = gains[at + 1]


def finish(own, pair, wide, after=()):
    half = own.shape[1]
    tall = own.shape[0] - 16 - wide
    model = 2 * half
    return call(
        "finish",
        finish_kernel,
        [(own, "v"), (pair, "v")],
        [
            ((wide, model), F32, "h"),
            ((tall, model), F32, "h"),
            ((model,), F32, "h"),
            ((model,), F32, "h"),
        ],
        (),
        16,
        after,
    )


def down_kernel(mixed_ref, w_ref, w_pair, middle_ref, keep_ref, *refs):
    send_refs, total = refs[:-1], refs[-1]
    part = keep_ref.shape[0]
    units = w_ref.shape[0]
    tp = lax.axis_index("tp")
    total[...] = mm(mixed_ref[:units, :], w_ref[...], TN)
    total[...] += mm(mixed_ref[units:, :], w_pair[...], TN)
    own = pl.ds(pl.multiple_of(tp // 2 * part, part), part)
    keep_ref[...] = total[own, :] + middle_ref[own, :]
    for n, ref in enumerate(send_refs):
        at = pl.ds(pl.multiple_of((tp ^ (2 * n + 2)) // 2 * part, part), part)
        ref[...] = total[at, :].astype(ref.dtype)


def down(n_tp, mixed, w_down, down_pair, middle, after):
    rows, model = middle.shape
    part = 2 * rows // n_tp
    return call(
        "down",
        down_kernel,
        kinds((mixed, w_down, down_pair, middle), "h"),
        [((part, model), F32, "h")] + [((part, model), BF16, "h")] * (n_tp // 2 - 1),
        [pltpu.VMEM((rows, model), F32)],
        16,
        after,
    )


def total_kernel(count, *refs):
    total = refs[0][...]
    for ref in refs[1:count]:
        total = total + ref[...].astype(F32)
    refs[count][...] = total.astype(refs[count].dtype)


def total_of(parts, dtype=BF16, kind="v", after=()):
    (out,) = call(
        "total_of",
        functools.partial(total_kernel, len(parts)),
        [(parts[0], kind)] + kinds(parts[1:], "v"),
        [(parts[0].shape, dtype, "v")],
        (),
        16,
        after,
    )
    return out


def body(
    n_seq,
    n_tp,
    tokens,
    gain_one,
    w_qkv,
    w_out,
    gain_two,
    w_in,
    w_down,
    cotangent,
    doc_lengths,
    roster,
):
    rows, model = tokens.shape
    width = w_qkv.shape[2]
    units = w_in.shape[2]
    count = n_seq // 2
    qkv_t = w_qkv.transpose(1, 2, 0).reshape(3 * width, model)
    in_t = w_in.transpose(1, 2, 0).reshape(2 * units, model)
    over_tp = lambda x, k: swap(x, "tp", k, n_tp)
    over_chips = lambda x, k: swap(x, "seq", 2 * k, n_seq)
    over_cores = lambda x: swap(x, "seq", 1, n_seq)
    everywhere = lambda xs: [xs[0]] + [over_tp(xs[k], k) for k in range(1, n_tp)]

    def by_steps(part):
        parts = {0: part}
        hop = n_tp // 2
        while hop:
            parts.update({k ^ hop: over_tp(x, hop) for k, x in parts.items()})
            hop //= 2
        return [parts[k] for k in range(n_tp)]

    docs = (doc_lengths, roster)

    queries, kv, h_one, cos_table, sin_table = project(*docs, tokens, gain_one, qkv_t)
    blocks = [kv] + [over_chips(kv, j) for j in range(1, count)]
    q_pair = over_cores(queries)
    w_full = lax.all_gather(w_out, "tp", axis=0, tiled=True)
    in_pair = over_tp(in_t, 1)
    down_pair = over_tp(w_down, 1)

    split = (count + 1) // 2
    (state,) = attention_forward(0, False, *docs, queries, q_pair, blocks[:split])
    state_own, state_pair = attention_forward(
        split, True, *docs, queries, q_pair, blocks[split:], state, kinds((in_pair, down_pair), "h")
    )
    out_b, totals, out_mine, out_other = join(state_own, over_cores(state_pair))
    outs = [out_mine] + [over_tp(out_other if k % 2 else out_mine, k) for k in range(1, n_tp)]
    out_pair = over_cores(out_b)
    totals_pair = over_cores(totals)

    staged = stage(tokens, cotangent, w_full, in_t, in_pair, w_down, down_pair)
    middle, middle_part, h_two, mixed, gate_grad, gain_two_part, own, *others = feed(
        gain_two, staged, outs
    )
    arrived = [own] + [over_tp(others[n], 2 * n + 2) for n in range(n_tp // 2 - 1)]
    own, *others = down(n_tp, mixed, w_down, down_pair, middle, ())
    middle_grad, branch_grad, *pieces = branch(
        n_tp, middle_part, cotangent, gain_two, w_full, arrived, [(own, "h")]
    )
    h_pair = over_tp(h_two, 1)
    early = early_grads(
        mixed, gate_grad, cotangent, h_two, in_t, w_down, h_pair, [(branch_grad, "h")]
    )
    early_sum = lax.psum(early, "seq")
    grad_down, grad_in = parted(early_sum, (units, 2 * units))
    out_grad = lay_turned(everywhere(pieces), [(early, "h")])
    grad_pair = over_cores(out_grad)
    branches = by_steps(branch_grad)

    total = total_of(
        [own] + [over_tp(others[n], 2 * n + 2) for n in range(n_tp // 2 - 1)],
        BF16,
        "h",
        [(out_grad, "v")],
    )
    totals_all = by_steps(total)

    held = (queries, q_pair, out_grad, grad_pair, out_b, out_pair, totals, totals_pair)
    *terms, dq = attention_backward(1, False, *docs, held, blocks[1:], None, [(total, "v")])
    dkv, dq_own, dq_pair = attention_backward(0, True, *docs, held, blocks[:1], dq)
    dkvs = [dkv] + [over_chips(terms[j - 1], j) for j in range(1, count)]

    proj_grad, *parts = unproject(
        n_tp,
        tokens,
        qkv_t,
        cos_table,
        sin_table,
        gain_two_part,
        dq_own,
        over_cores(dq_pair),
        dkvs,
        [(total, "v")],
    )
    layer_out = stack_parts(totals_all)
    keep, send = late_grads(proj_grad, h_one, out_b, branches, [(totals_all[n_tp // 2], "v")])
    own, *others = spread(count, keep, over_cores(send))
    chip_sum = total_of([own] + [over_chips(others[k - 1], k) for k in range(1, count)], F32)
    input_part, gains = input_side(
        tokens, gain_one, middle_grad, everywhere(parts), [(own, "v")]
    )
    inputs_all = everywhere([input_part] * n_tp)
    piece = sum_piece(gains, [chip_sum], [(layer_out, "h")])
    input_grad = stack_parts(inputs_all)
    collected = collect(
        [piece] + [over_chips(piece, k) for k in range(1, count)], [(input_grad, "h"), (grad_down, "h")]
    )
    grad_qkv, grad_out, grad_one, grad_two = finish(
        collected, over_cores(collected), 3 * width
    )

    back = lambda x, n: x.reshape(-1, n, model).transpose(2, 0, 1)
    return (
        layer_out,
        input_grad,
        grad_one,
        back(grad_qkv, width),
        grad_out,
        grad_two,
        back(grad_in, units),
        grad_down,
    )


def solution(mesh):
    placed = (
        P("seq", None),
        P(),
        P(None, None, "tp"),
        P("tp", None),
        P(),
        P(None, None, "tp"),
        P("tp", None),
        P("seq", None),
        P(),
        P(),
    )
    return jax.shard_map(
        functools.partial(body, mesh.shape["seq"], mesh.shape["tp"]),
        mesh=mesh,
        in_specs=placed,
        out_specs=(
            P("seq", None),
            P("seq", None),
            P(),
            P(None, None, "tp"),
            P("tp", None),
            P(),
            P(None, None, "tp"),
            P("tp", None),
        ),
        check_vma=False,
    )
```

```python
import functools

import jax
import jax.numpy as jnp
import numpy as np
from jax import lax
from jax.experimental import pallas as pl
from jax.experimental.pallas import tpu as pltpu
from jax.sharding import PartitionSpec as P

HDIM = 64
HALF = HDIM // 2
EPSILON = 1e-05
ROPE_THETA = 160000.0
MASKED = -1e30
AUG = 80
STRIP = 64
F32 = jnp.float32
BF16 = jnp.bfloat16
HBM = pl.BlockSpec(memory_space=pltpu.HBM)
VMEM = pl.BlockSpec(memory_space=pltpu.VMEM)

NN = (((1,), (0,)), ((), ()))
NT = (((1,), (1,)), ((), ()))
TN = (((0,), (0,)), ((), ()))


def params(mib):
    return pltpu.CompilerParams(vmem_limit_bytes=mib * 2**20)


def slot(tp, n_tp):
    return tp % 2 * (n_tp // 2) + tp // 2


def mm(a, b, dims):
    return lax.dot_general(a, b, dims, preferred_element_type=F32)


def shaped(shape, dtype):
    return jax.ShapeDtypeStruct(shape, dtype)


def kinds(arrays, kind):
    return [(array, kind) for array in arrays]


def pin(array, kind):
    return array if kind in ("v", "free") else pltpu.with_memory_space_constraint(array, pltpu.HBM)


def call(name, kernel, ins, outs, scratch=(), mib=16, after=(), lazy=False, flops=0):
    fetched = [i for i, given in enumerate(ins) if given[1] not in ("v", "raw", "free")]
    left = [i for i, out in enumerate(outs) if out[2] == "h"]

    def held(array, kind):
        rows = array.shape[0] if kind == "h" else kind
        return pltpu.VMEM((rows,) + array.shape[1:], array.dtype)

    def run(*refs):
        in_refs = list(refs[: len(ins)])
        at = len(ins) + len(after)
        out_refs = list(refs[at : at + len(outs)])
        at += len(outs)
        own = refs[at : at + len(scratch)]
        at += len(scratch)
        buffers = refs[at : at + len(fetched) + len(left)]
        sems = refs[-1]
        copies = []
        for n, i in enumerate(fetched):
            source = in_refs[i]
            if ins[i][1] != "h":
                rows = ins[i][1]
                n_tp = ins[i][0].shape[0] // rows
                at = pl.multiple_of(slot(lax.axis_index("tp"), n_tp) * rows, rows)
                source = source.at[pl.ds(at, rows)]
            copies.append(pltpu.make_async_copy(source, buffers[n], sems.at[n]))
            in_refs[i] = buffers[n]
        for copy in copies:
            copy.start()
        coming = dict(zip(fetched, copies))
        going = {}
        for n, i in enumerate(left):
            spot = len(fetched) + n
            going[i] = pltpu.make_async_copy(buffers[spot], out_refs[i], sems.at[spot])
            out_refs[i] = buffers[spot]
        gone = []

        def need(*which):
            for i in which:
                if i in coming:
                    coming.pop(i).wait()

        def give(*which):
            for i in which:
                if i in going:
                    gone.append(going.pop(i))
                    gone[-1].start()

        if lazy:
            kernel(need, give, *in_refs, *out_refs, *own)
        else:
            need(*fetched)
            kernel(*in_refs, *out_refs, *own)
        need(*fetched)
        give(*left)
        for copy in gone:
            copy.wait()

    spec = lambda kind: VMEM if kind == "v" else HBM
    count = len(fetched) + len(left)
    return pl.pallas_call(
        run,
        out_shape=tuple(
            shaped(shape, dtype) if kind == "v" else pltpu.HBM(shape, dtype)
            for shape, dtype, kind in outs
        ),
        in_specs=[spec(kind) for unused, kind in ins] + [spec(kind) for unused, kind in after],
        out_specs=tuple(spec(kind) for unused, unused, kind in outs),
        scratch_shapes=list(scratch)
        + [held(*ins[i]) for i in fetched]
        + [pltpu.VMEM(outs[i][0], outs[i][1]) for i in left]
        + [pltpu.SemaphoreType.DMA((max(count, 1),))],
        name=name,
        cost_estimate=pl.CostEstimate(flops=flops, bytes_accessed=0, transcendentals=0)
        if flops
        else None,
        compiler_params=params(mib),
    )(*[pin(*given) for given in ins], *[pin(*given) for given in after])


def swap(x, axis, hop, count):
    return lax.ppermute(x, axis, [(i, i ^ hop) for i in range(count)])


def doc_scratch(doc_lengths, roster):
    return [pltpu.SMEM(doc_lengths.shape, jnp.int32), pltpu.SMEM(roster.shape, jnp.int32)]


def fetch_docs(len_any, roster_any, len_ref, roster_ref, len_sem, roster_sem):
    one = pltpu.make_async_copy(len_any, len_ref, len_sem)
    two = pltpu.make_async_copy(roster_any, roster_ref, roster_sem)
    one.start()
    two.start()
    one.wait()
    two.wait()


def doc_bounds(len_ref):
    ends, total = [], jnp.int32(0)
    for d in range(len_ref.shape[0]):
        total = total + len_ref[d]
        ends.append(total)
    return ends


def doc_of(ends, position):
    found = jnp.int32(0)
    for end in ends:
        found = found + (end <= position).astype(jnp.int32)
    return found


def meet(ends, base_a, base_b, rows):
    low = jnp.maximum(doc_of(ends, base_a), doc_of(ends, base_b))
    high = jnp.minimum(doc_of(ends, base_a + rows - 1), doc_of(ends, base_b + rows - 1))
    return low <= high


def doc_rows(ends, base, rows):
    spot = base + lax.broadcasted_iota(jnp.int32, (16, rows), 1)
    line = lax.broadcasted_iota(jnp.int32, (16, rows), 0)
    held = jnp.zeros((16, rows), F32)
    start = jnp.int32(0)
    for d, end in enumerate(ends):
        inside = (line == d) & (spot >= start) & (spot < end)
        held = jnp.where(inside, 1.0, held)
        start = end
    return held


def ban_rows(ends, base, rows):
    line = lax.broadcasted_iota(jnp.int32, (16, rows), 0)
    held = doc_rows(ends, base, rows)
    return jnp.where((held > 0.5) | (line >= len(ends)), 0.0, MASKED)


def key_row(block, seq_index):
    return seq_index ^ (2 * block)


def place_row(ends, base, rows):
    spot = base + lax.broadcasted_iota(jnp.int32, (1, rows), 1)
    start = jnp.zeros((1, rows), jnp.int32)
    for end in ends:
        start = jnp.where(spot >= end, end, start)
    return (spot - start).astype(F32)


def normed(values):
    centre = jnp.mean(values, axis=-1, keepdims=True)
    shifted = values - centre
    spread = jnp.mean(shifted * shifted, axis=-1, keepdims=True)
    scale = lax.rsqrt(spread + EPSILON)
    return shifted * scale, scale


def norm_back(unit, scale, grad, gain):
    u = grad * gain
    mean_u = jnp.mean(u, axis=-1, keepdims=True)
    mean_un = jnp.mean(u * unit, axis=-1, keepdims=True)
    return scale * (u - mean_u - unit * mean_un)


def project_kernel(
    width, need, give, len_any, roster_any, x_ref, w_ref, gain_ref, freq_ref, *refs
):
    q_out, kv_out, h_out, cos_out, sin_out = refs[:5]
    proj, len_ref, roster_ref, sems = refs[5:]
    rows = x_ref.shape[0]
    fetch_docs(len_any, roster_any, len_ref, roster_ref, sems.at[0], sems.at[1])
    need(5)
    ends = doc_bounds(len_ref)
    place = place_row(ends, roster_ref[lax.axis_index("seq")] * rows, rows)
    angles = place * freq_ref[...]
    cos_table = jnp.cos(angles)
    sin_table = jnp.sin(angles)
    cos_out[...] = cos_table
    sin_out[...] = sin_table
    give(3, 4)
    need(2, 4)
    gain = gain_ref[...].reshape(1, -1)

    def strip(i, carry):
        at = pl.ds(i * STRIP, STRIP)
        unit, unused = normed(x_ref[at, :].astype(F32))
        h_out[at, :] = (unit * gain).astype(BF16)
        return carry

    lax.fori_loop(0, rows // STRIP, strip, 0)
    give(2)
    need(3)
    proj[...] = mm(w_ref[...], h_out[...], NT)
    for at in range(0, 2 * width, HDIM):
        low = proj[at : at + HALF, :]
        high = proj[at + HALF : at + HDIM, :]
        turned_low = (low * cos_out[...] - high * sin_out[...]).astype(BF16)
        turned_high = (high * cos_out[...] + low * sin_out[...]).astype(BF16)
        if at < width:
            q_out[at : at + HALF, :] = (turned_low.astype(F32) * HDIM**-0.5).astype(BF16)
            q_out[at + HALF : at + HDIM, :] = (turned_high.astype(F32) * HDIM**-0.5).astype(BF16)
        else:
            kv_out[at - width : at - width + HALF, :] = turned_low
            kv_out[at - width + HALF : at - width + HDIM, :] = turned_high
    kv_out[width:, :] = proj[2 * width :, :].astype(BF16)


def project(doc_lengths, roster, tokens, gain, qkv_t):
    rows, model = tokens.shape
    width = qkv_t.shape[0] // 3
    freq = (ROPE_THETA ** -(np.arange(HALF) * (2.0 / HDIM))).astype(np.float32)[:, None]
    return call(
        "project",
        functools.partial(project_kernel, width),
        kinds((doc_lengths, roster), "raw") + kinds((tokens, qkv_t, gain, jnp.asarray(freq)), "h"),
        [
            ((width, rows), BF16, "v"),
            ((2 * width, rows), BF16, "v"),
            ((rows, model), BF16, "h"),
            ((HALF, rows), F32, "h"),
            ((HALF, rows), F32, "h"),
        ],
        [pltpu.VMEM((3 * width, rows), F32)]
        + doc_scratch(doc_lengths, roster)
        + [pltpu.SemaphoreType.DMA((2,))],
        lazy=True,
    )


def forward_kernel(first, count, heads, last, len_any, roster_any, q_own, q_pair, *refs):
    kv_refs = refs[:count]
    refs = refs[count:]
    if first:
        state_in, refs = refs[0], refs[1:]
    outs = refs[: 2 if last else 1]
    kv, q_aug, state, len_ref, roster_ref, sems = refs[len(outs) :]
    rows = q_own.shape[1]
    width = heads * HDIM
    me = lax.axis_index("seq")
    copies = [pltpu.make_async_copy(kv_refs[j], kv.at[j], sems.at[j]) for j in range(count)]
    for copy in copies:
        copy.start()
    fetch_docs(len_any, roster_any, len_ref, roster_ref, sems.at[count], sems.at[count + 1])
    ends = doc_bounds(len_ref)
    bases = (roster_ref[me] * rows, roster_ref[me ^ 1] * rows)
    for g, q_ref in enumerate((q_own, q_pair)):
        mark = doc_rows(ends, bases[g], rows).astype(BF16)
        for h in range(heads):
            q_aug[g * heads + h, :HDIM, :] = q_ref[h * HDIM : (h + 1) * HDIM, :]
            q_aug[g * heads + h, HDIM:, :] = mark
    if first:
        state[...] = state_in[...]
    else:
        line = lax.broadcasted_iota(jnp.int32, (2 * heads, AUG, rows), 1)
        state[...] = jnp.where(line >= 72, MASKED, 0.0)
    for copy in copies:
        copy.wait()

    top = lax.broadcasted_iota(jnp.int32, (16, rows), 0) == 0
    ones = jnp.where(top, 1.0, 0.0).astype(BF16)

    def block(j, carry):
        key_base = roster_ref[key_row(j + first, me)] * rows
        ban = ban_rows(ends, key_base, rows).astype(BF16)
        for g in range(2):

            @pl.when(meet(ends, bases[g], key_base, rows))
            def _():
                for h in range(heads):
                    at = g * heads + h
                    keys = jnp.concatenate([kv[j, h * HDIM : (h + 1) * HDIM, :], ban], axis=0)
                    vals = jnp.concatenate(
                        [kv[j, width + h * HDIM : width + (h + 1) * HDIM, :], ones], axis=0
                    )
                    scores = mm(keys, q_aug[at], TN)
                    old = state[at, 72:73, :]
                    new = jnp.maximum(old, jnp.max(scores, axis=0, keepdims=True))
                    probs = jnp.exp(scores - new).astype(BF16)
                    part = mm(vals, probs, NN)
                    fade = jnp.exp(old - new)
                    state[at, :72, :] = state[at, :72, :] * fade + part[:72]
                    state[at, 72:, :] = jnp.broadcast_to(new, (8, rows))

        return carry

    lax.fori_loop(0, count, block, 0)
    if last:
        outs[0][...] = state[:heads]
        outs[1][...] = state[heads:]
    else:
        outs[0][...] = state[...]


def attention_forward(first, last, doc_lengths, roster, q_own, q_pair, blocks, state=None, after=()):
    width, rows = q_own.shape
    heads = width // HDIM
    count = len(blocks)
    half = ((heads, AUG, rows), F32, "v")
    whole = ((2 * heads, AUG, rows), F32, "v")
    given = [] if state is None else [(state, "v")]
    return call(
        "attention_forward",
        functools.partial(forward_kernel, first, count, heads, last),
        [(doc_lengths, "raw"), (roster, "raw"), (q_own, "v"), (q_pair, "v")]
        + kinds(blocks, "free")
        + given,
        [half, half] if last else [whole],
        [
            pltpu.VMEM((count, 2 * width, rows), BF16),
            pltpu.VMEM((2 * heads, AUG, rows), BF16),
            pltpu.VMEM((2 * heads, AUG, rows), F32),
        ]
        + doc_scratch(doc_lengths, roster)
        + [pltpu.SemaphoreType.DMA((count + 2,))],
        16 if count < 8 else 40,
        after,
    )


def backward_kernel(first, count, heads, more, last, len_any, roster_any, *refs):
    q_own, q_pair, g_own, g_pair, o_own, o_pair, t_own, t_pair = refs[:8]
    kv_refs, refs = refs[8 : 8 + count], refs[8 + count :]
    if more:
        dq_in, refs = refs[0], refs[1:]
    outs, refs = refs[:count], refs[count:]
    dq_outs, refs = (refs[:2], refs[2:]) if last else (refs[:1], refs[1:])
    kv, q_aug, delta, dq, dkv, len_ref, roster_ref, sems = refs
    rows = q_own.shape[1]
    width = heads * HDIM
    me = lax.axis_index("seq")
    copies = [pltpu.make_async_copy(kv_refs[j], kv.at[j], sems.at[j]) for j in range(count)]
    for copy in copies:
        copy.start()
    fetch_docs(len_any, roster_any, len_ref, roster_ref, sems.at[count], sems.at[count + 1])
    ends = doc_bounds(len_ref)
    bases = (roster_ref[me] * rows, roster_ref[me ^ 1] * rows)
    for g, (q_ref, g_ref, o_ref) in enumerate(((q_own, g_own, o_own), (q_pair, g_pair, o_pair))):
        mark = doc_rows(ends, bases[g], rows).astype(BF16)
        for h in range(heads):
            part = slice(h * HDIM, (h + 1) * HDIM)
            q_aug[g * heads + h, :HDIM, :] = q_ref[part, :]
            q_aug[g * heads + h, HDIM:, :] = mark
            product = g_ref[part, :].astype(F32) * o_ref[part, :].astype(F32)
            delta[g * heads + h] = jnp.broadcast_to(
                jnp.sum(product, axis=0, keepdims=True), (8, rows)
            )
    if more:
        dq[...] = dq_in[...]
    else:
        dq[...] = jnp.zeros_like(dq)
    for copy in copies:
        copy.wait()

    def block(j, carry):
        key_base = roster_ref[key_row(j + first, me)] * rows
        ban = ban_rows(ends, key_base, rows).astype(BF16)
        dkv[j] = jnp.zeros((2 * width, rows), F32)
        for g, (g_ref, t_ref) in enumerate(((g_own, t_own), (g_pair, t_pair))):

            @pl.when(meet(ends, bases[g], key_base, rows))
            def _():
                for h in range(heads):
                    at = g * heads + h
                    part = slice(h * HDIM, (h + 1) * HDIM)
                    late = slice(width + h * HDIM, width + (h + 1) * HDIM)
                    keys = kv[j, part, :]
                    scores = mm(jnp.concatenate([keys, ban], axis=0), q_aug[at], TN)
                    probs = jnp.exp(scores - t_ref[h, 0:1, :])
                    prob_grads = mm(kv[j, late, :], g_ref[part, :], TN)
                    score_grad = (probs * (prob_grads - delta[at, 0:1, :])).astype(BF16)
                    dkv[j, late, :] += mm(g_ref[part, :], probs.astype(BF16), NT)
                    dkv[j, part, :] += mm(q_aug[at, :HDIM, :], score_grad, NT)
                    dq[at] += mm(keys, score_grad, NN)

        return carry

    lax.fori_loop(0, count, block, 0)
    for j in range(count):
        outs[j][...] = dkv[j].astype(outs[j].dtype)
    if last:
        for h in range(heads):
            part = slice(h * HDIM, (h + 1) * HDIM)
            dq_outs[0][part, :] = dq[h] * HDIM**-0.5
            dq_outs[1][part, :] = (dq[heads + h] * HDIM**-0.5).astype(BF16)
    else:
        dq_outs[0][...] = dq[...]


def attention_backward(first, last, doc_lengths, roster, held, blocks, dq=None, after=()):
    width, rows = held[0].shape
    heads = width // HDIM
    count = len(blocks)
    given = [] if dq is None else [(dq, "v")]
    if last:
        queries = [((width, rows), F32, "v"), ((width, rows), BF16, "v")]
    else:
        queries = [((2 * heads, HDIM, rows), F32, "v")]
    return call(
        "attention_backward",
        functools.partial(backward_kernel, first, count, heads, bool(given), last),
        kinds((doc_lengths, roster), "raw") + kinds(held, "v") + kinds(blocks, "free") + given,
        [((2 * width, rows), BF16 if first else F32, "v")] * count + queries,
        [
            pltpu.VMEM((count, 2 * width, rows), BF16),
            pltpu.VMEM((2 * heads, AUG, rows), BF16),
            pltpu.VMEM((2 * heads, 8, rows), F32),
            pltpu.VMEM((2 * heads, HDIM, rows), F32),
            pltpu.VMEM((count, 2 * width, rows), F32),
        ]
        + doc_scratch(doc_lengths, roster)
        + [pltpu.SemaphoreType.DMA((count + 2,))],
        16 if count < 8 else 40,
        after,
    )


def join_kernel(heads, own_ref, back_ref, out_ref, total_ref, mine_ref, other_ref):
    rows = own_ref.shape[2]
    for h in range(heads):
        top_own = own_ref[h, 72:73, :]
        top_back = back_ref[h, 72:73, :]
        top = jnp.maximum(top_own, top_back)
        fade_own = jnp.exp(top_own - top)
        fade_back = jnp.exp(top_back - top)
        total = own_ref[h, 64:65, :] * fade_own + back_ref[h, 64:65, :] * fade_back
        share_own = fade_own / total
        share_back = fade_back / total
        value = own_ref[h, :HDIM, :] * share_own + back_ref[h, :HDIM, :] * share_back
        out_ref[h * HDIM : (h + 1) * HDIM, :] = value.astype(BF16)
        total_ref[h] = jnp.broadcast_to(top + jnp.log(total), (8, rows))
    half = rows // 2
    for bit in range(2):

        @pl.when(lax.axis_index("tp") % 2 == bit)
        def _():
            mine_ref[...] = out_ref[:, bit * half : (bit + 1) * half]
            other_ref[...] = out_ref[:, (1 - bit) * half : (2 - bit) * half]


def join(own, back):
    heads, unused, rows = own.shape
    return call(
        "join",
        functools.partial(join_kernel, heads),
        [(own, "v"), (back, "v")],
        [
            ((heads * HDIM, rows), BF16, "v"),
            ((heads, 8, rows), F32, "v"),
            ((heads * HDIM, rows // 2), BF16, "v"),
            ((heads * HDIM, rows // 2), BF16, "v"),
        ],
    )


def pick_kernel(in_any, down_any, out_ref, sems):
    core = lax.axis_index("seq") % 2
    at = 0
    copies = []
    for n, source in enumerate((in_any, down_any)):
        rows = source.shape[0] // 2
        mine = pl.ds(pl.multiple_of(core * rows, rows), rows)
        copies.append(
            pltpu.make_async_copy(source.at[mine], out_ref.at[pl.ds(at, rows)], sems.at[n])
        )
        at += rows
    for copy in copies:
        copy.start()
    for copy in copies:
        copy.wait()


def pick(in_t, w_down):
    (out,) = call(
        "pick",
        pick_kernel,
        kinds((in_t, w_down), "raw"),
        [(((in_t.shape[0] + w_down.shape[0]) // 2, in_t.shape[1]), BF16, "v")],
        [pltpu.SemaphoreType.DMA((2,))],
    )
    return out


def stage_kernel(x_any, cot_any, w_any, in_any, down_any, got_ref, rest_ref, *refs):
    x_ref, cot_ref, w_ref, in_ref, down_ref, sems = refs
    half = x_ref.shape[0]
    core = lax.axis_index("seq") % 2
    mine = pl.ds(pl.multiple_of(lax.axis_index("tp") % 2 * half, half), half)
    moves = [(w_any, w_ref), (x_any.at[mine], x_ref), (cot_any.at[mine], cot_ref)]
    at = 0
    for own, ref in ((in_any, in_ref), (down_any, down_ref)):
        rows = own.shape[0] // 2
        moves.append((own, ref.at[pl.ds(0, 2 * rows)]))
        for source, side in ((got_ref, core), (rest_ref, 1 - core)):
            spot = pl.multiple_of(2 * rows + side * rows, rows)
            moves.append((source.at[pl.ds(at, rows)], ref.at[pl.ds(spot, rows)]))
        at += rows
    copies = [pltpu.make_async_copy(*move, sems.at[n]) for n, move in enumerate(moves)]
    for copy in copies:
        copy.start()
    for copy in copies:
        copy.wait()


def stage(tokens, cotangent, w_full, in_t, w_down, got, rest):
    rows, model = tokens.shape
    return call(
        "stage",
        stage_kernel,
        kinds((tokens, cotangent, w_full, in_t, w_down), "raw") + kinds((got, rest), "free"),
        [
            ((rows // 2, model), BF16, "v"),
            ((rows // 2, model), BF16, "v"),
            (w_full.shape, BF16, "v"),
            ((2 * in_t.shape[0], model), BF16, "v"),
            ((2 * w_down.shape[0], model), BF16, "v"),
        ],
        [pltpu.SemaphoreType.DMA((9,))],
    )


def gated(units, first, gate_up, mixed_grad, mixed_out, gate_out):
    def wave(i, carry):
        spot = pl.ds(first + i * 32, 32)
        at = pl.ds(2 * first + i * 32, 32)
        late = pl.ds(2 * first + units + i * 32, 32)
        gate = gate_up[at, :]
        up = gate_up[late, :]
        back = mixed_grad[spot, :]
        bell = 0.5 * (1.0 + lax.erf(gate * (2.0**-0.5)))
        active = gate * bell
        slope = bell + gate * jnp.exp(-0.5 * gate * gate) * ((2.0 * jnp.pi) ** -0.5)
        mixed_out[spot, :] = (active * up).astype(BF16)
        gate_out[at, :] = (back * up * slope).astype(BF16)
        gate_out[late, :] = (back * active).astype(BF16)
        return carry

    lax.fori_loop(0, units // 32, wave, 0)


def feed_kernel(n_tp, need, give, x_ref, cot_ref, w_ref, in_ref, down_ref, gain_ref, *refs):
    out_refs = refs[:n_tp]
    middle_out, part_out, h_out, mixed_out, gate_out, gain_out = refs[n_tp : n_tp + 6]
    keep_ref, *send_refs = refs[n_tp + 6 : n_tp + 6 + n_tp // 2]
    outs, unit, gate_up, mixed_grad, grad = refs[n_tp + 6 + n_tp // 2 :]
    rows = x_ref.shape[0]
    part = keep_ref.shape[0]
    units = down_ref.shape[0] // 2
    width = out_refs[0].shape[0]
    tp = lax.axis_index("tp")
    for k in range(n_tp):
        at = pl.ds(pl.multiple_of((tp ^ k) * width, width), width)
        outs[at, :] = out_refs[k][...]
    mixed_grad[...] = mm(down_ref[...], cot_ref[...], NT)
    middle_out[...] = mm(outs[...], w_ref[...], TN)
    need(5)
    gain = gain_ref[...].reshape(1, -1)

    def strip(i, carry):
        at = pl.ds(i * 32, 32)
        middle = middle_out[at, :] + x_ref[at, :].astype(F32)
        middle_out[at, :] = middle
        held, unused = normed(middle)
        unit[at, :] = held
        h_out[at, :] = (held * gain).astype(BF16)
        return carry

    lax.fori_loop(0, rows // 32, strip, 0)
    give(0, 2)
    gate_up[...] = mm(in_ref[...], h_out[...], NT)
    for first in (0, units):
        gated(units, first, gate_up, mixed_grad, mixed_out, gate_out)
    give(3, 4)
    grad[...] = mm(gate_out[...], in_ref[...], TN)
    for n, ref in enumerate((keep_ref, *send_refs)):
        at = pl.ds(pl.multiple_of((tp ^ (2 * n)) // 2 * part, part), part)
        ref[...] = grad[at, :].astype(ref.dtype)
        give(6 + n)
    own = pl.ds(pl.multiple_of(tp // 2 * part, part), part)
    part_out[...] = middle_out[own, :]
    give(1)

    def gains(i, carry):
        at = pl.ds(i * 32, 32)
        product = grad[at, :] * unit[at, :]
        return carry + jnp.sum(product.reshape(4, 8, -1), axis=0)

    gain_out[...] = lax.fori_loop(0, rows // 32, gains, jnp.zeros(gain_out.shape, F32))


def feed(gain, staged, outs):
    rows, model = staged[0].shape
    n_tp = len(outs)
    units = staged[4].shape[0]
    part = 2 * rows // n_tp
    return call(
        "feed",
        functools.partial(feed_kernel, n_tp),
        kinds(staged, "v") + [(gain, "h")] + kinds(outs, "v"),
        [
            ((rows, model), F32, "h"),
            ((part, model), F32, "h"),
            ((rows, model), BF16, "h"),
            ((units, rows), BF16, "h"),
            ((2 * units, rows), BF16, "h"),
            ((8, model), F32, "h"),
            ((part, model), F32, "h"),
        ]
        + [((part, model), BF16, "h")] * (n_tp // 2 - 1),
        [
            pltpu.VMEM((n_tp * outs[0].shape[0], rows), BF16),
            pltpu.VMEM((rows, model), F32),
            pltpu.VMEM((2 * units, rows), F32),
            pltpu.VMEM((units, rows), F32),
            pltpu.VMEM((rows, model), F32),
        ],
        24,
        lazy=True,
    )


def branch_kernel(n_tp, count, need, give, middle_ref, cot_ref, gain_ref, w_ref, *refs):
    arrived = refs[:count]
    grad_out, branch_out = refs[count : count + 2]
    piece_refs = refs[count + 2 :]
    width = piece_refs[0].shape[1]
    tp = lax.axis_index("tp")
    need(0, 1, 2, 4)
    total = arrived[0][...]
    for ref in arrived[1:]:
        total = total + ref[...].astype(F32)
    unit, scale = normed(middle_ref[...])
    gain = gain_ref[...].reshape(1, -1)
    value = cot_ref[...].astype(F32) + norm_back(unit, scale, total, gain)
    grad_out[...] = value
    branch_out[...] = value.astype(BF16)
    give(0, 1)
    need(3)
    for k in range(n_tp):
        at = pl.ds(pl.multiple_of((tp ^ k) * width, width), width)
        piece_refs[k][...] = mm(branch_out[...], w_ref[at, :], NT).astype(BF16)


def branch(n_tp, middle_part, cotangent, gain, w_full, arrived, after):
    part, model = arrived[0].shape
    width = w_full.shape[0] // n_tp
    return call(
        "branch",
        functools.partial(branch_kernel, n_tp, len(arrived)),
        [(middle_part, "h"), (cotangent, part)]
        + kinds((gain, w_full, arrived[0]), "h")
        + kinds(arrived[1:], "v"),
        [((part, model), F32, "h"), ((part, model), BF16, "h")]
        + [((part, width), BF16, "v")] * n_tp,
        (),
        16,
        after,
        True,
    )


def lay_kernel(n_tp, *refs):
    out_ref, held = refs[n_tp:]
    part = refs[0].shape[0]
    tp = lax.axis_index("tp")
    for k in range(n_tp):
        at = pl.ds(pl.multiple_of(slot(tp ^ k, n_tp) * part, part), part)
        held[at, :] = refs[k][...].astype(F32)
    out_ref[...] = held[...].T.astype(BF16)


def lay_turned(pieces, after):
    part, width = pieces[0].shape
    rows = part * len(pieces)
    (out,) = call(
        "lay_turned",
        functools.partial(lay_kernel, len(pieces)),
        kinds(pieces, "v"),
        [((width, rows), BF16, "v")],
        [pltpu.VMEM((rows, width), F32)],
        16,
        after,
    )
    return out


def stack_kernel(n_tp, *refs):
    out_ref = refs[n_tp]
    part = refs[0].shape[0]
    tp = lax.axis_index("tp")
    for k in range(n_tp):
        at = pl.ds(pl.multiple_of(slot(tp ^ k, n_tp) * part, part), part)
        out_ref[at, :] = refs[k][...]


def stack_parts(pieces, after=()):
    part, model = pieces[0].shape
    (out,) = call(
        "stack_parts",
        functools.partial(stack_kernel, len(pieces)),
        kinds(pieces, "v"),
        [((part * len(pieces), model), pieces[0].dtype, "h")],
        (),
        16,
        after,
    )
    return out


def turn_back(out_ref, first, value, cos_table, sin_table):
    for at in range(0, value.shape[0], HDIM):
        low = value[at : at + HALF]
        high = value[at + HALF : at + HDIM]
        spot = first + at
        out_ref[spot : spot + HALF, :] = (low * cos_table + high * sin_table).astype(BF16)
        out_ref[spot + HALF : spot + HDIM, :] = (high * cos_table - low * sin_table).astype(BF16)


def unproject_kernel(
    count, n_tp, need, give, x_ref, w_ref, cos_ref, sin_ref, two_ref, dq_ref, dq_back, *refs
):
    dkv_refs = refs[:count]
    proj_out = refs[count]
    part_refs = refs[count + 1 : count + 1 + n_tp]
    grad, dkv = refs[count + 1 + n_tp :]
    rows, model = x_ref.shape
    part = rows // n_tp
    width = dq_ref.shape[0]
    tp = lax.axis_index("tp")
    need(2, 3)
    cos_table = cos_ref[...]
    sin_table = sin_ref[...]
    turn_back(proj_out, 0, dq_ref[...] + dq_back[...].astype(F32), cos_table, sin_table)
    total = dkv_refs[0][...]
    for ref in dkv_refs[1:]:
        total = total + ref[...].astype(F32)
    dkv[...] = total
    turn_back(proj_out, width, dkv[:width, :], cos_table, sin_table)
    proj_out[2 * width :, :] = dkv[width:, :].astype(BF16)
    need(1)
    grad[...] = mm(proj_out[...], w_ref[...], TN)
    need(0, 4)

    def gains(i, carry):
        at = pl.ds(i * STRIP, STRIP)
        unit, unused = normed(x_ref[at, :].astype(F32))
        product = grad[at, :] * unit
        return carry + jnp.sum(product.reshape(STRIP // 8, 8, -1), axis=0)

    gain = lax.fori_loop(0, rows // STRIP, gains, jnp.zeros((8, model), F32))
    line = lax.broadcasted_iota(jnp.int32, (16, model), 0)
    gain_two = jnp.sum(two_ref[...], axis=0, keepdims=True)
    gain = jnp.sum(gain, axis=0, keepdims=True)
    gain = jnp.where(line == 0, gain, jnp.where(line == 1, gain_two, 0.0))
    for k in range(n_tp):
        at = pl.ds(pl.multiple_of(slot(tp ^ k, n_tp) * part, part), part)
        part_refs[k][:part, :] = grad[at, :].astype(part_refs[k].dtype)
        part_refs[k][part:, :] = gain.astype(part_refs[k].dtype)


def unproject(n_tp, tokens, qkv_t, cos_table, sin_table, gain_two_part, dq, dq_back, dkvs, after):
    rows, model = tokens.shape
    part = rows // n_tp
    return call(
        "unproject",
        functools.partial(unproject_kernel, len(dkvs), n_tp),
        kinds((tokens, qkv_t, cos_table, sin_table, gain_two_part), "v")
        + kinds((dq, dq_back, *dkvs), "v"),
        [((qkv_t.shape[0], rows), BF16, "v"), ((part + 16, model), F32, "v")]
        + [((part + 16, model), BF16, "v")] * (n_tp - 1),
        [pltpu.VMEM((rows, model), F32), pltpu.VMEM(dkvs[0].shape, F32)],
        16,
        after,
        True,
    )


def input_kernel(x_ref, gain_ref, grad_ref, sum_ref, out_ref, gain_out):
    part, model = grad_ref.shape
    total = sum_ref[...]
    unit, scale = normed(x_ref[...].astype(F32))
    gain = gain_ref[...].reshape(1, -1)
    value = grad_ref[...] + norm_back(unit, scale, total[:part], gain)
    out_ref[...] = value.astype(BF16)
    gain_out[...] = total[part : part + 8]


def input_side(tokens, gain, middle_grad, summed, after):
    part, model = middle_grad.shape
    return call(
        "input_side",
        input_kernel,
        [(tokens, part), (gain, "h"), (middle_grad, "v"), (summed, "v")],
        [((part, model), BF16, "v"), ((8, model), F32, "v")],
        (),
        16,
        after,
    )


def early_kernel(mixed_ref, gate_ref, cot_ref, h_ref, in_ref, down_ref, h_pair, out_ref, *refs):
    gate_up, mixed_grad, mixed, gate = refs
    units = down_ref.shape[0]
    half = h_ref.shape[0]
    bit = lax.axis_index("tp") % 2
    mine = pl.ds(pl.multiple_of(bit * half, half), half)
    other = pl.ds(pl.multiple_of((1 - bit) * half, half), half)
    gate_up[...] = mm(in_ref[...], h_pair[...], NT)
    mixed_grad[...] = mm(down_ref[...], cot_ref[other, :], NT)
    gated(units, 0, gate_up, mixed_grad, mixed, gate)
    out_ref[:units, :] = mm(mixed_ref[:units, :], cot_ref[mine, :], NN)
    out_ref[:units, :] += mm(mixed[...], cot_ref[other, :], NN)
    out_ref[units : 3 * units, :] = mm(gate_ref[: 2 * units, :], h_ref[...], NN)
    out_ref[units : 3 * units, :] += mm(gate[...], h_pair[...], NN)
    if out_ref.shape[0] > 3 * units:
        out_ref[3 * units :, :] = jnp.zeros((out_ref.shape[0] - 3 * units, out_ref.shape[1]), F32)


def early_grads(mixed, gate_grad, cotangent, h_two, in_t, w_down, h_pair, after):
    units, model = w_down.shape
    half = h_two.shape[0]
    (out,) = call(
        "early_grads",
        early_kernel,
        kinds((mixed, gate_grad, cotangent, h_two, in_t, w_down), "h") + [(h_pair, "v")],
        [((25 * units // 6, model), F32, "h")],
        [
            pltpu.VMEM((2 * units, half), F32),
            pltpu.VMEM((units, half), F32),
            pltpu.VMEM((units, half), BF16),
            pltpu.VMEM((2 * units, half), BF16),
        ],
        24,
        after,
    )
    return out


def part_kernel(in_any, *refs):
    out_refs, held, sem = refs[:-2], refs[-2], refs[-1]
    rows = held.shape[0]
    copy = pltpu.make_async_copy(in_any.at[pl.ds(0, rows)], held, sem)
    copy.start()
    copy.wait()
    at = 0
    for ref in out_refs:
        ref[...] = held[at : at + ref.shape[0], :]
        at += ref.shape[0]


def parted(value, sizes):
    model = value.shape[1]
    return call(
        "parted",
        part_kernel,
        [(value, "raw")],
        [((size, model), F32, "h") for size in sizes],
        [pltpu.VMEM((sum(sizes), model), F32), pltpu.SemaphoreType.DMA],
    )


def late_kernel(n_tp, proj_ref, h_ref, out_ref, *refs):
    branch_refs = refs[:n_tp]
    keep_ref, send_ref, branch_full = refs[n_tp:]
    part = branch_refs[0].shape[0]
    half = keep_ref.shape[1]
    wide = proj_ref.shape[0]
    tp = lax.axis_index("tp")
    core = lax.axis_index("seq") % 2
    for k in range(n_tp):
        at = pl.ds(pl.multiple_of(slot(tp ^ k, n_tp) * part, part), part)
        branch_full[at, :] = branch_refs[k][...]
    for ref, side in ((send_ref, 1 - core), (keep_ref, core)):
        columns = pl.ds(pl.multiple_of(side * half, half), half)
        ref[:wide, :] = mm(proj_ref[...], h_ref[:, columns], NN).astype(ref.dtype)
        ref[wide:, :] = mm(out_ref[...], branch_full[:, columns], NN).astype(ref.dtype)


def late_grads(proj_grad, h_one, out_b, branches, after):
    rows, model = h_one.shape
    wide = proj_grad.shape[0] + out_b.shape[0]
    return call(
        "late_grads",
        functools.partial(late_kernel, len(branches)),
        [(proj_grad, "v"), (h_one, "v"), (out_b, "v"), (branches[0], "v")]
        + kinds(branches[1:], "v"),
        [((wide, model // 2), F32, "v"), ((wide, model // 2), BF16, "v")],
        [pltpu.VMEM((rows, model), BF16)],
        16,
        after,
    )


def spread_kernel(count, keep_ref, back_ref, *refs):
    held = refs[count]
    piece = refs[0].shape[0]
    chip = lax.axis_index("seq") // 2
    held[...] = keep_ref[...] + back_ref[...].astype(F32)
    for k in range(count):
        at = pl.ds(pl.multiple_of((chip ^ k) * piece, piece), piece)
        refs[k][...] = held[at, :].astype(refs[k].dtype)


def spread(count, keep, back):
    wide, half = keep.shape
    piece = wide // count
    return call(
        "spread",
        functools.partial(spread_kernel, count),
        [(keep, "v"), (back, "v")],
        [((piece, half), F32, "v")] + [((piece, half), BF16, "v")] * (count - 1),
        [pltpu.VMEM((wide, half), F32)],
    )


def piece_kernel(count, gain_ref, *refs):
    out_ref = refs[count]
    half = out_ref.shape[1]
    total = refs[0][...]
    for ref in refs[1:count]:
        total = total + ref[...].astype(F32)
    line = lax.broadcasted_iota(jnp.int32, (16, half), 0)
    gains = jnp.zeros((16, half), F32)
    for at in range(4):
        row = gain_ref[at // 2 : at // 2 + 1, at % 2 * half : (at % 2 + 1) * half]
        gains = jnp.where(line == at, row, gains)
    out_ref[...] = jnp.concatenate([total, gains], axis=0).astype(BF16)


def sum_piece(gains, pieces, after=()):
    piece, half = pieces[0].shape
    (out,) = call(
        "sum_piece",
        functools.partial(piece_kernel, len(pieces)),
        [(gains, "v")] + kinds(pieces, "v"),
        [((piece + 16, half), BF16, "v")],
        (),
        16,
        after,
    )
    return out


def collect_kernel(count, *refs):
    out_ref, held = refs[count:]
    piece = refs[0].shape[0] - 16
    wide = count * piece
    chip = lax.axis_index("seq") // 2
    gains = jnp.zeros((16, out_ref.shape[1]), F32)
    for k in range(count):
        at = pl.ds(pl.multiple_of((chip ^ k) * piece, piece), piece)
        whole = refs[k][...].astype(F32)
        held[at, :] = whole[:piece]
        gains = gains + whole[piece:]
    held[wide:, :] = gains
    out_ref[...] = held[...].astype(BF16)


def collect(pieces, after=()):
    piece, half = pieces[0].shape
    wide = (piece - 16) * len(pieces) + 16
    (out,) = call(
        "collect",
        functools.partial(collect_kernel, len(pieces)),
        kinds(pieces, "v"),
        [((wide, half), BF16, "v")],
        [pltpu.VMEM((wide, half), F32)],
        16,
        after,
    )
    return out


def finish_kernel(own_ref, pair_ref, qkv_ref, out_ref, one_ref, two_ref):
    half = own_ref.shape[1]
    wide, tall = qkv_ref.shape[0], out_ref.shape[0]
    core = lax.axis_index("seq") % 2
    for ref, side in ((own_ref, core), (pair_ref, 1 - core)):
        columns = pl.ds(pl.multiple_of(side * half, half), half)
        qkv_ref[:, columns] = ref[:wide, :].astype(F32)
        out_ref[:, columns] = ref[wide : wide + tall, :].astype(F32)
    gains = own_ref[wide + tall :, :].astype(F32) + pair_ref[wide + tall :, :].astype(F32)
    for at, ref in ((0, one_ref), (2, two_ref)):
        ref[pl.ds(0, half)] = gains[at]
        ref[pl.ds(half, half)] = gains[at + 1]


def finish(own, pair, wide, after=()):
    half = own.shape[1]
    tall = own.shape[0] - 16 - wide
    model = 2 * half
    return call(
        "finish",
        finish_kernel,
        [(own, "v"), (pair, "v")],
        [
            ((wide, model), F32, "h"),
            ((tall, model), F32, "h"),
            ((model,), F32, "h"),
            ((model,), F32, "h"),
        ],
        (),
        16,
        after,
    )


def down_kernel(mixed_ref, w_ref, middle_ref, keep_ref, *refs):
    send_refs, total = refs[:-1], refs[-1]
    part = keep_ref.shape[0]
    tp = lax.axis_index("tp")
    total[...] = mm(mixed_ref[...], w_ref[...], TN)
    own = pl.ds(pl.multiple_of(tp // 2 * part, part), part)
    keep_ref[...] = total[own, :] + middle_ref[own, :]
    for n, ref in enumerate(send_refs):
        at = pl.ds(pl.multiple_of((tp ^ (2 * n + 2)) // 2 * part, part), part)
        ref[...] = total[at, :].astype(ref.dtype)


def down(n_tp, mixed, w_both, middle, after):
    rows, model = middle.shape
    part = 2 * rows // n_tp
    return call(
        "down",
        down_kernel,
        [(mixed, "h"), (w_both, "v"), (middle, "h")],
        [((part, model), F32, "h")] + [((part, model), BF16, "h")] * (n_tp // 2 - 1),
        [pltpu.VMEM((rows, model), F32)],
        16,
        after,
    )


def total_kernel(count, *refs):
    total = refs[0][...]
    for ref in refs[1:count]:
        total = total + ref[...].astype(F32)
    refs[count][...] = total.astype(refs[count].dtype)


def total_of(parts, dtype=BF16, kind="v", after=(), flops=0):
    (out,) = call(
        "total_of",
        functools.partial(total_kernel, len(parts)),
        [(parts[0], kind)] + kinds(parts[1:], "v"),
        [(parts[0].shape, dtype, "v")],
        (),
        16,
        after,
        flops=flops,
    )
    return out


def body(
    n_seq,
    n_tp,
    tokens,
    gain_one,
    w_qkv,
    w_out,
    gain_two,
    w_in,
    w_down,
    cotangent,
    doc_lengths,
    roster,
):
    rows, model = tokens.shape
    width = w_qkv.shape[2]
    units = w_in.shape[2]
    count = n_seq // 2
    qkv_t = w_qkv.transpose(1, 2, 0).reshape(3 * width, model)
    in_t = w_in.transpose(1, 2, 0).reshape(2 * units, model)
    over_tp = lambda x, k: swap(x, "tp", k, n_tp)
    over_chips = lambda x, k: swap(x, "seq", 2 * k, n_seq)
    over_cores = lambda x: swap(x, "seq", 1, n_seq)
    everywhere = lambda xs: [xs[0]] + [over_tp(xs[k], k) for k in range(1, n_tp)]

    def by_steps(part):
        parts = {0: part}
        hop = n_tp // 2
        while hop:
            parts.update({k ^ hop: over_tp(x, hop) for k, x in parts.items()})
            hop //= 2
        return [parts[k] for k in range(n_tp)]

    docs = (doc_lengths, roster)

    queries, kv, h_one, cos_table, sin_table = project(*docs, tokens, gain_one, qkv_t)
    blocks = [kv] + [over_chips(kv, j) for j in range(1, count)]
    q_pair = over_cores(queries)
    w_full = lax.all_gather(w_out, "tp", axis=0, tiled=True)
    got = over_tp(pick(in_t, w_down), 1)

    split = (count + 1) // 2
    (state,) = attention_forward(0, False, *docs, queries, q_pair, blocks[:split])
    state_own, state_pair = attention_forward(
        split, True, *docs, queries, q_pair, blocks[split:], state
    )
    out_b, totals, out_mine, out_other = join(state_own, over_cores(state_pair))
    outs = [out_mine] + [over_tp(out_other if k % 2 else out_mine, k) for k in range(1, n_tp)]
    out_pair = over_cores(out_b)
    totals_pair = over_cores(totals)

    staged = stage(tokens, cotangent, w_full, in_t, w_down, got, over_cores(got))
    middle, middle_part, h_two, mixed, gate_grad, gain_two_part, own, *others = feed(
        gain_two, staged, outs
    )
    arrived = [own] + [over_tp(others[n], 2 * n + 2) for n in range(n_tp // 2 - 1)]
    early = early_grads(
        mixed, gate_grad, cotangent, h_two, in_t, w_down, over_tp(h_two, 1), ()
    )
    middle_grad, branch_grad, *pieces = branch(
        n_tp, middle_part, cotangent, gain_two, w_full, arrived, [(early, "h")]
    )
    early_sum = lax.psum(early, "seq")
    own, *others = down(n_tp, mixed, staged[4], middle, [(branch_grad, "h")])
    grad_down, grad_in = parted(early_sum, (units, 2 * units))
    out_grad = lay_turned(everywhere(pieces), [(own, "h")])
    grad_pair = over_cores(out_grad)
    branches = by_steps(branch_grad)

    held = (queries, q_pair, out_grad, grad_pair, out_b, out_pair, totals, totals_pair)
    *terms, dq = attention_backward(1, False, *docs, held, blocks[1:], None)
    total = total_of(
        [own] + [over_tp(others[n], 2 * n + 2) for n in range(n_tp // 2 - 1)],
        BF16,
        "h",
        [(dq, "v")],
    )
    totals_all = by_steps(total)

    dkv, dq_own, dq_pair = attention_backward(0, True, *docs, held, blocks[:1], dq)
    dkvs = [dkv] + [over_chips(terms[j - 1], j) for j in range(1, count)]

    proj_grad, *parts = unproject(
        n_tp,
        tokens,
        qkv_t,
        cos_table,
        sin_table,
        gain_two_part,
        dq_own,
        over_cores(dq_pair),
        dkvs,
        [(total, "v")],
    )
    layer_out = stack_parts(totals_all)
    keep, send = late_grads(proj_grad, h_one, out_b, branches, [(totals_all[n_tp // 2], "v")])
    own, *others = spread(count, keep, over_cores(send))
    came = everywhere(parts)
    summed = total_of(came[:2] + came[:1:-1], F32, flops=500_000_000)
    chip_sum = total_of(
        [own] + [over_chips(others[k - 1], k) for k in range(1, count)], F32, "v", [(summed, "v")]
    )
    input_part, gains = input_side(tokens, gain_one, middle_grad, summed, [(chip_sum, "v")])
    inputs_all = everywhere([input_part] * n_tp)
    piece = sum_piece(gains, [chip_sum], [])
    input_grad = stack_parts(inputs_all)
    collected = collect(
        [piece] + [over_chips(piece, k) for k in range(1, count)], [(input_grad, "h"), (layer_out, "h"), (grad_down, "h")]
    )
    grad_qkv, grad_out, grad_one, grad_two = finish(
        collected, over_cores(collected), 3 * width
    )

    back = lambda x, n: x.reshape(-1, n, model).transpose(2, 0, 1)
    return (
        layer_out,
        input_grad,
        grad_one,
        back(grad_qkv, width),
        grad_out,
        grad_two,
        back(grad_in, units),
        grad_down,
    )


def solution(mesh):
    placed = (
        P("seq", None),
        P(),
        P(None, None, "tp"),
        P("tp", None),
        P(),
        P(None, None, "tp"),
        P("tp", None),
        P("seq", None),
        P(),
        P(),
    )
    return jax.shard_map(
        functools.partial(body, mesh.shape["seq"], mesh.shape["tp"]),
        mesh=mesh,
        in_specs=placed,
        out_specs=(
            P("seq", None),
            P("seq", None),
            P(),
            P(None, None, "tp"),
            P("tp", None),
            P(),
            P(None, None, "tp"),
            P("tp", None),
        ),
        check_vma=False,
    )
```

```python
import functools

import jax
import jax.numpy as jnp
import numpy as np
from jax import lax
from jax.experimental import pallas as pl
from jax.experimental.pallas import tpu as pltpu
from jax.sharding import PartitionSpec as P

HDIM = 64
HALF = HDIM // 2
EPSILON = 1e-05
ROPE_THETA = 160000.0
MASKED = -1e30
AUG = 80
STRIP = 64
F32 = jnp.float32
BF16 = jnp.bfloat16
HBM = pl.BlockSpec(memory_space=pltpu.HBM)
VMEM = pl.BlockSpec(memory_space=pltpu.VMEM)

NN = (((1,), (0,)), ((), ()))
NT = (((1,), (1,)), ((), ()))
TN = (((0,), (0,)), ((), ()))


def params(mib):
    return pltpu.CompilerParams(vmem_limit_bytes=mib * 2**20)


def slot(tp, n_tp):
    return tp % 2 * (n_tp // 2) + tp // 2


def mm(a, b, dims):
    return lax.dot_general(a, b, dims, preferred_element_type=F32)


def shaped(shape, dtype):
    return jax.ShapeDtypeStruct(shape, dtype)


def kinds(arrays, kind):
    return [(array, kind) for array in arrays]


def pin(array, kind):
    return array if kind in ("v", "free") else pltpu.with_memory_space_constraint(array, pltpu.HBM)


def call(name, kernel, ins, outs, scratch=(), mib=16, after=(), lazy=False, flops=0):
    fetched = [i for i, given in enumerate(ins) if given[1] not in ("v", "raw", "free")]
    left = [i for i, out in enumerate(outs) if out[2] == "h"]

    def held(array, kind):
        rows = array.shape[0] if kind == "h" else kind
        return pltpu.VMEM((rows,) + array.shape[1:], array.dtype)

    def run(*refs):
        in_refs = list(refs[: len(ins)])
        at = len(ins) + len(after)
        out_refs = list(refs[at : at + len(outs)])
        at += len(outs)
        own = refs[at : at + len(scratch)]
        at += len(scratch)
        buffers = refs[at : at + len(fetched) + len(left)]
        sems = refs[-1]
        copies = []
        for n, i in enumerate(fetched):
            source = in_refs[i]
            if ins[i][1] != "h":
                rows = ins[i][1]
                n_tp = ins[i][0].shape[0] // rows
                at = pl.multiple_of(slot(lax.axis_index("tp"), n_tp) * rows, rows)
                source = source.at[pl.ds(at, rows)]
            copies.append(pltpu.make_async_copy(source, buffers[n], sems.at[n]))
            in_refs[i] = buffers[n]
        for copy in copies:
            copy.start()
        coming = dict(zip(fetched, copies))
        going = {}
        for n, i in enumerate(left):
            spot = len(fetched) + n
            going[i] = pltpu.make_async_copy(buffers[spot], out_refs[i], sems.at[spot])
            out_refs[i] = buffers[spot]
        gone = []

        def need(*which):
            for i in which:
                if i in coming:
                    coming.pop(i).wait()

        def give(*which):
            for i in which:
                if i in going:
                    gone.append(going.pop(i))
                    gone[-1].start()

        if lazy:
            kernel(need, give, *in_refs, *out_refs, *own)
        else:
            need(*fetched)
            kernel(*in_refs, *out_refs, *own)
        need(*fetched)
        give(*left)
        for copy in gone:
            copy.wait()

    spec = lambda kind: VMEM if kind == "v" else HBM
    count = len(fetched) + len(left)
    return pl.pallas_call(
        run,
        out_shape=tuple(
            shaped(shape, dtype) if kind == "v" else pltpu.HBM(shape, dtype)
            for shape, dtype, kind in outs
        ),
        in_specs=[spec(kind) for unused, kind in ins] + [spec(kind) for unused, kind in after],
        out_specs=tuple(spec(kind) for unused, unused, kind in outs),
        scratch_shapes=list(scratch)
        + [held(*ins[i]) for i in fetched]
        + [pltpu.VMEM(outs[i][0], outs[i][1]) for i in left]
        + [pltpu.SemaphoreType.DMA((max(count, 1),))],
        name=name,
        cost_estimate=pl.CostEstimate(flops=flops, bytes_accessed=0, transcendentals=0)
        if flops
        else None,
        compiler_params=params(mib),
    )(*[pin(*given) for given in ins], *[pin(*given) for given in after])


def swap(x, axis, hop, count):
    return lax.ppermute(x, axis, [(i, i ^ hop) for i in range(count)])


def doc_scratch(doc_lengths, roster):
    return [pltpu.SMEM(doc_lengths.shape, jnp.int32), pltpu.SMEM(roster.shape, jnp.int32)]


def fetch_docs(len_any, roster_any, len_ref, roster_ref, len_sem, roster_sem):
    one = pltpu.make_async_copy(len_any, len_ref, len_sem)
    two = pltpu.make_async_copy(roster_any, roster_ref, roster_sem)
    one.start()
    two.start()
    one.wait()
    two.wait()


def doc_bounds(len_ref):
    ends, total = [], jnp.int32(0)
    for d in range(len_ref.shape[0]):
        total = total + len_ref[d]
        ends.append(total)
    return ends


def doc_of(ends, position):
    found = jnp.int32(0)
    for end in ends:
        found = found + (end <= position).astype(jnp.int32)
    return found


def meet(ends, base_a, base_b, rows):
    low = jnp.maximum(doc_of(ends, base_a), doc_of(ends, base_b))
    high = jnp.minimum(doc_of(ends, base_a + rows - 1), doc_of(ends, base_b + rows - 1))
    return low <= high


def doc_rows(ends, base, rows):
    spot = base + lax.broadcasted_iota(jnp.int32, (16, rows), 1)
    line = lax.broadcasted_iota(jnp.int32, (16, rows), 0)
    held = jnp.zeros((16, rows), F32)
    start = jnp.int32(0)
    for d, end in enumerate(ends):
        inside = (line == d) & (spot >= start) & (spot < end)
        held = jnp.where(inside, 1.0, held)
        start = end
    return held


def ban_rows(ends, base, rows):
    line = lax.broadcasted_iota(jnp.int32, (16, rows), 0)
    held = doc_rows(ends, base, rows)
    return jnp.where((held > 0.5) | (line >= len(ends)), 0.0, MASKED)


def key_row(block, seq_index):
    return seq_index ^ (2 * block)


def place_row(ends, base, rows):
    spot = base + lax.broadcasted_iota(jnp.int32, (1, rows), 1)
    start = jnp.zeros((1, rows), jnp.int32)
    for end in ends:
        start = jnp.where(spot >= end, end, start)
    return (spot - start).astype(F32)


def normed(values):
    centre = jnp.mean(values, axis=-1, keepdims=True)
    shifted = values - centre
    spread = jnp.mean(shifted * shifted, axis=-1, keepdims=True)
    scale = lax.rsqrt(spread + EPSILON)
    return shifted * scale, scale


def norm_back(unit, scale, grad, gain):
    u = grad * gain
    mean_u = jnp.mean(u, axis=-1, keepdims=True)
    mean_un = jnp.mean(u * unit, axis=-1, keepdims=True)
    return scale * (u - mean_u - unit * mean_un)


def project_kernel(
    width, need, give, len_any, roster_any, x_ref, w_ref, gain_ref, freq_ref, *refs
):
    q_out, kv_out, h_out, cos_out, sin_out = refs[:5]
    proj, len_ref, roster_ref, sems = refs[5:]
    rows = x_ref.shape[0]
    fetch_docs(len_any, roster_any, len_ref, roster_ref, sems.at[0], sems.at[1])
    need(5)
    ends = doc_bounds(len_ref)
    place = place_row(ends, roster_ref[lax.axis_index("seq")] * rows, rows)
    angles = place * freq_ref[...]
    cos_table = jnp.cos(angles)
    sin_table = jnp.sin(angles)
    cos_out[...] = cos_table
    sin_out[...] = sin_table
    give(3, 4)
    need(2, 4)
    gain = gain_ref[...].reshape(1, -1)

    def strip(i, carry):
        at = pl.ds(i * STRIP, STRIP)
        unit, unused = normed(x_ref[at, :].astype(F32))
        h_out[at, :] = (unit * gain).astype(BF16)
        return carry

    lax.fori_loop(0, rows // STRIP, strip, 0)
    give(2)
    need(3)
    proj[...] = mm(w_ref[...], h_out[...], NT)
    for at in range(0, 2 * width, HDIM):
        low = proj[at : at + HALF, :]
        high = proj[at + HALF : at + HDIM, :]
        turned_low = (low * cos_out[...] - high * sin_out[...]).astype(BF16)
        turned_high = (high * cos_out[...] + low * sin_out[...]).astype(BF16)
        if at < width:
            q_out[at : at + HALF, :] = (turned_low.astype(F32) * HDIM**-0.5).astype(BF16)
            q_out[at + HALF : at + HDIM, :] = (turned_high.astype(F32) * HDIM**-0.5).astype(BF16)
        else:
            kv_out[at - width : at - width + HALF, :] = turned_low
            kv_out[at - width + HALF : at - width + HDIM, :] = turned_high
    kv_out[width:, :] = proj[2 * width :, :].astype(BF16)


def project(doc_lengths, roster, tokens, gain, qkv_t):
    rows, model = tokens.shape
    width = qkv_t.shape[0] // 3
    freq = (ROPE_THETA ** -(np.arange(HALF) * (2.0 / HDIM))).astype(np.float32)[:, None]
    return call(
        "project",
        functools.partial(project_kernel, width),
        kinds((doc_lengths, roster), "raw") + kinds((tokens, qkv_t, gain, jnp.asarray(freq)), "h"),
        [
            ((width, rows), BF16, "v"),
            ((2 * width, rows), BF16, "v"),
            ((rows, model), BF16, "h"),
            ((HALF, rows), F32, "h"),
            ((HALF, rows), F32, "h"),
        ],
        [pltpu.VMEM((3 * width, rows), F32)]
        + doc_scratch(doc_lengths, roster)
        + [pltpu.SemaphoreType.DMA((2,))],
        lazy=True,
    )


def forward_kernel(first, count, heads, last, len_any, roster_any, q_own, q_pair, *refs):
    kv_refs = refs[:count]
    refs = refs[count:]
    if first:
        state_in, refs = refs[0], refs[1:]
    outs = refs[: 2 if last else 1]
    kv, q_aug, state, len_ref, roster_ref, sems = refs[len(outs) :]
    rows = q_own.shape[1]
    width = heads * HDIM
    me = lax.axis_index("seq")
    copies = [pltpu.make_async_copy(kv_refs[j], kv.at[j], sems.at[j]) for j in range(count)]
    for copy in copies:
        copy.start()
    fetch_docs(len_any, roster_any, len_ref, roster_ref, sems.at[count], sems.at[count + 1])
    ends = doc_bounds(len_ref)
    bases = (roster_ref[me] * rows, roster_ref[me ^ 1] * rows)
    for g, q_ref in enumerate((q_own, q_pair)):
        mark = doc_rows(ends, bases[g], rows).astype(BF16)
        for h in range(heads):
            q_aug[g * heads + h, :HDIM, :] = q_ref[h * HDIM : (h + 1) * HDIM, :]
            q_aug[g * heads + h, HDIM:, :] = mark
    if first:
        state[...] = state_in[...]
    else:
        line = lax.broadcasted_iota(jnp.int32, (2 * heads, AUG, rows), 1)
        state[...] = jnp.where(line >= 72, MASKED, 0.0)
    for copy in copies:
        copy.wait()

    top = lax.broadcasted_iota(jnp.int32, (16, rows), 0) == 0
    ones = jnp.where(top, 1.0, 0.0).astype(BF16)

    def block(j, carry):
        key_base = roster_ref[key_row(j + first, me)] * rows
        ban = ban_rows(ends, key_base, rows).astype(BF16)
        for g in range(2):

            @pl.when(meet(ends, bases[g], key_base, rows))
            def _():
                for h in range(heads):
                    at = g * heads + h
                    keys = jnp.concatenate([kv[j, h * HDIM : (h + 1) * HDIM, :], ban], axis=0)
                    vals = jnp.concatenate(
                        [kv[j, width + h * HDIM : width + (h + 1) * HDIM, :], ones], axis=0
                    )
                    scores = mm(keys, q_aug[at], TN)
                    old = state[at, 72:73, :]
                    new = jnp.maximum(old, jnp.max(scores, axis=0, keepdims=True))
                    probs = jnp.exp(scores - new).astype(BF16)
                    part = mm(vals, probs, NN)
                    fade = jnp.exp(old - new)
                    state[at, :72, :] = state[at, :72, :] * fade + part[:72]
                    state[at, 72:, :] = jnp.broadcast_to(new, (8, rows))

        return carry

    lax.fori_loop(0, count, block, 0)
    if last:
        outs[0][...] = state[:heads]
        outs[1][...] = state[heads:]
    else:
        outs[0][...] = state[...]


def attention_forward(first, last, doc_lengths, roster, q_own, q_pair, blocks, state=None, after=()):
    width, rows = q_own.shape
    heads = width // HDIM
    count = len(blocks)
    half = ((heads, AUG, rows), F32, "v")
    whole = ((2 * heads, AUG, rows), F32, "v")
    given = [] if state is None else [(state, "v")]
    return call(
        "attention_forward",
        functools.partial(forward_kernel, first, count, heads, last),
        [(doc_lengths, "raw"), (roster, "raw"), (q_own, "v"), (q_pair, "v")]
        + kinds(blocks, "free")
        + given,
        [half, half] if last else [whole],
        [
            pltpu.VMEM((count, 2 * width, rows), BF16),
            pltpu.VMEM((2 * heads, AUG, rows), BF16),
            pltpu.VMEM((2 * heads, AUG, rows), F32),
        ]
        + doc_scratch(doc_lengths, roster)
        + [pltpu.SemaphoreType.DMA((count + 2,))],
        16 if count < 8 else 40,
        after,
    )


def backward_kernel(first, count, heads, more, last, len_any, roster_any, *refs):
    q_own, q_pair, g_own, g_pair, o_own, o_pair, t_own, t_pair = refs[:8]
    kv_refs, refs = refs[8 : 8 + count], refs[8 + count :]
    if more:
        dq_in, refs = refs[0], refs[1:]
    outs, refs = refs[:count], refs[count:]
    dq_outs, refs = (refs[:2], refs[2:]) if last else (refs[:1], refs[1:])
    kv, q_aug, delta, dq, dkv, len_ref, roster_ref, sems = refs
    rows = q_own.shape[1]
    width = heads * HDIM
    me = lax.axis_index("seq")
    copies = [pltpu.make_async_copy(kv_refs[j], kv.at[j], sems.at[j]) for j in range(count)]
    for copy in copies:
        copy.start()
    fetch_docs(len_any, roster_any, len_ref, roster_ref, sems.at[count], sems.at[count + 1])
    ends = doc_bounds(len_ref)
    bases = (roster_ref[me] * rows, roster_ref[me ^ 1] * rows)
    for g, (q_ref, g_ref, o_ref) in enumerate(((q_own, g_own, o_own), (q_pair, g_pair, o_pair))):
        mark = doc_rows(ends, bases[g], rows).astype(BF16)
        for h in range(heads):
            part = slice(h * HDIM, (h + 1) * HDIM)
            q_aug[g * heads + h, :HDIM, :] = q_ref[part, :]
            q_aug[g * heads + h, HDIM:, :] = mark
            product = g_ref[part, :].astype(F32) * o_ref[part, :].astype(F32)
            delta[g * heads + h] = jnp.broadcast_to(
                jnp.sum(product, axis=0, keepdims=True), (8, rows)
            )
    if more:
        dq[...] = dq_in[...]
    else:
        dq[...] = jnp.zeros_like(dq)
    for copy in copies:
        copy.wait()

    def block(j, carry):
        key_base = roster_ref[key_row(j + first, me)] * rows
        ban = ban_rows(ends, key_base, rows).astype(BF16)
        dkv[j] = jnp.zeros((2 * width, rows), F32)
        for g, (g_ref, t_ref) in enumerate(((g_own, t_own), (g_pair, t_pair))):

            @pl.when(meet(ends, bases[g], key_base, rows))
            def _():
                for h in range(heads):
                    at = g * heads + h
                    part = slice(h * HDIM, (h + 1) * HDIM)
                    late = slice(width + h * HDIM, width + (h + 1) * HDIM)
                    keys = kv[j, part, :]
                    scores = mm(jnp.concatenate([keys, ban], axis=0), q_aug[at], TN)
                    probs = jnp.exp(scores - t_ref[h, 0:1, :])
                    prob_grads = mm(kv[j, late, :], g_ref[part, :], TN)
                    score_grad = (probs * (prob_grads - delta[at, 0:1, :])).astype(BF16)
                    dkv[j, late, :] += mm(g_ref[part, :], probs.astype(BF16), NT)
                    dkv[j, part, :] += mm(q_aug[at, :HDIM, :], score_grad, NT)
                    dq[at] += mm(keys, score_grad, NN)

        return carry

    lax.fori_loop(0, count, block, 0)
    for j in range(count):
        outs[j][...] = dkv[j].astype(outs[j].dtype)
    if last:
        for h in range(heads):
            part = slice(h * HDIM, (h + 1) * HDIM)
            dq_outs[0][part, :] = dq[h] * HDIM**-0.5
            dq_outs[1][part, :] = (dq[heads + h] * HDIM**-0.5).astype(BF16)
    else:
        dq_outs[0][...] = dq[...]


def attention_backward(first, last, doc_lengths, roster, held, blocks, dq=None, after=()):
    width, rows = held[0].shape
    heads = width // HDIM
    count = len(blocks)
    given = [] if dq is None else [(dq, "v")]
    if last:
        queries = [((width, rows), F32, "v"), ((width, rows), BF16, "v")]
    else:
        queries = [((2 * heads, HDIM, rows), F32, "v")]
    return call(
        "attention_backward",
        functools.partial(backward_kernel, first, count, heads, bool(given), last),
        kinds((doc_lengths, roster), "raw") + kinds(held, "v") + kinds(blocks, "free") + given,
        [((2 * width, rows), BF16 if first else F32, "v")] * count + queries,
        [
            pltpu.VMEM((count, 2 * width, rows), BF16),
            pltpu.VMEM((2 * heads, AUG, rows), BF16),
            pltpu.VMEM((2 * heads, 8, rows), F32),
            pltpu.VMEM((2 * heads, HDIM, rows), F32),
            pltpu.VMEM((count, 2 * width, rows), F32),
        ]
        + doc_scratch(doc_lengths, roster)
        + [pltpu.SemaphoreType.DMA((count + 2,))],
        16 if count < 8 else 40,
        after,
    )


def join_kernel(heads, own_ref, back_ref, out_ref, total_ref, mine_ref, other_ref):
    rows = own_ref.shape[2]
    for h in range(heads):
        top_own = own_ref[h, 72:73, :]
        top_back = back_ref[h, 72:73, :]
        top = jnp.maximum(top_own, top_back)
        fade_own = jnp.exp(top_own - top)
        fade_back = jnp.exp(top_back - top)
        total = own_ref[h, 64:65, :] * fade_own + back_ref[h, 64:65, :] * fade_back
        share_own = fade_own / total
        share_back = fade_back / total
        value = own_ref[h, :HDIM, :] * share_own + back_ref[h, :HDIM, :] * share_back
        out_ref[h * HDIM : (h + 1) * HDIM, :] = value.astype(BF16)
        total_ref[h] = jnp.broadcast_to(top + jnp.log(total), (8, rows))
    half = rows // 2
    for bit in range(2):

        @pl.when(lax.axis_index("tp") % 2 == bit)
        def _():
            mine_ref[...] = out_ref[:, bit * half : (bit + 1) * half]
            other_ref[...] = out_ref[:, (1 - bit) * half : (2 - bit) * half]


def join(own, back):
    heads, unused, rows = own.shape
    return call(
        "join",
        functools.partial(join_kernel, heads),
        [(own, "v"), (back, "v")],
        [
            ((heads * HDIM, rows), BF16, "v"),
            ((heads, 8, rows), F32, "v"),
            ((heads * HDIM, rows // 2), BF16, "v"),
            ((heads * HDIM, rows // 2), BF16, "v"),
        ],
    )


def pick_kernel(in_any, down_any, out_ref, sems):
    core = lax.axis_index("seq") % 2
    at = 0
    copies = []
    for n, source in enumerate((in_any, down_any)):
        rows = source.shape[0] // 2
        mine = pl.ds(pl.multiple_of(core * rows, rows), rows)
        copies.append(
            pltpu.make_async_copy(source.at[mine], out_ref.at[pl.ds(at, rows)], sems.at[n])
        )
        at += rows
    for copy in copies:
        copy.start()
    for copy in copies:
        copy.wait()


def pick(in_t, w_down):
    (out,) = call(
        "pick",
        pick_kernel,
        kinds((in_t, w_down), "raw"),
        [(((in_t.shape[0] + w_down.shape[0]) // 2, in_t.shape[1]), BF16, "v")],
        [pltpu.SemaphoreType.DMA((2,))],
    )
    return out


def keep_kernel(in_ref, out_ref):
    out_ref[...] = in_ref[...]


def keep_until(value, after):
    (out,) = call("keep", keep_kernel, [(value, "v")], [(value.shape, value.dtype, "v")], (), 16, after)
    return out


def stage_kernel(x_any, cot_any, w_any, in_any, down_any, got_ref, rest_ref, *refs):
    x_ref, cot_ref, w_ref, in_ref, down_ref, sems = refs
    half = x_ref.shape[0]
    core = lax.axis_index("seq") % 2
    mine = pl.ds(pl.multiple_of(lax.axis_index("tp") % 2 * half, half), half)
    moves = [(w_any, w_ref), (x_any.at[mine], x_ref), (cot_any.at[mine], cot_ref)]
    at = 0
    for own, ref in ((in_any, in_ref), (down_any, down_ref)):
        rows = own.shape[0] // 2
        moves.append((own, ref.at[pl.ds(0, 2 * rows)]))
        for source, side in ((got_ref, core), (rest_ref, 1 - core)):
            spot = pl.multiple_of(2 * rows + side * rows, rows)
            moves.append((source.at[pl.ds(at, rows)], ref.at[pl.ds(spot, rows)]))
        at += rows
    copies = [pltpu.make_async_copy(*move, sems.at[n]) for n, move in enumerate(moves)]
    for copy in copies:
        copy.start()
    for copy in copies:
        copy.wait()


def stage(tokens, cotangent, w_full, in_t, w_down, got, rest):
    rows, model = tokens.shape
    return call(
        "stage",
        stage_kernel,
        kinds((tokens, cotangent, w_full, in_t, w_down), "raw") + kinds((got, rest), "v"),
        [
            ((rows // 2, model), BF16, "v"),
            ((rows // 2, model), BF16, "v"),
            (w_full.shape, BF16, "v"),
            ((2 * in_t.shape[0], model), BF16, "v"),
            ((2 * w_down.shape[0], model), BF16, "v"),
        ],
        [pltpu.SemaphoreType.DMA((9,))],
    )


def gated(units, first, gate_up, mixed_grad, mixed_out, gate_out):
    def wave(i, carry):
        spot = pl.ds(first + i * 32, 32)
        at = pl.ds(2 * first + i * 32, 32)
        late = pl.ds(2 * first + units + i * 32, 32)
        gate = gate_up[at, :]
        up = gate_up[late, :]
        back = mixed_grad[spot, :]
        bell = 0.5 * (1.0 + lax.erf(gate * (2.0**-0.5)))
        active = gate * bell
        slope = bell + gate * jnp.exp(-0.5 * gate * gate) * ((2.0 * jnp.pi) ** -0.5)
        mixed_out[spot, :] = (active * up).astype(BF16)
        gate_out[at, :] = (back * up * slope).astype(BF16)
        gate_out[late, :] = (back * active).astype(BF16)
        return carry

    lax.fori_loop(0, units // 32, wave, 0)


def feed_kernel(n_tp, need, give, x_ref, cot_ref, w_ref, in_ref, down_ref, gain_ref, *refs):
    out_refs = refs[:n_tp]
    middle_out, part_out, h_out, mixed_out, gate_out, gain_out = refs[n_tp : n_tp + 6]
    keep_ref, *send_refs = refs[n_tp + 6 : n_tp + 6 + n_tp // 2]
    outs, unit, gate_up, mixed_grad, grad = refs[n_tp + 6 + n_tp // 2 :]
    rows = x_ref.shape[0]
    part = keep_ref.shape[0]
    units = down_ref.shape[0] // 2
    width = out_refs[0].shape[0]
    tp = lax.axis_index("tp")
    for k in range(n_tp):
        at = pl.ds(pl.multiple_of((tp ^ k) * width, width), width)
        outs[at, :] = out_refs[k][...]
    mixed_grad[...] = mm(down_ref[...], cot_ref[...], NT)
    middle_out[...] = mm(outs[...], w_ref[...], TN)
    need(5)
    gain = gain_ref[...].reshape(1, -1)

    def strip(i, carry):
        at = pl.ds(i * 32, 32)
        middle = middle_out[at, :] + x_ref[at, :].astype(F32)
        middle_out[at, :] = middle
        held, unused = normed(middle)
        unit[at, :] = held
        h_out[at, :] = (held * gain).astype(BF16)
        return carry

    lax.fori_loop(0, rows // 32, strip, 0)
    give(0, 2)
    gate_up[...] = mm(in_ref[...], h_out[...], NT)
    for first in (0, units):
        gated(units, first, gate_up, mixed_grad, mixed_out, gate_out)
    give(3, 4)
    grad[...] = mm(gate_out[...], in_ref[...], TN)
    for n, ref in enumerate((keep_ref, *send_refs)):
        at = pl.ds(pl.multiple_of((tp ^ (2 * n)) // 2 * part, part), part)
        ref[...] = grad[at, :].astype(ref.dtype)
        give(6 + n)
    own = pl.ds(pl.multiple_of(tp // 2 * part, part), part)
    part_out[...] = middle_out[own, :]
    give(1)

    def gains(i, carry):
        at = pl.ds(i * 32, 32)
        product = grad[at, :] * unit[at, :]
        return carry + jnp.sum(product.reshape(4, 8, -1), axis=0)

    gain_out[...] = lax.fori_loop(0, rows // 32, gains, jnp.zeros(gain_out.shape, F32))


def feed(gain, staged, outs):
    rows, model = staged[0].shape
    n_tp = len(outs)
    units = staged[4].shape[0]
    part = 2 * rows // n_tp
    return call(
        "feed",
        functools.partial(feed_kernel, n_tp),
        kinds(staged, "v") + [(gain, "h")] + kinds(outs, "v"),
        [
            ((rows, model), F32, "h"),
            ((part, model), F32, "h"),
            ((rows, model), BF16, "h"),
            ((units, rows), BF16, "h"),
            ((2 * units, rows), BF16, "h"),
            ((8, model), F32, "h"),
            ((part, model), F32, "h"),
        ]
        + [((part, model), BF16, "h")] * (n_tp // 2 - 1),
        [
            pltpu.VMEM((n_tp * outs[0].shape[0], rows), BF16),
            pltpu.VMEM((rows, model), F32),
            pltpu.VMEM((2 * units, rows), F32),
            pltpu.VMEM((units, rows), F32),
            pltpu.VMEM((rows, model), F32),
        ],
        24,
        lazy=True,
    )


def branch_kernel(n_tp, count, need, give, middle_ref, cot_ref, gain_ref, w_ref, *refs):
    arrived = refs[:count]
    grad_out, branch_out = refs[count : count + 2]
    piece_refs = refs[count + 2 :]
    width = piece_refs[0].shape[1]
    tp = lax.axis_index("tp")
    need(0, 1, 2, 4)
    total = arrived[0][...]
    for ref in arrived[1:]:
        total = total + ref[...].astype(F32)
    unit, scale = normed(middle_ref[...])
    gain = gain_ref[...].reshape(1, -1)
    value = cot_ref[...].astype(F32) + norm_back(unit, scale, total, gain)
    grad_out[...] = value
    branch_out[...] = value.astype(BF16)
    give(0, 1)
    need(3)
    for k in range(n_tp):
        at = pl.ds(pl.multiple_of((tp ^ k) * width, width), width)
        piece_refs[k][...] = mm(branch_out[...], w_ref[at, :], NT).astype(BF16)


def branch(n_tp, middle_part, cotangent, gain, w_full, arrived, after):
    part, model = arrived[0].shape
    width = w_full.shape[0] // n_tp
    return call(
        "branch",
        functools.partial(branch_kernel, n_tp, len(arrived)),
        [(middle_part, "h"), (cotangent, part)]
        + [(gain, "h"), (w_full, "v"), (arrived[0], "h")]
        + kinds(arrived[1:], "v"),
        [((part, model), F32, "h"), ((part, model), BF16, "h")]
        + [((part, width), BF16, "v")] * n_tp,
        (),
        16,
        after,
        True,
    )


def lay_kernel(n_tp, *refs):
    out_ref, held = refs[n_tp:]
    part = refs[0].shape[0]
    tp = lax.axis_index("tp")
    for k in range(n_tp):
        at = pl.ds(pl.multiple_of(slot(tp ^ k, n_tp) * part, part), part)
        held[at, :] = refs[k][...].astype(F32)
    out_ref[...] = held[...].T.astype(BF16)


def lay_turned(pieces, after):
    part, width = pieces[0].shape
    rows = part * len(pieces)
    (out,) = call(
        "lay_turned",
        functools.partial(lay_kernel, len(pieces)),
        kinds(pieces, "v"),
        [((width, rows), BF16, "v")],
        [pltpu.VMEM((rows, width), F32)],
        16,
        after,
    )
    return out


def stack_kernel(n_tp, *refs):
    out_ref = refs[n_tp]
    part = refs[0].shape[0]
    tp = lax.axis_index("tp")
    for k in range(n_tp):
        at = pl.ds(pl.multiple_of(slot(tp ^ k, n_tp) * part, part), part)
        out_ref[at, :] = refs[k][...]


def stack_parts(pieces, after=(), flops=0):
    part, model = pieces[0].shape
    (out,) = call(
        "stack_parts",
        functools.partial(stack_kernel, len(pieces)),
        kinds(pieces, "v"),
        [((part * len(pieces), model), pieces[0].dtype, "h")],
        (),
        16,
        after,
        flops=flops,
    )
    return out


def turn_back(out_ref, first, value, cos_table, sin_table):
    for at in range(0, value.shape[0], HDIM):
        low = value[at : at + HALF]
        high = value[at + HALF : at + HDIM]
        spot = first + at
        out_ref[spot : spot + HALF, :] = (low * cos_table + high * sin_table).astype(BF16)
        out_ref[spot + HALF : spot + HDIM, :] = (high * cos_table - low * sin_table).astype(BF16)


def unproject_kernel(
    count, n_tp, need, give, x_ref, w_ref, cos_ref, sin_ref, two_ref, dq_ref, dq_back, *refs
):
    dkv_refs = refs[:count]
    proj_out = refs[count]
    part_refs = refs[count + 1 : count + 1 + n_tp]
    grad, dkv = refs[count + 1 + n_tp :]
    rows, model = x_ref.shape
    part = rows // n_tp
    width = dq_ref.shape[0]
    tp = lax.axis_index("tp")
    need(2, 3)
    cos_table = cos_ref[...]
    sin_table = sin_ref[...]
    turn_back(proj_out, 0, dq_ref[...] + dq_back[...].astype(F32), cos_table, sin_table)
    total = dkv_refs[0][...]
    for ref in dkv_refs[1:]:
        total = total + ref[...].astype(F32)
    dkv[...] = total
    turn_back(proj_out, width, dkv[:width, :], cos_table, sin_table)
    proj_out[2 * width :, :] = dkv[width:, :].astype(BF16)
    need(1)
    grad[...] = mm(proj_out[...], w_ref[...], TN)
    need(0, 4)

    def gains(i, carry):
        at = pl.ds(i * STRIP, STRIP)
        unit, unused = normed(x_ref[at, :].astype(F32))
        product = grad[at, :] * unit
        return carry + jnp.sum(product.reshape(STRIP // 8, 8, -1), axis=0)

    gain = lax.fori_loop(0, rows // STRIP, gains, jnp.zeros((8, model), F32))
    line = lax.broadcasted_iota(jnp.int32, (16, model), 0)
    gain_two = jnp.sum(two_ref[...], axis=0, keepdims=True)
    gain = jnp.sum(gain, axis=0, keepdims=True)
    gain = jnp.where(line == 0, gain, jnp.where(line == 1, gain_two, 0.0))
    for k in range(n_tp):
        at = pl.ds(pl.multiple_of(slot(tp ^ k, n_tp) * part, part), part)
        part_refs[k][:part, :] = grad[at, :].astype(part_refs[k].dtype)
        part_refs[k][part:, :] = gain.astype(part_refs[k].dtype)


def unproject(n_tp, tokens, qkv_t, cos_table, sin_table, gain_two_part, dq, dq_back, dkvs, after):
    rows, model = tokens.shape
    part = rows // n_tp
    return call(
        "unproject",
        functools.partial(unproject_kernel, len(dkvs), n_tp),
        kinds((tokens, qkv_t, cos_table, sin_table, gain_two_part), "v")
        + kinds((dq, dq_back, *dkvs), "v"),
        [((qkv_t.shape[0], rows), BF16, "v"), ((part + 16, model), F32, "v")]
        + [((part + 16, model), BF16, "v")] * (n_tp - 1),
        [pltpu.VMEM((rows, model), F32), pltpu.VMEM(dkvs[0].shape, F32)],
        16,
        after,
        True,
    )


def input_kernel(x_ref, gain_ref, grad_ref, sum_ref, out_ref, gain_out):
    part, model = grad_ref.shape
    total = sum_ref[...]
    unit, scale = normed(x_ref[...].astype(F32))
    gain = gain_ref[...].reshape(1, -1)
    value = grad_ref[...] + norm_back(unit, scale, total[:part], gain)
    out_ref[...] = value.astype(BF16)
    gain_out[...] = total[part : part + 8]


def input_side(tokens, gain, middle_grad, summed, after):
    part, model = middle_grad.shape
    return call(
        "input_side",
        input_kernel,
        [(tokens, part), (gain, "h"), (middle_grad, "v"), (summed, "v")],
        [((part, model), BF16, "v"), ((8, model), F32, "v")],
        (),
        16,
        after,
    )


def early_kernel(mixed_ref, gate_ref, cot_ref, h_ref, in_ref, down_ref, h_pair, *refs):
    keep_ref, send_ref, gate_up, mixed_grad, mixed, gate = refs
    units = down_ref.shape[0]
    half = h_ref.shape[0]
    bit = lax.axis_index("tp") % 2
    mine = pl.ds(pl.multiple_of(bit * half, half), half)
    other = pl.ds(pl.multiple_of((1 - bit) * half, half), half)
    gate_up[...] = mm(in_ref[...], h_pair[...], NT)
    mixed_grad[...] = mm(down_ref[...], cot_ref[other, :], NT)
    gated(units, 0, gate_up, mixed_grad, mixed, gate)
    width = keep_ref.shape[1]
    core = lax.axis_index("seq") % 2
    for ref, side in ((send_ref, 1 - core), (keep_ref, core)):
        columns = pl.ds(pl.multiple_of(side * width, width), width)
        down = mm(mixed_ref[:units, :], cot_ref[mine, columns], NN)
        down = down + mm(mixed[...], cot_ref[other, columns], NN)
        ref[:units, :] = down.astype(ref.dtype)
        both = mm(gate_ref[: 2 * units, :], h_ref[:, columns], NN)
        both = both + mm(gate[...], h_pair[:, columns], NN)
        ref[units:, :] = both.astype(ref.dtype)


def early_grads(mixed, gate_grad, cotangent, h_two, in_t, w_down, h_pair, after):
    units, model = w_down.shape
    half = h_two.shape[0]
    return call(
        "early_grads",
        early_kernel,
        kinds((mixed, gate_grad, cotangent, h_two, in_t, w_down), "h") + [(h_pair, "v")],
        [((3 * units, model // 2), F32, "v"), ((3 * units, model // 2), BF16, "v")],
        [
            pltpu.VMEM((2 * units, half), F32),
            pltpu.VMEM((units, half), F32),
            pltpu.VMEM((units, half), BF16),
            pltpu.VMEM((2 * units, half), BF16),
        ],
        24,
        after,
    )


def late_kernel(n_tp, proj_ref, h_ref, out_ref, *refs):
    branch_refs = refs[:n_tp]
    keep_ref, send_ref, branch_full = refs[n_tp:]
    part = branch_refs[0].shape[0]
    half = keep_ref.shape[1]
    wide = proj_ref.shape[0]
    tp = lax.axis_index("tp")
    core = lax.axis_index("seq") % 2
    for k in range(n_tp):
        at = pl.ds(pl.multiple_of(slot(tp ^ k, n_tp) * part, part), part)
        branch_full[at, :] = branch_refs[k][...]
    for ref, side in ((send_ref, 1 - core), (keep_ref, core)):
        columns = pl.ds(pl.multiple_of(side * half, half), half)
        ref[:wide, :] = mm(proj_ref[...], h_ref[:, columns], NN).astype(ref.dtype)
        ref[wide:, :] = mm(out_ref[...], branch_full[:, columns], NN).astype(ref.dtype)


def late_grads(proj_grad, h_one, out_b, branches, after):
    rows, model = h_one.shape
    wide = proj_grad.shape[0] + out_b.shape[0]
    return call(
        "late_grads",
        functools.partial(late_kernel, len(branches)),
        [(proj_grad, "v"), (h_one, "v"), (out_b, "v"), (branches[0], "v")]
        + kinds(branches[1:], "v"),
        [((wide, model // 2), F32, "v"), ((wide, model // 2), BF16, "v")],
        [pltpu.VMEM((rows, model), BF16)],
        16,
        after,
    )


def spread_kernel(count, *refs):
    given, outs, held = refs[: -count - 1], refs[-count - 1 : -1], refs[-1]
    piece = outs[0].shape[0]
    chip = lax.axis_index("seq") // 2
    at = 0
    for keep_ref, back_ref in zip(given[::2], given[1::2]):
        rows = keep_ref.shape[0]
        held[at : at + rows, :] = keep_ref[...] + back_ref[...].astype(F32)
        at += rows
    if at < held.shape[0]:
        held[at:, :] = jnp.zeros((held.shape[0] - at, held.shape[1]), F32)
    for k in range(count):
        at = pl.ds(pl.multiple_of((chip ^ k) * piece, piece), piece)
        outs[k][...] = held[at, :].astype(outs[k].dtype)


def spread(count, *pairs):
    half = pairs[0][0].shape[1]
    rows = sum(keep.shape[0] for keep, unused in pairs)
    piece = -(-rows // (8 * count)) * 8
    return call(
        "spread",
        functools.partial(spread_kernel, count),
        [(array, "v") for pair in pairs for array in pair],
        [((piece, half), F32, "v")] + [((piece, half), BF16, "v")] * (count - 1),
        [pltpu.VMEM((count * piece, half), F32)],
    )


def piece_kernel(count, gain_ref, *refs):
    out_ref = refs[count]
    half = out_ref.shape[1]
    total = refs[0][...]
    for ref in refs[1:count]:
        total = total + ref[...].astype(F32)
    line = lax.broadcasted_iota(jnp.int32, (16, half), 0)
    gains = jnp.zeros((16, half), F32)
    for at in range(4):
        row = gain_ref[at // 2 : at // 2 + 1, at % 2 * half : (at % 2 + 1) * half]
        gains = jnp.where(line == at, row, gains)
    out_ref[...] = jnp.concatenate([total, gains], axis=0).astype(BF16)


def sum_piece(gains, pieces, after=()):
    piece, half = pieces[0].shape
    (out,) = call(
        "sum_piece",
        functools.partial(piece_kernel, len(pieces)),
        [(gains, "v")] + kinds(pieces, "v"),
        [((piece + 16, half), BF16, "v")],
        (),
        16,
        after,
    )
    return out


def collect_kernel(count, *refs):
    out_ref, held = refs[count:]
    piece = refs[0].shape[0] - 16
    wide = count * piece
    chip = lax.axis_index("seq") // 2
    gains = jnp.zeros((16, out_ref.shape[1]), F32)
    for k in range(count):
        at = pl.ds(pl.multiple_of((chip ^ k) * piece, piece), piece)
        whole = refs[k][...].astype(F32)
        held[at, :] = whole[:piece]
        gains = gains + whole[piece:]
    held[wide:, :] = gains
    out_ref[...] = held[...].astype(BF16)


def collect(pieces, after=()):
    piece, half = pieces[0].shape
    wide = (piece - 16) * len(pieces) + 16
    (out,) = call(
        "collect",
        functools.partial(collect_kernel, len(pieces)),
        kinds(pieces, "v"),
        [((wide, half), BF16, "v")],
        [pltpu.VMEM((wide, half), F32)],
        16,
        after,
    )
    return out


def finish_kernel(sizes, own_ref, pair_ref, *refs):
    out_refs, gain_refs = refs[: len(sizes)], refs[len(sizes) :]
    half = own_ref.shape[1]
    core = lax.axis_index("seq") % 2
    for ref, side in ((own_ref, core), (pair_ref, 1 - core)):
        columns = pl.ds(pl.multiple_of(side * half, half), half)
        at = 0
        for out_ref, size in zip(out_refs, sizes):
            out_ref[:, columns] = ref[at : at + size, :].astype(F32)
            at += size
    first = own_ref.shape[0] - 16
    gains = own_ref[first:, :].astype(F32) + pair_ref[first:, :].astype(F32)
    for at, ref in zip((0, 2), gain_refs):
        ref[pl.ds(0, half)] = gains[at]
        ref[pl.ds(half, half)] = gains[at + 1]


def finish(own, pair, sizes):
    model = 2 * own.shape[1]
    return call(
        "finish",
        functools.partial(finish_kernel, sizes),
        [(own, "v"), (pair, "v")],
        [((size, model), F32, "h") for size in sizes] + [((model,), F32, "h")] * 2,
        (),
        24,
    )


def down_kernel(mixed_ref, w_ref, middle_ref, keep_ref, *refs):
    send_refs, total = refs[:-1], refs[-1]
    part = keep_ref.shape[0]
    tp = lax.axis_index("tp")
    total[...] = mm(mixed_ref[...], w_ref[...], TN)
    own = pl.ds(pl.multiple_of(tp // 2 * part, part), part)
    keep_ref[...] = total[own, :] + middle_ref[own, :]
    for n, ref in enumerate(send_refs):
        at = pl.ds(pl.multiple_of((tp ^ (2 * n + 2)) // 2 * part, part), part)
        ref[...] = total[at, :].astype(ref.dtype)


def down(n_tp, mixed, w_both, middle, after):
    rows, model = middle.shape
    part = 2 * rows // n_tp
    return call(
        "down",
        down_kernel,
        [(mixed, "h"), (w_both, "v"), (middle, "h")],
        [((part, model), F32, "h")] + [((part, model), BF16, "h")] * (n_tp // 2 - 1),
        [pltpu.VMEM((rows, model), F32)],
        16,
        after,
    )


def total_kernel(count, *refs):
    total = refs[0][...]
    for ref in refs[1:count]:
        total = total + ref[...].astype(F32)
    refs[count][...] = total.astype(refs[count].dtype)


def total_of(parts, dtype=BF16, kind="v", after=(), flops=0):
    (out,) = call(
        "total_of",
        functools.partial(total_kernel, len(parts)),
        [(parts[0], kind)] + kinds(parts[1:], "v"),
        [(parts[0].shape, dtype, "v")],
        (),
        16,
        after,
        flops=flops,
    )
    return out


def body(
    n_seq,
    n_tp,
    tokens,
    gain_one,
    w_qkv,
    w_out,
    gain_two,
    w_in,
    w_down,
    cotangent,
    doc_lengths,
    roster,
):
    rows, model = tokens.shape
    width = w_qkv.shape[2]
    units = w_in.shape[2]
    count = n_seq // 2
    qkv_t = w_qkv.transpose(1, 2, 0).reshape(3 * width, model)
    in_t = w_in.transpose(1, 2, 0).reshape(2 * units, model)
    over_tp = lambda x, k: swap(x, "tp", k, n_tp)
    over_chips = lambda x, k: swap(x, "seq", 2 * k, n_seq)
    over_cores = lambda x: swap(x, "seq", 1, n_seq)
    everywhere = lambda xs: [xs[0]] + [over_tp(xs[k], k) for k in range(1, n_tp)]

    def by_steps(part):
        parts = {0: part}
        hop = n_tp // 2
        while hop:
            parts.update({k ^ hop: over_tp(x, hop) for k, x in parts.items()})
            hop //= 2
        return [parts[k] for k in range(n_tp)]

    docs = (doc_lengths, roster)

    queries, kv, h_one, cos_table, sin_table = project(*docs, tokens, gain_one, qkv_t)
    blocks = [kv] + [over_chips(kv, j) for j in range(1, count)]
    q_pair = over_cores(queries)
    w_full = lax.all_gather(w_out, "tp", axis=0, tiled=True)
    got = over_tp(pick(in_t, w_down), 1)

    split = (count + 1) // 2
    (state,) = attention_forward(0, False, *docs, queries, q_pair, blocks[:split])
    state_own, state_pair = attention_forward(
        split, True, *docs, queries, q_pair, blocks[split:], state
    )
    out_b, totals, out_mine, out_other = join(state_own, over_cores(state_pair))
    outs = [out_mine] + [over_tp(out_other if k % 2 else out_mine, k) for k in range(1, n_tp)]
    out_pair = over_cores(out_b)
    totals_pair = over_cores(totals)

    got = keep_until(got, [(state_pair, "v")])
    staged = stage(tokens, cotangent, w_full, in_t, w_down, got, over_cores(got))
    middle, middle_part, h_two, mixed, gate_grad, gain_two_part, own, *others = feed(
        gain_two, staged, outs
    )
    arrived = [own] + [over_tp(others[n], 2 * n + 2) for n in range(n_tp // 2 - 1)]
    own, *others = down(n_tp, mixed, staged[4], middle, ())
    middle_grad, branch_grad, *pieces = branch(
        n_tp, middle_part, cotangent, gain_two, staged[2], arrived, [(own, "h")]
    )
    early, early_send = early_grads(
        mixed, gate_grad, cotangent, h_two, in_t, w_down, over_tp(h_two, 1), [(branch_grad, "h")]
    )
    out_grad = lay_turned(everywhere(pieces), [(early, "v")])
    grad_pair = over_cores(out_grad)
    branches = by_steps(branch_grad)

    held = (queries, q_pair, out_grad, grad_pair, out_b, out_pair, totals, totals_pair)
    *terms, dq = attention_backward(1, False, *docs, held, blocks[1:], None)
    total = total_of(
        [own] + [over_tp(others[n], 2 * n + 2) for n in range(n_tp // 2 - 1)],
        BF16,
        "h",
        [(dq, "v")],
    )
    totals_all = by_steps(total)

    dkv, dq_own, dq_pair = attention_backward(0, True, *docs, held, blocks[:1], dq)
    dkvs = [dkv] + [over_chips(terms[j - 1], j) for j in range(1, count)]

    proj_grad, *parts = unproject(
        n_tp,
        tokens,
        qkv_t,
        cos_table,
        sin_table,
        gain_two_part,
        dq_own,
        over_cores(dq_pair),
        dkvs,
        [(total, "v")],
    )
    layer_out = stack_parts(totals_all)
    keep, send = late_grads(proj_grad, h_one, out_b, branches, [(totals_all[n_tp // 2], "v")])
    own, *others = spread(count, (keep, over_cores(send)), (early, over_cores(early_send)))
    came = everywhere(parts)
    summed = total_of(came[:2] + came[:1:-1], F32, flops=2_000_000_000)
    chip_sum = total_of(
        [own] + [over_chips(others[k - 1], k) for k in range(1, count)], F32, "v", ()
    )
    input_part, gains = input_side(tokens, gain_one, middle_grad, summed, [(own, "v")])
    inputs_all = everywhere([input_part] * n_tp)
    piece = sum_piece(gains, [chip_sum], ())
    input_grad = stack_parts(inputs_all, (), 3_000_000_000)
    collected = collect(
        [piece] + [over_chips(piece, k) for k in range(1, count)], [(input_grad, "h"), (layer_out, "h")]
    )
    grad_qkv, grad_out, grad_down, grad_in, grad_one, grad_two = finish(
        collected, over_cores(collected), (3 * width, width, units, 2 * units)
    )

    back = lambda x, n: x.reshape(-1, n, model).transpose(2, 0, 1)
    return (
        layer_out,
        input_grad,
        grad_one,
        back(grad_qkv, width),
        grad_out,
        grad_two,
        back(grad_in, units),
        grad_down,
    )


def solution(mesh):
    placed = (
        P("seq", None),
        P(),
        P(None, None, "tp"),
        P("tp", None),
        P(),
        P(None, None, "tp"),
        P("tp", None),
        P("seq", None),
        P(),
        P(),
    )
    return jax.shard_map(
        functools.partial(body, mesh.shape["seq"], mesh.shape["tp"]),
        mesh=mesh,
        in_specs=placed,
        out_specs=(
            P("seq", None),
            P("seq", None),
            P(),
            P(None, None, "tp"),
            P("tp", None),
            P(),
            P(None, None, "tp"),
            P("tp", None),
        ),
        check_vma=False,
    )
```

```python
import functools
import math

import jax
import jax.numpy as jnp
import numpy as np
from jax import lax
from jax.experimental import pallas as pl
from jax.experimental.pallas import tpu as pltpu
from jax.sharding import PartitionSpec as P

HDIM = 64
HALF = HDIM // 2
EPSILON = 1e-05
ROPE_THETA = 160000.0
MASKED = -1e30
AUG = 80
STRIP = 64
F32 = jnp.float32
BF16 = jnp.bfloat16
HBM = pl.BlockSpec(memory_space=pltpu.HBM)
VMEM = pl.BlockSpec(memory_space=pltpu.VMEM)

NN = (((1,), (0,)), ((), ()))
NT = (((1,), (1,)), ((), ()))
TN = (((0,), (0,)), ((), ()))


def params(mib):
    return pltpu.CompilerParams(vmem_limit_bytes=mib * 2**20)


def slot(tp, n_tp):
    return tp % 2 * (n_tp // 2) + tp // 2


def hop(n, count):
    return (count - n) % count


def came(count, send):
    return [send(hop(n, count)) for n in range(1, count)]


def mm(a, b, dims):
    return lax.dot_general(a, b, dims, preferred_element_type=F32)


def shaped(shape, dtype):
    return jax.ShapeDtypeStruct(shape, dtype)


def kinds(arrays, kind):
    return [(array, kind) for array in arrays]


def pin(array, kind):
    return array if kind in ("v", "free") else pltpu.with_memory_space_constraint(array, pltpu.HBM)


def call(name, kernel, ins, outs, scratch=(), mib=16, after=(), lazy=False, flops=0):
    fetched = [i for i, given in enumerate(ins) if given[1] not in ("v", "raw", "free")]
    left = [i for i, out in enumerate(outs) if out[2] == "h"]

    def held(array, kind):
        rows = array.shape[0] if kind == "h" else kind
        return pltpu.VMEM((rows,) + array.shape[1:], array.dtype)

    def run(*refs):
        in_refs = list(refs[: len(ins)])
        at = len(ins) + len(after)
        out_refs = list(refs[at : at + len(outs)])
        at += len(outs)
        own = refs[at : at + len(scratch)]
        at += len(scratch)
        buffers = refs[at : at + len(fetched) + len(left)]
        sems = refs[-1]
        copies = []
        for n, i in enumerate(fetched):
            source = in_refs[i]
            if ins[i][1] != "h":
                rows = ins[i][1]
                n_tp = ins[i][0].shape[0] // rows
                at = pl.multiple_of(slot(lax.axis_index("tp"), n_tp) * rows, rows)
                source = source.at[pl.ds(at, rows)]
            copies.append(pltpu.make_async_copy(source, buffers[n], sems.at[n]))
            in_refs[i] = buffers[n]
        for copy in copies:
            copy.start()
        coming = dict(zip(fetched, copies))
        going = {}
        for n, i in enumerate(left):
            spot = len(fetched) + n
            going[i] = pltpu.make_async_copy(buffers[spot], out_refs[i], sems.at[spot])
            out_refs[i] = buffers[spot]
        gone = []

        def need(*which):
            for i in which:
                if i in coming:
                    coming.pop(i).wait()

        def give(*which):
            for i in which:
                if i in going:
                    gone.append(going.pop(i))
                    gone[-1].start()

        if lazy:
            kernel(need, give, *in_refs, *out_refs, *own)
        else:
            need(*fetched)
            kernel(*in_refs, *out_refs, *own)
        need(*fetched)
        give(*left)
        for copy in gone:
            copy.wait()

    spec = lambda kind: VMEM if kind == "v" else HBM
    count = len(fetched) + len(left)
    return pl.pallas_call(
        run,
        out_shape=tuple(
            shaped(shape, dtype) if kind == "v" else pltpu.HBM(shape, dtype)
            for shape, dtype, kind in outs
        ),
        in_specs=[spec(kind) for unused, kind in ins] + [spec(kind) for unused, kind in after],
        out_specs=tuple(spec(kind) for unused, unused, kind in outs),
        scratch_shapes=list(scratch)
        + [held(*ins[i]) for i in fetched]
        + [pltpu.VMEM(outs[i][0], outs[i][1]) for i in left]
        + [pltpu.SemaphoreType.DMA((max(count, 1),))],
        name=name,
        cost_estimate=pl.CostEstimate(flops=flops, bytes_accessed=0, transcendentals=0)
        if flops
        else None,
        compiler_params=params(mib),
    )(*[pin(*given) for given in ins], *[pin(*given) for given in after])


def swap(x, axis, hop, count):
    return lax.ppermute(x, axis, [(i, i ^ hop) for i in range(count)])


def doc_scratch(doc_lengths, roster):
    return [pltpu.SMEM(doc_lengths.shape, jnp.int32), pltpu.SMEM(roster.shape, jnp.int32)]


def fetch_docs(len_any, roster_any, len_ref, roster_ref, len_sem, roster_sem):
    one = pltpu.make_async_copy(len_any, len_ref, len_sem)
    two = pltpu.make_async_copy(roster_any, roster_ref, roster_sem)
    one.start()
    two.start()
    one.wait()
    two.wait()


def doc_bounds(len_ref):
    ends, total = [], jnp.int32(0)
    for d in range(len_ref.shape[0]):
        total = total + len_ref[d]
        ends.append(total)
    return ends


def doc_of(ends, position):
    found = jnp.int32(0)
    for end in ends:
        found = found + (end <= position).astype(jnp.int32)
    return found


def meet(ends, base_a, base_b, rows):
    low = jnp.maximum(doc_of(ends, base_a), doc_of(ends, base_b))
    high = jnp.minimum(doc_of(ends, base_a + rows - 1), doc_of(ends, base_b + rows - 1))
    return low <= high


def doc_rows(ends, base, rows):
    spot = base + lax.broadcasted_iota(jnp.int32, (16, rows), 1)
    line = lax.broadcasted_iota(jnp.int32, (16, rows), 0)
    held = jnp.zeros((16, rows), F32)
    start = jnp.int32(0)
    for d, end in enumerate(ends):
        inside = (line == d) & (spot >= start) & (spot < end)
        held = jnp.where(inside, 1.0, held)
        start = end
    return held


def ban_rows(ends, base, rows):
    line = lax.broadcasted_iota(jnp.int32, (16, rows), 0)
    held = doc_rows(ends, base, rows)
    return jnp.where((held > 0.5) | (line >= len(ends)), 0.0, MASKED)


def key_row(block, seq_index):
    return seq_index ^ (2 * block)


def place_row(ends, base, rows):
    spot = base + lax.broadcasted_iota(jnp.int32, (1, rows), 1)
    start = jnp.zeros((1, rows), jnp.int32)
    for end in ends:
        start = jnp.where(spot >= end, end, start)
    return (spot - start).astype(F32)


def normed(values):
    centre = jnp.mean(values, axis=-1, keepdims=True)
    shifted = values - centre
    spread = jnp.mean(shifted * shifted, axis=-1, keepdims=True)
    scale = lax.rsqrt(spread + EPSILON)
    return shifted * scale, scale


def norm_back(unit, scale, grad, gain):
    u = grad * gain
    mean_u = jnp.mean(u, axis=-1, keepdims=True)
    mean_un = jnp.mean(u * unit, axis=-1, keepdims=True)
    return scale * (u - mean_u - unit * mean_un)


def project_kernel(
    width, need, give, len_any, roster_any, x_ref, w_ref, gain_ref, freq_ref, *refs
):
    q_out, kv_out, h_out, cos_out, sin_out = refs[:5]
    proj, len_ref, roster_ref, sems = refs[5:]
    rows = x_ref.shape[0]
    fetch_docs(len_any, roster_any, len_ref, roster_ref, sems.at[0], sems.at[1])
    need(5)
    ends = doc_bounds(len_ref)
    place = place_row(ends, roster_ref[lax.axis_index("seq")] * rows, rows)
    angles = place * freq_ref[...]
    cos_table = jnp.cos(angles)
    sin_table = jnp.sin(angles)
    cos_out[...] = cos_table
    sin_out[...] = sin_table
    give(3, 4)
    need(2, 4)
    gain = gain_ref[...].reshape(1, -1)

    def strip(i, carry):
        at = pl.ds(i * STRIP, STRIP)
        unit, unused = normed(x_ref[at, :].astype(F32))
        h_out[at, :] = (unit * gain).astype(BF16)
        return carry

    lax.fori_loop(0, rows // STRIP, strip, 0)
    give(2)
    need(3)
    proj[...] = mm(w_ref[...], h_out[...], NT)
    for at in range(0, 2 * width, HDIM):
        low = proj[at : at + HALF, :]
        high = proj[at + HALF : at + HDIM, :]
        turned_low = (low * cos_out[...] - high * sin_out[...]).astype(BF16)
        turned_high = (high * cos_out[...] + low * sin_out[...]).astype(BF16)
        if at < width:
            q_out[at : at + HALF, :] = (turned_low.astype(F32) * HDIM**-0.5).astype(BF16)
            q_out[at + HALF : at + HDIM, :] = (turned_high.astype(F32) * HDIM**-0.5).astype(BF16)
        else:
            kv_out[at - width : at - width + HALF, :] = turned_low
            kv_out[at - width + HALF : at - width + HDIM, :] = turned_high
    kv_out[width:, :] = proj[2 * width :, :].astype(BF16)


def project(doc_lengths, roster, tokens, gain, qkv_t):
    rows, model = tokens.shape
    width = qkv_t.shape[0] // 3
    freq = (ROPE_THETA ** -(np.arange(HALF) * (2.0 / HDIM))).astype(np.float32)[:, None]
    return call(
        "project",
        functools.partial(project_kernel, width),
        kinds((doc_lengths, roster), "raw") + kinds((tokens, qkv_t, gain, jnp.asarray(freq)), "h"),
        [
            ((width, rows), BF16, "v"),
            ((2 * width, rows), BF16, "v"),
            ((rows, model), BF16, "h"),
            ((HALF, rows), F32, "h"),
            ((HALF, rows), F32, "h"),
        ],
        [pltpu.VMEM((3 * width, rows), F32)]
        + doc_scratch(doc_lengths, roster)
        + [pltpu.SemaphoreType.DMA((2,))],
        lazy=True,
    )


def forward_kernel(first, count, heads, last, len_any, roster_any, q_own, q_pair, *refs):
    kv_refs = refs[:count]
    refs = refs[count:]
    if first:
        state_in, refs = refs[0], refs[1:]
    outs = refs[: 2 if last else 1]
    kv, q_aug, state, len_ref, roster_ref, sems = refs[len(outs) :]
    rows = q_own.shape[1]
    width = heads * HDIM
    me = lax.axis_index("seq")
    copies = [pltpu.make_async_copy(kv_refs[j], kv.at[j], sems.at[j]) for j in range(count)]
    for copy in copies:
        copy.start()
    fetch_docs(len_any, roster_any, len_ref, roster_ref, sems.at[count], sems.at[count + 1])
    ends = doc_bounds(len_ref)
    bases = (roster_ref[me] * rows, roster_ref[me ^ 1] * rows)
    for g, q_ref in enumerate((q_own, q_pair)):
        mark = doc_rows(ends, bases[g], rows).astype(BF16)
        for h in range(heads):
            q_aug[g * heads + h, :HDIM, :] = q_ref[h * HDIM : (h + 1) * HDIM, :]
            q_aug[g * heads + h, HDIM:, :] = mark
    if first:
        state[...] = state_in[...]
    else:
        line = lax.broadcasted_iota(jnp.int32, (2 * heads, AUG, rows), 1)
        state[...] = jnp.where(line >= 72, MASKED, 0.0)
    for copy in copies:
        copy.wait()

    top = lax.broadcasted_iota(jnp.int32, (16, rows), 0) == 0
    ones = jnp.where(top, 1.0, 0.0).astype(BF16)

    def block(j, carry):
        key_base = roster_ref[key_row(j + first, me)] * rows
        ban = ban_rows(ends, key_base, rows).astype(BF16)
        for g in range(2):

            @pl.when(meet(ends, bases[g], key_base, rows))
            def _():
                for h in range(heads):
                    at = g * heads + h
                    keys = jnp.concatenate([kv[j, h * HDIM : (h + 1) * HDIM, :], ban], axis=0)
                    vals = jnp.concatenate(
                        [kv[j, width + h * HDIM : width + (h + 1) * HDIM, :], ones], axis=0
                    )
                    scores = mm(keys, q_aug[at], TN)
                    old = state[at, 72:73, :]
                    new = jnp.maximum(old, jnp.max(scores, axis=0, keepdims=True))
                    probs = jnp.exp(scores - new).astype(BF16)
                    part = mm(vals, probs, NN)
                    fade = jnp.exp(old - new)
                    state[at, :72, :] = state[at, :72, :] * fade + part[:72]
                    state[at, 72:, :] = jnp.broadcast_to(new, (8, rows))

        return carry

    lax.fori_loop(0, count, block, 0)
    if last:
        outs[0][...] = state[:heads]
        outs[1][...] = state[heads:]
    else:
        outs[0][...] = state[...]


def attention_forward(first, last, doc_lengths, roster, q_own, q_pair, blocks, state=None, after=()):
    width, rows = q_own.shape
    heads = width // HDIM
    count = len(blocks)
    half = ((heads, AUG, rows), F32, "v")
    whole = ((2 * heads, AUG, rows), F32, "v")
    given = [] if state is None else [(state, "v")]
    return call(
        "attention_forward",
        functools.partial(forward_kernel, first, count, heads, last),
        [(doc_lengths, "raw"), (roster, "raw"), (q_own, "v"), (q_pair, "v")]
        + kinds(blocks, "free")
        + given,
        [half, half] if last else [whole],
        [
            pltpu.VMEM((count, 2 * width, rows), BF16),
            pltpu.VMEM((2 * heads, AUG, rows), BF16),
            pltpu.VMEM((2 * heads, AUG, rows), F32),
        ]
        + doc_scratch(doc_lengths, roster)
        + [pltpu.SemaphoreType.DMA((count + 2,))],
        16 if count < 8 else 40,
        after,
    )


def backward_kernel(first, count, heads, more, last, len_any, roster_any, *refs):
    q_own, q_pair, g_own, g_pair, o_own, o_pair, t_own, t_pair = refs[:8]
    kv_refs, refs = refs[8 : 8 + count], refs[8 + count :]
    if more:
        dq_in, refs = refs[0], refs[1:]
    outs, refs = refs[:count], refs[count:]
    dq_outs, refs = (refs[:2], refs[2:]) if last else (refs[:1], refs[1:])
    kv, q_aug, delta, dq, dkv, len_ref, roster_ref, sems = refs
    rows = q_own.shape[1]
    width = heads * HDIM
    me = lax.axis_index("seq")
    copies = [pltpu.make_async_copy(kv_refs[j], kv.at[j], sems.at[j]) for j in range(count)]
    for copy in copies:
        copy.start()
    fetch_docs(len_any, roster_any, len_ref, roster_ref, sems.at[count], sems.at[count + 1])
    ends = doc_bounds(len_ref)
    bases = (roster_ref[me] * rows, roster_ref[me ^ 1] * rows)
    for g, (q_ref, g_ref, o_ref) in enumerate(((q_own, g_own, o_own), (q_pair, g_pair, o_pair))):
        mark = doc_rows(ends, bases[g], rows).astype(BF16)
        for h in range(heads):
            part = slice(h * HDIM, (h + 1) * HDIM)
            q_aug[g * heads + h, :HDIM, :] = q_ref[part, :]
            q_aug[g * heads + h, HDIM:, :] = mark
            product = g_ref[part, :].astype(F32) * o_ref[part, :].astype(F32)
            delta[g * heads + h] = jnp.broadcast_to(
                jnp.sum(product, axis=0, keepdims=True), (8, rows)
            )
    if more:
        dq[...] = dq_in[...]
    else:
        dq[...] = jnp.zeros_like(dq)
    for copy in copies:
        copy.wait()

    def block(j, carry):
        key_base = roster_ref[key_row(j + first, me)] * rows
        ban = ban_rows(ends, key_base, rows).astype(BF16)
        dkv[j] = jnp.zeros((2 * width, rows), F32)
        for g, (g_ref, t_ref) in enumerate(((g_own, t_own), (g_pair, t_pair))):

            @pl.when(meet(ends, bases[g], key_base, rows))
            def _():
                for h in range(heads):
                    at = g * heads + h
                    part = slice(h * HDIM, (h + 1) * HDIM)
                    late = slice(width + h * HDIM, width + (h + 1) * HDIM)
                    keys = kv[j, part, :]
                    scores = mm(jnp.concatenate([keys, ban], axis=0), q_aug[at], TN)
                    probs = jnp.exp(scores - t_ref[h, 0:1, :])
                    prob_grads = mm(kv[j, late, :], g_ref[part, :], TN)
                    score_grad = (probs * (prob_grads - delta[at, 0:1, :])).astype(BF16)
                    dkv[j, late, :] += mm(g_ref[part, :], probs.astype(BF16), NT)
                    dkv[j, part, :] += mm(q_aug[at, :HDIM, :], score_grad, NT)
                    dq[at] += mm(keys, score_grad, NN)

        return carry

    lax.fori_loop(0, count, block, 0)
    for j in range(count):
        outs[j][...] = dkv[j].astype(outs[j].dtype)
    if last:
        for h in range(heads):
            part = slice(h * HDIM, (h + 1) * HDIM)
            dq_outs[0][part, :] = dq[h] * HDIM**-0.5
            dq_outs[1][part, :] = (dq[heads + h] * HDIM**-0.5).astype(BF16)
    else:
        dq_outs[0][...] = dq[...]


def attention_backward(first, last, doc_lengths, roster, held, blocks, dq=None, after=()):
    width, rows = held[0].shape
    heads = width // HDIM
    count = len(blocks)
    given = [] if dq is None else [(dq, "v")]
    if last:
        queries = [((width, rows), F32, "v"), ((width, rows), BF16, "v")]
    else:
        queries = [((2 * heads, HDIM, rows), F32, "v")]
    return call(
        "attention_backward",
        functools.partial(backward_kernel, first, count, heads, bool(given), last),
        kinds((doc_lengths, roster), "raw") + kinds(held, "v") + kinds(blocks, "free") + given,
        [((2 * width, rows), BF16 if first else F32, "v")] * count + queries,
        [
            pltpu.VMEM((count, 2 * width, rows), BF16),
            pltpu.VMEM((2 * heads, AUG, rows), BF16),
            pltpu.VMEM((2 * heads, 8, rows), F32),
            pltpu.VMEM((2 * heads, HDIM, rows), F32),
            pltpu.VMEM((count, 2 * width, rows), F32),
        ]
        + doc_scratch(doc_lengths, roster)
        + [pltpu.SemaphoreType.DMA((count + 2,))],
        16 if count < 8 else 40,
        after,
        flops=0 if last else 0,
    )


def join_kernel(heads, own_ref, back_ref, out_ref, total_ref, mine_ref, other_ref):
    rows = own_ref.shape[2]
    for h in range(heads):
        top_own = own_ref[h, 72:73, :]
        top_back = back_ref[h, 72:73, :]
        top = jnp.maximum(top_own, top_back)
        fade_own = jnp.exp(top_own - top)
        fade_back = jnp.exp(top_back - top)
        total = own_ref[h, 64:65, :] * fade_own + back_ref[h, 64:65, :] * fade_back
        share_own = fade_own / total
        share_back = fade_back / total
        value = own_ref[h, :HDIM, :] * share_own + back_ref[h, :HDIM, :] * share_back
        out_ref[h * HDIM : (h + 1) * HDIM, :] = value.astype(BF16)
        total_ref[h] = jnp.broadcast_to(top + jnp.log(total), (8, rows))
    half = rows // 2
    for bit in range(2):

        @pl.when(lax.axis_index("tp") % 2 == bit)
        def _():
            mine_ref[...] = out_ref[:, bit * half : (bit + 1) * half]
            other_ref[...] = out_ref[:, (1 - bit) * half : (2 - bit) * half]


def join(own, back):
    heads, unused, rows = own.shape
    return call(
        "join",
        functools.partial(join_kernel, heads),
        [(own, "v"), (back, "v")],
        [
            ((heads * HDIM, rows), BF16, "v"),
            ((heads, 8, rows), F32, "v"),
            ((heads * HDIM, rows // 2), BF16, "v"),
            ((heads * HDIM, rows // 2), BF16, "v"),
        ],
    )


def pick_kernel(in_any, down_any, out_ref, sems):
    core = lax.axis_index("seq") % 2
    at = 0
    copies = []
    for n, source in enumerate((in_any, down_any)):
        rows = source.shape[0] // 2
        mine = pl.ds(pl.multiple_of(core * rows, rows), rows)
        copies.append(
            pltpu.make_async_copy(source.at[mine], out_ref.at[pl.ds(at, rows)], sems.at[n])
        )
        at += rows
    for copy in copies:
        copy.start()
    for copy in copies:
        copy.wait()


def pick(in_t, w_down):
    (out,) = call(
        "pick",
        pick_kernel,
        kinds((in_t, w_down), "raw"),
        [(((in_t.shape[0] + w_down.shape[0]) // 2, in_t.shape[1]), BF16, "v")],
        [pltpu.SemaphoreType.DMA((2,))],
    )
    return out


def keep_kernel(in_ref, out_ref):
    out_ref[...] = in_ref[...]


def keep_until(value, after):
    (out,) = call("keep", keep_kernel, [(value, "v")], [(value.shape, value.dtype, "v")], (), 16, after)
    return out


def stage_kernel(x_any, cot_any, w_any, in_any, down_any, got_ref, rest_ref, *refs):
    x_ref, cot_ref, w_ref, in_ref, down_ref, sems = refs
    half = x_ref.shape[0]
    core = lax.axis_index("seq") % 2
    mine = pl.ds(pl.multiple_of(lax.axis_index("tp") % 2 * half, half), half)
    moves = [(w_any, w_ref), (x_any.at[mine], x_ref), (cot_any.at[mine], cot_ref)]
    at = 0
    for own, ref in ((in_any, in_ref), (down_any, down_ref)):
        rows = own.shape[0] // 2
        moves.append((own, ref.at[pl.ds(0, 2 * rows)]))
        for source, side in ((got_ref, core), (rest_ref, 1 - core)):
            spot = pl.multiple_of(2 * rows + side * rows, rows)
            moves.append((source.at[pl.ds(at, rows)], ref.at[pl.ds(spot, rows)]))
        at += rows
    copies = [pltpu.make_async_copy(*move, sems.at[n]) for n, move in enumerate(moves)]
    for copy in copies:
        copy.start()
    for copy in copies:
        copy.wait()


def stage(tokens, cotangent, w_full, in_t, w_down, got, rest):
    rows, model = tokens.shape
    return call(
        "stage",
        stage_kernel,
        kinds((tokens, cotangent, w_full, in_t, w_down), "raw") + kinds((got, rest), "v"),
        [
            ((rows // 2, model), BF16, "v"),
            ((rows // 2, model), BF16, "v"),
            (w_full.shape, BF16, "v"),
            ((2 * in_t.shape[0], model), BF16, "v"),
            ((2 * w_down.shape[0], model), BF16, "v"),
        ],
        [pltpu.SemaphoreType.DMA((9,))],
    )


def gated(units, first, gate_up, mixed_grad, mixed_out, gate_out):
    rows = math.gcd(units, 96)

    def wave(i, carry):
        spot = pl.ds(first + i * rows, rows)
        at = pl.ds(2 * first + i * rows, rows)
        late = pl.ds(2 * first + units + i * rows, rows)
        gate = gate_up[at, :]
        up = gate_up[late, :]
        back = mixed_grad[spot, :]
        bell = 0.5 * (1.0 + lax.erf(gate * (2.0**-0.5)))
        active = gate * bell
        slope = bell + gate * jnp.exp(-0.5 * gate * gate) * ((2.0 * jnp.pi) ** -0.5)
        mixed_out[spot, :] = (active * up).astype(BF16)
        gate_out[at, :] = (back * up * slope).astype(BF16)
        gate_out[late, :] = (back * active).astype(BF16)
        return carry

    lax.fori_loop(0, units // rows, wave, 0)


def feed_kernel(n_tp, need, give, x_ref, cot_ref, w_ref, in_ref, down_ref, gain_ref, *refs):
    out_refs = refs[:n_tp]
    middle_out, part_out, h_out, mixed_out, gate_out, gain_out = refs[n_tp : n_tp + 6]
    keep_ref, *send_refs = refs[n_tp + 6 : n_tp + 6 + n_tp // 2]
    outs, unit, gate_up, mixed_grad, grad = refs[n_tp + 6 + n_tp // 2 :]
    rows = x_ref.shape[0]
    part = keep_ref.shape[0]
    units = down_ref.shape[0] // 2
    width = out_refs[0].shape[0]
    tp = lax.axis_index("tp")
    for k in range(n_tp):
        at = pl.ds(pl.multiple_of((tp ^ hop(k, n_tp)) * width, width), width)
        outs[at, :] = out_refs[k][...]
    mixed_grad[...] = mm(down_ref[...], cot_ref[...], NT)
    middle_out[...] = mm(outs[...], w_ref[...], TN)
    need(5)
    gain = gain_ref[...].reshape(1, -1)

    def strip(i, carry):
        at = pl.ds(i * 32, 32)
        middle = middle_out[at, :] + x_ref[at, :].astype(F32)
        middle_out[at, :] = middle
        held, unused = normed(middle)
        unit[at, :] = held
        h_out[at, :] = (held * gain).astype(BF16)
        return carry

    lax.fori_loop(0, rows // 32, strip, 0)
    give(0, 2)
    gate_up[...] = mm(in_ref[...], h_out[...], NT)
    for first in (0, units):
        gated(units, first, gate_up, mixed_grad, mixed_out, gate_out)
    give(3, 4)
    grad[...] = mm(gate_out[...], in_ref[...], TN)
    for n, ref in enumerate((keep_ref, *send_refs)):
        at = pl.ds(pl.multiple_of((tp ^ (2 * n)) // 2 * part, part), part)
        ref[...] = grad[at, :].astype(ref.dtype)
        give(6 + n)
    own = pl.ds(pl.multiple_of(tp // 2 * part, part), part)
    part_out[...] = middle_out[own, :]
    give(1)

    def gains(i, carry):
        at = pl.ds(i * 32, 32)
        product = grad[at, :] * unit[at, :]
        return carry + jnp.sum(product.reshape(4, 8, -1), axis=0)

    gain_out[...] = lax.fori_loop(0, rows // 32, gains, jnp.zeros(gain_out.shape, F32))


def feed(gain, staged, outs):
    rows, model = staged[0].shape
    n_tp = len(outs)
    units = staged[4].shape[0]
    part = 2 * rows // n_tp
    return call(
        "feed",
        functools.partial(feed_kernel, n_tp),
        kinds(staged, "v") + [(gain, "h")] + kinds(outs, "v"),
        [
            ((rows, model), F32, "h"),
            ((part, model), F32, "h"),
            ((rows, model), BF16, "h"),
            ((units, rows), BF16, "h"),
            ((2 * units, rows), BF16, "h"),
            ((8, model), F32, "h"),
            ((part, model), F32, "h"),
        ]
        + [((part, model), BF16, "h")] * (n_tp // 2 - 1),
        [
            pltpu.VMEM((n_tp * outs[0].shape[0], rows), BF16),
            pltpu.VMEM((rows, model), F32),
            pltpu.VMEM((2 * units, rows), F32),
            pltpu.VMEM((units, rows), F32),
            pltpu.VMEM((rows, model), F32),
        ],
        24,
        lazy=True,
    )


def branch_kernel(n_tp, count, need, give, middle_ref, cot_ref, gain_ref, w_ref, *refs):
    arrived = refs[:count]
    grad_out, branch_out = refs[count : count + 2]
    piece_refs = refs[count + 2 :]
    width = piece_refs[0].shape[1]
    tp = lax.axis_index("tp")
    need(0, 1, 2, 4)
    total = arrived[0][...]
    for ref in arrived[1:]:
        total = total + ref[...].astype(F32)
    unit, scale = normed(middle_ref[...])
    gain = gain_ref[...].reshape(1, -1)
    value = cot_ref[...].astype(F32) + norm_back(unit, scale, total, gain)
    grad_out[...] = value
    branch_out[...] = value.astype(BF16)
    give(0, 1)
    need(3)
    for k in range(n_tp):
        at = pl.ds(pl.multiple_of((tp ^ k) * width, width), width)
        piece_refs[k][...] = mm(branch_out[...], w_ref[at, :], NT).astype(BF16)


def branch(n_tp, middle_part, cotangent, gain, w_full, arrived, after):
    part, model = arrived[0].shape
    width = w_full.shape[0] // n_tp
    return call(
        "branch",
        functools.partial(branch_kernel, n_tp, len(arrived)),
        [(middle_part, "h"), (cotangent, part)]
        + [(gain, "h"), (w_full, "v"), (arrived[0], "h")]
        + kinds(arrived[1:], "v"),
        [((part, model), F32, "h"), ((part, model), BF16, "h")]
        + [((part, width), BF16, "v")] * n_tp,
        (),
        16,
        after,
        True,
    )


def lay_kernel(n_tp, *refs):
    out_ref, held = refs[n_tp:]
    part = refs[0].shape[0]
    tp = lax.axis_index("tp")
    for k in range(n_tp):
        at = pl.ds(pl.multiple_of(slot(tp ^ hop(k, n_tp), n_tp) * part, part), part)
        held[at, :] = refs[k][...].astype(F32)
    out_ref[...] = held[...].T.astype(BF16)


def lay_turned(pieces, after):
    part, width = pieces[0].shape
    rows = part * len(pieces)
    (out,) = call(
        "lay_turned",
        functools.partial(lay_kernel, len(pieces)),
        kinds(pieces, "v"),
        [((width, rows), BF16, "v")],
        [pltpu.VMEM((rows, width), F32)],
        16,
        after,
    )
    return out


def stack_kernel(n_tp, *refs):
    out_ref = refs[n_tp]
    part = refs[0].shape[0]
    tp = lax.axis_index("tp")
    for k in range(n_tp):
        at = pl.ds(pl.multiple_of(slot(tp ^ hop(k, n_tp), n_tp) * part, part), part)
        out_ref[at, :] = refs[k][...]


def stack_parts(pieces, after=(), flops=0):
    part, model = pieces[0].shape
    (out,) = call(
        "stack_parts",
        functools.partial(stack_kernel, len(pieces)),
        kinds(pieces, "v"),
        [((part * len(pieces), model), pieces[0].dtype, "h")],
        (),
        16,
        after,
        flops=flops,
    )
    return out


def turn_back(out_ref, first, value, cos_table, sin_table):
    for at in range(0, value.shape[0], HDIM):
        low = value[at : at + HALF]
        high = value[at + HALF : at + HDIM]
        spot = first + at
        out_ref[spot : spot + HALF, :] = (low * cos_table + high * sin_table).astype(BF16)
        out_ref[spot + HALF : spot + HDIM, :] = (high * cos_table - low * sin_table).astype(BF16)


def unproject_kernel(
    count, n_tp, need, give, x_ref, w_ref, cos_ref, sin_ref, two_ref, dq_ref, dq_back, *refs
):
    dkv_refs = refs[:count]
    proj_out = refs[count]
    part_refs = refs[count + 1 : count + 1 + n_tp]
    grad, dkv = refs[count + 1 + n_tp :]
    rows, model = x_ref.shape
    part = rows // n_tp
    width = dq_ref.shape[0]
    tp = lax.axis_index("tp")
    need(2, 3)
    cos_table = cos_ref[...]
    sin_table = sin_ref[...]
    turn_back(proj_out, 0, dq_ref[...] + dq_back[...].astype(F32), cos_table, sin_table)
    total = dkv_refs[0][...]
    for ref in dkv_refs[1:]:
        total = total + ref[...].astype(F32)
    dkv[...] = total
    turn_back(proj_out, width, dkv[:width, :], cos_table, sin_table)
    proj_out[2 * width :, :] = dkv[width:, :].astype(BF16)
    need(1)
    grad[...] = mm(proj_out[...], w_ref[...], TN)
    need(0, 4)

    def gains(i, carry):
        at = pl.ds(i * STRIP, STRIP)
        unit, unused = normed(x_ref[at, :].astype(F32))
        product = grad[at, :] * unit
        return carry + jnp.sum(product.reshape(STRIP // 8, 8, -1), axis=0)

    gain = lax.fori_loop(0, rows // STRIP, gains, jnp.zeros((8, model), F32))
    line = lax.broadcasted_iota(jnp.int32, (16, model), 0)
    gain_two = jnp.sum(two_ref[...], axis=0, keepdims=True)
    gain = jnp.sum(gain, axis=0, keepdims=True)
    gain = jnp.where(line == 0, gain, jnp.where(line == 1, gain_two, 0.0))
    for k in range(n_tp):
        at = pl.ds(pl.multiple_of(slot(tp ^ k, n_tp) * part, part), part)
        part_refs[k][:part, :] = grad[at, :].astype(part_refs[k].dtype)
        part_refs[k][part:, :] = gain.astype(part_refs[k].dtype)


def unproject(n_tp, tokens, qkv_t, cos_table, sin_table, gain_two_part, dq, dq_back, dkvs, after):
    rows, model = tokens.shape
    part = rows // n_tp
    return call(
        "unproject",
        functools.partial(unproject_kernel, len(dkvs), n_tp),
        kinds((tokens, qkv_t, cos_table, sin_table, gain_two_part), "v")
        + kinds((dq, dq_back, *dkvs), "v"),
        [((qkv_t.shape[0], rows), BF16, "v"), ((part + 16, model), F32, "v")]
        + [((part + 16, model), BF16, "v")] * (n_tp - 1),
        [pltpu.VMEM((rows, model), F32), pltpu.VMEM(dkvs[0].shape, F32)],
        16,
        after,
        True,
    )


def input_kernel(x_ref, gain_ref, grad_ref, sum_ref, out_ref, gain_out):
    part, model = grad_ref.shape
    total = sum_ref[...]
    unit, scale = normed(x_ref[...].astype(F32))
    gain = gain_ref[...].reshape(1, -1)
    value = grad_ref[...] + norm_back(unit, scale, total[:part], gain)
    out_ref[...] = value.astype(BF16)
    gain_out[...] = total[part : part + 8]


def input_side(tokens, gain, middle_grad, summed, after):
    part, model = middle_grad.shape
    return call(
        "input_side",
        input_kernel,
        [(tokens, part), (gain, "h"), (middle_grad, "v"), (summed, "v")],
        [((part, model), BF16, "v"), ((8, model), F32, "v")],
        (),
        16,
        after,
    )


def early_kernel(mixed_ref, gate_ref, cot_ref, h_ref, in_ref, down_ref, h_pair, *refs):
    keep_ref, send_ref, gate_up, mixed_grad, mixed, gate = refs
    units = down_ref.shape[0]
    half = h_ref.shape[0]
    bit = lax.axis_index("tp") % 2
    mine = pl.ds(pl.multiple_of(bit * half, half), half)
    other = pl.ds(pl.multiple_of((1 - bit) * half, half), half)
    gate_up[...] = mm(in_ref[...], h_pair[...], NT)
    mixed_grad[...] = mm(down_ref[...], cot_ref[other, :], NT)
    gated(units, 0, gate_up, mixed_grad, mixed, gate)
    width = keep_ref.shape[1]
    core = lax.axis_index("seq") % 2
    for ref, side in ((send_ref, 1 - core), (keep_ref, core)):
        columns = pl.ds(pl.multiple_of(side * width, width), width)
        down = mm(mixed_ref[:units, :], cot_ref[mine, columns], NN)
        down = down + mm(mixed[...], cot_ref[other, columns], NN)
        ref[:units, :] = down.astype(ref.dtype)
        both = mm(gate_ref[: 2 * units, :], h_ref[:, columns], NN)
        both = both + mm(gate[...], h_pair[:, columns], NN)
        ref[units:, :] = both.astype(ref.dtype)


def early_grads(mixed, gate_grad, cotangent, h_two, in_t, w_down, h_pair, after):
    units, model = w_down.shape
    half = h_two.shape[0]
    return call(
        "early_grads",
        early_kernel,
        kinds((mixed, gate_grad, cotangent, h_two, in_t, w_down), "h") + [(h_pair, "v")],
        [((3 * units, model // 2), F32, "v"), ((3 * units, model // 2), BF16, "v")],
        [
            pltpu.VMEM((2 * units, half), F32),
            pltpu.VMEM((units, half), F32),
            pltpu.VMEM((units, half), BF16),
            pltpu.VMEM((2 * units, half), BF16),
        ],
        24,
        after,
    )


def late_kernel(n_tp, proj_ref, h_ref, out_ref, *refs):
    branch_refs = refs[:n_tp]
    keep_ref, send_ref, branch_full = refs[n_tp:]
    part = branch_refs[0].shape[0]
    half = keep_ref.shape[1]
    wide = proj_ref.shape[0]
    tp = lax.axis_index("tp")
    core = lax.axis_index("seq") % 2
    for k in range(n_tp):
        at = pl.ds(pl.multiple_of(slot(tp ^ hop(k, n_tp), n_tp) * part, part), part)
        branch_full[at, :] = branch_refs[k][...]
    for ref, side in ((send_ref, 1 - core), (keep_ref, core)):
        columns = pl.ds(pl.multiple_of(side * half, half), half)
        ref[:wide, :] = mm(proj_ref[...], h_ref[:, columns], NN).astype(ref.dtype)
        ref[wide:, :] = mm(out_ref[...], branch_full[:, columns], NN).astype(ref.dtype)


def late_grads(proj_grad, h_one, out_b, branches, after):
    rows, model = h_one.shape
    wide = proj_grad.shape[0] + out_b.shape[0]
    return call(
        "late_grads",
        functools.partial(late_kernel, len(branches)),
        [(proj_grad, "v"), (h_one, "v"), (out_b, "v"), (branches[0], "v")]
        + kinds(branches[1:], "v"),
        [((wide, model // 2), F32, "v"), ((wide, model // 2), BF16, "v")],
        [pltpu.VMEM((rows, model), BF16)],
        16,
        after,
    )


def spread_kernel(count, *refs):
    given, outs, held = refs[: -count - 1], refs[-count - 1 : -1], refs[-1]
    piece = outs[0].shape[0]
    chip = lax.axis_index("seq") // 2
    at = 0
    for keep_ref, back_ref in zip(given[::2], given[1::2]):
        rows = keep_ref.shape[0]
        held[at : at + rows, :] = keep_ref[...] + back_ref[...].astype(F32)
        at += rows
    if at < held.shape[0]:
        held[at:, :] = jnp.zeros((held.shape[0] - at, held.shape[1]), F32)
    for k in range(count):
        at = pl.ds(pl.multiple_of((chip ^ k) * piece, piece), piece)
        outs[k][...] = held[at, :].astype(outs[k].dtype)


def spread(count, *pairs):
    half = pairs[0][0].shape[1]
    rows = sum(keep.shape[0] for keep, unused in pairs)
    piece = -(-rows // (8 * count)) * 8
    return call(
        "spread",
        functools.partial(spread_kernel, count),
        [(array, "v") for pair in pairs for array in pair],
        [((piece, half), F32, "v")] + [((piece, half), BF16, "v")] * (count - 1),
        [pltpu.VMEM((count * piece, half), F32)],
    )


def piece_kernel(count, gain_ref, *refs):
    out_ref = refs[count]
    half = out_ref.shape[1]
    total = refs[0][...]
    for ref in refs[1:count]:
        total = total + ref[...].astype(F32)
    line = lax.broadcasted_iota(jnp.int32, (16, half), 0)
    gains = jnp.zeros((16, half), F32)
    for at in range(4):
        row = gain_ref[at // 2 : at // 2 + 1, at % 2 * half : (at % 2 + 1) * half]
        gains = jnp.where(line == at, row, gains)
    out_ref[...] = jnp.concatenate([total, gains], axis=0).astype(BF16)


def sum_piece(gains, pieces, after=()):
    piece, half = pieces[0].shape
    (out,) = call(
        "sum_piece",
        functools.partial(piece_kernel, len(pieces)),
        [(gains, "v")] + kinds(pieces, "v"),
        [((piece + 16, half), BF16, "v")],
        (),
        16,
        after,
    )
    return out


def collect_kernel(count, *refs):
    out_ref, held = refs[count:]
    piece = refs[0].shape[0] - 16
    wide = count * piece
    chip = lax.axis_index("seq") // 2
    gains = jnp.zeros((16, out_ref.shape[1]), F32)
    for k in range(count):
        at = pl.ds(pl.multiple_of((chip ^ hop(k, count)) * piece, piece), piece)
        whole = refs[k][...].astype(F32)
        held[at, :] = whole[:piece]
        gains = gains + whole[piece:]
    held[wide:, :] = gains
    out_ref[...] = held[...].astype(BF16)


def collect(pieces, after=()):
    piece, half = pieces[0].shape
    wide = (piece - 16) * len(pieces) + 16
    (out,) = call(
        "collect",
        functools.partial(collect_kernel, len(pieces)),
        kinds(pieces, "v"),
        [((wide, half), BF16, "v")],
        [pltpu.VMEM((wide, half), F32)],
        16,
        after,
    )
    return out


def finish_kernel(sizes, need, give, own_ref, pair_ref, *refs):
    out_refs, gain_refs = refs[: len(sizes)], refs[len(sizes) :]
    half = own_ref.shape[1]
    core = lax.axis_index("seq") % 2
    at = 0
    for n, (out_ref, size) in enumerate(zip(out_refs, sizes)):
        for ref, side in ((own_ref, core), (pair_ref, 1 - core)):
            columns = pl.ds(pl.multiple_of(side * half, half), half)
            out_ref[:, columns] = ref[at : at + size, :].astype(F32)
        give(n)
        at += size
    first = own_ref.shape[0] - 16
    gains = own_ref[first:, :].astype(F32) + pair_ref[first:, :].astype(F32)
    for at, ref in zip((0, 2), gain_refs):
        ref[pl.ds(0, half)] = gains[at]
        ref[pl.ds(half, half)] = gains[at + 1]


def finish(own, pair, sizes):
    model = 2 * own.shape[1]
    return call(
        "finish",
        functools.partial(finish_kernel, sizes),
        [(own, "v"), (pair, "v")],
        [((size, model), F32, "h") for size in sizes] + [((model,), F32, "h")] * 2,
        (),
        24,
        lazy=True,
    )


def down_kernel(mixed_ref, w_ref, middle_ref, keep_ref, *refs):
    send_refs, total = refs[:-1], refs[-1]
    part = keep_ref.shape[0]
    tp = lax.axis_index("tp")
    total[...] = mm(mixed_ref[...], w_ref[...], TN)
    own = pl.ds(pl.multiple_of(tp // 2 * part, part), part)
    keep_ref[...] = total[own, :] + middle_ref[own, :]
    for n, ref in enumerate(send_refs):
        at = pl.ds(pl.multiple_of((tp ^ (2 * n + 2)) // 2 * part, part), part)
        ref[...] = total[at, :].astype(ref.dtype)


def down(n_tp, mixed, w_both, middle, after):
    rows, model = middle.shape
    part = 2 * rows // n_tp
    return call(
        "down",
        down_kernel,
        [(mixed, "h"), (w_both, "v"), (middle, "h")],
        [((part, model), F32, "h")] + [((part, model), BF16, "h")] * (n_tp // 2 - 1),
        [pltpu.VMEM((rows, model), F32)],
        16,
        after,
    )


def total_kernel(count, *refs):
    total = refs[0][...]
    for ref in refs[1:count]:
        total = total + ref[...].astype(F32)
    refs[count][...] = total.astype(refs[count].dtype)


def total_of(parts, dtype=BF16, kind="v", after=(), flops=0):
    (out,) = call(
        "total_of",
        functools.partial(total_kernel, len(parts)),
        [(parts[0], kind)] + kinds(parts[1:], "v"),
        [(parts[0].shape, dtype, "v")],
        (),
        16,
        after,
        flops=flops,
    )
    return out


def body(
    n_seq,
    n_tp,
    tokens,
    gain_one,
    w_qkv,
    w_out,
    gain_two,
    w_in,
    w_down,
    cotangent,
    doc_lengths,
    roster,
):
    rows, model = tokens.shape
    width = w_qkv.shape[2]
    units = w_in.shape[2]
    count = n_seq // 2
    qkv_t = w_qkv.transpose(1, 2, 0).reshape(3 * width, model)
    in_t = w_in.transpose(1, 2, 0).reshape(2 * units, model)
    over_tp = lambda x, k: swap(x, "tp", k, n_tp)
    over_chips = lambda x, k: swap(x, "seq", 2 * k, n_seq)
    over_cores = lambda x: swap(x, "seq", 1, n_seq)
    everywhere = lambda xs: [xs[0]] + came(n_tp, lambda k: over_tp(xs[k], k))

    def by_steps(part):
        parts = {0: part}
        step = n_tp // 2
        while step:
            parts.update({k ^ step: over_tp(x, step) for k, x in parts.items()})
            step //= 2
        return [parts[hop(n, n_tp)] for n in range(n_tp)]

    docs = (doc_lengths, roster)

    queries, kv, h_one, cos_table, sin_table = project(*docs, tokens, gain_one, qkv_t)
    blocks = [kv] + [over_chips(kv, j) for j in range(1, count)]
    q_pair = over_cores(queries)
    w_full = lax.all_gather(w_out, "tp", axis=0, tiled=True)
    got = over_tp(pick(in_t, w_down), 1)

    split = (count + 1) // 2
    (state,) = attention_forward(0, False, *docs, queries, q_pair, blocks[:split])
    state_own, state_pair = attention_forward(
        split, True, *docs, queries, q_pair, blocks[split:], state
    )
    out_b, totals, out_mine, out_other = join(state_own, over_cores(state_pair))
    outs = everywhere([out_other if k % 2 else out_mine for k in range(n_tp)])
    out_pair = over_cores(out_b)
    totals_pair = over_cores(totals)

    got = keep_until(got, [(state_pair, "v")])
    staged = stage(tokens, cotangent, w_full, in_t, w_down, got, over_cores(got))
    middle, middle_part, h_two, mixed, gate_grad, gain_two_part, own, *others = feed(
        gain_two, staged, outs
    )
    arrived = [own] + [over_tp(others[n], 2 * n + 2) for n in range(n_tp // 2 - 1)]
    own, *others = down(n_tp, mixed, staged[4], middle, ())
    middle_grad, branch_grad, *pieces = branch(
        n_tp, middle_part, cotangent, gain_two, staged[2], arrived, [(own, "h")]
    )
    early, early_send = early_grads(
        mixed, gate_grad, cotangent, h_two, in_t, w_down, over_tp(h_two, 1), [(branch_grad, "h")]
    )
    out_grad = lay_turned(everywhere(pieces), [(early, "v")])
    grad_pair = over_cores(out_grad)
    branches = by_steps(branch_grad)

    held = (queries, q_pair, out_grad, grad_pair, out_b, out_pair, totals, totals_pair)
    *terms, dq = attention_backward(1, False, *docs, held, blocks[1:], None)
    total = total_of(
        [own] + [over_tp(others[n], 2 * n + 2) for n in range(n_tp // 2 - 1)],
        BF16,
        "h",
        [(dq, "v")],
    )
    totals_all = by_steps(total)

    dkv, dq_own, dq_pair = attention_backward(0, True, *docs, held, blocks[:1], dq)
    dkvs = [dkv] + [over_chips(terms[j - 1], j) for j in range(1, count)]

    proj_grad, *parts = unproject(
        n_tp,
        tokens,
        qkv_t,
        cos_table,
        sin_table,
        gain_two_part,
        dq_own,
        over_cores(dq_pair),
        dkvs,
        [(total, "v")],
    )
    layer_out = stack_parts(totals_all)
    keep, send = late_grads(proj_grad, h_one, out_b, branches, [(totals_all[n_tp // 2], "v")])
    own, *others = spread(count, (keep, over_cores(send)), (early, over_cores(early_send)))
    summed = total_of(everywhere(parts), F32, flops=2_000_000_000)
    chip_sum = total_of(
        [own] + came(count, lambda k: over_chips(others[k - 1], k)), F32, "v", ()
    )
    input_part, gains = input_side(tokens, gain_one, middle_grad, summed, [(own, "v")])
    inputs_all = everywhere([input_part] * n_tp)
    piece = sum_piece(gains, [chip_sum], ())
    input_grad = stack_parts(inputs_all, (), 3_000_000_000)
    collected = collect(
        [piece] + came(count, lambda k: over_chips(piece, k)), [(input_grad, "h"), (layer_out, "h")]
    )
    grad_qkv, grad_out, grad_down, grad_in, grad_one, grad_two = finish(
        collected, over_cores(collected), (3 * width, width, units, 2 * units)
    )

    back = lambda x, n: x.reshape(-1, n, model).transpose(2, 0, 1)
    return (
        layer_out,
        input_grad,
        grad_one,
        back(grad_qkv, width),
        grad_out,
        grad_two,
        back(grad_in, units),
        grad_down,
    )


def solution(mesh):
    placed = (
        P("seq", None),
        P(),
        P(None, None, "tp"),
        P("tp", None),
        P(),
        P(None, None, "tp"),
        P("tp", None),
        P("seq", None),
        P(),
        P(),
    )
    return jax.shard_map(
        functools.partial(body, mesh.shape["seq"], mesh.shape["tp"]),
        mesh=mesh,
        in_specs=placed,
        out_specs=(
            P("seq", None),
            P("seq", None),
            P(),
            P(None, None, "tp"),
            P("tp", None),
            P(),
            P(None, None, "tp"),
            P("tp", None),
        ),
        check_vma=False,
    )
```

```python
import functools
import math

import jax
import jax.numpy as jnp
import numpy as np
from jax import lax
from jax.experimental import pallas as pl
from jax.experimental.pallas import tpu as pltpu
from jax.sharding import PartitionSpec as P

HDIM = 64
HALF = HDIM // 2
EPSILON = 1e-05
ROPE_THETA = 160000.0
MASKED = -1e30
AUG = 80
STRIP = 64
F32 = jnp.float32
BF16 = jnp.bfloat16
HBM = pl.BlockSpec(memory_space=pltpu.HBM)
VMEM = pl.BlockSpec(memory_space=pltpu.VMEM)

NN = (((1,), (0,)), ((), ()))
NT = (((1,), (1,)), ((), ()))
TN = (((0,), (0,)), ((), ()))


def params(mib):
    return pltpu.CompilerParams(vmem_limit_bytes=mib * 2**20)


def slot(tp, n_tp):
    return tp % 2 * (n_tp // 2) + tp // 2


def hop(n, count):
    return (count - n) % count


def came(count, send):
    return [send(hop(n, count)) for n in range(1, count)]


def mm(a, b, dims):
    return lax.dot_general(a, b, dims, preferred_element_type=F32)


def shaped(shape, dtype):
    return jax.ShapeDtypeStruct(shape, dtype)


def kinds(arrays, kind):
    return [(array, kind) for array in arrays]


def pin(array, kind):
    return array if kind in ("v", "free") else pltpu.with_memory_space_constraint(array, pltpu.HBM)


def call(name, kernel, ins, outs, scratch=(), mib=16, after=(), lazy=False, flops=0):
    fetched = [i for i, given in enumerate(ins) if given[1] not in ("v", "raw", "free")]
    left = [i for i, out in enumerate(outs) if out[2] == "h"]

    def held(array, kind):
        rows = array.shape[0] if kind == "h" else kind
        return pltpu.VMEM((rows,) + array.shape[1:], array.dtype)

    def run(*refs):
        in_refs = list(refs[: len(ins)])
        at = len(ins) + len(after)
        out_refs = list(refs[at : at + len(outs)])
        at += len(outs)
        own = refs[at : at + len(scratch)]
        at += len(scratch)
        buffers = refs[at : at + len(fetched) + len(left)]
        sems = refs[-1]
        copies = []
        for n, i in enumerate(fetched):
            source = in_refs[i]
            if ins[i][1] != "h":
                rows = ins[i][1]
                n_tp = ins[i][0].shape[0] // rows
                at = pl.multiple_of(slot(lax.axis_index("tp"), n_tp) * rows, rows)
                source = source.at[pl.ds(at, rows)]
            copies.append(pltpu.make_async_copy(source, buffers[n], sems.at[n]))
            in_refs[i] = buffers[n]
        for copy in copies:
            copy.start()
        coming = dict(zip(fetched, copies))
        going = {}
        for n, i in enumerate(left):
            spot = len(fetched) + n
            going[i] = pltpu.make_async_copy(buffers[spot], out_refs[i], sems.at[spot])
            out_refs[i] = buffers[spot]
        gone = []

        def need(*which):
            for i in which:
                if i in coming:
                    coming.pop(i).wait()

        def give(*which):
            for i in which:
                if i in going:
                    gone.append(going.pop(i))
                    gone[-1].start()

        if lazy:
            kernel(need, give, *in_refs, *out_refs, *own)
        else:
            need(*fetched)
            kernel(*in_refs, *out_refs, *own)
        need(*fetched)
        give(*left)
        for copy in gone:
            copy.wait()

    spec = lambda kind: VMEM if kind == "v" else HBM
    count = len(fetched) + len(left)
    return pl.pallas_call(
        run,
        out_shape=tuple(
            shaped(shape, dtype) if kind == "v" else pltpu.HBM(shape, dtype)
            for shape, dtype, kind in outs
        ),
        in_specs=[spec(kind) for unused, kind in ins] + [spec(kind) for unused, kind in after],
        out_specs=tuple(spec(kind) for unused, unused, kind in outs),
        scratch_shapes=list(scratch)
        + [held(*ins[i]) for i in fetched]
        + [pltpu.VMEM(outs[i][0], outs[i][1]) for i in left]
        + [pltpu.SemaphoreType.DMA((max(count, 1),))],
        name=name,
        cost_estimate=pl.CostEstimate(flops=flops, bytes_accessed=0, transcendentals=0)
        if flops
        else None,
        compiler_params=params(mib),
    )(*[pin(*given) for given in ins], *[pin(*given) for given in after])


def swap(x, axis, hop, count):
    return lax.ppermute(x, axis, [(i, i ^ hop) for i in range(count)])


def doc_scratch(doc_lengths, roster):
    return [pltpu.SMEM(doc_lengths.shape, jnp.int32), pltpu.SMEM(roster.shape, jnp.int32)]


def fetch_docs(len_any, roster_any, len_ref, roster_ref, len_sem, roster_sem):
    one = pltpu.make_async_copy(len_any, len_ref, len_sem)
    two = pltpu.make_async_copy(roster_any, roster_ref, roster_sem)
    one.start()
    two.start()
    one.wait()
    two.wait()


def doc_bounds(len_ref):
    ends, total = [], jnp.int32(0)
    for d in range(len_ref.shape[0]):
        total = total + len_ref[d]
        ends.append(total)
    return ends


def doc_of(ends, position):
    found = jnp.int32(0)
    for end in ends:
        found = found + (end <= position).astype(jnp.int32)
    return found


def meet(ends, base_a, base_b, rows):
    low = jnp.maximum(doc_of(ends, base_a), doc_of(ends, base_b))
    high = jnp.minimum(doc_of(ends, base_a + rows - 1), doc_of(ends, base_b + rows - 1))
    return low <= high


def doc_rows(ends, base, rows):
    spot = base + lax.broadcasted_iota(jnp.int32, (16, rows), 1)
    line = lax.broadcasted_iota(jnp.int32, (16, rows), 0)
    held = jnp.zeros((16, rows), F32)
    start = jnp.int32(0)
    for d, end in enumerate(ends):
        inside = (line == d) & (spot >= start) & (spot < end)
        held = jnp.where(inside, 1.0, held)
        start = end
    return held


def ban_rows(ends, base, rows):
    line = lax.broadcasted_iota(jnp.int32, (16, rows), 0)
    held = doc_rows(ends, base, rows)
    return jnp.where((held > 0.5) | (line >= len(ends)), 0.0, MASKED)


def key_row(block, seq_index):
    return seq_index ^ (2 * block)


def place_row(ends, base, rows):
    spot = base + lax.broadcasted_iota(jnp.int32, (1, rows), 1)
    start = jnp.zeros((1, rows), jnp.int32)
    for end in ends:
        start = jnp.where(spot >= end, end, start)
    return (spot - start).astype(F32)


def normed(values):
    centre = jnp.mean(values, axis=-1, keepdims=True)
    shifted = values - centre
    spread = jnp.mean(shifted * shifted, axis=-1, keepdims=True)
    scale = lax.rsqrt(spread + EPSILON)
    return shifted * scale, scale


def norm_back(unit, scale, grad, gain):
    u = grad * gain
    mean_u = jnp.mean(u, axis=-1, keepdims=True)
    mean_un = jnp.mean(u * unit, axis=-1, keepdims=True)
    return scale * (u - mean_u - unit * mean_un)


def project_kernel(
    width, need, give, len_any, roster_any, x_ref, w_ref, gain_ref, freq_ref, *refs
):
    q_out, kv_out, h_out, cos_out, sin_out = refs[:5]
    proj, len_ref, roster_ref, sems = refs[5:]
    rows = x_ref.shape[0]
    fetch_docs(len_any, roster_any, len_ref, roster_ref, sems.at[0], sems.at[1])
    need(5)
    ends = doc_bounds(len_ref)
    place = place_row(ends, roster_ref[lax.axis_index("seq")] * rows, rows)
    angles = place * freq_ref[...]
    cos_table = jnp.cos(angles)
    sin_table = jnp.sin(angles)
    cos_out[...] = cos_table
    sin_out[...] = sin_table
    give(3, 4)
    need(2, 4)
    gain = gain_ref[...].reshape(1, -1)

    def strip(i, carry):
        at = pl.ds(i * STRIP, STRIP)
        unit, unused = normed(x_ref[at, :].astype(F32))
        h_out[at, :] = (unit * gain).astype(BF16)
        return carry

    lax.fori_loop(0, rows // STRIP, strip, 0)
    give(2)
    need(3)
    proj[...] = mm(w_ref[...], h_out[...], NT)
    for at in range(0, 2 * width, HDIM):
        low = proj[at : at + HALF, :]
        high = proj[at + HALF : at + HDIM, :]
        turned_low = (low * cos_out[...] - high * sin_out[...]).astype(BF16)
        turned_high = (high * cos_out[...] + low * sin_out[...]).astype(BF16)
        if at < width:
            q_out[at : at + HALF, :] = (turned_low.astype(F32) * HDIM**-0.5).astype(BF16)
            q_out[at + HALF : at + HDIM, :] = (turned_high.astype(F32) * HDIM**-0.5).astype(BF16)
        else:
            kv_out[at - width : at - width + HALF, :] = turned_low
            kv_out[at - width + HALF : at - width + HDIM, :] = turned_high
    kv_out[width:, :] = proj[2 * width :, :].astype(BF16)


def project(doc_lengths, roster, tokens, gain, qkv_t):
    rows, model = tokens.shape
    width = qkv_t.shape[0] // 3
    freq = (ROPE_THETA ** -(np.arange(HALF) * (2.0 / HDIM))).astype(np.float32)[:, None]
    return call(
        "project",
        functools.partial(project_kernel, width),
        kinds((doc_lengths, roster), "raw") + kinds((tokens, qkv_t, gain, jnp.asarray(freq)), "h"),
        [
            ((width, rows), BF16, "v"),
            ((2 * width, rows), BF16, "v"),
            ((rows, model), BF16, "h"),
            ((HALF, rows), F32, "h"),
            ((HALF, rows), F32, "h"),
        ],
        [pltpu.VMEM((3 * width, rows), F32)]
        + doc_scratch(doc_lengths, roster)
        + [pltpu.SemaphoreType.DMA((2,))],
        lazy=True,
    )


def forward_kernel(first, count, heads, last, len_any, roster_any, q_own, q_pair, *refs):
    kv_refs = refs[:count]
    refs = refs[count:]
    if first:
        state_in, refs = refs[0], refs[1:]
    outs = refs[: 2 if last else 1]
    kv, q_aug, state, len_ref, roster_ref, sems = refs[len(outs) :]
    rows = q_own.shape[1]
    width = heads * HDIM
    me = lax.axis_index("seq")
    copies = [pltpu.make_async_copy(kv_refs[j], kv.at[j], sems.at[j]) for j in range(count)]
    for copy in copies:
        copy.start()
    fetch_docs(len_any, roster_any, len_ref, roster_ref, sems.at[count], sems.at[count + 1])
    ends = doc_bounds(len_ref)
    bases = (roster_ref[me] * rows, roster_ref[me ^ 1] * rows)
    for g, q_ref in enumerate((q_own, q_pair)):
        mark = doc_rows(ends, bases[g], rows).astype(BF16)
        for h in range(heads):
            q_aug[g * heads + h, :HDIM, :] = q_ref[h * HDIM : (h + 1) * HDIM, :]
            q_aug[g * heads + h, HDIM:, :] = mark
    if first:
        state[...] = state_in[...]
    else:
        line = lax.broadcasted_iota(jnp.int32, (2 * heads, AUG, rows), 1)
        state[...] = jnp.where(line >= 72, MASKED, 0.0)
    for copy in copies:
        copy.wait()

    top = lax.broadcasted_iota(jnp.int32, (16, rows), 0) == 0
    ones = jnp.where(top, 1.0, 0.0).astype(BF16)

    def block(j, carry):
        key_base = roster_ref[key_row(j + first, me)] * rows
        ban = ban_rows(ends, key_base, rows).astype(BF16)
        for g in range(2):

            @pl.when(meet(ends, bases[g], key_base, rows))
            def _():
                for h in range(heads):
                    at = g * heads + h
                    keys = jnp.concatenate([kv[j, h * HDIM : (h + 1) * HDIM, :], ban], axis=0)
                    vals = jnp.concatenate(
                        [kv[j, width + h * HDIM : width + (h + 1) * HDIM, :], ones], axis=0
                    )
                    scores = mm(keys, q_aug[at], TN)
                    old = state[at, 72:73, :]
                    new = jnp.maximum(old, jnp.max(scores, axis=0, keepdims=True))
                    probs = jnp.exp(scores - new).astype(BF16)
                    part = mm(vals, probs, NN)
                    fade = jnp.exp(old - new)
                    state[at, :72, :] = state[at, :72, :] * fade + part[:72]
                    state[at, 72:, :] = jnp.broadcast_to(new, (8, rows))

        return carry

    lax.fori_loop(0, count, block, 0)
    if last:
        outs[0][...] = state[:heads]
        outs[1][...] = state[heads:]
    else:
        outs[0][...] = state[...]


def attention_forward(first, last, doc_lengths, roster, q_own, q_pair, blocks, state=None, after=()):
    width, rows = q_own.shape
    heads = width // HDIM
    count = len(blocks)
    half = ((heads, AUG, rows), F32, "v")
    whole = ((2 * heads, AUG, rows), F32, "v")
    given = [] if state is None else [(state, "v")]
    return call(
        "attention_forward",
        functools.partial(forward_kernel, first, count, heads, last),
        [(doc_lengths, "raw"), (roster, "raw"), (q_own, "v"), (q_pair, "v")]
        + kinds(blocks, "free")
        + given,
        [half, half] if last else [whole],
        [
            pltpu.VMEM((count, 2 * width, rows), BF16),
            pltpu.VMEM((2 * heads, AUG, rows), BF16),
            pltpu.VMEM((2 * heads, AUG, rows), F32),
        ]
        + doc_scratch(doc_lengths, roster)
        + [pltpu.SemaphoreType.DMA((count + 2,))],
        16 if count < 8 else 40,
        after,
    )


def backward_kernel(first, count, heads, more, last, len_any, roster_any, *refs):
    q_own, q_pair, g_own, g_pair, o_own, o_pair, t_own, t_pair = refs[:8]
    kv_refs, refs = refs[8 : 8 + count], refs[8 + count :]
    if more:
        dq_in, refs = refs[0], refs[1:]
    outs, refs = refs[:count], refs[count:]
    dq_outs, refs = (refs[:2], refs[2:]) if last else (refs[:1], refs[1:])
    kv, q_aug, delta, dq, dkv, len_ref, roster_ref, sems = refs
    rows = q_own.shape[1]
    width = heads * HDIM
    me = lax.axis_index("seq")
    copies = [pltpu.make_async_copy(kv_refs[j], kv.at[j], sems.at[j]) for j in range(count)]
    for copy in copies:
        copy.start()
    fetch_docs(len_any, roster_any, len_ref, roster_ref, sems.at[count], sems.at[count + 1])
    ends = doc_bounds(len_ref)
    bases = (roster_ref[me] * rows, roster_ref[me ^ 1] * rows)
    for g, (q_ref, g_ref, o_ref) in enumerate(((q_own, g_own, o_own), (q_pair, g_pair, o_pair))):
        mark = doc_rows(ends, bases[g], rows).astype(BF16)
        for h in range(heads):
            part = slice(h * HDIM, (h + 1) * HDIM)
            q_aug[g * heads + h, :HDIM, :] = q_ref[part, :]
            q_aug[g * heads + h, HDIM:, :] = mark
            product = g_ref[part, :].astype(F32) * o_ref[part, :].astype(F32)
            delta[g * heads + h] = jnp.broadcast_to(
                jnp.sum(product, axis=0, keepdims=True), (8, rows)
            )
    if more:
        dq[...] = dq_in[...]
    else:
        dq[...] = jnp.zeros_like(dq)
    for copy in copies:
        copy.wait()

    def block(j, carry):
        key_base = roster_ref[key_row(j + first, me)] * rows
        ban = ban_rows(ends, key_base, rows).astype(BF16)
        dkv[j] = jnp.zeros((2 * width, rows), F32)
        for g, (g_ref, t_ref) in enumerate(((g_own, t_own), (g_pair, t_pair))):

            @pl.when(meet(ends, bases[g], key_base, rows))
            def _():
                for h in range(heads):
                    at = g * heads + h
                    part = slice(h * HDIM, (h + 1) * HDIM)
                    late = slice(width + h * HDIM, width + (h + 1) * HDIM)
                    keys = kv[j, part, :]
                    scores = mm(jnp.concatenate([keys, ban], axis=0), q_aug[at], TN)
                    probs = jnp.exp(scores - t_ref[h, 0:1, :])
                    prob_grads = mm(kv[j, late, :], g_ref[part, :], TN)
                    score_grad = (probs * (prob_grads - delta[at, 0:1, :])).astype(BF16)
                    dkv[j, late, :] += mm(g_ref[part, :], probs.astype(BF16), NT)
                    dkv[j, part, :] += mm(q_aug[at, :HDIM, :], score_grad, NT)
                    dq[at] += mm(keys, score_grad, NN)

        return carry

    lax.fori_loop(0, count, block, 0)
    for j in range(count):
        outs[j][...] = dkv[j].astype(outs[j].dtype)
    if last:
        for h in range(heads):
            part = slice(h * HDIM, (h + 1) * HDIM)
            dq_outs[0][part, :] = dq[h] * HDIM**-0.5
            dq_outs[1][part, :] = (dq[heads + h] * HDIM**-0.5).astype(BF16)
    else:
        dq_outs[0][...] = dq[...]


def attention_backward(first, last, doc_lengths, roster, held, blocks, dq=None, after=()):
    width, rows = held[0].shape
    heads = width // HDIM
    count = len(blocks)
    given = [] if dq is None else [(dq, "v")]
    if last:
        queries = [((width, rows), F32, "v"), ((width, rows), BF16, "v")]
    else:
        queries = [((2 * heads, HDIM, rows), F32, "v")]
    return call(
        "attention_backward",
        functools.partial(backward_kernel, first, count, heads, bool(given), last),
        kinds((doc_lengths, roster), "raw") + kinds(held, "v") + kinds(blocks, "free") + given,
        [((2 * width, rows), BF16 if first else F32, "v")] * count + queries,
        [
            pltpu.VMEM((count, 2 * width, rows), BF16),
            pltpu.VMEM((2 * heads, AUG, rows), BF16),
            pltpu.VMEM((2 * heads, 8, rows), F32),
            pltpu.VMEM((2 * heads, HDIM, rows), F32),
            pltpu.VMEM((count, 2 * width, rows), F32),
        ]
        + doc_scratch(doc_lengths, roster)
        + [pltpu.SemaphoreType.DMA((count + 2,))],
        16 if count < 8 else 40,
        after,
        flops=0 if last else 0,
    )


def join_kernel(heads, own_ref, back_ref, out_ref, total_ref, mine_ref, other_ref):
    rows = own_ref.shape[2]
    for h in range(heads):
        top_own = own_ref[h, 72:73, :]
        top_back = back_ref[h, 72:73, :]
        top = jnp.maximum(top_own, top_back)
        fade_own = jnp.exp(top_own - top)
        fade_back = jnp.exp(top_back - top)
        total = own_ref[h, 64:65, :] * fade_own + back_ref[h, 64:65, :] * fade_back
        share_own = fade_own / total
        share_back = fade_back / total
        value = own_ref[h, :HDIM, :] * share_own + back_ref[h, :HDIM, :] * share_back
        out_ref[h * HDIM : (h + 1) * HDIM, :] = value.astype(BF16)
        total_ref[h] = jnp.broadcast_to(top + jnp.log(total), (8, rows))
    half = rows // 2
    for bit in range(2):

        @pl.when(lax.axis_index("tp") % 2 == bit)
        def _():
            mine_ref[...] = out_ref[:, bit * half : (bit + 1) * half]
            other_ref[...] = out_ref[:, (1 - bit) * half : (2 - bit) * half]


def join(own, back):
    heads, unused, rows = own.shape
    return call(
        "join",
        functools.partial(join_kernel, heads),
        [(own, "v"), (back, "v")],
        [
            ((heads * HDIM, rows), BF16, "v"),
            ((heads, 8, rows), F32, "v"),
            ((heads * HDIM, rows // 2), BF16, "v"),
            ((heads * HDIM, rows // 2), BF16, "v"),
        ],
    )


def pick_kernel(in_any, down_any, w_any, all_ref, w_ref, sems):
    core = lax.axis_index("seq") % 2
    at = 0
    copies = []
    for source in (in_any, down_any, w_any):
        rows = source.shape[0] // 2
        mine = pl.ds(pl.multiple_of(core * rows, rows), rows)
        copies.append((source.at[mine], all_ref.at[pl.ds(at, rows)]))
        at += rows
    copies.append((w_any.at[mine], w_ref))
    copies = [pltpu.make_async_copy(*move, sems.at[n]) for n, move in enumerate(copies)]
    for copy in copies:
        copy.start()
    for copy in copies:
        copy.wait()


def pick(in_t, w_down, w_out):
    rows = (in_t.shape[0] + w_down.shape[0] + w_out.shape[0]) // 2
    model = w_out.shape[1]
    return call(
        "pick",
        pick_kernel,
        kinds((in_t, w_down, w_out), "raw"),
        [((rows, model), BF16, "v"), ((w_out.shape[0] // 2, model), BF16, "v")],
        [pltpu.SemaphoreType.DMA((4,))],
    )


def pile_kernel(*refs):
    out_ref = refs[-1]
    at = 0
    for ref in refs[:-1]:
        out_ref[at : at + ref.shape[0], :] = ref[...]
        at += ref.shape[0]


def pile(values, after):
    rows = sum(value.shape[0] for value in values)
    (out,) = call(
        "pile",
        pile_kernel,
        kinds(values, "v"),
        [((rows, values[0].shape[1]), BF16, "v")],
        (),
        16,
        after,
    )
    return out


def stage_kernel(x_any, cot_any, in_any, down_any, w_any, got_ref, rest_ref, *refs):
    x_ref, cot_ref, w_ref, in_ref, down_ref, sems = refs
    half = x_ref.shape[0]
    core = lax.axis_index("seq") % 2
    tp = lax.axis_index("tp")
    n_tp = w_ref.shape[0] // w_any.shape[0]
    mine = pl.ds(pl.multiple_of(tp % 2 * half, half), half)
    width = w_any.shape[0]
    rows = width // 2
    own = pl.ds(pl.multiple_of(tp * width, width), width)
    moves = [(w_any, w_ref.at[own]), (x_any.at[mine], x_ref), (cot_any.at[mine], cot_ref)]
    sides = ((got_ref, core), (rest_ref, 1 - core))
    first = got_ref.shape[0] - (n_tp - 1) * rows
    for k in range(1, n_tp):
        for source, side in sides:
            spot = pl.multiple_of((tp ^ k) * width + side * rows, rows)
            piece = source.at[pl.ds(first + (k - 1) * rows, rows)]
            moves.append((piece, w_ref.at[pl.ds(spot, rows)]))
    at = 0
    for own, ref in ((in_any, in_ref), (down_any, down_ref)):
        rows = own.shape[0] // 2
        moves.append((own, ref.at[pl.ds(0, 2 * rows)]))
        for source, side in sides:
            spot = pl.multiple_of(2 * rows + side * rows, rows)
            moves.append((source.at[pl.ds(at, rows)], ref.at[pl.ds(spot, rows)]))
        at += rows
    copies = [pltpu.make_async_copy(*move, sems.at[n]) for n, move in enumerate(moves)]
    for copy in copies:
        copy.start()
    for copy in copies:
        copy.wait()


def stage(n_tp, tokens, cotangent, in_t, w_down, w_out, got, rest):
    rows, model = tokens.shape
    return call(
        "stage",
        stage_kernel,
        kinds((tokens, cotangent, in_t, w_down, w_out), "raw") + kinds((got, rest), "v"),
        [
            ((rows // 2, model), BF16, "v"),
            ((rows // 2, model), BF16, "v"),
            ((n_tp * w_out.shape[0], model), BF16, "v"),
            ((2 * in_t.shape[0], model), BF16, "v"),
            ((2 * w_down.shape[0], model), BF16, "v"),
        ],
        [pltpu.SemaphoreType.DMA((7 + 2 * n_tp,))],
    )


def gated(units, first, gate_up, mixed_grad, mixed_out, gate_out):
    rows = math.gcd(units, 96)

    def wave(i, carry):
        spot = pl.ds(first + i * rows, rows)
        at = pl.ds(2 * first + i * rows, rows)
        late = pl.ds(2 * first + units + i * rows, rows)
        gate = gate_up[at, :]
        up = gate_up[late, :]
        back = mixed_grad[spot, :]
        bell = 0.5 * (1.0 + lax.erf(gate * (2.0**-0.5)))
        active = gate * bell
        slope = bell + gate * jnp.exp(-0.5 * gate * gate) * ((2.0 * jnp.pi) ** -0.5)
        mixed_out[spot, :] = (active * up).astype(BF16)
        gate_out[at, :] = (back * up * slope).astype(BF16)
        gate_out[late, :] = (back * active).astype(BF16)
        return carry

    lax.fori_loop(0, units // rows, wave, 0)


def feed_kernel(n_tp, need, give, x_ref, cot_ref, w_ref, in_ref, down_ref, gain_ref, *refs):
    out_refs = refs[:n_tp]
    middle_out, part_out, h_out, mixed_out, gate_out, gain_out = refs[n_tp : n_tp + 6]
    keep_ref, *send_refs = refs[n_tp + 6 : n_tp + 6 + n_tp // 2]
    outs, unit, gate_up, mixed_grad, grad = refs[n_tp + 6 + n_tp // 2 :]
    rows = x_ref.shape[0]
    part = keep_ref.shape[0]
    units = down_ref.shape[0] // 2
    width = out_refs[0].shape[0]
    tp = lax.axis_index("tp")
    for k in range(n_tp):
        at = pl.ds(pl.multiple_of((tp ^ hop(k, n_tp)) * width, width), width)
        outs[at, :] = out_refs[k][...]
    mixed_grad[...] = mm(down_ref[...], cot_ref[...], NT)
    middle_out[...] = mm(outs[...], w_ref[...], TN)
    need(5)
    gain = gain_ref[...].reshape(1, -1)

    def strip(i, carry):
        at = pl.ds(i * 32, 32)
        middle = middle_out[at, :] + x_ref[at, :].astype(F32)
        middle_out[at, :] = middle
        held, unused = normed(middle)
        unit[at, :] = held
        h_out[at, :] = (held * gain).astype(BF16)
        return carry

    lax.fori_loop(0, rows // 32, strip, 0)
    give(0, 2)
    gate_up[...] = mm(in_ref[...], h_out[...], NT)
    for first in (0, units):
        gated(units, first, gate_up, mixed_grad, mixed_out, gate_out)
    give(3, 4)
    grad[...] = mm(gate_out[...], in_ref[...], TN)
    for n, ref in enumerate((keep_ref, *send_refs)):
        at = pl.ds(pl.multiple_of((tp ^ (2 * n)) // 2 * part, part), part)
        ref[...] = grad[at, :].astype(ref.dtype)
        give(6 + n)
    own = pl.ds(pl.multiple_of(tp // 2 * part, part), part)
    part_out[...] = middle_out[own, :]
    give(1)

    def gains(i, carry):
        at = pl.ds(i * 32, 32)
        product = grad[at, :] * unit[at, :]
        return carry + jnp.sum(product.reshape(4, 8, -1), axis=0)

    gain_out[...] = lax.fori_loop(0, rows // 32, gains, jnp.zeros(gain_out.shape, F32))


def feed(gain, staged, outs):
    rows, model = staged[0].shape
    n_tp = len(outs)
    units = staged[4].shape[0]
    part = 2 * rows // n_tp
    return call(
        "feed",
        functools.partial(feed_kernel, n_tp),
        kinds(staged, "v") + [(gain, "h")] + kinds(outs, "v"),
        [
            ((rows, model), F32, "h"),
            ((part, model), F32, "h"),
            ((rows, model), BF16, "h"),
            ((units, rows), BF16, "h"),
            ((2 * units, rows), BF16, "h"),
            ((8, model), F32, "h"),
            ((part, model), F32, "h"),
        ]
        + [((part, model), BF16, "h")] * (n_tp // 2 - 1),
        [
            pltpu.VMEM((n_tp * outs[0].shape[0], rows), BF16),
            pltpu.VMEM((rows, model), F32),
            pltpu.VMEM((2 * units, rows), F32),
            pltpu.VMEM((units, rows), F32),
            pltpu.VMEM((rows, model), F32),
        ],
        24,
        lazy=True,
    )


def branch_kernel(n_tp, count, need, give, middle_ref, cot_ref, gain_ref, w_ref, *refs):
    arrived = refs[:count]
    grad_out, branch_out = refs[count : count + 2]
    piece_refs = refs[count + 2 :]
    width = piece_refs[0].shape[1]
    tp = lax.axis_index("tp")
    need(0, 1, 2, 4)
    total = arrived[0][...]
    for ref in arrived[1:]:
        total = total + ref[...].astype(F32)
    unit, scale = normed(middle_ref[...])
    gain = gain_ref[...].reshape(1, -1)
    value = cot_ref[...].astype(F32) + norm_back(unit, scale, total, gain)
    grad_out[...] = value
    branch_out[...] = value.astype(BF16)
    give(0, 1)
    need(3)
    for k in range(n_tp):
        at = pl.ds(pl.multiple_of((tp ^ k) * width, width), width)
        piece_refs[k][...] = mm(branch_out[...], w_ref[at, :], NT).astype(BF16)


def branch(n_tp, middle_part, cotangent, gain, w_full, arrived, after):
    part, model = arrived[0].shape
    width = w_full.shape[0] // n_tp
    return call(
        "branch",
        functools.partial(branch_kernel, n_tp, len(arrived)),
        [(middle_part, "h"), (cotangent, part)]
        + [(gain, "h"), (w_full, "v"), (arrived[0], "h")]
        + kinds(arrived[1:], "v"),
        [((part, model), F32, "h"), ((part, model), BF16, "h")]
        + [((part, width), BF16, "v")] * n_tp,
        (),
        16,
        after,
        True,
    )


def lay_kernel(n_tp, *refs):
    out_ref, held = refs[n_tp:]
    part = refs[0].shape[0]
    tp = lax.axis_index("tp")
    for k in range(n_tp):
        at = pl.ds(pl.multiple_of(slot(tp ^ hop(k, n_tp), n_tp) * part, part), part)
        held[at, :] = refs[k][...].astype(F32)
    out_ref[...] = held[...].T.astype(BF16)


def lay_turned(pieces, after):
    part, width = pieces[0].shape
    rows = part * len(pieces)
    (out,) = call(
        "lay_turned",
        functools.partial(lay_kernel, len(pieces)),
        kinds(pieces, "v"),
        [((width, rows), BF16, "v")],
        [pltpu.VMEM((rows, width), F32)],
        16,
        after,
    )
    return out


def stack_kernel(n_tp, *refs):
    out_ref = refs[n_tp]
    part = refs[0].shape[0]
    tp = lax.axis_index("tp")
    for k in range(n_tp):
        at = pl.ds(pl.multiple_of(slot(tp ^ hop(k, n_tp), n_tp) * part, part), part)
        out_ref[at, :] = refs[k][...]


def stack_parts(pieces, after=(), flops=0):
    part, model = pieces[0].shape
    (out,) = call(
        "stack_parts",
        functools.partial(stack_kernel, len(pieces)),
        kinds(pieces, "v"),
        [((part * len(pieces), model), pieces[0].dtype, "h")],
        (),
        16,
        after,
        flops=flops,
    )
    return out


def turn_back(out_ref, first, value, cos_table, sin_table):
    for at in range(0, value.shape[0], HDIM):
        low = value[at : at + HALF]
        high = value[at + HALF : at + HDIM]
        spot = first + at
        out_ref[spot : spot + HALF, :] = (low * cos_table + high * sin_table).astype(BF16)
        out_ref[spot + HALF : spot + HDIM, :] = (high * cos_table - low * sin_table).astype(BF16)


def unproject_kernel(
    count, n_tp, need, give, x_ref, w_ref, cos_ref, sin_ref, two_ref, dq_ref, dq_back, *refs
):
    dkv_refs = refs[:count]
    proj_out = refs[count]
    part_refs = refs[count + 1 : count + 1 + n_tp]
    grad, dkv = refs[count + 1 + n_tp :]
    rows, model = x_ref.shape
    part = rows // n_tp
    width = dq_ref.shape[0]
    tp = lax.axis_index("tp")
    need(2, 3)
    cos_table = cos_ref[...]
    sin_table = sin_ref[...]
    turn_back(proj_out, 0, dq_ref[...] + dq_back[...].astype(F32), cos_table, sin_table)
    total = dkv_refs[0][...]
    for ref in dkv_refs[1:]:
        total = total + ref[...].astype(F32)
    dkv[...] = total
    turn_back(proj_out, width, dkv[:width, :], cos_table, sin_table)
    proj_out[2 * width :, :] = dkv[width:, :].astype(BF16)
    need(1)
    grad[...] = mm(proj_out[...], w_ref[...], TN)
    need(0, 4)

    def gains(i, carry):
        at = pl.ds(i * STRIP, STRIP)
        unit, unused = normed(x_ref[at, :].astype(F32))
        product = grad[at, :] * unit
        return carry + jnp.sum(product.reshape(STRIP // 8, 8, -1), axis=0)

    gain = lax.fori_loop(0, rows // STRIP, gains, jnp.zeros((8, model), F32))
    line = lax.broadcasted_iota(jnp.int32, (16, model), 0)
    gain_two = jnp.sum(two_ref[...], axis=0, keepdims=True)
    gain = jnp.sum(gain, axis=0, keepdims=True)
    gain = jnp.where(line == 0, gain, jnp.where(line == 1, gain_two, 0.0))
    for k in range(n_tp):
        at = pl.ds(pl.multiple_of(slot(tp ^ k, n_tp) * part, part), part)
        part_refs[k][:part, :] = grad[at, :].astype(part_refs[k].dtype)
        part_refs[k][part:, :] = gain.astype(part_refs[k].dtype)


def unproject(n_tp, tokens, qkv_t, cos_table, sin_table, gain_two_part, dq, dq_back, dkvs, after):
    rows, model = tokens.shape
    part = rows // n_tp
    return call(
        "unproject",
        functools.partial(unproject_kernel, len(dkvs), n_tp),
        kinds((tokens, qkv_t, cos_table, sin_table, gain_two_part), "v")
        + kinds((dq, dq_back, *dkvs), "v"),
        [((qkv_t.shape[0], rows), BF16, "v"), ((part + 16, model), F32, "v")]
        + [((part + 16, model), BF16, "v")] * (n_tp - 1),
        [pltpu.VMEM((rows, model), F32), pltpu.VMEM(dkvs[0].shape, F32)],
        16,
        after,
        True,
    )


def input_kernel(x_ref, gain_ref, grad_ref, sum_ref, out_ref, gain_out):
    part, model = grad_ref.shape
    total = sum_ref[...]
    unit, scale = normed(x_ref[...].astype(F32))
    gain = gain_ref[...].reshape(1, -1)
    value = grad_ref[...] + norm_back(unit, scale, total[:part], gain)
    out_ref[...] = value.astype(BF16)
    gain_out[...] = total[part : part + 8]


def input_side(tokens, gain, middle_grad, summed, after):
    part, model = middle_grad.shape
    return call(
        "input_side",
        input_kernel,
        [(tokens, part), (gain, "h"), (middle_grad, "v"), (summed, "v")],
        [((part, model), BF16, "v"), ((8, model), F32, "v")],
        (),
        16,
        after,
    )


def early_kernel(mixed_ref, gate_ref, cot_ref, h_ref, in_ref, down_ref, h_pair, *refs):
    keep_ref, send_ref, gate_up, mixed_grad, mixed, gate = refs
    units = down_ref.shape[0]
    half = h_ref.shape[0]
    bit = lax.axis_index("tp") % 2
    mine = pl.ds(pl.multiple_of(bit * half, half), half)
    other = pl.ds(pl.multiple_of((1 - bit) * half, half), half)
    gate_up[...] = mm(in_ref[...], h_pair[...], NT)
    mixed_grad[...] = mm(down_ref[...], cot_ref[other, :], NT)
    gated(units, 0, gate_up, mixed_grad, mixed, gate)
    width = keep_ref.shape[1]
    core = lax.axis_index("seq") % 2
    for ref, side in ((send_ref, 1 - core), (keep_ref, core)):
        columns = pl.ds(pl.multiple_of(side * width, width), width)
        down = mm(mixed_ref[:units, :], cot_ref[mine, columns], NN)
        down = down + mm(mixed[...], cot_ref[other, columns], NN)
        ref[:units, :] = down.astype(ref.dtype)
        both = mm(gate_ref[: 2 * units, :], h_ref[:, columns], NN)
        both = both + mm(gate[...], h_pair[:, columns], NN)
        ref[units:, :] = both.astype(ref.dtype)


def early_grads(mixed, gate_grad, cotangent, h_two, in_t, w_down, h_pair, after):
    units, model = w_down.shape
    half = h_two.shape[0]
    return call(
        "early_grads",
        early_kernel,
        kinds((mixed, gate_grad, cotangent, h_two, in_t, w_down), "h") + [(h_pair, "v")],
        [((3 * units, model // 2), F32, "v"), ((3 * units, model // 2), BF16, "v")],
        [
            pltpu.VMEM((2 * units, half), F32),
            pltpu.VMEM((units, half), F32),
            pltpu.VMEM((units, half), BF16),
            pltpu.VMEM((2 * units, half), BF16),
        ],
        24,
        after,
    )


def late_kernel(n_tp, proj_ref, h_ref, out_ref, *refs):
    branch_refs = refs[:n_tp]
    keep_ref, send_ref, branch_full = refs[n_tp:]
    part = branch_refs[0].shape[0]
    half = keep_ref.shape[1]
    wide = proj_ref.shape[0]
    tp = lax.axis_index("tp")
    core = lax.axis_index("seq") % 2
    for k in range(n_tp):
        at = pl.ds(pl.multiple_of(slot(tp ^ hop(k, n_tp), n_tp) * part, part), part)
        branch_full[at, :] = branch_refs[k][...]
    for ref, side in ((send_ref, 1 - core), (keep_ref, core)):
        columns = pl.ds(pl.multiple_of(side * half, half), half)
        ref[:wide, :] = mm(proj_ref[...], h_ref[:, columns], NN).astype(ref.dtype)
        ref[wide:, :] = mm(out_ref[...], branch_full[:, columns], NN).astype(ref.dtype)


def late_grads(proj_grad, h_one, out_b, branches, after):
    rows, model = h_one.shape
    wide = proj_grad.shape[0] + out_b.shape[0]
    return call(
        "late_grads",
        functools.partial(late_kernel, len(branches)),
        [(proj_grad, "v"), (h_one, "v"), (out_b, "v"), (branches[0], "v")]
        + kinds(branches[1:], "v"),
        [((wide, model // 2), F32, "v"), ((wide, model // 2), BF16, "v")],
        [pltpu.VMEM((rows, model), BF16)],
        16,
        after,
    )


def spread_kernel(count, *refs):
    given, outs, held = refs[: -count - 1], refs[-count - 1 : -1], refs[-1]
    piece = outs[0].shape[0]
    chip = lax.axis_index("seq") // 2
    at = 0
    for keep_ref, back_ref in zip(given[::2], given[1::2]):
        rows = keep_ref.shape[0]
        held[at : at + rows, :] = keep_ref[...] + back_ref[...].astype(F32)
        at += rows
    if at < held.shape[0]:
        held[at:, :] = jnp.zeros((held.shape[0] - at, held.shape[1]), F32)
    for k in range(count):
        at = pl.ds(pl.multiple_of((chip ^ k) * piece, piece), piece)
        outs[k][...] = held[at, :].astype(outs[k].dtype)


def spread(count, *pairs):
    half = pairs[0][0].shape[1]
    rows = sum(keep.shape[0] for keep, unused in pairs)
    piece = -(-rows // (8 * count)) * 8
    return call(
        "spread",
        functools.partial(spread_kernel, count),
        [(array, "v") for pair in pairs for array in pair],
        [((piece, half), F32, "v")] + [((piece, half), BF16, "v")] * (count - 1),
        [pltpu.VMEM((count * piece, half), F32)],
    )


def piece_kernel(count, gain_ref, *refs):
    out_ref = refs[count]
    half = out_ref.shape[1]
    total = refs[0][...]
    for ref in refs[1:count]:
        total = total + ref[...].astype(F32)
    line = lax.broadcasted_iota(jnp.int32, (16, half), 0)
    gains = jnp.zeros((16, half), F32)
    for at in range(4):
        row = gain_ref[at // 2 : at // 2 + 1, at % 2 * half : (at % 2 + 1) * half]
        gains = jnp.where(line == at, row, gains)
    out_ref[...] = jnp.concatenate([total, gains], axis=0).astype(BF16)


def sum_piece(gains, pieces, after=()):
    piece, half = pieces[0].shape
    (out,) = call(
        "sum_piece",
        functools.partial(piece_kernel, len(pieces)),
        [(gains, "v")] + kinds(pieces, "v"),
        [((piece + 16, half), BF16, "v")],
        (),
        16,
        after,
    )
    return out


def collect_kernel(count, *refs):
    out_ref, held = refs[count:]
    piece = refs[0].shape[0] - 16
    wide = count * piece
    chip = lax.axis_index("seq") // 2
    gains = jnp.zeros((16, out_ref.shape[1]), F32)
    for k in range(count):
        at = pl.ds(pl.multiple_of((chip ^ hop(k, count)) * piece, piece), piece)
        whole = refs[k][...].astype(F32)
        held[at, :] = whole[:piece]
        gains = gains + whole[piece:]
    held[wide:, :] = gains
    out_ref[...] = held[...].astype(BF16)


def collect(pieces, after=()):
    piece, half = pieces[0].shape
    wide = (piece - 16) * len(pieces) + 16
    (out,) = call(
        "collect",
        functools.partial(collect_kernel, len(pieces)),
        kinds(pieces, "v"),
        [((wide, half), BF16, "v")],
        [pltpu.VMEM((wide, half), F32)],
        16,
        after,
    )
    return out


def finish_kernel(sizes, need, give, own_ref, pair_ref, *refs):
    out_refs, gain_refs = refs[: len(sizes)], refs[len(sizes) :]
    half = own_ref.shape[1]
    core = lax.axis_index("seq") % 2
    at = 0
    for n, (out_ref, size) in enumerate(zip(out_refs, sizes)):
        for ref, side in ((own_ref, core), (pair_ref, 1 - core)):
            columns = pl.ds(pl.multiple_of(side * half, half), half)
            out_ref[:, columns] = ref[at : at + size, :].astype(F32)
        give(n)
        at += size
    first = own_ref.shape[0] - 16
    gains = own_ref[first:, :].astype(F32) + pair_ref[first:, :].astype(F32)
    for at, ref in zip((0, 2), gain_refs):
        ref[pl.ds(0, half)] = gains[at]
        ref[pl.ds(half, half)] = gains[at + 1]


def finish(own, pair, sizes):
    model = 2 * own.shape[1]
    return call(
        "finish",
        functools.partial(finish_kernel, sizes),
        [(own, "v"), (pair, "v")],
        [((size, model), F32, "h") for size in sizes] + [((model,), F32, "h")] * 2,
        (),
        24,
        lazy=True,
    )


def down_kernel(mixed_ref, w_ref, middle_ref, keep_ref, *refs):
    send_refs, total = refs[:-1], refs[-1]
    part = keep_ref.shape[0]
    tp = lax.axis_index("tp")
    total[...] = mm(mixed_ref[...], w_ref[...], TN)
    own = pl.ds(pl.multiple_of(tp // 2 * part, part), part)
    keep_ref[...] = total[own, :] + middle_ref[own, :]
    for n, ref in enumerate(send_refs):
        at = pl.ds(pl.multiple_of((tp ^ (2 * n + 2)) // 2 * part, part), part)
        ref[...] = total[at, :].astype(ref.dtype)


def down(n_tp, mixed, w_both, middle, after):
    rows, model = middle.shape
    part = 2 * rows // n_tp
    return call(
        "down",
        down_kernel,
        [(mixed, "h"), (w_both, "v"), (middle, "h")],
        [((part, model), F32, "h")] + [((part, model), BF16, "h")] * (n_tp // 2 - 1),
        [pltpu.VMEM((rows, model), F32)],
        16,
        after,
    )


def total_kernel(count, *refs):
    total = refs[0][...]
    for ref in refs[1:count]:
        total = total + ref[...].astype(F32)
    refs[count][...] = total.astype(refs[count].dtype)


def total_of(parts, dtype=BF16, kind="v", after=(), flops=0):
    (out,) = call(
        "total_of",
        functools.partial(total_kernel, len(parts)),
        [(parts[0], kind)] + kinds(parts[1:], "v"),
        [(parts[0].shape, dtype, "v")],
        (),
        16,
        after,
        flops=flops,
    )
    return out


def body(
    n_seq,
    n_tp,
    tokens,
    gain_one,
    w_qkv,
    w_out,
    gain_two,
    w_in,
    w_down,
    cotangent,
    doc_lengths,
    roster,
):
    rows, model = tokens.shape
    width = w_qkv.shape[2]
    units = w_in.shape[2]
    count = n_seq // 2
    qkv_t = w_qkv.transpose(1, 2, 0).reshape(3 * width, model)
    in_t = w_in.transpose(1, 2, 0).reshape(2 * units, model)
    over_tp = lambda x, k: swap(x, "tp", k, n_tp)
    over_chips = lambda x, k: swap(x, "seq", 2 * k, n_seq)
    over_cores = lambda x: swap(x, "seq", 1, n_seq)
    everywhere = lambda xs: [xs[0]] + came(n_tp, lambda k: over_tp(xs[k], k))

    def by_steps(part):
        parts = {0: part}
        step = n_tp // 2
        while step:
            parts.update({k ^ step: over_tp(x, step) for k, x in parts.items()})
            step //= 2
        return [parts[hop(n, n_tp)] for n in range(n_tp)]

    docs = (doc_lengths, roster)

    queries, kv, h_one, cos_table, sin_table = project(*docs, tokens, gain_one, qkv_t)
    blocks = [kv] + [over_chips(kv, j) for j in range(1, count)]
    q_pair = over_cores(queries)
    picked, w_half = pick(in_t, w_down, w_out)
    got = [over_tp(picked, 1)] + [over_tp(w_half, k) for k in range(2, n_tp)]

    split = (count + 1) // 2
    (state,) = attention_forward(0, False, *docs, queries, q_pair, blocks[:split])
    state_own, state_pair = attention_forward(
        split, True, *docs, queries, q_pair, blocks[split:], state, kinds(got[1:], "v")
    )
    out_b, totals, out_mine, out_other = join(state_own, over_cores(state_pair))
    outs = everywhere([out_other if k % 2 else out_mine for k in range(n_tp)])
    out_pair = over_cores(out_b)
    totals_pair = over_cores(totals)

    got = pile(got, [(state_pair, "v")])
    staged = stage(n_tp, tokens, cotangent, in_t, w_down, w_out, got, over_cores(got))
    middle, middle_part, h_two, mixed, gate_grad, gain_two_part, own, *others = feed(
        gain_two, staged, outs
    )
    arrived = [own] + [over_tp(others[n], 2 * n + 2) for n in range(n_tp // 2 - 1)]
    own, *others = down(n_tp, mixed, staged[4], middle, ())
    middle_grad, branch_grad, *pieces = branch(
        n_tp, middle_part, cotangent, gain_two, staged[2], arrived, [(own, "h")]
    )
    early, early_send = early_grads(
        mixed, gate_grad, cotangent, h_two, in_t, w_down, over_tp(h_two, 1), [(branch_grad, "h")]
    )
    out_grad = lay_turned(everywhere(pieces), [(early, "v")])
    grad_pair = over_cores(out_grad)
    branches = by_steps(branch_grad)

    held = (queries, q_pair, out_grad, grad_pair, out_b, out_pair, totals, totals_pair)
    *terms, dq = attention_backward(1, False, *docs, held, blocks[1:], None)
    total = total_of(
        [own] + [over_tp(others[n], 2 * n + 2) for n in range(n_tp // 2 - 1)],
        BF16,
        "h",
        [(dq, "v")],
    )
    totals_all = by_steps(total)

    dkv, dq_own, dq_pair = attention_backward(0, True, *docs, held, blocks[:1], dq)
    dkvs = [dkv] + [over_chips(terms[j - 1], j) for j in range(1, count)]

    proj_grad, *parts = unproject(
        n_tp,
        tokens,
        qkv_t,
        cos_table,
        sin_table,
        gain_two_part,
        dq_own,
        over_cores(dq_pair),
        dkvs,
        [(total, "v")],
    )
    layer_out = stack_parts(totals_all)
    keep, send = late_grads(proj_grad, h_one, out_b, branches, [(totals_all[n_tp // 2], "v")])
    own, *others = spread(count, (keep, over_cores(send)), (early, over_cores(early_send)))
    summed = total_of(everywhere(parts), F32, flops=2_000_000_000)
    chip_sum = total_of(
        [own] + came(count, lambda k: over_chips(others[k - 1], k)), F32, "v", ()
    )
    input_part, gains = input_side(tokens, gain_one, middle_grad, summed, [(own, "v")])
    inputs_all = everywhere([input_part] * n_tp)
    piece = sum_piece(gains, [chip_sum], ())
    input_grad = stack_parts(inputs_all, (), 3_000_000_000)
    collected = collect(
        [piece] + came(count, lambda k: over_chips(piece, k)), [(input_grad, "h"), (layer_out, "h")]
    )
    grad_qkv, grad_out, grad_down, grad_in, grad_one, grad_two = finish(
        collected, over_cores(collected), (3 * width, width, units, 2 * units)
    )

    back = lambda x, n: x.reshape(-1, n, model).transpose(2, 0, 1)
    return (
        layer_out,
        input_grad,
        grad_one,
        back(grad_qkv, width),
        grad_out,
        grad_two,
        back(grad_in, units),
        grad_down,
    )


def solution(mesh):
    placed = (
        P("seq", None),
        P(),
        P(None, None, "tp"),
        P("tp", None),
        P(),
        P(None, None, "tp"),
        P("tp", None),
        P("seq", None),
        P(),
        P(),
    )
    return jax.shard_map(
        functools.partial(body, mesh.shape["seq"], mesh.shape["tp"]),
        mesh=mesh,
        in_specs=placed,
        out_specs=(
            P("seq", None),
            P("seq", None),
            P(),
            P(None, None, "tp"),
            P("tp", None),
            P(),
            P(None, None, "tp"),
            P("tp", None),
        ),
        check_vma=False,
    )
```

```python
import functools
import math

import jax
import jax.numpy as jnp
import numpy as np
from jax import lax
from jax.experimental import pallas as pl
from jax.experimental.pallas import tpu as pltpu
from jax.sharding import PartitionSpec as P

HDIM = 64
HALF = HDIM // 2
EPSILON = 1e-05
ROPE_THETA = 160000.0
MASKED = -1e30
AUG = 80
STRIP = 64
F32 = jnp.float32
BF16 = jnp.bfloat16
HBM = pl.BlockSpec(memory_space=pltpu.HBM)
VMEM = pl.BlockSpec(memory_space=pltpu.VMEM)

NN = (((1,), (0,)), ((), ()))
NT = (((1,), (1,)), ((), ()))
TN = (((0,), (0,)), ((), ()))


def params(mib):
    return pltpu.CompilerParams(vmem_limit_bytes=mib * 2**20)


def slot(tp, n_tp):
    return tp % 2 * (n_tp // 2) + tp // 2


def hop(n, count):
    return (count - n) % count


def came(count, send):
    return [send(hop(n, count)) for n in range(1, count)]


def mm(a, b, dims):
    return lax.dot_general(a, b, dims, preferred_element_type=F32)


def shaped(shape, dtype):
    return jax.ShapeDtypeStruct(shape, dtype)


def kinds(arrays, kind):
    return [(array, kind) for array in arrays]


def pin(array, kind):
    return array if kind in ("v", "free") else pltpu.with_memory_space_constraint(array, pltpu.HBM)


def call(name, kernel, ins, outs, scratch=(), mib=16, after=(), lazy=False, flops=0):
    fetched = [i for i, given in enumerate(ins) if given[1] not in ("v", "raw", "free")]
    left = [i for i, out in enumerate(outs) if out[2] == "h"]

    def held(array, kind):
        rows = array.shape[0] if kind == "h" else kind
        return pltpu.VMEM((rows,) + array.shape[1:], array.dtype)

    def run(*refs):
        in_refs = list(refs[: len(ins)])
        at = len(ins) + len(after)
        out_refs = list(refs[at : at + len(outs)])
        at += len(outs)
        own = refs[at : at + len(scratch)]
        at += len(scratch)
        buffers = refs[at : at + len(fetched) + len(left)]
        sems = refs[-1]
        copies = []
        for n, i in enumerate(fetched):
            source = in_refs[i]
            if ins[i][1] != "h":
                rows = ins[i][1]
                n_tp = ins[i][0].shape[0] // rows
                at = pl.multiple_of(slot(lax.axis_index("tp"), n_tp) * rows, rows)
                source = source.at[pl.ds(at, rows)]
            copies.append(pltpu.make_async_copy(source, buffers[n], sems.at[n]))
            in_refs[i] = buffers[n]
        for copy in copies:
            copy.start()
        coming = dict(zip(fetched, copies))
        going = {}
        for n, i in enumerate(left):
            spot = len(fetched) + n
            going[i] = pltpu.make_async_copy(buffers[spot], out_refs[i], sems.at[spot])
            out_refs[i] = buffers[spot]
        gone = []

        def need(*which):
            for i in which:
                if i in coming:
                    coming.pop(i).wait()

        def give(*which):
            for i in which:
                if i in going:
                    gone.append(going.pop(i))
                    gone[-1].start()

        if lazy:
            kernel(need, give, *in_refs, *out_refs, *own)
        else:
            need(*fetched)
            kernel(*in_refs, *out_refs, *own)
        need(*fetched)
        give(*left)
        for copy in gone:
            copy.wait()

    spec = lambda kind: VMEM if kind == "v" else HBM
    count = len(fetched) + len(left)
    return pl.pallas_call(
        run,
        out_shape=tuple(
            shaped(shape, dtype) if kind == "v" else pltpu.HBM(shape, dtype)
            for shape, dtype, kind in outs
        ),
        in_specs=[spec(kind) for unused, kind in ins] + [spec(kind) for unused, kind in after],
        out_specs=tuple(spec(kind) for unused, unused, kind in outs),
        scratch_shapes=list(scratch)
        + [held(*ins[i]) for i in fetched]
        + [pltpu.VMEM(outs[i][0], outs[i][1]) for i in left]
        + [pltpu.SemaphoreType.DMA((max(count, 1),))],
        name=name,
        cost_estimate=pl.CostEstimate(flops=flops, bytes_accessed=0, transcendentals=0)
        if flops
        else None,
        compiler_params=params(mib),
    )(*[pin(*given) for given in ins], *[pin(*given) for given in after])


def swap(x, axis, hop, count):
    return lax.ppermute(x, axis, [(i, i ^ hop) for i in range(count)])


def doc_scratch(doc_lengths, roster):
    return [pltpu.SMEM(doc_lengths.shape, jnp.int32), pltpu.SMEM(roster.shape, jnp.int32)]


def fetch_docs(len_any, roster_any, len_ref, roster_ref, len_sem, roster_sem):
    one = pltpu.make_async_copy(len_any, len_ref, len_sem)
    two = pltpu.make_async_copy(roster_any, roster_ref, roster_sem)
    one.start()
    two.start()
    one.wait()
    two.wait()


def doc_bounds(len_ref):
    ends, total = [], jnp.int32(0)
    for d in range(len_ref.shape[0]):
        total = total + len_ref[d]
        ends.append(total)
    return ends


def doc_of(ends, position):
    found = jnp.int32(0)
    for end in ends:
        found = found + (end <= position).astype(jnp.int32)
    return found


def meet(ends, base_a, base_b, rows):
    low = jnp.maximum(doc_of(ends, base_a), doc_of(ends, base_b))
    high = jnp.minimum(doc_of(ends, base_a + rows - 1), doc_of(ends, base_b + rows - 1))
    return low <= high


def doc_rows(ends, base, rows):
    spot = base + lax.broadcasted_iota(jnp.int32, (16, rows), 1)
    line = lax.broadcasted_iota(jnp.int32, (16, rows), 0)
    held = jnp.zeros((16, rows), F32)
    start = jnp.int32(0)
    for d, end in enumerate(ends):
        inside = (line == d) & (spot >= start) & (spot < end)
        held = jnp.where(inside, 1.0, held)
        start = end
    return held


def ban_rows(ends, base, rows):
    line = lax.broadcasted_iota(jnp.int32, (16, rows), 0)
    held = doc_rows(ends, base, rows)
    return jnp.where((held > 0.5) | (line >= len(ends)), 0.0, MASKED)


def key_row(block, seq_index):
    return seq_index ^ (2 * block)


def place_row(ends, base, rows):
    spot = base + lax.broadcasted_iota(jnp.int32, (1, rows), 1)
    start = jnp.zeros((1, rows), jnp.int32)
    for end in ends:
        start = jnp.where(spot >= end, end, start)
    return (spot - start).astype(F32)


def normed(values):
    centre = jnp.mean(values, axis=-1, keepdims=True)
    shifted = values - centre
    spread = jnp.mean(shifted * shifted, axis=-1, keepdims=True)
    scale = lax.rsqrt(spread + EPSILON)
    return shifted * scale, scale


def norm_back(unit, scale, grad, gain):
    u = grad * gain
    mean_u = jnp.mean(u, axis=-1, keepdims=True)
    mean_un = jnp.mean(u * unit, axis=-1, keepdims=True)
    return scale * (u - mean_u - unit * mean_un)


def project_kernel(
    width, need, give, len_any, roster_any, x_ref, w_ref, gain_ref, freq_ref, *refs
):
    q_out, kv_out, h_out, cos_out, sin_out = refs[:5]
    proj, len_ref, roster_ref, sems = refs[5:]
    rows = x_ref.shape[0]
    fetch_docs(len_any, roster_any, len_ref, roster_ref, sems.at[0], sems.at[1])
    need(5)
    ends = doc_bounds(len_ref)
    place = place_row(ends, roster_ref[lax.axis_index("seq")] * rows, rows)
    angles = place * freq_ref[...]
    cos_table = jnp.cos(angles)
    sin_table = jnp.sin(angles)
    cos_out[...] = cos_table
    sin_out[...] = sin_table
    give(3, 4)
    need(2, 4)
    gain = gain_ref[...].reshape(1, -1)

    def strip(i, carry):
        at = pl.ds(i * STRIP, STRIP)
        unit, unused = normed(x_ref[at, :].astype(F32))
        h_out[at, :] = (unit * gain).astype(BF16)
        return carry

    lax.fori_loop(0, rows // STRIP, strip, 0)
    give(2)
    need(3)
    proj[...] = mm(w_ref[...], h_out[...], NT)
    for at in range(0, 2 * width, HDIM):
        low = proj[at : at + HALF, :]
        high = proj[at + HALF : at + HDIM, :]
        turned_low = (low * cos_out[...] - high * sin_out[...]).astype(BF16)
        turned_high = (high * cos_out[...] + low * sin_out[...]).astype(BF16)
        if at < width:
            q_out[at : at + HALF, :] = (turned_low.astype(F32) * HDIM**-0.5).astype(BF16)
            q_out[at + HALF : at + HDIM, :] = (turned_high.astype(F32) * HDIM**-0.5).astype(BF16)
        else:
            kv_out[at - width : at - width + HALF, :] = turned_low
            kv_out[at - width + HALF : at - width + HDIM, :] = turned_high
    kv_out[width:, :] = proj[2 * width :, :].astype(BF16)


def project(doc_lengths, roster, tokens, gain, qkv_t):
    rows, model = tokens.shape
    width = qkv_t.shape[0] // 3
    freq = (ROPE_THETA ** -(np.arange(HALF) * (2.0 / HDIM))).astype(np.float32)[:, None]
    return call(
        "project",
        functools.partial(project_kernel, width),
        kinds((doc_lengths, roster), "raw") + kinds((tokens, qkv_t, gain, jnp.asarray(freq)), "h"),
        [
            ((width, rows), BF16, "v"),
            ((2 * width, rows), BF16, "v"),
            ((rows, model), BF16, "v"),
            ((HALF, rows), F32, "v"),
            ((HALF, rows), F32, "v"),
        ],
        [pltpu.VMEM((3 * width, rows), F32)]
        + doc_scratch(doc_lengths, roster)
        + [pltpu.SemaphoreType.DMA((2,))],
        lazy=True,
    )


def forward_kernel(first, count, heads, last, len_any, roster_any, q_own, q_pair, *refs):
    kv_refs = refs[:count]
    refs = refs[count:]
    if first:
        state_in, refs = refs[0], refs[1:]
    outs = refs[: 2 if last else 1]
    kv, q_aug, state, len_ref, roster_ref, sems = refs[len(outs) :]
    rows = q_own.shape[1]
    width = heads * HDIM
    me = lax.axis_index("seq")
    copies = [pltpu.make_async_copy(kv_refs[j], kv.at[j], sems.at[j]) for j in range(count)]
    for copy in copies:
        copy.start()
    fetch_docs(len_any, roster_any, len_ref, roster_ref, sems.at[count], sems.at[count + 1])
    ends = doc_bounds(len_ref)
    bases = (roster_ref[me] * rows, roster_ref[me ^ 1] * rows)
    for g, q_ref in enumerate((q_own, q_pair)):
        mark = doc_rows(ends, bases[g], rows).astype(BF16)
        for h in range(heads):
            q_aug[g * heads + h, :HDIM, :] = q_ref[h * HDIM : (h + 1) * HDIM, :]
            q_aug[g * heads + h, HDIM:, :] = mark
    if first:
        state[...] = state_in[...]
    else:
        line = lax.broadcasted_iota(jnp.int32, (2 * heads, AUG, rows), 1)
        state[...] = jnp.where(line >= 72, MASKED, 0.0)
    for copy in copies:
        copy.wait()

    top = lax.broadcasted_iota(jnp.int32, (16, rows), 0) == 0
    ones = jnp.where(top, 1.0, 0.0).astype(BF16)

    def block(j, carry):
        key_base = roster_ref[key_row(j + first, me)] * rows
        ban = ban_rows(ends, key_base, rows).astype(BF16)
        for g in range(2):

            @pl.when(meet(ends, bases[g], key_base, rows))
            def _():
                for h in range(heads):
                    at = g * heads + h
                    keys = jnp.concatenate([kv[j, h * HDIM : (h + 1) * HDIM, :], ban], axis=0)
                    vals = jnp.concatenate(
                        [kv[j, width + h * HDIM : width + (h + 1) * HDIM, :], ones], axis=0
                    )
                    scores = mm(keys, q_aug[at], TN)
                    old = state[at, 72:73, :]
                    new = jnp.maximum(old, jnp.max(scores, axis=0, keepdims=True))
                    probs = jnp.exp(scores - new).astype(BF16)
                    part = mm(vals, probs, NN)
                    fade = jnp.exp(old - new)
                    state[at, :72, :] = state[at, :72, :] * fade + part[:72]
                    state[at, 72:, :] = jnp.broadcast_to(new, (8, rows))

        return carry

    lax.fori_loop(0, count, block, 0)
    if last:
        outs[0][...] = state[:heads]
        outs[1][...] = state[heads:]
    else:
        outs[0][...] = state[...]


def attention_forward(first, last, doc_lengths, roster, q_own, q_pair, blocks, state=None, after=()):
    width, rows = q_own.shape
    heads = width // HDIM
    count = len(blocks)
    half = ((heads, AUG, rows), F32, "v")
    whole = ((2 * heads, AUG, rows), F32, "v")
    given = [] if state is None else [(state, "v")]
    return call(
        "attention_forward",
        functools.partial(forward_kernel, first, count, heads, last),
        [(doc_lengths, "raw"), (roster, "raw"), (q_own, "v"), (q_pair, "v")]
        + kinds(blocks, "free")
        + given,
        [half, half] if last else [whole],
        [
            pltpu.VMEM((count, 2 * width, rows), BF16),
            pltpu.VMEM((2 * heads, AUG, rows), BF16),
            pltpu.VMEM((2 * heads, AUG, rows), F32),
        ]
        + doc_scratch(doc_lengths, roster)
        + [pltpu.SemaphoreType.DMA((count + 2,))],
        16 if count < 8 else 40,
        after,
    )


def backward_kernel(first, count, heads, more, last, len_any, roster_any, *refs):
    q_own, q_pair, g_own, g_pair, o_own, o_pair, t_own, t_pair = refs[:8]
    kv_refs, refs = refs[8 : 8 + count], refs[8 + count :]
    if more:
        dq_in, refs = refs[0], refs[1:]
    outs, refs = refs[:count], refs[count:]
    dq_outs, refs = (refs[:2], refs[2:]) if last else (refs[:1], refs[1:])
    kv, q_aug, delta, dq, dkv, len_ref, roster_ref, sems = refs
    rows = q_own.shape[1]
    width = heads * HDIM
    me = lax.axis_index("seq")
    copies = [pltpu.make_async_copy(kv_refs[j], kv.at[j], sems.at[j]) for j in range(count)]
    for copy in copies:
        copy.start()
    fetch_docs(len_any, roster_any, len_ref, roster_ref, sems.at[count], sems.at[count + 1])
    ends = doc_bounds(len_ref)
    bases = (roster_ref[me] * rows, roster_ref[me ^ 1] * rows)
    for g, (q_ref, g_ref, o_ref) in enumerate(((q_own, g_own, o_own), (q_pair, g_pair, o_pair))):
        mark = doc_rows(ends, bases[g], rows).astype(BF16)
        for h in range(heads):
            part = slice(h * HDIM, (h + 1) * HDIM)
            q_aug[g * heads + h, :HDIM, :] = q_ref[part, :]
            q_aug[g * heads + h, HDIM:, :] = mark
            product = g_ref[part, :].astype(F32) * o_ref[part, :].astype(F32)
            delta[g * heads + h] = jnp.broadcast_to(
                jnp.sum(product, axis=0, keepdims=True), (8, rows)
            )
    if more:
        dq[...] = dq_in[...]
    else:
        dq[...] = jnp.zeros_like(dq)
    for copy in copies:
        copy.wait()

    def block(j, carry):
        key_base = roster_ref[key_row(j + first, me)] * rows
        ban = ban_rows(ends, key_base, rows).astype(BF16)
        dkv[j] = jnp.zeros((2 * width, rows), F32)
        for g, (g_ref, t_ref) in enumerate(((g_own, t_own), (g_pair, t_pair))):

            @pl.when(meet(ends, bases[g], key_base, rows))
            def _():
                for h in range(heads):
                    at = g * heads + h
                    part = slice(h * HDIM, (h + 1) * HDIM)
                    late = slice(width + h * HDIM, width + (h + 1) * HDIM)
                    keys = kv[j, part, :]
                    scores = mm(jnp.concatenate([keys, ban], axis=0), q_aug[at], TN)
                    probs = jnp.exp(scores - t_ref[h, 0:1, :])
                    prob_grads = mm(kv[j, late, :], g_ref[part, :], TN)
                    score_grad = (probs * (prob_grads - delta[at, 0:1, :])).astype(BF16)
                    dkv[j, late, :] += mm(g_ref[part, :], probs.astype(BF16), NT)
                    dkv[j, part, :] += mm(q_aug[at, :HDIM, :], score_grad, NT)
                    dq[at] += mm(keys, score_grad, NN)

        return carry

    lax.fori_loop(0, count, block, 0)
    for j in range(count):
        outs[j][...] = dkv[j].astype(outs[j].dtype)
    if last:
        for h in range(heads):
            part = slice(h * HDIM, (h + 1) * HDIM)
            dq_outs[0][part, :] = dq[h] * HDIM**-0.5
            dq_outs[1][part, :] = (dq[heads + h] * HDIM**-0.5).astype(BF16)
    else:
        dq_outs[0][...] = dq[...]


def attention_backward(first, last, doc_lengths, roster, held, blocks, dq=None, after=()):
    width, rows = held[0].shape
    heads = width // HDIM
    count = len(blocks)
    given = [] if dq is None else [(dq, "v")]
    if last:
        queries = [((width, rows), F32, "v"), ((width, rows), BF16, "v")]
    else:
        queries = [((2 * heads, HDIM, rows), F32, "v")]
    return call(
        "attention_backward",
        functools.partial(backward_kernel, first, count, heads, bool(given), last),
        kinds((doc_lengths, roster), "raw") + kinds(held, "v") + kinds(blocks, "free") + given,
        [((2 * width, rows), BF16 if first else F32, "v")] * count + queries,
        [
            pltpu.VMEM((count, 2 * width, rows), BF16),
            pltpu.VMEM((2 * heads, AUG, rows), BF16),
            pltpu.VMEM((2 * heads, 8, rows), F32),
            pltpu.VMEM((2 * heads, HDIM, rows), F32),
            pltpu.VMEM((count, 2 * width, rows), F32),
        ]
        + doc_scratch(doc_lengths, roster)
        + [pltpu.SemaphoreType.DMA((count + 2,))],
        16 if count < 8 else 40,
        after,
        flops=0 if last else 0,
    )


def join_kernel(heads, own_ref, back_ref, out_ref, total_ref, mine_ref, other_ref):
    rows = own_ref.shape[2]
    for h in range(heads):
        top_own = own_ref[h, 72:73, :]
        top_back = back_ref[h, 72:73, :]
        top = jnp.maximum(top_own, top_back)
        fade_own = jnp.exp(top_own - top)
        fade_back = jnp.exp(top_back - top)
        total = own_ref[h, 64:65, :] * fade_own + back_ref[h, 64:65, :] * fade_back
        share_own = fade_own / total
        share_back = fade_back / total
        value = own_ref[h, :HDIM, :] * share_own + back_ref[h, :HDIM, :] * share_back
        out_ref[h * HDIM : (h + 1) * HDIM, :] = value.astype(BF16)
        total_ref[h] = jnp.broadcast_to(top + jnp.log(total), (8, rows))
    half = rows // 2
    for bit in range(2):

        @pl.when(lax.axis_index("tp") % 2 == bit)
        def _():
            mine_ref[...] = out_ref[:, bit * half : (bit + 1) * half]
            other_ref[...] = out_ref[:, (1 - bit) * half : (2 - bit) * half]


def join(own, back):
    heads, unused, rows = own.shape
    return call(
        "join",
        functools.partial(join_kernel, heads),
        [(own, "v"), (back, "v")],
        [
            ((heads * HDIM, rows), BF16, "v"),
            ((heads, 8, rows), F32, "v"),
            ((heads * HDIM, rows // 2), BF16, "v"),
            ((heads * HDIM, rows // 2), BF16, "v"),
        ],
    )


def pick_kernel(in_any, down_any, w_any, all_ref, w_ref, sems):
    core = lax.axis_index("seq") % 2
    at = 0
    copies = []
    for source in (in_any, down_any, w_any):
        rows = source.shape[0] // 2
        mine = pl.ds(pl.multiple_of(core * rows, rows), rows)
        copies.append((source.at[mine], all_ref.at[pl.ds(at, rows)]))
        at += rows
    copies.append((w_any.at[mine], w_ref))
    copies = [pltpu.make_async_copy(*move, sems.at[n]) for n, move in enumerate(copies)]
    for copy in copies:
        copy.start()
    for copy in copies:
        copy.wait()


def pick(in_t, w_down, w_out):
    rows = (in_t.shape[0] + w_down.shape[0] + w_out.shape[0]) // 2
    model = w_out.shape[1]
    return call(
        "pick",
        pick_kernel,
        kinds((in_t, w_down, w_out), "raw"),
        [((rows, model), BF16, "v"), ((w_out.shape[0] // 2, model), BF16, "v")],
        [pltpu.SemaphoreType.DMA((4,))],
    )


def pile_kernel(*refs):
    out_ref = refs[-1]
    at = 0
    for ref in refs[:-1]:
        out_ref[at : at + ref.shape[0], :] = ref[...]
        at += ref.shape[0]


def pile(values, after):
    rows = sum(value.shape[0] for value in values)
    (out,) = call(
        "pile",
        pile_kernel,
        kinds(values, "v"),
        [((rows, values[0].shape[1]), BF16, "v")],
        (),
        16,
        after,
    )
    return out


def stage_kernel(x_any, cot_any, in_any, down_any, w_any, got_ref, rest_ref, *refs):
    x_ref, cot_ref, w_ref, in_ref, down_ref, sems = refs
    half = x_ref.shape[0]
    core = lax.axis_index("seq") % 2
    tp = lax.axis_index("tp")
    n_tp = w_ref.shape[0] // w_any.shape[0]
    mine = pl.ds(pl.multiple_of(tp % 2 * half, half), half)
    width = w_any.shape[0]
    rows = width // 2
    own = pl.ds(pl.multiple_of(tp * width, width), width)
    moves = [(w_any, w_ref.at[own]), (x_any.at[mine], x_ref), (cot_any.at[mine], cot_ref)]
    sides = ((got_ref, core), (rest_ref, 1 - core))
    first = got_ref.shape[0] - (n_tp - 1) * rows
    for k in range(1, n_tp):
        for source, side in sides:
            spot = pl.multiple_of((tp ^ k) * width + side * rows, rows)
            piece = source.at[pl.ds(first + (k - 1) * rows, rows)]
            moves.append((piece, w_ref.at[pl.ds(spot, rows)]))
    at = 0
    for own, ref in ((in_any, in_ref), (down_any, down_ref)):
        rows = own.shape[0] // 2
        moves.append((own, ref.at[pl.ds(0, 2 * rows)]))
        for source, side in sides:
            spot = pl.multiple_of(2 * rows + side * rows, rows)
            moves.append((source.at[pl.ds(at, rows)], ref.at[pl.ds(spot, rows)]))
        at += rows
    copies = [pltpu.make_async_copy(*move, sems.at[n]) for n, move in enumerate(moves)]
    for copy in copies:
        copy.start()
    for copy in copies:
        copy.wait()


def stage(n_tp, tokens, cotangent, in_t, w_down, w_out, got, rest):
    rows, model = tokens.shape
    return call(
        "stage",
        stage_kernel,
        kinds((tokens, cotangent, in_t, w_down, w_out), "raw") + kinds((got, rest), "v"),
        [
            ((rows // 2, model), BF16, "v"),
            ((rows // 2, model), BF16, "v"),
            ((n_tp * w_out.shape[0], model), BF16, "v"),
            ((2 * in_t.shape[0], model), BF16, "v"),
            ((2 * w_down.shape[0], model), BF16, "v"),
        ],
        [pltpu.SemaphoreType.DMA((7 + 2 * n_tp,))],
    )


def gated(units, first, gate_up, mixed_grad, mixed_out, gate_out):
    rows = math.gcd(units, 96)

    def wave(i, carry):
        spot = pl.ds(first + i * rows, rows)
        at = pl.ds(2 * first + i * rows, rows)
        late = pl.ds(2 * first + units + i * rows, rows)
        gate = gate_up[at, :]
        up = gate_up[late, :]
        back = mixed_grad[spot, :]
        bell = 0.5 * (1.0 + lax.erf(gate * (2.0**-0.5)))
        active = gate * bell
        slope = bell + gate * jnp.exp(-0.5 * gate * gate) * ((2.0 * jnp.pi) ** -0.5)
        mixed_out[spot, :] = (active * up).astype(BF16)
        gate_out[at, :] = (back * up * slope).astype(BF16)
        gate_out[late, :] = (back * active).astype(BF16)
        return carry

    lax.fori_loop(0, units // rows, wave, 0)


def feed_kernel(n_tp, need, give, x_ref, cot_ref, w_ref, in_ref, down_ref, gain_ref, *refs):
    out_refs = refs[:n_tp]
    middle_out, part_out, h_out, mixed_out, gate_out, gain_out = refs[n_tp : n_tp + 6]
    keep_ref, *send_refs = refs[n_tp + 6 : n_tp + 6 + n_tp // 2]
    outs, unit, gate_up, mixed_grad, grad = refs[n_tp + 6 + n_tp // 2 :]
    rows = x_ref.shape[0]
    part = keep_ref.shape[0]
    units = down_ref.shape[0] // 2
    width = out_refs[0].shape[0]
    tp = lax.axis_index("tp")
    for k in range(n_tp):
        at = pl.ds(pl.multiple_of((tp ^ hop(k, n_tp)) * width, width), width)
        outs[at, :] = out_refs[k][...]
    mixed_grad[...] = mm(down_ref[...], cot_ref[...], NT)
    middle_out[...] = mm(outs[...], w_ref[...], TN)
    need(5)
    gain = gain_ref[...].reshape(1, -1)

    def strip(i, carry):
        at = pl.ds(i * 32, 32)
        middle = middle_out[at, :] + x_ref[at, :].astype(F32)
        middle_out[at, :] = middle
        held, unused = normed(middle)
        unit[at, :] = held
        h_out[at, :] = (held * gain).astype(BF16)
        return carry

    lax.fori_loop(0, rows // 32, strip, 0)
    give(0, 2)
    gate_up[...] = mm(in_ref[...], h_out[...], NT)
    for first in (0, units):
        gated(units, first, gate_up, mixed_grad, mixed_out, gate_out)
    give(3, 4)
    grad[...] = mm(gate_out[...], in_ref[...], TN)
    for n, ref in enumerate((keep_ref, *send_refs)):
        at = pl.ds(pl.multiple_of((tp ^ (2 * n)) // 2 * part, part), part)
        ref[...] = grad[at, :].astype(ref.dtype)
        give(6 + n)
    own = pl.ds(pl.multiple_of(tp // 2 * part, part), part)
    part_out[...] = middle_out[own, :]
    give(1)

    def gains(i, carry):
        at = pl.ds(i * 32, 32)
        product = grad[at, :] * unit[at, :]
        return carry + jnp.sum(product.reshape(4, 8, -1), axis=0)

    gain_out[...] = lax.fori_loop(0, rows // 32, gains, jnp.zeros(gain_out.shape, F32))


def feed(gain, staged, outs):
    rows, model = staged[0].shape
    n_tp = len(outs)
    units = staged[4].shape[0]
    part = 2 * rows // n_tp
    return call(
        "feed",
        functools.partial(feed_kernel, n_tp),
        kinds(staged, "v") + [(gain, "h")] + kinds(outs, "v"),
        [
            ((rows, model), F32, "v"),
            ((part, model), F32, "v"),
            ((rows, model), BF16, "v"),
            ((units, rows), BF16, "v"),
            ((2 * units, rows), BF16, "v"),
            ((8, model), F32, "v"),
            ((part, model), F32, "v"),
        ]
        + [((part, model), BF16, "v")] * (n_tp // 2 - 1),
        [
            pltpu.VMEM((n_tp * outs[0].shape[0], rows), BF16),
            pltpu.VMEM((rows, model), F32),
            pltpu.VMEM((2 * units, rows), F32),
            pltpu.VMEM((units, rows), F32),
            pltpu.VMEM((rows, model), F32),
        ],
        24,
        lazy=True,
    )


def branch_kernel(n_tp, count, need, give, middle_ref, cot_ref, gain_ref, w_ref, *refs):
    arrived = refs[:count]
    grad_out, branch_out = refs[count : count + 2]
    piece_refs = refs[count + 2 :]
    width = piece_refs[0].shape[1]
    tp = lax.axis_index("tp")
    need(0, 1, 2, 4)
    total = arrived[0][...]
    for ref in arrived[1:]:
        total = total + ref[...].astype(F32)
    unit, scale = normed(middle_ref[...])
    gain = gain_ref[...].reshape(1, -1)
    value = cot_ref[...].astype(F32) + norm_back(unit, scale, total, gain)
    grad_out[...] = value
    branch_out[...] = value.astype(BF16)
    give(0, 1)
    need(3)
    for k in range(n_tp):
        at = pl.ds(pl.multiple_of((tp ^ k) * width, width), width)
        piece_refs[k][...] = mm(branch_out[...], w_ref[at, :], NT).astype(BF16)


def branch(n_tp, middle_part, cotangent, gain, w_full, arrived, after):
    part, model = arrived[0].shape
    width = w_full.shape[0] // n_tp
    return call(
        "branch",
        functools.partial(branch_kernel, n_tp, len(arrived)),
        [(middle_part, "v"), (cotangent, part)]
        + [(gain, "h"), (w_full, "v"), (arrived[0], "v")]
        + kinds(arrived[1:], "v"),
        [((part, model), F32, "v"), ((part, model), BF16, "v")]
        + [((part, width), BF16, "v")] * n_tp,
        (),
        16,
        after,
        True,
    )


def lay_kernel(n_tp, *refs):
    out_ref, held = refs[n_tp:]
    part = refs[0].shape[0]
    tp = lax.axis_index("tp")
    for k in range(n_tp):
        at = pl.ds(pl.multiple_of(slot(tp ^ hop(k, n_tp), n_tp) * part, part), part)
        held[at, :] = refs[k][...].astype(F32)
    out_ref[...] = held[...].T.astype(BF16)


def lay_turned(pieces, after):
    part, width = pieces[0].shape
    rows = part * len(pieces)
    (out,) = call(
        "lay_turned",
        functools.partial(lay_kernel, len(pieces)),
        kinds(pieces, "v"),
        [((width, rows), BF16, "v")],
        [pltpu.VMEM((rows, width), F32)],
        16,
        after,
    )
    return out


def stack_kernel(n_tp, *refs):
    out_ref = refs[n_tp]
    part = refs[0].shape[0]
    tp = lax.axis_index("tp")
    for k in range(n_tp):
        at = pl.ds(pl.multiple_of(slot(tp ^ hop(k, n_tp), n_tp) * part, part), part)
        out_ref[at, :] = refs[k][...]


def stack_parts(pieces, after=(), flops=0):
    part, model = pieces[0].shape
    (out,) = call(
        "stack_parts",
        functools.partial(stack_kernel, len(pieces)),
        kinds(pieces, "v"),
        [((part * len(pieces), model), pieces[0].dtype, "h")],
        (),
        16,
        after,
        flops=flops,
    )
    return out


def turn_back(out_ref, first, value, cos_table, sin_table):
    for at in range(0, value.shape[0], HDIM):
        low = value[at : at + HALF]
        high = value[at + HALF : at + HDIM]
        spot = first + at
        out_ref[spot : spot + HALF, :] = (low * cos_table + high * sin_table).astype(BF16)
        out_ref[spot + HALF : spot + HDIM, :] = (high * cos_table - low * sin_table).astype(BF16)


def unproject_kernel(
    count, n_tp, need, give, x_ref, w_ref, cos_ref, sin_ref, two_ref, dq_ref, dq_back, *refs
):
    dkv_refs = refs[:count]
    proj_out = refs[count]
    part_refs = refs[count + 1 : count + 1 + n_tp]
    grad, dkv = refs[count + 1 + n_tp :]
    rows, model = x_ref.shape
    part = rows // n_tp
    width = dq_ref.shape[0]
    tp = lax.axis_index("tp")
    need(2, 3)
    cos_table = cos_ref[...]
    sin_table = sin_ref[...]
    turn_back(proj_out, 0, dq_ref[...] + dq_back[...].astype(F32), cos_table, sin_table)
    total = dkv_refs[0][...]
    for ref in dkv_refs[1:]:
        total = total + ref[...].astype(F32)
    dkv[...] = total
    turn_back(proj_out, width, dkv[:width, :], cos_table, sin_table)
    proj_out[2 * width :, :] = dkv[width:, :].astype(BF16)
    need(1)
    grad[...] = mm(proj_out[...], w_ref[...], TN)
    need(0, 4)

    def gains(i, carry):
        at = pl.ds(i * STRIP, STRIP)
        unit, unused = normed(x_ref[at, :].astype(F32))
        product = grad[at, :] * unit
        return carry + jnp.sum(product.reshape(STRIP // 8, 8, -1), axis=0)

    gain = lax.fori_loop(0, rows // STRIP, gains, jnp.zeros((8, model), F32))
    line = lax.broadcasted_iota(jnp.int32, (16, model), 0)
    gain_two = jnp.sum(two_ref[...], axis=0, keepdims=True)
    gain = jnp.sum(gain, axis=0, keepdims=True)
    gain = jnp.where(line == 0, gain, jnp.where(line == 1, gain_two, 0.0))
    for k in range(n_tp):
        at = pl.ds(pl.multiple_of(slot(tp ^ k, n_tp) * part, part), part)
        part_refs[k][:part, :] = grad[at, :].astype(part_refs[k].dtype)
        part_refs[k][part:, :] = gain.astype(part_refs[k].dtype)


def unproject(n_tp, tokens, qkv_t, cos_table, sin_table, gain_two_part, dq, dq_back, dkvs, after):
    rows, model = tokens.shape
    part = rows // n_tp
    return call(
        "unproject",
        functools.partial(unproject_kernel, len(dkvs), n_tp),
        kinds((tokens, qkv_t, cos_table, sin_table, gain_two_part), "v")
        + kinds((dq, dq_back, *dkvs), "v"),
        [((qkv_t.shape[0], rows), BF16, "v"), ((part + 16, model), F32, "v")]
        + [((part + 16, model), BF16, "v")] * (n_tp - 1),
        [pltpu.VMEM((rows, model), F32), pltpu.VMEM(dkvs[0].shape, F32)],
        16,
        after,
        True,
    )


def input_kernel(x_ref, gain_ref, grad_ref, sum_ref, out_ref, gain_out):
    part, model = grad_ref.shape
    total = sum_ref[...]
    unit, scale = normed(x_ref[...].astype(F32))
    gain = gain_ref[...].reshape(1, -1)
    value = grad_ref[...] + norm_back(unit, scale, total[:part], gain)
    out_ref[...] = value.astype(BF16)
    gain_out[...] = total[part : part + 8]


def input_side(tokens, gain, middle_grad, summed, after):
    part, model = middle_grad.shape
    return call(
        "input_side",
        input_kernel,
        [(tokens, part), (gain, "h"), (middle_grad, "v"), (summed, "v")],
        [((part, model), BF16, "v"), ((8, model), F32, "v")],
        (),
        16,
        after,
    )


def early_kernel(mixed_ref, gate_ref, cot_ref, h_ref, in_ref, down_ref, h_pair, *refs):
    keep_ref, send_ref, gate_up, mixed_grad, mixed, gate = refs
    units = down_ref.shape[0]
    half = h_ref.shape[0]
    bit = lax.axis_index("tp") % 2
    mine = pl.ds(pl.multiple_of(bit * half, half), half)
    other = pl.ds(pl.multiple_of((1 - bit) * half, half), half)
    gate_up[...] = mm(in_ref[...], h_pair[...], NT)
    mixed_grad[...] = mm(down_ref[...], cot_ref[other, :], NT)
    gated(units, 0, gate_up, mixed_grad, mixed, gate)
    width = keep_ref.shape[1]
    core = lax.axis_index("seq") % 2
    for ref, side in ((send_ref, 1 - core), (keep_ref, core)):
        columns = pl.ds(pl.multiple_of(side * width, width), width)
        down = mm(mixed_ref[:units, :], cot_ref[mine, columns], NN)
        down = down + mm(mixed[...], cot_ref[other, columns], NN)
        ref[:units, :] = down.astype(ref.dtype)
        both = mm(gate_ref[: 2 * units, :], h_ref[:, columns], NN)
        both = both + mm(gate[...], h_pair[:, columns], NN)
        ref[units:, :] = both.astype(ref.dtype)


def early_grads(mixed, gate_grad, cotangent, h_two, in_t, w_down, h_pair, after):
    units, model = w_down.shape
    half = h_two.shape[0]
    return call(
        "early_grads",
        early_kernel,
        kinds((mixed, gate_grad, cotangent, h_two, in_t, w_down, h_pair), "v"),
        [((3 * units, model // 2), F32, "v"), ((3 * units, model // 2), BF16, "v")],
        [
            pltpu.VMEM((2 * units, half), F32),
            pltpu.VMEM((units, half), F32),
            pltpu.VMEM((units, half), BF16),
            pltpu.VMEM((2 * units, half), BF16),
        ],
        24,
        after,
    )


def late_kernel(n_tp, proj_ref, h_ref, out_ref, *refs):
    branch_refs = refs[:n_tp]
    keep_ref, send_ref, branch_full = refs[n_tp:]
    part = branch_refs[0].shape[0]
    half = keep_ref.shape[1]
    wide = proj_ref.shape[0]
    tp = lax.axis_index("tp")
    core = lax.axis_index("seq") % 2
    for k in range(n_tp):
        at = pl.ds(pl.multiple_of(slot(tp ^ hop(k, n_tp), n_tp) * part, part), part)
        branch_full[at, :] = branch_refs[k][...]
    for ref, side in ((send_ref, 1 - core), (keep_ref, core)):
        columns = pl.ds(pl.multiple_of(side * half, half), half)
        ref[:wide, :] = mm(proj_ref[...], h_ref[:, columns], NN).astype(ref.dtype)
        ref[wide:, :] = mm(out_ref[...], branch_full[:, columns], NN).astype(ref.dtype)


def late_grads(proj_grad, h_one, out_b, branches, after):
    rows, model = h_one.shape
    wide = proj_grad.shape[0] + out_b.shape[0]
    return call(
        "late_grads",
        functools.partial(late_kernel, len(branches)),
        [(proj_grad, "v"), (h_one, "v"), (out_b, "v"), (branches[0], "v")]
        + kinds(branches[1:], "v"),
        [((wide, model // 2), F32, "v"), ((wide, model // 2), BF16, "v")],
        [pltpu.VMEM((rows, model), BF16)],
        16,
        after,
    )


def spread_kernel(count, *refs):
    given, outs, held = refs[: -count - 1], refs[-count - 1 : -1], refs[-1]
    piece = outs[0].shape[0]
    chip = lax.axis_index("seq") // 2
    at = 0
    for keep_ref, back_ref in zip(given[::2], given[1::2]):
        rows = keep_ref.shape[0]
        held[at : at + rows, :] = keep_ref[...] + back_ref[...].astype(F32)
        at += rows
    if at < held.shape[0]:
        held[at:, :] = jnp.zeros((held.shape[0] - at, held.shape[1]), F32)
    for k in range(count):
        at = pl.ds(pl.multiple_of((chip ^ k) * piece, piece), piece)
        outs[k][...] = held[at, :].astype(outs[k].dtype)


def spread(count, *pairs):
    half = pairs[0][0].shape[1]
    rows = sum(keep.shape[0] for keep, unused in pairs)
    piece = -(-rows // (8 * count)) * 8
    return call(
        "spread",
        functools.partial(spread_kernel, count),
        [(array, "v") for pair in pairs for array in pair],
        [((piece, half), F32, "v")] + [((piece, half), BF16, "v")] * (count - 1),
        [pltpu.VMEM((count * piece, half), F32)],
    )


def piece_kernel(count, gain_ref, *refs):
    out_ref = refs[count]
    half = out_ref.shape[1]
    total = refs[0][...]
    for ref in refs[1:count]:
        total = total + ref[...].astype(F32)
    line = lax.broadcasted_iota(jnp.int32, (16, half), 0)
    gains = jnp.zeros((16, half), F32)
    for at in range(4):
        row = gain_ref[at // 2 : at // 2 + 1, at % 2 * half : (at % 2 + 1) * half]
        gains = jnp.where(line == at, row, gains)
    out_ref[...] = jnp.concatenate([total, gains], axis=0).astype(BF16)


def sum_piece(gains, pieces, after=()):
    piece, half = pieces[0].shape
    (out,) = call(
        "sum_piece",
        functools.partial(piece_kernel, len(pieces)),
        [(gains, "v")] + kinds(pieces, "v"),
        [((piece + 16, half), BF16, "v")],
        (),
        16,
        after,
    )
    return out


def collect_kernel(count, *refs):
    out_ref, held = refs[count:]
    piece = refs[0].shape[0] - 16
    wide = count * piece
    chip = lax.axis_index("seq") // 2
    gains = jnp.zeros((16, out_ref.shape[1]), F32)
    for k in range(count):
        at = pl.ds(pl.multiple_of((chip ^ hop(k, count)) * piece, piece), piece)
        whole = refs[k][...].astype(F32)
        held[at, :] = whole[:piece]
        gains = gains + whole[piece:]
    held[wide:, :] = gains
    out_ref[...] = held[...].astype(BF16)


def collect(pieces, after=()):
    piece, half = pieces[0].shape
    wide = (piece - 16) * len(pieces) + 16
    (out,) = call(
        "collect",
        functools.partial(collect_kernel, len(pieces)),
        kinds(pieces, "v"),
        [((wide, half), BF16, "v")],
        [pltpu.VMEM((wide, half), F32)],
        16,
        after,
    )
    return out


def finish_kernel(sizes, need, give, own_ref, pair_ref, *refs):
    out_refs, gain_refs = refs[: len(sizes)], refs[len(sizes) :]
    half = own_ref.shape[1]
    core = lax.axis_index("seq") % 2
    at = 0
    for n, (out_ref, size) in enumerate(zip(out_refs, sizes)):
        for ref, side in ((own_ref, core), (pair_ref, 1 - core)):
            columns = pl.ds(pl.multiple_of(side * half, half), half)
            out_ref[:, columns] = ref[at : at + size, :].astype(F32)
        give(n)
        at += size
    first = own_ref.shape[0] - 16
    gains = own_ref[first:, :].astype(F32) + pair_ref[first:, :].astype(F32)
    for at, ref in zip((0, 2), gain_refs):
        ref[pl.ds(0, half)] = gains[at]
        ref[pl.ds(half, half)] = gains[at + 1]


def finish(own, pair, sizes):
    model = 2 * own.shape[1]
    return call(
        "finish",
        functools.partial(finish_kernel, sizes),
        [(own, "v"), (pair, "v")],
        [((size, model), F32, "h") for size in sizes] + [((model,), F32, "h")] * 2,
        (),
        24,
        lazy=True,
    )


def down_kernel(mixed_ref, w_ref, middle_ref, keep_ref, *refs):
    send_refs, total = refs[:-1], refs[-1]
    part = keep_ref.shape[0]
    tp = lax.axis_index("tp")
    total[...] = mm(mixed_ref[...], w_ref[...], TN)
    own = pl.ds(pl.multiple_of(tp // 2 * part, part), part)
    keep_ref[...] = total[own, :] + middle_ref[own, :]
    for n, ref in enumerate(send_refs):
        at = pl.ds(pl.multiple_of((tp ^ (2 * n + 2)) // 2 * part, part), part)
        ref[...] = total[at, :].astype(ref.dtype)


def down(n_tp, mixed, w_both, middle, after):
    rows, model = middle.shape
    part = 2 * rows // n_tp
    return call(
        "down",
        down_kernel,
        kinds((mixed, w_both, middle), "v"),
        [((part, model), F32, "v")] + [((part, model), BF16, "v")] * (n_tp // 2 - 1),
        [pltpu.VMEM((rows, model), F32)],
        16,
        after,
    )


def total_kernel(count, *refs):
    total = refs[0][...]
    for ref in refs[1:count]:
        total = total + ref[...].astype(F32)
    refs[count][...] = total.astype(refs[count].dtype)


def total_of(parts, dtype=BF16, kind="v", after=(), flops=0):
    (out,) = call(
        "total_of",
        functools.partial(total_kernel, len(parts)),
        [(parts[0], kind)] + kinds(parts[1:], "v"),
        [(parts[0].shape, dtype, "v")],
        (),
        16,
        after,
        flops=flops,
    )
    return out


def body(
    n_seq,
    n_tp,
    tokens,
    gain_one,
    w_qkv,
    w_out,
    gain_two,
    w_in,
    w_down,
    cotangent,
    doc_lengths,
    roster,
):
    rows, model = tokens.shape
    width = w_qkv.shape[2]
    units = w_in.shape[2]
    count = n_seq // 2
    qkv_t = w_qkv.transpose(1, 2, 0).reshape(3 * width, model)
    in_t = w_in.transpose(1, 2, 0).reshape(2 * units, model)
    over_tp = lambda x, k: swap(x, "tp", k, n_tp)
    over_chips = lambda x, k: swap(x, "seq", 2 * k, n_seq)
    over_cores = lambda x: swap(x, "seq", 1, n_seq)
    everywhere = lambda xs: [xs[0]] + came(n_tp, lambda k: over_tp(xs[k], k))

    def by_steps(part):
        parts = {0: part}
        step = n_tp // 2
        while step:
            parts.update({k ^ step: over_tp(x, step) for k, x in parts.items()})
            step //= 2
        return [parts[hop(n, n_tp)] for n in range(n_tp)]

    docs = (doc_lengths, roster)

    queries, kv, h_one, cos_table, sin_table = project(*docs, tokens, gain_one, qkv_t)
    blocks = [kv] + [over_chips(kv, j) for j in range(1, count)]
    q_pair = over_cores(queries)
    picked, w_half = pick(in_t, w_down, w_out)
    got = [over_tp(picked, 1)] + [over_tp(w_half, k) for k in range(2, n_tp)]

    split = (count + 1) // 2
    (state,) = attention_forward(0, False, *docs, queries, q_pair, blocks[:split])
    state_own, state_pair = attention_forward(
        split, True, *docs, queries, q_pair, blocks[split:], state
    )
    out_b, totals, out_mine, out_other = join(state_own, over_cores(state_pair))
    outs = everywhere([out_other if k % 2 else out_mine for k in range(n_tp)])
    out_pair = over_cores(out_b)
    totals_pair = over_cores(totals)

    got = pile(got, [(state_pair, "v")])
    staged = stage(n_tp, tokens, cotangent, in_t, w_down, w_out, got, over_cores(got))
    middle, middle_part, h_two, mixed, gate_grad, gain_two_part, own, *others = feed(
        gain_two, staged, outs
    )
    arrived = [own] + [over_tp(others[n], 2 * n + 2) for n in range(n_tp // 2 - 1)]
    own, *others = down(n_tp, mixed, staged[4], middle, ())
    middle_grad, branch_grad, *pieces = branch(
        n_tp, middle_part, cotangent, gain_two, staged[2], arrived, [(own, "v")]
    )
    early, early_send = early_grads(
        mixed, gate_grad, cotangent, h_two, in_t, w_down, over_tp(h_two, 1), [(branch_grad, "v")]
    )
    early_back = over_cores(early_send)
    out_grad = lay_turned(everywhere(pieces), ())
    grad_pair = over_cores(out_grad)
    branches = by_steps(branch_grad)

    held = (queries, q_pair, out_grad, grad_pair, out_b, out_pair, totals, totals_pair)
    *terms, dq = attention_backward(1, False, *docs, held, blocks[1:], None)
    total = total_of(
        [own] + [over_tp(others[n], 2 * n + 2) for n in range(n_tp // 2 - 1)],
        BF16,
        "v",
        [(dq, "v")],
    )
    totals_all = by_steps(total)

    dkv, dq_own, dq_pair = attention_backward(
        0, True, *docs, held, blocks[:1], dq, ()
    )
    dkvs = [dkv] + [over_chips(terms[j - 1], j) for j in range(1, count)]

    proj_grad, *parts = unproject(
        n_tp,
        tokens,
        qkv_t,
        cos_table,
        sin_table,
        gain_two_part,
        dq_own,
        over_cores(dq_pair),
        dkvs,
        [(total, "v")],
    )
    layer_out = stack_parts(totals_all)
    keep, send = late_grads(proj_grad, h_one, out_b, branches, [(totals_all[n_tp // 2], "v")])
    own, *others = spread(count, (keep, over_cores(send)), (early, early_back))
    summed = total_of(everywhere(parts), F32, flops=2_000_000_000)
    chip_sum = total_of(
        [own] + came(count, lambda k: over_chips(others[k - 1], k)), F32, "v", ()
    )
    input_part, gains = input_side(tokens, gain_one, middle_grad, summed, [(own, "v")])
    inputs_all = everywhere([input_part] * n_tp)
    piece = sum_piece(gains, [chip_sum], ())
    input_grad = stack_parts(inputs_all, (), 3_000_000_000)
    collected = collect(
        [piece] + came(count, lambda k: over_chips(piece, k)), [(input_grad, "h"), (layer_out, "h")]
    )
    grad_qkv, grad_out, grad_down, grad_in, grad_one, grad_two = finish(
        collected, over_cores(collected), (3 * width, width, units, 2 * units)
    )

    back = lambda x, n: x.reshape(-1, n, model).transpose(2, 0, 1)
    return (
        layer_out,
        input_grad,
        grad_one,
        back(grad_qkv, width),
        grad_out,
        grad_two,
        back(grad_in, units),
        grad_down,
    )


def solution(mesh):
    placed = (
        P("seq", None),
        P(),
        P(None, None, "tp"),
        P("tp", None),
        P(),
        P(None, None, "tp"),
        P("tp", None),
        P("seq", None),
        P(),
        P(),
    )
    return jax.shard_map(
        functools.partial(body, mesh.shape["seq"], mesh.shape["tp"]),
        mesh=mesh,
        in_specs=placed,
        out_specs=(
            P("seq", None),
            P("seq", None),
            P(),
            P(None, None, "tp"),
            P("tp", None),
            P(),
            P(None, None, "tp"),
            P("tp", None),
        ),
        check_vma=False,
    )
```

```python
import functools
import math

import jax
import jax.numpy as jnp
import numpy as np
from jax import lax
from jax.experimental import pallas as pl
from jax.experimental.pallas import tpu as pltpu
from jax.sharding import PartitionSpec as P

HDIM = 64
HALF = HDIM // 2
EPSILON = 1e-05
ROPE_THETA = 160000.0
MASKED = -1e30
AUG = 80
STRIP = 64
F32 = jnp.float32
BF16 = jnp.bfloat16
HBM = pl.BlockSpec(memory_space=pltpu.HBM)
VMEM = pl.BlockSpec(memory_space=pltpu.VMEM)

NN = (((1,), (0,)), ((), ()))
NT = (((1,), (1,)), ((), ()))
TN = (((0,), (0,)), ((), ()))


def params(mib):
    return pltpu.CompilerParams(vmem_limit_bytes=mib * 2**20)


def slot(tp, n_tp):
    return tp % 2 * (n_tp // 2) + tp // 2


def hop(n, count):
    return (count - n) % count


def came(count, send):
    return [send(hop(n, count)) for n in range(1, count)]


def mm(a, b, dims):
    return lax.dot_general(a, b, dims, preferred_element_type=F32)


def shaped(shape, dtype):
    return jax.ShapeDtypeStruct(shape, dtype)


def kinds(arrays, kind):
    return [(array, kind) for array in arrays]


def pin(array, kind):
    return array if kind in ("v", "free") else pltpu.with_memory_space_constraint(array, pltpu.HBM)


def call(name, kernel, ins, outs, scratch=(), mib=16, after=(), lazy=False, flops=0, alias=None):
    fetched = [i for i, given in enumerate(ins) if given[1] not in ("v", "raw", "free")]
    left = [i for i, out in enumerate(outs) if out[2] == "h"]

    def held(array, kind):
        rows = array.shape[0] if kind == "h" else kind
        return pltpu.VMEM((rows,) + array.shape[1:], array.dtype)

    def run(*refs):
        in_refs = list(refs[: len(ins)])
        at = len(ins) + len(after)
        out_refs = list(refs[at : at + len(outs)])
        at += len(outs)
        own = refs[at : at + len(scratch)]
        at += len(scratch)
        buffers = refs[at : at + len(fetched) + len(left)]
        sems = refs[-1]
        copies = []
        for n, i in enumerate(fetched):
            source = in_refs[i]
            if ins[i][1] != "h":
                rows = ins[i][1]
                n_tp = ins[i][0].shape[0] // rows
                at = pl.multiple_of(slot(lax.axis_index("tp"), n_tp) * rows, rows)
                source = source.at[pl.ds(at, rows)]
            copies.append(pltpu.make_async_copy(source, buffers[n], sems.at[n]))
            in_refs[i] = buffers[n]
        for copy in copies:
            copy.start()
        coming = dict(zip(fetched, copies))
        going = {}
        for n, i in enumerate(left):
            spot = len(fetched) + n
            going[i] = pltpu.make_async_copy(buffers[spot], out_refs[i], sems.at[spot])
            out_refs[i] = buffers[spot]
        gone = []

        def need(*which):
            for i in which:
                if i in coming:
                    coming.pop(i).wait()

        def give(*which):
            for i in which:
                if i in going:
                    gone.append(going.pop(i))
                    gone[-1].start()

        if lazy:
            kernel(need, give, *in_refs, *out_refs, *own)
        else:
            need(*fetched)
            kernel(*in_refs, *out_refs, *own)
        need(*fetched)
        give(*left)
        for copy in gone:
            copy.wait()

    spec = lambda kind: VMEM if kind == "v" else HBM
    count = len(fetched) + len(left)
    return pl.pallas_call(
        run,
        out_shape=tuple(
            shaped(shape, dtype) if kind == "v" else pltpu.HBM(shape, dtype)
            for shape, dtype, kind in outs
        ),
        in_specs=[spec(kind) for unused, kind in ins] + [spec(kind) for unused, kind in after],
        out_specs=tuple(spec(kind) for unused, unused, kind in outs),
        scratch_shapes=list(scratch)
        + [held(*ins[i]) for i in fetched]
        + [pltpu.VMEM(outs[i][0], outs[i][1]) for i in left]
        + [pltpu.SemaphoreType.DMA((max(count, 1),))],
        name=name,
        input_output_aliases=alias or {},
        cost_estimate=pl.CostEstimate(flops=flops, bytes_accessed=0, transcendentals=0)
        if flops
        else None,
        compiler_params=params(mib),
    )(*[pin(*given) for given in ins], *[pin(*given) for given in after])


def swap(x, axis, hop, count):
    return lax.ppermute(x, axis, [(i, i ^ hop) for i in range(count)])


def doc_scratch(doc_lengths, roster):
    return [pltpu.SMEM(doc_lengths.shape, jnp.int32), pltpu.SMEM(roster.shape, jnp.int32)]


def fetch_docs(len_any, roster_any, len_ref, roster_ref, len_sem, roster_sem):
    one = pltpu.make_async_copy(len_any, len_ref, len_sem)
    two = pltpu.make_async_copy(roster_any, roster_ref, roster_sem)
    one.start()
    two.start()
    one.wait()
    two.wait()


def doc_bounds(len_ref):
    ends, total = [], jnp.int32(0)
    for d in range(len_ref.shape[0]):
        total = total + len_ref[d]
        ends.append(total)
    return ends


def doc_of(ends, position):
    found = jnp.int32(0)
    for end in ends:
        found = found + (end <= position).astype(jnp.int32)
    return found


def meet(ends, base_a, base_b, rows):
    low = jnp.maximum(doc_of(ends, base_a), doc_of(ends, base_b))
    high = jnp.minimum(doc_of(ends, base_a + rows - 1), doc_of(ends, base_b + rows - 1))
    return low <= high


def doc_rows(ends, base, rows):
    spot = base + lax.broadcasted_iota(jnp.int32, (16, rows), 1)
    line = lax.broadcasted_iota(jnp.int32, (16, rows), 0)
    held = jnp.zeros((16, rows), F32)
    start = jnp.int32(0)
    for d, end in enumerate(ends):
        inside = (line == d) & (spot >= start) & (spot < end)
        held = jnp.where(inside, 1.0, held)
        start = end
    return held


def ban_rows(ends, base, rows):
    line = lax.broadcasted_iota(jnp.int32, (16, rows), 0)
    held = doc_rows(ends, base, rows)
    return jnp.where((held > 0.5) | (line >= len(ends)), 0.0, MASKED)


def key_row(block, seq_index):
    return seq_index ^ (2 * block)


def place_row(ends, base, rows):
    spot = base + lax.broadcasted_iota(jnp.int32, (1, rows), 1)
    start = jnp.zeros((1, rows), jnp.int32)
    for end in ends:
        start = jnp.where(spot >= end, end, start)
    return (spot - start).astype(F32)


def normed(values):
    centre = jnp.mean(values, axis=-1, keepdims=True)
    shifted = values - centre
    spread = jnp.mean(shifted * shifted, axis=-1, keepdims=True)
    scale = lax.rsqrt(spread + EPSILON)
    return shifted * scale, scale


def norm_back(unit, scale, grad, gain):
    u = grad * gain
    mean_u = jnp.mean(u, axis=-1, keepdims=True)
    mean_un = jnp.mean(u * unit, axis=-1, keepdims=True)
    return scale * (u - mean_u - unit * mean_un)


def project_kernel(
    width, need, give, len_any, roster_any, x_ref, w_ref, gain_ref, freq_ref, *refs
):
    q_out, kv_out, h_out, cos_out, sin_out = refs[:5]
    proj, len_ref, roster_ref, sems = refs[5:]
    rows = x_ref.shape[0]
    fetch_docs(len_any, roster_any, len_ref, roster_ref, sems.at[0], sems.at[1])
    need(5)
    ends = doc_bounds(len_ref)
    place = place_row(ends, roster_ref[lax.axis_index("seq")] * rows, rows)
    angles = place * freq_ref[...]
    cos_table = jnp.cos(angles)
    sin_table = jnp.sin(angles)
    cos_out[...] = cos_table
    sin_out[...] = sin_table
    give(3, 4)
    need(2, 4)
    gain = gain_ref[...].reshape(1, -1)

    def strip(i, carry):
        at = pl.ds(i * STRIP, STRIP)
        unit, unused = normed(x_ref[at, :].astype(F32))
        h_out[at, :] = (unit * gain).astype(BF16)
        return carry

    lax.fori_loop(0, rows // STRIP, strip, 0)
    give(2)
    need(3)
    proj[...] = mm(w_ref[...], h_out[...], NT)
    for at in range(0, 2 * width, HDIM):
        low = proj[at : at + HALF, :]
        high = proj[at + HALF : at + HDIM, :]
        turned_low = (low * cos_out[...] - high * sin_out[...]).astype(BF16)
        turned_high = (high * cos_out[...] + low * sin_out[...]).astype(BF16)
        if at < width:
            q_out[at : at + HALF, :] = (turned_low.astype(F32) * HDIM**-0.5).astype(BF16)
            q_out[at + HALF : at + HDIM, :] = (turned_high.astype(F32) * HDIM**-0.5).astype(BF16)
        else:
            kv_out[at - width : at - width + HALF, :] = turned_low
            kv_out[at - width + HALF : at - width + HDIM, :] = turned_high
    kv_out[width:, :] = proj[2 * width :, :].astype(BF16)


def project(doc_lengths, roster, tokens, gain, qkv_t):
    rows, model = tokens.shape
    width = qkv_t.shape[0] // 3
    freq = (ROPE_THETA ** -(np.arange(HALF) * (2.0 / HDIM))).astype(np.float32)[:, None]
    return call(
        "project",
        functools.partial(project_kernel, width),
        kinds((doc_lengths, roster), "raw") + kinds((tokens, qkv_t, gain, jnp.asarray(freq)), "h"),
        [
            ((width, rows), BF16, "v"),
            ((2 * width, rows), BF16, "v"),
            ((rows, model), BF16, "v"),
            ((HALF, rows), F32, "v"),
            ((HALF, rows), F32, "v"),
        ],
        [pltpu.VMEM((3 * width, rows), F32)]
        + doc_scratch(doc_lengths, roster)
        + [pltpu.SemaphoreType.DMA((2,))],
        lazy=True,
    )


def forward_kernel(first, count, heads, last, len_any, roster_any, q_own, q_pair, *refs):
    kv_refs = refs[:count]
    refs = refs[count:]
    if first:
        state_in, refs = refs[0], refs[1:]
    outs = refs[: 2 if last else 1]
    kv, q_aug, state, len_ref, roster_ref, sems = refs[len(outs) :]
    rows = q_own.shape[1]
    width = heads * HDIM
    me = lax.axis_index("seq")
    copies = [pltpu.make_async_copy(kv_refs[j], kv.at[j], sems.at[j]) for j in range(count)]
    for copy in copies:
        copy.start()
    fetch_docs(len_any, roster_any, len_ref, roster_ref, sems.at[count], sems.at[count + 1])
    ends = doc_bounds(len_ref)
    bases = (roster_ref[me] * rows, roster_ref[me ^ 1] * rows)
    for g, q_ref in enumerate((q_own, q_pair)):
        mark = doc_rows(ends, bases[g], rows).astype(BF16)
        for h in range(heads):
            q_aug[g * heads + h, :HDIM, :] = q_ref[h * HDIM : (h + 1) * HDIM, :]
            q_aug[g * heads + h, HDIM:, :] = mark
    if first:
        state[...] = state_in[...]
    else:
        line = lax.broadcasted_iota(jnp.int32, (2 * heads, AUG, rows), 1)
        state[...] = jnp.where(line >= 72, MASKED, 0.0)
    for copy in copies:
        copy.wait()

    top = lax.broadcasted_iota(jnp.int32, (16, rows), 0) == 0
    ones = jnp.where(top, 1.0, 0.0).astype(BF16)

    def block(j, carry):
        key_base = roster_ref[key_row(j + first, me)] * rows
        ban = ban_rows(ends, key_base, rows).astype(BF16)
        for g in range(2):

            @pl.when(meet(ends, bases[g], key_base, rows))
            def _():
                for h in range(heads):
                    at = g * heads + h
                    keys = jnp.concatenate([kv[j, h * HDIM : (h + 1) * HDIM, :], ban], axis=0)
                    vals = jnp.concatenate(
                        [kv[j, width + h * HDIM : width + (h + 1) * HDIM, :], ones], axis=0
                    )
                    scores = mm(keys, q_aug[at], TN)
                    old = state[at, 72:73, :]
                    new = jnp.maximum(old, jnp.max(scores, axis=0, keepdims=True))
                    probs = jnp.exp(scores - new).astype(BF16)
                    part = mm(vals, probs, NN)
                    fade = jnp.exp(old - new)
                    state[at, :72, :] = state[at, :72, :] * fade + part[:72]
                    state[at, 72:, :] = jnp.broadcast_to(new, (8, rows))

        return carry

    lax.fori_loop(0, count, block, 0)
    if last:
        outs[0][...] = state[:heads]
        outs[1][...] = state[heads:]
    else:
        outs[0][...] = state[...]


def attention_forward(first, last, doc_lengths, roster, q_own, q_pair, blocks, state=None, after=()):
    width, rows = q_own.shape
    heads = width // HDIM
    count = len(blocks)
    half = ((heads, AUG, rows), F32, "v")
    whole = ((2 * heads, AUG, rows), F32, "v")
    given = [] if state is None else [(state, "v")]
    return call(
        "attention_forward",
        functools.partial(forward_kernel, first, count, heads, last),
        [(doc_lengths, "raw"), (roster, "raw"), (q_own, "v"), (q_pair, "v")]
        + kinds(blocks, "free")
        + given,
        [half, half] if last else [whole],
        [
            pltpu.VMEM((count, 2 * width, rows), BF16),
            pltpu.VMEM((2 * heads, AUG, rows), BF16),
            pltpu.VMEM((2 * heads, AUG, rows), F32),
        ]
        + doc_scratch(doc_lengths, roster)
        + [pltpu.SemaphoreType.DMA((count + 2,))],
        16 if count < 8 else 40,
        after,
    )


def backward_kernel(first, count, heads, more, last, len_any, roster_any, *refs):
    q_own, q_pair, g_own, g_pair, o_own, o_pair, t_own, t_pair = refs[:8]
    kv_refs, refs = refs[8 : 8 + count], refs[8 + count :]
    if more:
        dq_in, refs = refs[0], refs[1:]
    outs, refs = refs[:count], refs[count:]
    dq_outs, refs = (refs[:2], refs[2:]) if last else (refs[:1], refs[1:])
    kv, q_aug, delta, dq, dkv, len_ref, roster_ref, sems = refs
    rows = q_own.shape[1]
    width = heads * HDIM
    me = lax.axis_index("seq")
    copies = [pltpu.make_async_copy(kv_refs[j], kv.at[j], sems.at[j]) for j in range(count)]
    for copy in copies:
        copy.start()
    fetch_docs(len_any, roster_any, len_ref, roster_ref, sems.at[count], sems.at[count + 1])
    ends = doc_bounds(len_ref)
    bases = (roster_ref[me] * rows, roster_ref[me ^ 1] * rows)
    for g, (q_ref, g_ref, o_ref) in enumerate(((q_own, g_own, o_own), (q_pair, g_pair, o_pair))):
        mark = doc_rows(ends, bases[g], rows).astype(BF16)
        for h in range(heads):
            part = slice(h * HDIM, (h + 1) * HDIM)
            q_aug[g * heads + h, :HDIM, :] = q_ref[part, :]
            q_aug[g * heads + h, HDIM:, :] = mark
            product = g_ref[part, :].astype(F32) * o_ref[part, :].astype(F32)
            delta[g * heads + h] = jnp.broadcast_to(
                jnp.sum(product, axis=0, keepdims=True), (8, rows)
            )
    if more:
        dq[...] = dq_in[...]
    else:
        dq[...] = jnp.zeros_like(dq)
    for copy in copies:
        copy.wait()

    def block(j, carry):
        key_base = roster_ref[key_row(j + first, me)] * rows
        ban = ban_rows(ends, key_base, rows).astype(BF16)
        dkv[j] = jnp.zeros((2 * width, rows), F32)
        for g, (g_ref, t_ref) in enumerate(((g_own, t_own), (g_pair, t_pair))):

            @pl.when(meet(ends, bases[g], key_base, rows))
            def _():
                for h in range(heads):
                    at = g * heads + h
                    part = slice(h * HDIM, (h + 1) * HDIM)
                    late = slice(width + h * HDIM, width + (h + 1) * HDIM)
                    keys = kv[j, part, :]
                    scores = mm(jnp.concatenate([keys, ban], axis=0), q_aug[at], TN)
                    probs = jnp.exp(scores - t_ref[h, 0:1, :])
                    prob_grads = mm(kv[j, late, :], g_ref[part, :], TN)
                    score_grad = (probs * (prob_grads - delta[at, 0:1, :])).astype(BF16)
                    dkv[j, late, :] += mm(g_ref[part, :], probs.astype(BF16), NT)
                    dkv[j, part, :] += mm(q_aug[at, :HDIM, :], score_grad, NT)
                    dq[at] += mm(keys, score_grad, NN)

        return carry

    lax.fori_loop(0, count, block, 0)
    for j in range(count):
        outs[j][...] = dkv[j].astype(outs[j].dtype)
    if last:
        for h in range(heads):
            part = slice(h * HDIM, (h + 1) * HDIM)
            dq_outs[0][part, :] = dq[h] * HDIM**-0.5
            dq_outs[1][part, :] = (dq[heads + h] * HDIM**-0.5).astype(BF16)
    else:
        dq_outs[0][...] = dq[...]


def attention_backward(first, last, doc_lengths, roster, held, blocks, dq=None, after=()):
    width, rows = held[0].shape
    heads = width // HDIM
    count = len(blocks)
    given = [] if dq is None else [(dq, "v")]
    if last:
        queries = [((width, rows), F32, "v"), ((width, rows), BF16, "v")]
    else:
        queries = [((2 * heads, HDIM, rows), F32, "v")]
    return call(
        "attention_backward",
        functools.partial(backward_kernel, first, count, heads, bool(given), last),
        kinds((doc_lengths, roster), "raw") + kinds(held, "v") + kinds(blocks, "free") + given,
        [((2 * width, rows), BF16 if first else F32, "v")] * count + queries,
        [
            pltpu.VMEM((count, 2 * width, rows), BF16),
            pltpu.VMEM((2 * heads, AUG, rows), BF16),
            pltpu.VMEM((2 * heads, 8, rows), F32),
            pltpu.VMEM((2 * heads, HDIM, rows), F32),
            pltpu.VMEM((count, 2 * width, rows), F32),
        ]
        + doc_scratch(doc_lengths, roster)
        + [pltpu.SemaphoreType.DMA((count + 2,))],
        16 if count < 8 else 40,
        after,
        flops=0 if last else 0,
    )


def join_kernel(heads, own_ref, back_ref, out_ref, total_ref, mine_ref, other_ref):
    rows = own_ref.shape[2]
    for h in range(heads):
        top_own = own_ref[h, 72:73, :]
        top_back = back_ref[h, 72:73, :]
        top = jnp.maximum(top_own, top_back)
        fade_own = jnp.exp(top_own - top)
        fade_back = jnp.exp(top_back - top)
        total = own_ref[h, 64:65, :] * fade_own + back_ref[h, 64:65, :] * fade_back
        share_own = fade_own / total
        share_back = fade_back / total
        value = own_ref[h, :HDIM, :] * share_own + back_ref[h, :HDIM, :] * share_back
        out_ref[h * HDIM : (h + 1) * HDIM, :] = value.astype(BF16)
        total_ref[h] = jnp.broadcast_to(top + jnp.log(total), (8, rows))
    half = rows // 2
    for bit in range(2):

        @pl.when(lax.axis_index("tp") % 2 == bit)
        def _():
            mine_ref[...] = out_ref[:, bit * half : (bit + 1) * half]
            other_ref[...] = out_ref[:, (1 - bit) * half : (2 - bit) * half]


def join(own, back):
    heads, unused, rows = own.shape
    return call(
        "join",
        functools.partial(join_kernel, heads),
        [(own, "v"), (back, "v")],
        [
            ((heads * HDIM, rows), BF16, "v"),
            ((heads, 8, rows), F32, "v"),
            ((heads * HDIM, rows // 2), BF16, "v"),
            ((heads * HDIM, rows // 2), BF16, "v"),
        ],
    )


def pick_kernel(in_any, down_any, w_any, all_ref, w_ref, sems):
    core = lax.axis_index("seq") % 2
    at = 0
    copies = []
    for source in (in_any, down_any, w_any):
        rows = source.shape[0] // 2
        mine = pl.ds(pl.multiple_of(core * rows, rows), rows)
        copies.append((source.at[mine], all_ref.at[pl.ds(at, rows)]))
        at += rows
    copies.append((w_any.at[mine], w_ref))
    copies = [pltpu.make_async_copy(*move, sems.at[n]) for n, move in enumerate(copies)]
    for copy in copies:
        copy.start()
    for copy in copies:
        copy.wait()


def pick(in_t, w_down, w_out):
    rows = (in_t.shape[0] + w_down.shape[0] + w_out.shape[0]) // 2
    model = w_out.shape[1]
    return call(
        "pick",
        pick_kernel,
        kinds((in_t, w_down, w_out), "raw"),
        [((rows, model), BF16, "v"), ((w_out.shape[0] // 2, model), BF16, "v")],
        [pltpu.SemaphoreType.DMA((4,))],
    )


def pile_kernel(*refs):
    out_ref = refs[-1]
    at = 0
    for ref in refs[:-1]:
        out_ref[at : at + ref.shape[0], :] = ref[...]
        at += ref.shape[0]


def pile(values, after):
    rows = sum(value.shape[0] for value in values)
    (out,) = call(
        "pile",
        pile_kernel,
        kinds(values, "v"),
        [((rows, values[0].shape[1]), BF16, "v")],
        (),
        16,
        after,
    )
    return out


def stage_kernel(x_any, cot_any, in_any, down_any, w_any, got_ref, rest_ref, *refs):
    x_ref, cot_ref, w_ref, in_ref, down_ref, sems = refs
    half = x_ref.shape[0]
    core = lax.axis_index("seq") % 2
    tp = lax.axis_index("tp")
    n_tp = w_ref.shape[0] // w_any.shape[0]
    mine = pl.ds(pl.multiple_of(tp % 2 * half, half), half)
    width = w_any.shape[0]
    rows = width // 2
    own = pl.ds(pl.multiple_of(tp * width, width), width)
    moves = [(w_any, w_ref.at[own]), (x_any.at[mine], x_ref), (cot_any.at[mine], cot_ref)]
    sides = ((got_ref, core), (rest_ref, 1 - core))
    first = got_ref.shape[0] - (n_tp - 1) * rows
    for k in range(1, n_tp):
        for source, side in sides:
            spot = pl.multiple_of((tp ^ k) * width + side * rows, rows)
            piece = source.at[pl.ds(first + (k - 1) * rows, rows)]
            moves.append((piece, w_ref.at[pl.ds(spot, rows)]))
    at = 0
    for own, ref in ((in_any, in_ref), (down_any, down_ref)):
        rows = own.shape[0] // 2
        moves.append((own, ref.at[pl.ds(0, 2 * rows)]))
        for source, side in sides:
            spot = pl.multiple_of(2 * rows + side * rows, rows)
            moves.append((source.at[pl.ds(at, rows)], ref.at[pl.ds(spot, rows)]))
        at += rows
    copies = [pltpu.make_async_copy(*move, sems.at[n]) for n, move in enumerate(moves)]
    for copy in copies:
        copy.start()
    for copy in copies:
        copy.wait()


def stage(n_tp, tokens, cotangent, in_t, w_down, w_out, got, rest):
    rows, model = tokens.shape
    return call(
        "stage",
        stage_kernel,
        kinds((tokens, cotangent, in_t, w_down, w_out), "raw") + kinds((got, rest), "v"),
        [
            ((rows // 2, model), BF16, "v"),
            ((rows // 2, model), BF16, "v"),
            ((n_tp * w_out.shape[0], model), BF16, "v"),
            ((2 * in_t.shape[0], model), BF16, "v"),
            ((2 * w_down.shape[0], model), BF16, "v"),
        ],
        [pltpu.SemaphoreType.DMA((7 + 2 * n_tp,))],
    )


def gated(units, first, gate_up, mixed_grad, mixed_out, gate_out):
    rows = math.gcd(units, 96)

    def wave(i, carry):
        spot = pl.ds(first + i * rows, rows)
        at = pl.ds(2 * first + i * rows, rows)
        late = pl.ds(2 * first + units + i * rows, rows)
        gate = gate_up[at, :]
        up = gate_up[late, :]
        back = mixed_grad[spot, :]
        bell = 0.5 * (1.0 + lax.erf(gate * (2.0**-0.5)))
        active = gate * bell
        slope = bell + gate * jnp.exp(-0.5 * gate * gate) * ((2.0 * jnp.pi) ** -0.5)
        mixed_out[spot, :] = (active * up).astype(BF16)
        gate_out[at, :] = (back * up * slope).astype(BF16)
        gate_out[late, :] = (back * active).astype(BF16)
        return carry

    lax.fori_loop(0, units // rows, wave, 0)


def feed_kernel(n_tp, need, give, x_ref, cot_ref, w_ref, in_ref, down_ref, gain_ref, *refs):
    out_refs = refs[:n_tp]
    middle_out, part_out, h_out, mixed_out, gate_out, gain_out = refs[n_tp : n_tp + 6]
    keep_ref, *send_refs = refs[n_tp + 6 : n_tp + 6 + n_tp // 2]
    outs, unit, gate_up, mixed_grad, grad = refs[n_tp + 6 + n_tp // 2 :]
    rows = x_ref.shape[0]
    part = keep_ref.shape[0]
    units = down_ref.shape[0] // 2
    width = out_refs[0].shape[0]
    tp = lax.axis_index("tp")
    for k in range(n_tp):
        at = pl.ds(pl.multiple_of((tp ^ hop(k, n_tp)) * width, width), width)
        outs[at, :] = out_refs[k][...]
    mixed_grad[...] = mm(down_ref[...], cot_ref[...], NT)
    middle_out[...] = mm(outs[...], w_ref[...], TN)
    need(5)
    gain = gain_ref[...].reshape(1, -1)

    def strip(i, carry):
        at = pl.ds(i * 32, 32)
        middle = middle_out[at, :] + x_ref[at, :].astype(F32)
        middle_out[at, :] = middle
        held, unused = normed(middle)
        unit[at, :] = held
        h_out[at, :] = (held * gain).astype(BF16)
        return carry

    lax.fori_loop(0, rows // 32, strip, 0)
    give(0, 2)
    gate_up[...] = mm(in_ref[...], h_out[...], NT)
    for first in (0, units):
        gated(units, first, gate_up, mixed_grad, mixed_out, gate_out)
    give(3, 4)
    grad[...] = mm(gate_out[...], in_ref[...], TN)
    for n, ref in enumerate((keep_ref, *send_refs)):
        at = pl.ds(pl.multiple_of((tp ^ (2 * n)) // 2 * part, part), part)
        ref[...] = grad[at, :].astype(ref.dtype)
        give(6 + n)
    own = pl.ds(pl.multiple_of(tp // 2 * part, part), part)
    part_out[...] = middle_out[own, :]
    give(1)

    def gains(i, carry):
        at = pl.ds(i * 32, 32)
        product = grad[at, :] * unit[at, :]
        return carry + jnp.sum(product.reshape(4, 8, -1), axis=0)

    gain_out[...] = lax.fori_loop(0, rows // 32, gains, jnp.zeros(gain_out.shape, F32))


def feed(gain, staged, outs):
    rows, model = staged[0].shape
    n_tp = len(outs)
    units = staged[4].shape[0]
    part = 2 * rows // n_tp
    return call(
        "feed",
        functools.partial(feed_kernel, n_tp),
        kinds(staged, "v") + [(gain, "h")] + kinds(outs, "v"),
        [
            ((rows, model), F32, "v"),
            ((part, model), F32, "v"),
            ((rows, model), BF16, "v"),
            ((units, rows), BF16, "v"),
            ((2 * units, rows), BF16, "v"),
            ((8, model), F32, "v"),
            ((part, model), F32, "v"),
        ]
        + [((part, model), BF16, "v")] * (n_tp // 2 - 1),
        [
            pltpu.VMEM((n_tp * outs[0].shape[0], rows), BF16),
            pltpu.VMEM((rows, model), F32),
            pltpu.VMEM((2 * units, rows), F32),
            pltpu.VMEM((units, rows), F32),
            pltpu.VMEM((rows, model), F32),
        ],
        24,
        lazy=True,
    )


def branch_kernel(n_tp, count, need, give, middle_ref, cot_ref, gain_ref, w_ref, *refs):
    arrived = refs[:count]
    grad_out, branch_out = refs[count : count + 2]
    piece_refs = refs[count + 2 :]
    width = piece_refs[0].shape[1]
    tp = lax.axis_index("tp")
    need(0, 1, 2, 4)
    total = arrived[0][...]
    for ref in arrived[1:]:
        total = total + ref[...].astype(F32)
    unit, scale = normed(middle_ref[...])
    gain = gain_ref[...].reshape(1, -1)
    value = cot_ref[...].astype(F32) + norm_back(unit, scale, total, gain)
    grad_out[...] = value
    branch_out[...] = value.astype(BF16)
    give(0, 1)
    need(3)
    for k in range(n_tp):
        at = pl.ds(pl.multiple_of((tp ^ k) * width, width), width)
        piece_refs[k][...] = mm(branch_out[...], w_ref[at, :], NT).astype(BF16)


def branch(n_tp, middle_part, cotangent, gain, w_full, arrived, after):
    part, model = arrived[0].shape
    width = w_full.shape[0] // n_tp
    return call(
        "branch",
        functools.partial(branch_kernel, n_tp, len(arrived)),
        [(middle_part, "v"), (cotangent, part)]
        + [(gain, "h"), (w_full, "v"), (arrived[0], "v")]
        + kinds(arrived[1:], "v"),
        [((part, model), F32, "v"), ((part, model), BF16, "v")]
        + [((part, width), BF16, "v")] * n_tp,
        (),
        16,
        after,
        True,
    )


def lay_kernel(n_tp, *refs):
    out_ref, held = refs[n_tp:]
    part = refs[0].shape[0]
    tp = lax.axis_index("tp")
    for k in range(n_tp):
        at = pl.ds(pl.multiple_of(slot(tp ^ hop(k, n_tp), n_tp) * part, part), part)
        held[at, :] = refs[k][...].astype(F32)
    out_ref[...] = held[...].T.astype(BF16)


def lay_turned(pieces, after):
    part, width = pieces[0].shape
    rows = part * len(pieces)
    (out,) = call(
        "lay_turned",
        functools.partial(lay_kernel, len(pieces)),
        kinds(pieces, "v"),
        [((width, rows), BF16, "v")],
        [pltpu.VMEM((rows, width), F32)],
        16,
        after,
    )
    return out


def stack_kernel(n_tp, *refs):
    out_ref = refs[n_tp]
    part = refs[0].shape[0]
    tp = lax.axis_index("tp")
    for k in range(n_tp):
        at = pl.ds(pl.multiple_of(slot(tp ^ hop(k, n_tp), n_tp) * part, part), part)
        out_ref[at, :] = refs[k][...]


def stack_parts(pieces, after=(), flops=0):
    part, model = pieces[0].shape
    (out,) = call(
        "stack_parts",
        functools.partial(stack_kernel, len(pieces)),
        kinds(pieces, "v"),
        [((part * len(pieces), model), pieces[0].dtype, "h")],
        (),
        16,
        after,
        flops=flops,
    )
    return out


def turn_back(out_ref, first, value, cos_table, sin_table):
    for at in range(0, value.shape[0], HDIM):
        low = value[at : at + HALF]
        high = value[at + HALF : at + HDIM]
        spot = first + at
        out_ref[spot : spot + HALF, :] = (low * cos_table + high * sin_table).astype(BF16)
        out_ref[spot + HALF : spot + HDIM, :] = (high * cos_table - low * sin_table).astype(BF16)


def unproject_kernel(
    count, n_tp, need, give, x_ref, w_ref, cos_ref, sin_ref, two_ref, dq_ref, dq_back, *refs
):
    dkv_refs = refs[:count]
    proj_out = refs[count]
    part_refs = refs[count + 1 : count + 1 + n_tp]
    grad, dkv = refs[count + 1 + n_tp :]
    rows, model = x_ref.shape
    part = rows // n_tp
    width = dq_ref.shape[0]
    tp = lax.axis_index("tp")
    need(2, 3)
    cos_table = cos_ref[...]
    sin_table = sin_ref[...]
    turn_back(proj_out, 0, dq_ref[...] + dq_back[...].astype(F32), cos_table, sin_table)
    total = dkv_refs[0][...]
    for ref in dkv_refs[1:]:
        total = total + ref[...].astype(F32)
    dkv[...] = total
    turn_back(proj_out, width, dkv[:width, :], cos_table, sin_table)
    proj_out[2 * width :, :] = dkv[width:, :].astype(BF16)
    need(1)
    grad[...] = mm(proj_out[...], w_ref[...], TN)
    need(0, 4)

    def gains(i, carry):
        at = pl.ds(i * STRIP, STRIP)
        unit, unused = normed(x_ref[at, :].astype(F32))
        product = grad[at, :] * unit
        return carry + jnp.sum(product.reshape(STRIP // 8, 8, -1), axis=0)

    gain = lax.fori_loop(0, rows // STRIP, gains, jnp.zeros((8, model), F32))
    line = lax.broadcasted_iota(jnp.int32, (16, model), 0)
    gain_two = jnp.sum(two_ref[...], axis=0, keepdims=True)
    gain = jnp.sum(gain, axis=0, keepdims=True)
    gain = jnp.where(line == 0, gain, jnp.where(line == 1, gain_two, 0.0))
    for k in range(n_tp):
        at = pl.ds(pl.multiple_of(slot(tp ^ k, n_tp) * part, part), part)
        part_refs[k][:part, :] = grad[at, :].astype(part_refs[k].dtype)
        part_refs[k][part:, :] = gain.astype(part_refs[k].dtype)


def unproject(n_tp, tokens, qkv_t, cos_table, sin_table, gain_two_part, dq, dq_back, dkvs, after):
    rows, model = tokens.shape
    part = rows // n_tp
    return call(
        "unproject",
        functools.partial(unproject_kernel, len(dkvs), n_tp),
        kinds((tokens, qkv_t, cos_table, sin_table, gain_two_part), "v")
        + kinds((dq, dq_back, *dkvs), "v"),
        [((qkv_t.shape[0], rows), BF16, "v"), ((part + 16, model), F32, "v")]
        + [((part + 16, model), BF16, "v")] * (n_tp - 1),
        [pltpu.VMEM((rows, model), F32), pltpu.VMEM(dkvs[0].shape, F32)],
        16,
        after,
        True,
    )


def input_kernel(x_ref, gain_ref, grad_ref, sum_ref, out_ref, gain_out):
    part, model = grad_ref.shape
    total = sum_ref[...]
    unit, scale = normed(x_ref[...].astype(F32))
    gain = gain_ref[...].reshape(1, -1)
    value = grad_ref[...] + norm_back(unit, scale, total[:part], gain)
    out_ref[...] = value.astype(BF16)
    gain_out[...] = total[part : part + 8]


def input_side(tokens, gain, middle_grad, summed, after):
    part, model = middle_grad.shape
    return call(
        "input_side",
        input_kernel,
        [(tokens, part), (gain, "h"), (middle_grad, "v"), (summed, "v")],
        [((part, model), BF16, "v"), ((8, model), F32, "v")],
        (),
        16,
        after,
    )


def early_kernel(mixed_ref, gate_ref, cot_ref, h_ref, in_ref, down_ref, h_pair, *refs):
    keep_ref, send_ref, gate_up, mixed_grad, mixed, gate = refs
    units = down_ref.shape[0]
    half = h_ref.shape[0]
    bit = lax.axis_index("tp") % 2
    mine = pl.ds(pl.multiple_of(bit * half, half), half)
    other = pl.ds(pl.multiple_of((1 - bit) * half, half), half)
    gate_up[...] = mm(in_ref[...], h_pair[...], NT)
    mixed_grad[...] = mm(down_ref[...], cot_ref[other, :], NT)
    gated(units, 0, gate_up, mixed_grad, mixed, gate)
    width = keep_ref.shape[1]
    core = lax.axis_index("seq") % 2
    for ref, side in ((send_ref, 1 - core), (keep_ref, core)):
        columns = pl.ds(pl.multiple_of(side * width, width), width)
        down = mm(mixed_ref[:units, :], cot_ref[mine, columns], NN)
        down = down + mm(mixed[...], cot_ref[other, columns], NN)
        ref[:units, :] = down.astype(ref.dtype)
        both = mm(gate_ref[: 2 * units, :], h_ref[:, columns], NN)
        both = both + mm(gate[...], h_pair[:, columns], NN)
        ref[units:, :] = both.astype(ref.dtype)


def early_grads(mixed, gate_grad, cotangent, h_two, in_t, w_down, h_pair, after):
    units, model = w_down.shape
    half = h_two.shape[0]
    return call(
        "early_grads",
        early_kernel,
        kinds((mixed, gate_grad, cotangent, h_two, in_t, w_down, h_pair), "v"),
        [((3 * units, model // 2), F32, "v"), ((3 * units, model // 2), BF16, "v")],
        [
            pltpu.VMEM((2 * units, half), F32),
            pltpu.VMEM((units, half), F32),
            pltpu.VMEM((units, half), BF16),
            pltpu.VMEM((2 * units, half), BF16),
        ],
        24,
        after,
    )


def late_kernel(n_tp, proj_ref, h_ref, out_ref, *refs):
    branch_refs = refs[:n_tp]
    keep_ref, send_ref, branch_full = refs[n_tp:]
    part = branch_refs[0].shape[0]
    half = keep_ref.shape[1]
    wide = proj_ref.shape[0]
    tp = lax.axis_index("tp")
    core = lax.axis_index("seq") % 2
    for k in range(n_tp):
        at = pl.ds(pl.multiple_of(slot(tp ^ hop(k, n_tp), n_tp) * part, part), part)
        branch_full[at, :] = branch_refs[k][...]
    for ref, side in ((send_ref, 1 - core), (keep_ref, core)):
        columns = pl.ds(pl.multiple_of(side * half, half), half)
        ref[:wide, :] = mm(proj_ref[...], h_ref[:, columns], NN).astype(ref.dtype)
        ref[wide:, :] = mm(out_ref[...], branch_full[:, columns], NN).astype(ref.dtype)


def late_grads(proj_grad, h_one, out_b, branches, after):
    rows, model = h_one.shape
    wide = proj_grad.shape[0] + out_b.shape[0]
    return call(
        "late_grads",
        functools.partial(late_kernel, len(branches)),
        [(proj_grad, "v"), (h_one, "v"), (out_b, "v"), (branches[0], "v")]
        + kinds(branches[1:], "v"),
        [((wide, model // 2), F32, "v"), ((wide, model // 2), BF16, "v")],
        [pltpu.VMEM((rows, model), BF16)],
        16,
        after,
    )


def spread_kernel(count, *refs):
    given, outs, held = refs[: -count - 1], refs[-count - 1 : -1], refs[-1]
    piece = outs[0].shape[0]
    chip = lax.axis_index("seq") // 2
    at = 0
    for keep_ref, back_ref in zip(given[::2], given[1::2]):
        rows = keep_ref.shape[0]
        held[at : at + rows, :] = keep_ref[...] + back_ref[...].astype(F32)
        at += rows
    if at < held.shape[0]:
        held[at:, :] = jnp.zeros((held.shape[0] - at, held.shape[1]), F32)
    for k in range(count):
        at = pl.ds(pl.multiple_of((chip ^ k) * piece, piece), piece)
        outs[k][...] = held[at, :].astype(outs[k].dtype)


def spread(count, *pairs):
    half = pairs[0][0].shape[1]
    rows = sum(keep.shape[0] for keep, unused in pairs)
    piece = -(-rows // (8 * count)) * 8
    return call(
        "spread",
        functools.partial(spread_kernel, count),
        [(array, "v") for pair in pairs for array in pair],
        [((piece, half), F32, "v")] + [((piece, half), BF16, "v")] * (count - 1),
        [pltpu.VMEM((count * piece, half), F32)],
    )


def piece_kernel(count, gain_ref, *refs):
    out_ref = refs[count]
    half = out_ref.shape[1]
    total = refs[0][...]
    for ref in refs[1:count]:
        total = total + ref[...].astype(F32)
    line = lax.broadcasted_iota(jnp.int32, (16, half), 0)
    gains = jnp.zeros((16, half), F32)
    for at in range(4):
        row = gain_ref[at // 2 : at // 2 + 1, at % 2 * half : (at % 2 + 1) * half]
        gains = jnp.where(line == at, row, gains)
    out_ref[...] = jnp.concatenate([total, gains], axis=0).astype(BF16)


def sum_piece(gains, pieces, after=()):
    piece, half = pieces[0].shape
    (out,) = call(
        "sum_piece",
        functools.partial(piece_kernel, len(pieces)),
        [(gains, "v")] + kinds(pieces, "v"),
        [((piece + 16, half), BF16, "v")],
        (),
        16,
        after,
    )
    return out


def collect_kernel(count, *refs):
    out_ref, held = refs[count:]
    piece = refs[0].shape[0] - 16
    wide = count * piece
    chip = lax.axis_index("seq") // 2
    gains = jnp.zeros((16, out_ref.shape[1]), F32)
    for k in range(count):
        at = pl.ds(pl.multiple_of((chip ^ hop(k, count)) * piece, piece), piece)
        whole = refs[k][...].astype(F32)
        held[at, :] = whole[:piece]
        gains = gains + whole[piece:]
    held[wide:, :] = gains
    out_ref[...] = held[...].astype(BF16)


def collect(pieces, after=()):
    piece, half = pieces[0].shape
    wide = (piece - 16) * len(pieces) + 16
    (out,) = call(
        "collect",
        functools.partial(collect_kernel, len(pieces)),
        kinds(pieces, "v"),
        [((wide, half), BF16, "v")],
        [pltpu.VMEM((wide, half), F32)],
        16,
        after,
    )
    return out


def write_half(sizes, source, side, out_refs, held, sems):
    half = source.shape[1]
    columns = pl.ds(pl.multiple_of(side * half, half), half)
    at = 0
    copies = []
    for n, (ref, size) in enumerate(zip(out_refs, sizes)):
        rows = pl.ds(at, size)
        held[rows, :] = source[rows, :].astype(F32)
        copies.append(pltpu.make_async_copy(held.at[rows], ref.at[:, columns], sems.at[n]))
        copies[-1].start()
        at += size
    return copies


def own_kernel(sizes, own_ref, *refs):
    out_refs, held, sems = refs[:-2], refs[-2], refs[-1]
    core = lax.axis_index("seq") % 2
    for copy in write_half(sizes, own_ref, core, out_refs, held, sems):
        copy.wait()


def pair_kernel(sizes, own_ref, pair_ref, *refs):
    refs = refs[len(sizes) :]
    out_refs, gain_refs = refs[: len(sizes)], refs[len(sizes) : len(sizes) + 2]
    held, sems = refs[-2:]
    core = lax.axis_index("seq") % 2
    copies = write_half(sizes, pair_ref, 1 - core, out_refs, held, sems)
    half = own_ref.shape[1]
    first = own_ref.shape[0] - 16
    gains = own_ref[first:, :].astype(F32) + pair_ref[first:, :].astype(F32)
    for at, ref in zip((0, 2), gain_refs):
        ref[pl.ds(0, half)] = gains[at]
        ref[pl.ds(half, half)] = gains[at + 1]
    for copy in copies:
        copy.wait()


def finish(own, over_cores, sizes):
    half = own.shape[1]
    shapes = [((size, 2 * half), F32, "raw") for size in sizes]
    scratch = [pltpu.VMEM((sum(sizes), half), F32), pltpu.SemaphoreType.DMA((len(sizes),))]
    pair = over_cores(own)
    begun = call("own_half", functools.partial(own_kernel, sizes), [(own, "v")], shapes, scratch)
    return call(
        "pair_half",
        functools.partial(pair_kernel, sizes),
        [(own, "v"), (pair, "v")] + kinds(begun, "raw"),
        shapes + [((2 * half,), F32, "h")] * 2,
        scratch,
        alias={2 + n: n for n in range(len(sizes))},
    )


def down_kernel(mixed_ref, w_ref, middle_ref, keep_ref, *refs):
    send_refs, total = refs[:-1], refs[-1]
    part = keep_ref.shape[0]
    tp = lax.axis_index("tp")
    total[...] = mm(mixed_ref[...], w_ref[...], TN)
    own = pl.ds(pl.multiple_of(tp // 2 * part, part), part)
    keep_ref[...] = total[own, :] + middle_ref[own, :]
    for n, ref in enumerate(send_refs):
        at = pl.ds(pl.multiple_of((tp ^ (2 * n + 2)) // 2 * part, part), part)
        ref[...] = total[at, :].astype(ref.dtype)


def down(n_tp, mixed, w_both, middle, after):
    rows, model = middle.shape
    part = 2 * rows // n_tp
    return call(
        "down",
        down_kernel,
        kinds((mixed, w_both, middle), "v"),
        [((part, model), F32, "v")] + [((part, model), BF16, "v")] * (n_tp // 2 - 1),
        [pltpu.VMEM((rows, model), F32)],
        16,
        after,
    )


def total_kernel(count, *refs):
    total = refs[0][...]
    for ref in refs[1:count]:
        total = total + ref[...].astype(F32)
    refs[count][...] = total.astype(refs[count].dtype)


def total_of(parts, dtype=BF16, kind="v", after=(), flops=0):
    (out,) = call(
        "total_of",
        functools.partial(total_kernel, len(parts)),
        [(parts[0], kind)] + kinds(parts[1:], "v"),
        [(parts[0].shape, dtype, "v")],
        (),
        16,
        after,
        flops=flops,
    )
    return out


def body(
    n_seq,
    n_tp,
    tokens,
    gain_one,
    w_qkv,
    w_out,
    gain_two,
    w_in,
    w_down,
    cotangent,
    doc_lengths,
    roster,
):
    rows, model = tokens.shape
    width = w_qkv.shape[2]
    units = w_in.shape[2]
    count = n_seq // 2
    qkv_t = w_qkv.transpose(1, 2, 0).reshape(3 * width, model)
    in_t = w_in.transpose(1, 2, 0).reshape(2 * units, model)
    over_tp = lambda x, k: swap(x, "tp", k, n_tp)
    over_chips = lambda x, k: swap(x, "seq", 2 * k, n_seq)
    over_cores = lambda x: swap(x, "seq", 1, n_seq)
    everywhere = lambda xs: [xs[0]] + came(n_tp, lambda k: over_tp(xs[k], k))

    def by_steps(part):
        parts = {0: part}
        step = n_tp // 2
        while step:
            parts.update({k ^ step: over_tp(x, step) for k, x in parts.items()})
            step //= 2
        return [parts[hop(n, n_tp)] for n in range(n_tp)]

    docs = (doc_lengths, roster)

    queries, kv, h_one, cos_table, sin_table = project(*docs, tokens, gain_one, qkv_t)
    blocks = [kv] + [over_chips(kv, j) for j in range(1, count)]
    q_pair = over_cores(queries)
    picked, w_half = pick(in_t, w_down, w_out)
    got = [over_tp(picked, 1)] + [over_tp(w_half, k) for k in range(2, n_tp)]

    split = (count + 1) // 2
    (state,) = attention_forward(0, False, *docs, queries, q_pair, blocks[:split])
    state_own, state_pair = attention_forward(
        split, True, *docs, queries, q_pair, blocks[split:], state
    )
    out_b, totals, out_mine, out_other = join(state_own, over_cores(state_pair))
    outs = everywhere([out_other if k % 2 else out_mine for k in range(n_tp)])
    out_pair = over_cores(out_b)
    totals_pair = over_cores(totals)

    got = pile(got, [(state_pair, "v")])
    staged = stage(n_tp, tokens, cotangent, in_t, w_down, w_out, got, over_cores(got))
    middle, middle_part, h_two, mixed, gate_grad, gain_two_part, own, *others = feed(
        gain_two, staged, outs
    )
    arrived = [own] + [over_tp(others[n], 2 * n + 2) for n in range(n_tp // 2 - 1)]
    own, *others = down(n_tp, mixed, staged[4], middle, [(out_pair, "v"), (totals_pair, "v")])
    middle_grad, branch_grad, *pieces = branch(
        n_tp, middle_part, cotangent, gain_two, staged[2], arrived, [(own, "v")]
    )
    early, early_send = early_grads(
        mixed, gate_grad, cotangent, h_two, in_t, w_down, over_tp(h_two, 1), [(branch_grad, "v")]
    )
    early_back = over_cores(early_send)
    out_grad = lay_turned(everywhere(pieces), ())
    grad_pair = over_cores(out_grad)
    branches = by_steps(branch_grad)

    held = (queries, q_pair, out_grad, grad_pair, out_b, out_pair, totals, totals_pair)
    *terms, dq = attention_backward(1, False, *docs, held, blocks[1:], None)
    total = total_of(
        [own] + [over_tp(others[n], 2 * n + 2) for n in range(n_tp // 2 - 1)],
        BF16,
        "v",
        [(dq, "v"), (branches[2], "v")],
    )
    totals_all = by_steps(total)

    dkv, dq_own, dq_pair = attention_backward(
        0, True, *docs, held, blocks[:1], dq, ()
    )
    dkvs = [dkv] + [over_chips(terms[j - 1], j) for j in range(1, count)]

    proj_grad, *parts = unproject(
        n_tp,
        tokens,
        qkv_t,
        cos_table,
        sin_table,
        gain_two_part,
        dq_own,
        over_cores(dq_pair),
        dkvs,
        [(total, "v")],
    )
    layer_out = stack_parts(totals_all)
    keep, send = late_grads(proj_grad, h_one, out_b, branches, [(totals_all[n_tp // 2], "v")])
    own, *others = spread(count, (keep, over_cores(send)), (early, early_back))
    summed = total_of(everywhere(parts), F32, flops=2_000_000_000)
    chip_sum = total_of(
        [own] + came(count, lambda k: over_chips(others[k - 1], k)), F32, "v", ()
    )
    input_part, gains = input_side(tokens, gain_one, middle_grad, summed, [(own, "v")])
    inputs_all = everywhere([input_part] * n_tp)
    piece = sum_piece(gains, [chip_sum], ())
    input_grad = stack_parts(inputs_all, (), 3_000_000_000)
    collected = collect(
        [piece] + came(count, lambda k: over_chips(piece, k)), [(input_grad, "h"), (layer_out, "h")]
    )
    grad_qkv, grad_out, grad_down, grad_in, grad_one, grad_two = finish(
        collected, over_cores, (3 * width, width, units, 2 * units)
    )

    back = lambda x, n: x.reshape(-1, n, model).transpose(2, 0, 1)
    return (
        layer_out,
        input_grad,
        grad_one,
        back(grad_qkv, width),
        grad_out,
        grad_two,
        back(grad_in, units),
        grad_down,
    )


def solution(mesh):
    placed = (
        P("seq", None),
        P(),
        P(None, None, "tp"),
        P("tp", None),
        P(),
        P(None, None, "tp"),
        P("tp", None),
        P("seq", None),
        P(),
        P(),
    )
    return jax.shard_map(
        functools.partial(body, mesh.shape["seq"], mesh.shape["tp"]),
        mesh=mesh,
        in_specs=placed,
        out_specs=(
            P("seq", None),
            P("seq", None),
            P(),
            P(None, None, "tp"),
            P("tp", None),
            P(),
            P(None, None, "tp"),
            P("tp", None),
        ),
        check_vma=False,
    )
```

```python
import functools
import math

import jax
import jax.numpy as jnp
import numpy as np
from jax import lax
from jax.experimental import pallas as pl
from jax.experimental.pallas import tpu as pltpu
from jax.sharding import PartitionSpec as P

HDIM = 64
HALF = HDIM // 2
EPSILON = 1e-05
ROPE_THETA = 160000.0
MASKED = -1e30
AUG = 80
STRIP = 64
F32 = jnp.float32
BF16 = jnp.bfloat16
HBM = pl.BlockSpec(memory_space=pltpu.HBM)
VMEM = pl.BlockSpec(memory_space=pltpu.VMEM)

NN = (((1,), (0,)), ((), ()))
NT = (((1,), (1,)), ((), ()))
TN = (((0,), (0,)), ((), ()))


def params(mib):
    return pltpu.CompilerParams(vmem_limit_bytes=mib * 2**20)


def slot(tp, n_tp):
    return tp % 2 * (n_tp // 2) + tp // 2


def hop(n, count):
    return (count - n) % count


def came(count, send):
    return [send(hop(n, count)) for n in range(1, count)]


def mm(a, b, dims):
    return lax.dot_general(a, b, dims, preferred_element_type=F32)


def shaped(shape, dtype):
    return jax.ShapeDtypeStruct(shape, dtype)


def kinds(arrays, kind):
    return [(array, kind) for array in arrays]


def pin(array, kind):
    return array if kind in ("v", "free") else pltpu.with_memory_space_constraint(array, pltpu.HBM)


def call(name, kernel, ins, outs, scratch=(), mib=16, after=(), lazy=False, flops=0, alias=None):
    fetched = [i for i, given in enumerate(ins) if given[1] not in ("v", "raw", "free")]
    left = [i for i, out in enumerate(outs) if out[2] == "h"]

    def held(array, kind):
        rows = array.shape[0] if kind == "h" else kind
        return pltpu.VMEM((rows,) + array.shape[1:], array.dtype)

    def run(*refs):
        in_refs = list(refs[: len(ins)])
        at = len(ins) + len(after)
        out_refs = list(refs[at : at + len(outs)])
        at += len(outs)
        own = refs[at : at + len(scratch)]
        at += len(scratch)
        buffers = refs[at : at + len(fetched) + len(left)]
        sems = refs[-1]
        copies = []
        for n, i in enumerate(fetched):
            source = in_refs[i]
            if ins[i][1] != "h":
                rows = ins[i][1]
                n_tp = ins[i][0].shape[0] // rows
                at = pl.multiple_of(slot(lax.axis_index("tp"), n_tp) * rows, rows)
                source = source.at[pl.ds(at, rows)]
            copies.append(pltpu.make_async_copy(source, buffers[n], sems.at[n]))
            in_refs[i] = buffers[n]
        for copy in copies:
            copy.start()
        coming = dict(zip(fetched, copies))
        going = {}
        for n, i in enumerate(left):
            spot = len(fetched) + n
            going[i] = pltpu.make_async_copy(buffers[spot], out_refs[i], sems.at[spot])
            out_refs[i] = buffers[spot]
        gone = []

        def need(*which):
            for i in which:
                if i in coming:
                    coming.pop(i).wait()

        def give(*which):
            for i in which:
                if i in going:
                    gone.append(going.pop(i))
                    gone[-1].start()

        if lazy:
            kernel(need, give, *in_refs, *out_refs, *own)
        else:
            need(*fetched)
            kernel(*in_refs, *out_refs, *own)
        need(*fetched)
        give(*left)
        for copy in gone:
            copy.wait()

    spec = lambda kind: VMEM if kind == "v" else HBM
    count = len(fetched) + len(left)
    return pl.pallas_call(
        run,
        out_shape=tuple(
            shaped(shape, dtype) if kind == "v" else pltpu.HBM(shape, dtype)
            for shape, dtype, kind in outs
        ),
        in_specs=[spec(kind) for unused, kind in ins] + [spec(kind) for unused, kind in after],
        out_specs=tuple(spec(kind) for unused, unused, kind in outs),
        scratch_shapes=list(scratch)
        + [held(*ins[i]) for i in fetched]
        + [pltpu.VMEM(outs[i][0], outs[i][1]) for i in left]
        + [pltpu.SemaphoreType.DMA((max(count, 1),))],
        name=name,
        input_output_aliases=alias or {},
        cost_estimate=pl.CostEstimate(flops=flops, bytes_accessed=0, transcendentals=0)
        if flops
        else None,
        compiler_params=params(mib),
    )(*[pin(*given) for given in ins], *[pin(*given) for given in after])


def swap(x, axis, hop, count):
    return lax.ppermute(x, axis, [(i, i ^ hop) for i in range(count)])


def doc_scratch(doc_lengths, roster):
    return [pltpu.SMEM(doc_lengths.shape, jnp.int32), pltpu.SMEM(roster.shape, jnp.int32)]


def fetch_docs(len_any, roster_any, len_ref, roster_ref, len_sem, roster_sem):
    one = pltpu.make_async_copy(len_any, len_ref, len_sem)
    two = pltpu.make_async_copy(roster_any, roster_ref, roster_sem)
    one.start()
    two.start()
    one.wait()
    two.wait()


def doc_bounds(len_ref):
    ends, total = [], jnp.int32(0)
    for d in range(len_ref.shape[0]):
        total = total + len_ref[d]
        ends.append(total)
    return ends


def doc_of(ends, position):
    found = jnp.int32(0)
    for end in ends:
        found = found + (end <= position).astype(jnp.int32)
    return found


def meet(ends, base_a, base_b, rows):
    low = jnp.maximum(doc_of(ends, base_a), doc_of(ends, base_b))
    high = jnp.minimum(doc_of(ends, base_a + rows - 1), doc_of(ends, base_b + rows - 1))
    return low <= high


def doc_rows(ends, base, rows):
    spot = base + lax.broadcasted_iota(jnp.int32, (16, rows), 1)
    line = lax.broadcasted_iota(jnp.int32, (16, rows), 0)
    held = jnp.zeros((16, rows), F32)
    start = jnp.int32(0)
    for d, end in enumerate(ends):
        inside = (line == d) & (spot >= start) & (spot < end)
        held = jnp.where(inside, 1.0, held)
        start = end
    return held


def ban_rows(ends, base, rows):
    line = lax.broadcasted_iota(jnp.int32, (16, rows), 0)
    held = doc_rows(ends, base, rows)
    return jnp.where((held > 0.5) | (line >= len(ends)), 0.0, MASKED)


def key_row(block, seq_index):
    return seq_index ^ (2 * block)


def place_row(ends, base, rows):
    spot = base + lax.broadcasted_iota(jnp.int32, (1, rows), 1)
    start = jnp.zeros((1, rows), jnp.int32)
    for end in ends:
        start = jnp.where(spot >= end, end, start)
    return (spot - start).astype(F32)


def normed(values):
    centre = jnp.mean(values, axis=-1, keepdims=True)
    shifted = values - centre
    spread = jnp.mean(shifted * shifted, axis=-1, keepdims=True)
    scale = lax.rsqrt(spread + EPSILON)
    return shifted * scale, scale


def norm_back(unit, scale, grad, gain):
    u = grad * gain
    mean_u = jnp.mean(u, axis=-1, keepdims=True)
    mean_un = jnp.mean(u * unit, axis=-1, keepdims=True)
    return scale * (u - mean_u - unit * mean_un)


def project_kernel(
    width, need, give, len_any, roster_any, x_ref, w_ref, gain_ref, freq_ref, *refs
):
    q_out, kv_out, h_out, cos_out, sin_out = refs[:5]
    proj, len_ref, roster_ref, sems = refs[5:]
    rows = x_ref.shape[0]
    fetch_docs(len_any, roster_any, len_ref, roster_ref, sems.at[0], sems.at[1])
    need(5)
    ends = doc_bounds(len_ref)
    place = place_row(ends, roster_ref[lax.axis_index("seq")] * rows, rows)
    angles = place * freq_ref[...]
    cos_table = jnp.cos(angles)
    sin_table = jnp.sin(angles)
    cos_out[...] = cos_table
    sin_out[...] = sin_table
    give(3, 4)
    need(2, 4)
    gain = gain_ref[...].reshape(1, -1)

    def strip(i, carry):
        at = pl.ds(i * STRIP, STRIP)
        unit, unused = normed(x_ref[at, :].astype(F32))
        h_out[at, :] = (unit * gain).astype(BF16)
        return carry

    lax.fori_loop(0, rows // STRIP, strip, 0)
    give(2)
    need(3)
    proj[...] = mm(w_ref[...], h_out[...], NT)
    for at in range(0, 2 * width, HDIM):
        low = proj[at : at + HALF, :]
        high = proj[at + HALF : at + HDIM, :]
        turned_low = (low * cos_out[...] - high * sin_out[...]).astype(BF16)
        turned_high = (high * cos_out[...] + low * sin_out[...]).astype(BF16)
        if at < width:
            q_out[at : at + HALF, :] = (turned_low.astype(F32) * HDIM**-0.5).astype(BF16)
            q_out[at + HALF : at + HDIM, :] = (turned_high.astype(F32) * HDIM**-0.5).astype(BF16)
        else:
            kv_out[at - width : at - width + HALF, :] = turned_low
            kv_out[at - width + HALF : at - width + HDIM, :] = turned_high
    kv_out[width:, :] = proj[2 * width :, :].astype(BF16)


def project(doc_lengths, roster, tokens, gain, qkv_t):
    rows, model = tokens.shape
    width = qkv_t.shape[0] // 3
    freq = (ROPE_THETA ** -(np.arange(HALF) * (2.0 / HDIM))).astype(np.float32)[:, None]
    return call(
        "project",
        functools.partial(project_kernel, width),
        kinds((doc_lengths, roster), "raw") + kinds((tokens, qkv_t, gain, jnp.asarray(freq)), "h"),
        [
            ((width, rows), BF16, "v"),
            ((2 * width, rows), BF16, "v"),
            ((rows, model), BF16, "v"),
            ((HALF, rows), F32, "v"),
            ((HALF, rows), F32, "v"),
        ],
        [pltpu.VMEM((3 * width, rows), F32)]
        + doc_scratch(doc_lengths, roster)
        + [pltpu.SemaphoreType.DMA((2,))],
        lazy=True,
    )


def forward_kernel(first, count, heads, last, len_any, roster_any, q_own, q_pair, *refs):
    kv_refs = refs[:count]
    refs = refs[count:]
    if first:
        state_in, refs = refs[0], refs[1:]
    outs = refs[: 2 if last else 1]
    kv, q_aug, state, len_ref, roster_ref, sems = refs[len(outs) :]
    rows = q_own.shape[1]
    width = heads * HDIM
    me = lax.axis_index("seq")
    copies = [pltpu.make_async_copy(kv_refs[j], kv.at[j], sems.at[j]) for j in range(count)]
    for copy in copies:
        copy.start()
    fetch_docs(len_any, roster_any, len_ref, roster_ref, sems.at[count], sems.at[count + 1])
    ends = doc_bounds(len_ref)
    bases = (roster_ref[me] * rows, roster_ref[me ^ 1] * rows)
    for g, q_ref in enumerate((q_own, q_pair)):
        mark = doc_rows(ends, bases[g], rows).astype(BF16)
        for h in range(heads):
            q_aug[g * heads + h, :HDIM, :] = q_ref[h * HDIM : (h + 1) * HDIM, :]
            q_aug[g * heads + h, HDIM:, :] = mark
    if first:
        state[...] = state_in[...]
    else:
        line = lax.broadcasted_iota(jnp.int32, (2 * heads, AUG, rows), 1)
        state[...] = jnp.where(line >= 72, MASKED, 0.0)
    for copy in copies:
        copy.wait()

    top = lax.broadcasted_iota(jnp.int32, (16, rows), 0) == 0
    ones = jnp.where(top, 1.0, 0.0).astype(BF16)

    def block(j, carry):
        key_base = roster_ref[key_row(j + first, me)] * rows
        ban = ban_rows(ends, key_base, rows).astype(BF16)
        for g in range(2):

            @pl.when(meet(ends, bases[g], key_base, rows))
            def _():
                for h in range(heads):
                    at = g * heads + h
                    keys = jnp.concatenate([kv[j, h * HDIM : (h + 1) * HDIM, :], ban], axis=0)
                    vals = jnp.concatenate(
                        [kv[j, width + h * HDIM : width + (h + 1) * HDIM, :], ones], axis=0
                    )
                    scores = mm(keys, q_aug[at], TN)
                    old = state[at, 72:73, :]
                    new = jnp.maximum(old, jnp.max(scores, axis=0, keepdims=True))
                    probs = jnp.exp(scores - new).astype(BF16)
                    part = mm(vals, probs, NN)
                    fade = jnp.exp(old - new)
                    state[at, :72, :] = state[at, :72, :] * fade + part[:72]
                    state[at, 72:, :] = jnp.broadcast_to(new, (8, rows))

        return carry

    lax.fori_loop(0, count, block, 0)
    if last:
        outs[0][...] = state[:heads]
        outs[1][...] = state[heads:]
    else:
        outs[0][...] = state[...]


def attention_forward(first, last, doc_lengths, roster, q_own, q_pair, blocks, state=None, after=()):
    width, rows = q_own.shape
    heads = width // HDIM
    count = len(blocks)
    half = ((heads, AUG, rows), F32, "v")
    whole = ((2 * heads, AUG, rows), F32, "v")
    given = [] if state is None else [(state, "v")]
    return call(
        "attention_forward",
        functools.partial(forward_kernel, first, count, heads, last),
        [(doc_lengths, "raw"), (roster, "raw"), (q_own, "v"), (q_pair, "v")]
        + kinds(blocks, "free")
        + given,
        [half, half] if last else [whole],
        [
            pltpu.VMEM((count, 2 * width, rows), BF16),
            pltpu.VMEM((2 * heads, AUG, rows), BF16),
            pltpu.VMEM((2 * heads, AUG, rows), F32),
        ]
        + doc_scratch(doc_lengths, roster)
        + [pltpu.SemaphoreType.DMA((count + 2,))],
        16 if count < 8 else 40,
        after,
    )


def backward_kernel(first, count, heads, more, last, len_any, roster_any, *refs):
    q_own, q_pair, g_own, g_pair, o_own, o_pair, t_own, t_pair = refs[:8]
    kv_refs, refs = refs[8 : 8 + count], refs[8 + count :]
    if more:
        dq_in, refs = refs[0], refs[1:]
    outs, refs = refs[:count], refs[count:]
    dq_outs, refs = (refs[:2], refs[2:]) if last else (refs[:1], refs[1:])
    kv, q_aug, delta, dq, dkv, len_ref, roster_ref, sems = refs
    rows = q_own.shape[1]
    width = heads * HDIM
    me = lax.axis_index("seq")
    copies = [pltpu.make_async_copy(kv_refs[j], kv.at[j], sems.at[j]) for j in range(count)]
    for copy in copies:
        copy.start()
    fetch_docs(len_any, roster_any, len_ref, roster_ref, sems.at[count], sems.at[count + 1])
    ends = doc_bounds(len_ref)
    bases = (roster_ref[me] * rows, roster_ref[me ^ 1] * rows)
    for g, (q_ref, g_ref, o_ref) in enumerate(((q_own, g_own, o_own), (q_pair, g_pair, o_pair))):
        mark = doc_rows(ends, bases[g], rows).astype(BF16)
        for h in range(heads):
            part = slice(h * HDIM, (h + 1) * HDIM)
            q_aug[g * heads + h, :HDIM, :] = q_ref[part, :]
            q_aug[g * heads + h, HDIM:, :] = mark
            product = g_ref[part, :].astype(F32) * o_ref[part, :].astype(F32)
            delta[g * heads + h] = jnp.broadcast_to(
                jnp.sum(product, axis=0, keepdims=True), (8, rows)
            )
    if more:
        dq[...] = dq_in[...]
    else:
        dq[...] = jnp.zeros_like(dq)
    for copy in copies:
        copy.wait()

    def block(j, carry):
        key_base = roster_ref[key_row(j + first, me)] * rows
        ban = ban_rows(ends, key_base, rows).astype(BF16)
        dkv[j] = jnp.zeros((2 * width, rows), F32)
        for g, (g_ref, t_ref) in enumerate(((g_own, t_own), (g_pair, t_pair))):

            @pl.when(meet(ends, bases[g], key_base, rows))
            def _():
                for h in range(heads):
                    at = g * heads + h
                    part = slice(h * HDIM, (h + 1) * HDIM)
                    late = slice(width + h * HDIM, width + (h + 1) * HDIM)
                    keys = kv[j, part, :]
                    scores = mm(jnp.concatenate([keys, ban], axis=0), q_aug[at], TN)
                    probs = jnp.exp(scores - t_ref[h, 0:1, :])
                    prob_grads = mm(kv[j, late, :], g_ref[part, :], TN)
                    score_grad = (probs * (prob_grads - delta[at, 0:1, :])).astype(BF16)
                    dkv[j, late, :] += mm(g_ref[part, :], probs.astype(BF16), NT)
                    dkv[j, part, :] += mm(q_aug[at, :HDIM, :], score_grad, NT)
                    dq[at] += mm(keys, score_grad, NN)

        return carry

    lax.fori_loop(0, count, block, 0)
    for j in range(count):
        outs[j][...] = dkv[j].astype(outs[j].dtype)
    if last:
        for h in range(heads):
            part = slice(h * HDIM, (h + 1) * HDIM)
            dq_outs[0][part, :] = dq[h] * HDIM**-0.5
            dq_outs[1][part, :] = (dq[heads + h] * HDIM**-0.5).astype(BF16)
    else:
        dq_outs[0][...] = dq[...]


def attention_backward(first, last, doc_lengths, roster, held, blocks, dq=None, after=()):
    width, rows = held[0].shape
    heads = width // HDIM
    count = len(blocks)
    given = [] if dq is None else [(dq, "v")]
    if last:
        queries = [((width, rows), F32, "v"), ((width, rows), BF16, "v")]
    else:
        queries = [((2 * heads, HDIM, rows), F32, "v")]
    return call(
        "attention_backward",
        functools.partial(backward_kernel, first, count, heads, bool(given), last),
        kinds((doc_lengths, roster), "raw") + kinds(held, "v") + kinds(blocks, "free") + given,
        [((2 * width, rows), BF16 if first else F32, "v")] * count + queries,
        [
            pltpu.VMEM((count, 2 * width, rows), BF16),
            pltpu.VMEM((2 * heads, AUG, rows), BF16),
            pltpu.VMEM((2 * heads, 8, rows), F32),
            pltpu.VMEM((2 * heads, HDIM, rows), F32),
            pltpu.VMEM((count, 2 * width, rows), F32),
        ]
        + doc_scratch(doc_lengths, roster)
        + [pltpu.SemaphoreType.DMA((count + 2,))],
        16 if count < 8 else 40,
        after,
        flops=0 if last else 0,
    )


def join_kernel(heads, own_ref, back_ref, out_ref, total_ref, mine_ref, other_ref):
    rows = own_ref.shape[2]
    for h in range(heads):
        top_own = own_ref[h, 72:73, :]
        top_back = back_ref[h, 72:73, :]
        top = jnp.maximum(top_own, top_back)
        fade_own = jnp.exp(top_own - top)
        fade_back = jnp.exp(top_back - top)
        total = own_ref[h, 64:65, :] * fade_own + back_ref[h, 64:65, :] * fade_back
        share_own = fade_own / total
        share_back = fade_back / total
        value = own_ref[h, :HDIM, :] * share_own + back_ref[h, :HDIM, :] * share_back
        out_ref[h * HDIM : (h + 1) * HDIM, :] = value.astype(BF16)
        total_ref[h] = jnp.broadcast_to(top + jnp.log(total), (8, rows))
    half = rows // 2
    for bit in range(2):

        @pl.when(lax.axis_index("tp") % 2 == bit)
        def _():
            mine_ref[...] = out_ref[:, bit * half : (bit + 1) * half]
            other_ref[...] = out_ref[:, (1 - bit) * half : (2 - bit) * half]


def join(own, back):
    heads, unused, rows = own.shape
    return call(
        "join",
        functools.partial(join_kernel, heads),
        [(own, "v"), (back, "v")],
        [
            ((heads * HDIM, rows), BF16, "v"),
            ((heads, 8, rows), F32, "v"),
            ((heads * HDIM, rows // 2), BF16, "v"),
            ((heads * HDIM, rows // 2), BF16, "v"),
        ],
    )


def pick_kernel(in_any, down_any, w_any, all_ref, w_ref, sems):
    core = lax.axis_index("seq") % 2
    at = 0
    copies = []
    for source in (in_any, down_any, w_any):
        rows = source.shape[0] // 2
        mine = pl.ds(pl.multiple_of(core * rows, rows), rows)
        copies.append((source.at[mine], all_ref.at[pl.ds(at, rows)]))
        at += rows
    copies.append((w_any.at[mine], w_ref))
    copies = [pltpu.make_async_copy(*move, sems.at[n]) for n, move in enumerate(copies)]
    for copy in copies:
        copy.start()
    for copy in copies:
        copy.wait()


def pick(in_t, w_down, w_out):
    rows = (in_t.shape[0] + w_down.shape[0] + w_out.shape[0]) // 2
    model = w_out.shape[1]
    return call(
        "pick",
        pick_kernel,
        kinds((in_t, w_down, w_out), "raw"),
        [((rows, model), BF16, "v"), ((w_out.shape[0] // 2, model), BF16, "v")],
        [pltpu.SemaphoreType.DMA((4,))],
    )


def pile_kernel(*refs):
    out_ref = refs[-1]
    at = 0
    for ref in refs[:-1]:
        out_ref[at : at + ref.shape[0], :] = ref[...]
        at += ref.shape[0]


def pile(values, after):
    rows = sum(value.shape[0] for value in values)
    (out,) = call(
        "pile",
        pile_kernel,
        kinds(values, "v"),
        [((rows, values[0].shape[1]), BF16, "v")],
        (),
        16,
        after,
    )
    return out


def stage_kernel(x_any, cot_any, in_any, down_any, w_any, got_ref, rest_ref, *refs):
    x_ref, cot_ref, w_ref, in_ref, down_ref, sems = refs
    half = x_ref.shape[0]
    core = lax.axis_index("seq") % 2
    tp = lax.axis_index("tp")
    n_tp = w_ref.shape[0] // w_any.shape[0]
    mine = pl.ds(pl.multiple_of(tp % 2 * half, half), half)
    width = w_any.shape[0]
    rows = width // 2
    own = pl.ds(pl.multiple_of(tp * width, width), width)
    moves = [(w_any, w_ref.at[own]), (x_any.at[mine], x_ref), (cot_any.at[mine], cot_ref)]
    sides = ((got_ref, core), (rest_ref, 1 - core))
    first = got_ref.shape[0] - (n_tp - 1) * rows
    for k in range(1, n_tp):
        for source, side in sides:
            spot = pl.multiple_of((tp ^ k) * width + side * rows, rows)
            piece = source.at[pl.ds(first + (k - 1) * rows, rows)]
            moves.append((piece, w_ref.at[pl.ds(spot, rows)]))
    at = 0
    for own, ref in ((in_any, in_ref), (down_any, down_ref)):
        rows = own.shape[0] // 2
        moves.append((own, ref.at[pl.ds(0, 2 * rows)]))
        for source, side in sides:
            spot = pl.multiple_of(2 * rows + side * rows, rows)
            moves.append((source.at[pl.ds(at, rows)], ref.at[pl.ds(spot, rows)]))
        at += rows
    copies = [pltpu.make_async_copy(*move, sems.at[n]) for n, move in enumerate(moves)]
    for copy in copies:
        copy.start()
    for copy in copies:
        copy.wait()


def stage(n_tp, tokens, cotangent, in_t, w_down, w_out, got, rest):
    rows, model = tokens.shape
    return call(
        "stage",
        stage_kernel,
        kinds((tokens, cotangent, in_t, w_down, w_out), "raw") + kinds((got, rest), "v"),
        [
            ((rows // 2, model), BF16, "v"),
            ((rows // 2, model), BF16, "v"),
            ((n_tp * w_out.shape[0], model), BF16, "v"),
            ((2 * in_t.shape[0], model), BF16, "v"),
            ((2 * w_down.shape[0], model), BF16, "v"),
        ],
        [pltpu.SemaphoreType.DMA((7 + 2 * n_tp,))],
    )


def gated(units, first, gate_up, mixed_grad, mixed_out, gate_out):
    rows = math.gcd(units, 96)

    def wave(i, carry):
        spot = pl.ds(first + i * rows, rows)
        at = pl.ds(2 * first + i * rows, rows)
        late = pl.ds(2 * first + units + i * rows, rows)
        gate = gate_up[at, :]
        up = gate_up[late, :]
        back = mixed_grad[spot, :]
        bell = 0.5 * (1.0 + lax.erf(gate * (2.0**-0.5)))
        active = gate * bell
        slope = bell + gate * jnp.exp(-0.5 * gate * gate) * ((2.0 * jnp.pi) ** -0.5)
        mixed_out[spot, :] = (active * up).astype(BF16)
        gate_out[at, :] = (back * up * slope).astype(BF16)
        gate_out[late, :] = (back * active).astype(BF16)
        return carry

    lax.fori_loop(0, units // rows, wave, 0)


def feed_kernel(n_tp, need, give, x_ref, cot_ref, w_ref, in_ref, down_ref, gain_ref, *refs):
    out_refs = refs[:n_tp]
    middle_out, part_out, h_out, mixed_out, gate_out, gain_out = refs[n_tp : n_tp + 6]
    keep_ref, *send_refs = refs[n_tp + 6 : n_tp + 6 + n_tp // 2]
    outs, unit, gate_up, mixed_grad, grad = refs[n_tp + 6 + n_tp // 2 :]
    rows = x_ref.shape[0]
    part = keep_ref.shape[0]
    units = down_ref.shape[0] // 2
    width = out_refs[0].shape[0]
    tp = lax.axis_index("tp")
    for k in range(n_tp):
        at = pl.ds(pl.multiple_of((tp ^ hop(k, n_tp)) * width, width), width)
        outs[at, :] = out_refs[k][...]
    mixed_grad[...] = mm(down_ref[...], cot_ref[...], NT)
    middle_out[...] = mm(outs[...], w_ref[...], TN)
    need(5)
    gain = gain_ref[...].reshape(1, -1)

    def strip(i, carry):
        at = pl.ds(i * 32, 32)
        middle = middle_out[at, :] + x_ref[at, :].astype(F32)
        middle_out[at, :] = middle
        held, unused = normed(middle)
        unit[at, :] = held
        h_out[at, :] = (held * gain).astype(BF16)
        return carry

    lax.fori_loop(0, rows // 32, strip, 0)
    give(0, 2)
    gate_up[...] = mm(in_ref[...], h_out[...], NT)
    for first in (0, units):
        gated(units, first, gate_up, mixed_grad, mixed_out, gate_out)
    give(3, 4)
    grad[...] = mm(gate_out[...], in_ref[...], TN)
    for n, ref in enumerate((keep_ref, *send_refs)):
        at = pl.ds(pl.multiple_of((tp ^ (2 * n)) // 2 * part, part), part)
        ref[...] = grad[at, :].astype(ref.dtype)
        give(6 + n)
    own = pl.ds(pl.multiple_of(tp // 2 * part, part), part)
    part_out[...] = middle_out[own, :]
    give(1)

    def gains(i, carry):
        at = pl.ds(i * 32, 32)
        product = grad[at, :] * unit[at, :]
        return carry + jnp.sum(product.reshape(4, 8, -1), axis=0)

    gain_out[...] = lax.fori_loop(0, rows // 32, gains, jnp.zeros(gain_out.shape, F32))


def feed(gain, staged, outs):
    rows, model = staged[0].shape
    n_tp = len(outs)
    units = staged[4].shape[0]
    part = 2 * rows // n_tp
    return call(
        "feed",
        functools.partial(feed_kernel, n_tp),
        kinds(staged, "v") + [(gain, "h")] + kinds(outs, "v"),
        [
            ((rows, model), F32, "v"),
            ((part, model), F32, "v"),
            ((rows, model), BF16, "v"),
            ((units, rows), BF16, "v"),
            ((2 * units, rows), BF16, "v"),
            ((8, model), F32, "v"),
            ((part, model), F32, "v"),
        ]
        + [((part, model), BF16, "v")] * (n_tp // 2 - 1),
        [
            pltpu.VMEM((n_tp * outs[0].shape[0], rows), BF16),
            pltpu.VMEM((rows, model), F32),
            pltpu.VMEM((2 * units, rows), F32),
            pltpu.VMEM((units, rows), F32),
            pltpu.VMEM((rows, model), F32),
        ],
        24,
        lazy=True,
    )


def branch_kernel(n_tp, count, need, give, middle_ref, cot_ref, gain_ref, w_ref, *refs):
    arrived = refs[:count]
    grad_out, branch_out = refs[count : count + 2]
    piece_refs = refs[count + 2 :]
    width = piece_refs[0].shape[1]
    tp = lax.axis_index("tp")
    need(0, 1, 2, 4)
    total = arrived[0][...]
    for ref in arrived[1:]:
        total = total + ref[...].astype(F32)
    unit, scale = normed(middle_ref[...])
    gain = gain_ref[...].reshape(1, -1)
    value = cot_ref[...].astype(F32) + norm_back(unit, scale, total, gain)
    grad_out[...] = value
    branch_out[...] = value.astype(BF16)
    give(0, 1)
    need(3)
    for k in range(n_tp):
        at = pl.ds(pl.multiple_of((tp ^ k) * width, width), width)
        piece_refs[k][...] = mm(branch_out[...], w_ref[at, :], NT).astype(BF16)


def branch(n_tp, middle_part, cotangent, gain, w_full, arrived, after):
    part, model = arrived[0].shape
    width = w_full.shape[0] // n_tp
    return call(
        "branch",
        functools.partial(branch_kernel, n_tp, len(arrived)),
        [(middle_part, "v"), (cotangent, part)]
        + [(gain, "h"), (w_full, "v"), (arrived[0], "v")]
        + kinds(arrived[1:], "v"),
        [((part, model), F32, "v"), ((part, model), BF16, "v")]
        + [((part, width), BF16, "v")] * n_tp,
        (),
        16,
        after,
        True,
    )


def lay_kernel(n_tp, *refs):
    out_ref, held = refs[n_tp:]
    part = refs[0].shape[0]
    tp = lax.axis_index("tp")
    for k in range(n_tp):
        at = pl.ds(pl.multiple_of(slot(tp ^ hop(k, n_tp), n_tp) * part, part), part)
        held[at, :] = refs[k][...].astype(F32)
    out_ref[...] = held[...].T.astype(BF16)


def lay_turned(pieces, after):
    part, width = pieces[0].shape
    rows = part * len(pieces)
    (out,) = call(
        "lay_turned",
        functools.partial(lay_kernel, len(pieces)),
        kinds(pieces, "v"),
        [((width, rows), BF16, "v")],
        [pltpu.VMEM((rows, width), F32)],
        16,
        after,
    )
    return out


def stack_kernel(n_tp, *refs):
    out_ref = refs[n_tp]
    part = refs[0].shape[0]
    tp = lax.axis_index("tp")
    for k in range(n_tp):
        at = pl.ds(pl.multiple_of(slot(tp ^ hop(k, n_tp), n_tp) * part, part), part)
        out_ref[at, :] = refs[k][...]


def stack_parts(pieces, after=(), flops=0):
    part, model = pieces[0].shape
    (out,) = call(
        "stack_parts",
        functools.partial(stack_kernel, len(pieces)),
        kinds(pieces, "v"),
        [((part * len(pieces), model), pieces[0].dtype, "h")],
        (),
        16,
        after,
        flops=flops,
    )
    return out


def turn_back(out_ref, first, value, cos_table, sin_table):
    for at in range(0, value.shape[0], HDIM):
        low = value[at : at + HALF]
        high = value[at + HALF : at + HDIM]
        spot = first + at
        out_ref[spot : spot + HALF, :] = (low * cos_table + high * sin_table).astype(BF16)
        out_ref[spot + HALF : spot + HDIM, :] = (high * cos_table - low * sin_table).astype(BF16)


def unproject_kernel(
    count, n_tp, need, give, x_ref, w_ref, cos_ref, sin_ref, two_ref, dq_ref, dq_back, *refs
):
    dkv_refs = refs[:count]
    proj_out = refs[count]
    part_refs = refs[count + 1 : count + 1 + n_tp]
    grad, dkv = refs[count + 1 + n_tp :]
    rows, model = x_ref.shape
    part = rows // n_tp
    width = dq_ref.shape[0]
    tp = lax.axis_index("tp")
    need(2, 3)
    cos_table = cos_ref[...]
    sin_table = sin_ref[...]
    turn_back(proj_out, 0, dq_ref[...] + dq_back[...].astype(F32), cos_table, sin_table)
    total = dkv_refs[0][...]
    for ref in dkv_refs[1:]:
        total = total + ref[...].astype(F32)
    dkv[...] = total
    turn_back(proj_out, width, dkv[:width, :], cos_table, sin_table)
    proj_out[2 * width :, :] = dkv[width:, :].astype(BF16)
    need(1)
    grad[...] = mm(proj_out[...], w_ref[...], TN)
    need(0, 4)

    def gains(i, carry):
        at = pl.ds(i * STRIP, STRIP)
        unit, unused = normed(x_ref[at, :].astype(F32))
        product = grad[at, :] * unit
        return carry + jnp.sum(product.reshape(STRIP // 8, 8, -1), axis=0)

    gain = lax.fori_loop(0, rows // STRIP, gains, jnp.zeros((8, model), F32))
    line = lax.broadcasted_iota(jnp.int32, (16, model), 0)
    gain_two = jnp.sum(two_ref[...], axis=0, keepdims=True)
    gain = jnp.sum(gain, axis=0, keepdims=True)
    gain = jnp.where(line == 0, gain, jnp.where(line == 1, gain_two, 0.0))
    for k in range(n_tp):
        at = pl.ds(pl.multiple_of(slot(tp ^ k, n_tp) * part, part), part)
        part_refs[k][:part, :] = grad[at, :].astype(part_refs[k].dtype)
        part_refs[k][part:, :] = gain.astype(part_refs[k].dtype)


def unproject(n_tp, tokens, qkv_t, cos_table, sin_table, gain_two_part, dq, dq_back, dkvs, after):
    rows, model = tokens.shape
    part = rows // n_tp
    return call(
        "unproject",
        functools.partial(unproject_kernel, len(dkvs), n_tp),
        kinds((tokens, qkv_t, cos_table, sin_table, gain_two_part), "v")
        + kinds((dq, dq_back, *dkvs), "v"),
        [((qkv_t.shape[0], rows), BF16, "v"), ((part + 16, model), F32, "v")]
        + [((part + 16, model), BF16, "v")] * (n_tp - 1),
        [pltpu.VMEM((rows, model), F32), pltpu.VMEM(dkvs[0].shape, F32)],
        16,
        after,
        True,
    )


def input_kernel(x_ref, gain_ref, grad_ref, sum_ref, out_ref, gain_out):
    part, model = grad_ref.shape
    total = sum_ref[...]
    unit, scale = normed(x_ref[...].astype(F32))
    gain = gain_ref[...].reshape(1, -1)
    value = grad_ref[...] + norm_back(unit, scale, total[:part], gain)
    out_ref[...] = value.astype(BF16)
    gain_out[...] = total[part : part + 8]


def input_side(tokens, gain, middle_grad, summed, after):
    part, model = middle_grad.shape
    return call(
        "input_side",
        input_kernel,
        [(tokens, part), (gain, "h"), (middle_grad, "v"), (summed, "v")],
        [((part, model), BF16, "v"), ((8, model), F32, "v")],
        (),
        16,
        after,
    )


def early_kernel(mixed_ref, gate_ref, cot_ref, h_ref, in_ref, down_ref, h_pair, *refs):
    keep_ref, send_ref, gate_up, mixed_grad, mixed, gate = refs
    units = down_ref.shape[0]
    half = h_ref.shape[0]
    bit = lax.axis_index("tp") % 2
    mine = pl.ds(pl.multiple_of(bit * half, half), half)
    other = pl.ds(pl.multiple_of((1 - bit) * half, half), half)
    gate_up[...] = mm(in_ref[...], h_pair[...], NT)
    mixed_grad[...] = mm(down_ref[...], cot_ref[other, :], NT)
    gated(units, 0, gate_up, mixed_grad, mixed, gate)
    width = keep_ref.shape[1]
    core = lax.axis_index("seq") % 2
    for ref, side in ((send_ref, 1 - core), (keep_ref, core)):
        columns = pl.ds(pl.multiple_of(side * width, width), width)
        down = mm(mixed_ref[:units, :], cot_ref[mine, columns], NN)
        down = down + mm(mixed[...], cot_ref[other, columns], NN)
        ref[:units, :] = down.astype(ref.dtype)
        both = mm(gate_ref[: 2 * units, :], h_ref[:, columns], NN)
        both = both + mm(gate[...], h_pair[:, columns], NN)
        ref[units:, :] = both.astype(ref.dtype)


def early_grads(mixed, gate_grad, cotangent, h_two, in_t, w_down, h_pair, after):
    units, model = w_down.shape
    half = h_two.shape[0]
    return call(
        "early_grads",
        early_kernel,
        kinds((mixed, gate_grad, cotangent, h_two, in_t, w_down, h_pair), "v"),
        [((3 * units, model // 2), F32, "v"), ((3 * units, model // 2), BF16, "v")],
        [
            pltpu.VMEM((2 * units, half), F32),
            pltpu.VMEM((units, half), F32),
            pltpu.VMEM((units, half), BF16),
            pltpu.VMEM((2 * units, half), BF16),
        ],
        24,
        after,
    )


def late_kernel(n_tp, proj_ref, h_ref, out_ref, *refs):
    branch_refs = refs[:n_tp]
    keep_ref, send_ref, branch_full = refs[n_tp:]
    part = branch_refs[0].shape[0]
    half = keep_ref.shape[1]
    wide = proj_ref.shape[0]
    tp = lax.axis_index("tp")
    core = lax.axis_index("seq") % 2
    for k in range(n_tp):
        at = pl.ds(pl.multiple_of(slot(tp ^ hop(k, n_tp), n_tp) * part, part), part)
        branch_full[at, :] = branch_refs[k][...]
    for ref, side in ((send_ref, 1 - core), (keep_ref, core)):
        columns = pl.ds(pl.multiple_of(side * half, half), half)
        ref[:wide, :] = mm(proj_ref[...], h_ref[:, columns], NN).astype(ref.dtype)
        ref[wide:, :] = mm(out_ref[...], branch_full[:, columns], NN).astype(ref.dtype)


def late_grads(proj_grad, h_one, out_b, branches, after):
    rows, model = h_one.shape
    wide = proj_grad.shape[0] + out_b.shape[0]
    return call(
        "late_grads",
        functools.partial(late_kernel, len(branches)),
        [(proj_grad, "v"), (h_one, "v"), (out_b, "v"), (branches[0], "v")]
        + kinds(branches[1:], "v"),
        [((wide, model // 2), F32, "v"), ((wide, model // 2), BF16, "v")],
        [pltpu.VMEM((rows, model), BF16)],
        16,
        after,
    )


def spread_kernel(count, *refs):
    given, outs, held = refs[: -count - 1], refs[-count - 1 : -1], refs[-1]
    piece = outs[0].shape[0]
    chip = lax.axis_index("seq") // 2
    at = 0
    for keep_ref, back_ref in zip(given[::2], given[1::2]):
        rows = keep_ref.shape[0]
        held[at : at + rows, :] = keep_ref[...] + back_ref[...].astype(F32)
        at += rows
    if at < held.shape[0]:
        held[at:, :] = jnp.zeros((held.shape[0] - at, held.shape[1]), F32)
    for k in range(count):
        at = pl.ds(pl.multiple_of((chip ^ k) * piece, piece), piece)
        outs[k][...] = held[at, :].astype(outs[k].dtype)


def spread(count, *pairs):
    half = pairs[0][0].shape[1]
    rows = sum(keep.shape[0] for keep, unused in pairs)
    piece = -(-rows // (8 * count)) * 8
    return call(
        "spread",
        functools.partial(spread_kernel, count),
        [(array, "v") for pair in pairs for array in pair],
        [((piece, half), F32, "v")] + [((piece, half), BF16, "v")] * (count - 1),
        [pltpu.VMEM((count * piece, half), F32)],
    )


def piece_kernel(count, gain_ref, *refs):
    out_ref = refs[count]
    half = out_ref.shape[1]
    total = refs[0][...]
    for ref in refs[1:count]:
        total = total + ref[...].astype(F32)
    line = lax.broadcasted_iota(jnp.int32, (16, half), 0)
    gains = jnp.zeros((16, half), F32)
    for at in range(4):
        row = gain_ref[at // 2 : at // 2 + 1, at % 2 * half : (at % 2 + 1) * half]
        gains = jnp.where(line == at, row, gains)
    out_ref[...] = jnp.concatenate([total, gains], axis=0).astype(BF16)


def sum_piece(gains, pieces, after=()):
    piece, half = pieces[0].shape
    (out,) = call(
        "sum_piece",
        functools.partial(piece_kernel, len(pieces)),
        [(gains, "v")] + kinds(pieces, "v"),
        [((piece + 16, half), BF16, "v")],
        (),
        16,
        after,
    )
    return out


def collect_kernel(count, *refs):
    out_ref, held = refs[count:]
    piece = refs[0].shape[0] - 16
    wide = count * piece
    chip = lax.axis_index("seq") // 2
    gains = jnp.zeros((16, out_ref.shape[1]), F32)
    for k in range(count):
        at = pl.ds(pl.multiple_of((chip ^ hop(k, count)) * piece, piece), piece)
        whole = refs[k][...].astype(F32)
        held[at, :] = whole[:piece]
        gains = gains + whole[piece:]
    held[wide:, :] = gains
    out_ref[...] = held[...].astype(BF16)


def collect(pieces, after=()):
    piece, half = pieces[0].shape
    wide = (piece - 16) * len(pieces) + 16
    (out,) = call(
        "collect",
        functools.partial(collect_kernel, len(pieces)),
        kinds(pieces, "v"),
        [((wide, half), BF16, "v")],
        [pltpu.VMEM((wide, half), F32)],
        16,
        after,
    )
    return out


def write_half(sizes, source, side, out_refs, held, sems):
    half = source.shape[1]
    columns = pl.ds(pl.multiple_of(side * half, half), half)
    at = 0
    copies = []
    for n, (ref, size) in enumerate(zip(out_refs, sizes)):
        rows = pl.ds(at, size)
        held[rows, :] = source[rows, :].astype(F32)
        copies.append(pltpu.make_async_copy(held.at[rows], ref.at[:, columns], sems.at[n]))
        copies[-1].start()
        at += size
    return copies


def own_kernel(sizes, own_ref, *refs):
    out_refs, held, sems = refs[:-2], refs[-2], refs[-1]
    core = lax.axis_index("seq") % 2
    for copy in write_half(sizes, own_ref, core, out_refs, held, sems):
        copy.wait()


def pair_kernel(sizes, own_ref, pair_ref, *refs):
    refs = refs[len(sizes) :]
    out_refs, gain_refs = refs[: len(sizes)], refs[len(sizes) : len(sizes) + 2]
    held, sems = refs[-2:]
    core = lax.axis_index("seq") % 2
    copies = write_half(sizes, pair_ref, 1 - core, out_refs, held, sems)
    half = own_ref.shape[1]
    first = own_ref.shape[0] - 16
    gains = own_ref[first:, :].astype(F32) + pair_ref[first:, :].astype(F32)
    for at, ref in zip((0, 2), gain_refs):
        ref[pl.ds(0, half)] = gains[at]
        ref[pl.ds(half, half)] = gains[at + 1]
    for copy in copies:
        copy.wait()


def half_scratch(sizes, half):
    return [pltpu.VMEM((sum(sizes), half), F32), pltpu.SemaphoreType.DMA((len(sizes),))]


def begin(own, sizes):
    half = own.shape[1]
    return call(
        "own_half",
        functools.partial(own_kernel, sizes),
        [(own, "v")],
        [((size, 2 * half), F32, "raw") for size in sizes],
        half_scratch(sizes, half),
    )


def finish(begun, own, pair, sizes):
    half = own.shape[1]
    return call(
        "pair_half",
        functools.partial(pair_kernel, sizes),
        [(own, "v"), (pair, "v")] + kinds(begun, "raw"),
        [((size, 2 * half), F32, "raw") for size in sizes] + [((2 * half,), F32, "h")] * 2,
        half_scratch(sizes, half),
        alias={2 + n: n for n in range(len(sizes))},
    )


def down_kernel(mixed_ref, w_ref, middle_ref, keep_ref, *refs):
    send_refs, total = refs[:-1], refs[-1]
    part = keep_ref.shape[0]
    tp = lax.axis_index("tp")
    total[...] = mm(mixed_ref[...], w_ref[...], TN)
    own = pl.ds(pl.multiple_of(tp // 2 * part, part), part)
    keep_ref[...] = total[own, :] + middle_ref[own, :]
    for n, ref in enumerate(send_refs):
        at = pl.ds(pl.multiple_of((tp ^ (2 * n + 2)) // 2 * part, part), part)
        ref[...] = total[at, :].astype(ref.dtype)


def down(n_tp, mixed, w_both, middle, after):
    rows, model = middle.shape
    part = 2 * rows // n_tp
    return call(
        "down",
        down_kernel,
        kinds((mixed, w_both, middle), "v"),
        [((part, model), F32, "v")] + [((part, model), BF16, "v")] * (n_tp // 2 - 1),
        [pltpu.VMEM((rows, model), F32)],
        16,
        after,
    )


def total_kernel(count, *refs):
    total = refs[0][...]
    for ref in refs[1:count]:
        total = total + ref[...].astype(F32)
    refs[count][...] = total.astype(refs[count].dtype)


def total_of(parts, dtype=BF16, kind="v", after=(), flops=0):
    (out,) = call(
        "total_of",
        functools.partial(total_kernel, len(parts)),
        [(parts[0], kind)] + kinds(parts[1:], "v"),
        [(parts[0].shape, dtype, "v")],
        (),
        16,
        after,
        flops=flops,
    )
    return out


def body(
    n_seq,
    n_tp,
    tokens,
    gain_one,
    w_qkv,
    w_out,
    gain_two,
    w_in,
    w_down,
    cotangent,
    doc_lengths,
    roster,
):
    rows, model = tokens.shape
    width = w_qkv.shape[2]
    units = w_in.shape[2]
    count = n_seq // 2
    qkv_t = w_qkv.transpose(1, 2, 0).reshape(3 * width, model)
    in_t = w_in.transpose(1, 2, 0).reshape(2 * units, model)
    over_tp = lambda x, k: swap(x, "tp", k, n_tp)
    over_chips = lambda x, k: swap(x, "seq", 2 * k, n_seq)
    over_cores = lambda x: swap(x, "seq", 1, n_seq)
    everywhere = lambda xs: [xs[0]] + came(n_tp, lambda k: over_tp(xs[k], k))

    def by_steps(part):
        parts = {0: part}
        step = n_tp // 2
        while step:
            parts.update({k ^ step: over_tp(x, step) for k, x in parts.items()})
            step //= 2
        return [parts[hop(n, n_tp)] for n in range(n_tp)]

    docs = (doc_lengths, roster)

    queries, kv, h_one, cos_table, sin_table = project(*docs, tokens, gain_one, qkv_t)
    blocks = [kv] + [over_chips(kv, j) for j in range(1, count)]
    q_pair = over_cores(queries)
    picked, w_half = pick(in_t, w_down, w_out)
    got = [over_tp(picked, 1)] + [over_tp(w_half, k) for k in range(2, n_tp)]

    split = (count + 1) // 2
    (state,) = attention_forward(0, False, *docs, queries, q_pair, blocks[:split])
    state_own, state_pair = attention_forward(
        split, True, *docs, queries, q_pair, blocks[split:], state
    )
    out_b, totals, out_mine, out_other = join(state_own, over_cores(state_pair))
    outs = everywhere([out_other if k % 2 else out_mine for k in range(n_tp)])
    out_pair = over_cores(out_b)
    totals_pair = over_cores(totals)

    got = pile(got, [(state_pair, "v")])
    staged = stage(n_tp, tokens, cotangent, in_t, w_down, w_out, got, over_cores(got))
    middle, middle_part, h_two, mixed, gate_grad, gain_two_part, own, *others = feed(
        gain_two, staged, outs
    )
    arrived = [own] + [over_tp(others[n], 2 * n + 2) for n in range(n_tp // 2 - 1)]
    own, *others = down(n_tp, mixed, staged[4], middle, [(out_pair, "v"), (totals_pair, "v")])
    middle_grad, branch_grad, *pieces = branch(
        n_tp, middle_part, cotangent, gain_two, staged[2], arrived, [(own, "v")]
    )
    early, early_send = early_grads(
        mixed, gate_grad, cotangent, h_two, in_t, w_down, over_tp(h_two, 1), [(branch_grad, "v")]
    )
    early_back = over_cores(early_send)
    out_grad = lay_turned(everywhere(pieces), ())
    grad_pair = over_cores(out_grad)
    branches = by_steps(branch_grad)

    held = (queries, q_pair, out_grad, grad_pair, out_b, out_pair, totals, totals_pair)
    *terms, dq = attention_backward(1, False, *docs, held, blocks[1:], None)
    total = total_of(
        [own] + [over_tp(others[n], 2 * n + 2) for n in range(n_tp // 2 - 1)],
        BF16,
        "v",
        [(dq, "v"), (branches[2], "v")],
    )
    totals_all = by_steps(total)

    dkv, dq_own, dq_pair = attention_backward(
        0, True, *docs, held, blocks[:1], dq, ()
    )
    dkvs = [dkv] + [over_chips(terms[j - 1], j) for j in range(1, count)]

    proj_grad, *parts = unproject(
        n_tp,
        tokens,
        qkv_t,
        cos_table,
        sin_table,
        gain_two_part,
        dq_own,
        over_cores(dq_pair),
        dkvs,
        [(total, "v")],
    )
    keep, send = late_grads(proj_grad, h_one, out_b, branches, [(totals_all[n_tp // 2], "v")])
    own, *others = spread(count, (keep, over_cores(send)), (early, early_back))
    summed = total_of(everywhere(parts), F32, flops=2_000_000_000)
    chip_sum = total_of(
        [own] + came(count, lambda k: over_chips(others[k - 1], k)), F32, "v", ()
    )
    input_part, gains = input_side(tokens, gain_one, middle_grad, summed, [(own, "v")])
    inputs_all = everywhere([input_part] * n_tp)
    piece = sum_piece(gains, [chip_sum], ())
    input_grad = stack_parts(inputs_all, (), 3_000_000_000)
    collected = collect(
        [piece] + came(count, lambda k: over_chips(piece, k)), [(input_grad, "h")]
    )
    sizes = (3 * width, width, units, 2 * units)
    pair = over_cores(collected)
    begun = begin(collected, sizes)
    layer_out = stack_parts(totals_all, [(begun[0], "h")])
    grad_qkv, grad_out, grad_down, grad_in, grad_one, grad_two = finish(
        begun, collected, pair, sizes
    )

    back = lambda x, n: x.reshape(-1, n, model).transpose(2, 0, 1)
    return (
        layer_out,
        input_grad,
        grad_one,
        back(grad_qkv, width),
        grad_out,
        grad_two,
        back(grad_in, units),
        grad_down,
    )


def solution(mesh):
    placed = (
        P("seq", None),
        P(),
        P(None, None, "tp"),
        P("tp", None),
        P(),
        P(None, None, "tp"),
        P("tp", None),
        P("seq", None),
        P(),
        P(),
    )
    return jax.shard_map(
        functools.partial(body, mesh.shape["seq"], mesh.shape["tp"]),
        mesh=mesh,
        in_specs=placed,
        out_specs=(
            P("seq", None),
            P("seq", None),
            P(),
            P(None, None, "tp"),
            P("tp", None),
            P(),
            P(None, None, "tp"),
            P("tp", None),
        ),
        check_vma=False,
    )
```

```python
import functools
import math

import jax
import jax.numpy as jnp
import numpy as np
from jax import lax
from jax.experimental import pallas as pl
from jax.experimental.pallas import tpu as pltpu
from jax.sharding import PartitionSpec as P

HDIM = 64
HALF = HDIM // 2
EPSILON = 1e-05
ROPE_THETA = 160000.0
MASKED = -1e30
AUG = 80
STRIP = 64
F32 = jnp.float32
BF16 = jnp.bfloat16
HBM = pl.BlockSpec(memory_space=pltpu.HBM)
VMEM = pl.BlockSpec(memory_space=pltpu.VMEM)

NN = (((1,), (0,)), ((), ()))
NT = (((1,), (1,)), ((), ()))
TN = (((0,), (0,)), ((), ()))


def params(mib):
    return pltpu.CompilerParams(vmem_limit_bytes=mib * 2**20)


def slot(tp, n_tp):
    return tp % 2 * (n_tp // 2) + tp // 2


def hop(n, count):
    return (count - n) % count


def came(count, send):
    return [send(hop(n, count)) for n in range(1, count)]


def mm(a, b, dims):
    return lax.dot_general(a, b, dims, preferred_element_type=F32)


def shaped(shape, dtype):
    return jax.ShapeDtypeStruct(shape, dtype)


def kinds(arrays, kind):
    return [(array, kind) for array in arrays]


def pin(array, kind):
    return array if kind in ("v", "free") else pltpu.with_memory_space_constraint(array, pltpu.HBM)


def call(name, kernel, ins, outs, scratch=(), mib=16, after=(), lazy=False, flops=0, alias=None):
    fetched = [i for i, given in enumerate(ins) if given[1] not in ("v", "raw", "free")]
    left = [i for i, out in enumerate(outs) if out[2] == "h"]

    def held(array, kind):
        rows = array.shape[0] if kind == "h" else kind
        return pltpu.VMEM((rows,) + array.shape[1:], array.dtype)

    def run(*refs):
        in_refs = list(refs[: len(ins)])
        at = len(ins) + len(after)
        out_refs = list(refs[at : at + len(outs)])
        at += len(outs)
        own = refs[at : at + len(scratch)]
        at += len(scratch)
        buffers = refs[at : at + len(fetched) + len(left)]
        sems = refs[-1]
        copies = []
        for n, i in enumerate(fetched):
            source = in_refs[i]
            if ins[i][1] != "h":
                rows = ins[i][1]
                n_tp = ins[i][0].shape[0] // rows
                at = pl.multiple_of(slot(lax.axis_index("tp"), n_tp) * rows, rows)
                source = source.at[pl.ds(at, rows)]
            copies.append(pltpu.make_async_copy(source, buffers[n], sems.at[n]))
            in_refs[i] = buffers[n]
        for copy in copies:
            copy.start()
        coming = dict(zip(fetched, copies))
        going = {}
        for n, i in enumerate(left):
            spot = len(fetched) + n
            going[i] = pltpu.make_async_copy(buffers[spot], out_refs[i], sems.at[spot])
            out_refs[i] = buffers[spot]
        gone = []

        def need(*which):
            for i in which:
                if i in coming:
                    coming.pop(i).wait()

        def give(*which):
            for i in which:
                if i in going:
                    gone.append(going.pop(i))
                    gone[-1].start()

        if lazy:
            kernel(need, give, *in_refs, *out_refs, *own)
        else:
            need(*fetched)
            kernel(*in_refs, *out_refs, *own)
        need(*fetched)
        give(*left)
        for copy in gone:
            copy.wait()

    spec = lambda kind: VMEM if kind == "v" else HBM
    count = len(fetched) + len(left)
    return pl.pallas_call(
        run,
        out_shape=tuple(
            shaped(shape, dtype) if kind == "v" else pltpu.HBM(shape, dtype)
            for shape, dtype, kind in outs
        ),
        in_specs=[spec(kind) for unused, kind in ins] + [spec(kind) for unused, kind in after],
        out_specs=tuple(spec(kind) for unused, unused, kind in outs),
        scratch_shapes=list(scratch)
        + [held(*ins[i]) for i in fetched]
        + [pltpu.VMEM(outs[i][0], outs[i][1]) for i in left]
        + [pltpu.SemaphoreType.DMA((max(count, 1),))],
        name=name,
        input_output_aliases=alias or {},
        cost_estimate=pl.CostEstimate(flops=flops, bytes_accessed=0, transcendentals=0)
        if flops
        else None,
        compiler_params=params(mib),
    )(*[pin(*given) for given in ins], *[pin(*given) for given in after])


def swap(x, axis, hop, count):
    return lax.ppermute(x, axis, [(i, i ^ hop) for i in range(count)])


def doc_scratch(doc_lengths, roster):
    return [pltpu.SMEM(doc_lengths.shape, jnp.int32), pltpu.SMEM(roster.shape, jnp.int32)]


def fetch_docs(len_any, roster_any, len_ref, roster_ref, len_sem, roster_sem):
    one = pltpu.make_async_copy(len_any, len_ref, len_sem)
    two = pltpu.make_async_copy(roster_any, roster_ref, roster_sem)
    one.start()
    two.start()
    one.wait()
    two.wait()


def doc_bounds(len_ref):
    ends, total = [], jnp.int32(0)
    for d in range(len_ref.shape[0]):
        total = total + len_ref[d]
        ends.append(total)
    return ends


def doc_of(ends, position):
    found = jnp.int32(0)
    for end in ends:
        found = found + (end <= position).astype(jnp.int32)
    return found


def meet(ends, base_a, base_b, rows):
    low = jnp.maximum(doc_of(ends, base_a), doc_of(ends, base_b))
    high = jnp.minimum(doc_of(ends, base_a + rows - 1), doc_of(ends, base_b + rows - 1))
    return low <= high


def doc_rows(ends, base, rows):
    spot = base + lax.broadcasted_iota(jnp.int32, (16, rows), 1)
    line = lax.broadcasted_iota(jnp.int32, (16, rows), 0)
    held = jnp.zeros((16, rows), F32)
    start = jnp.int32(0)
    for d, end in enumerate(ends):
        inside = (line == d) & (spot >= start) & (spot < end)
        held = jnp.where(inside, 1.0, held)
        start = end
    return held


def ban_rows(ends, base, rows):
    line = lax.broadcasted_iota(jnp.int32, (16, rows), 0)
    held = doc_rows(ends, base, rows)
    return jnp.where((held > 0.5) | (line >= len(ends)), 0.0, MASKED)


def key_row(block, seq_index):
    return seq_index ^ (2 * block)


def place_row(ends, base, rows):
    spot = base + lax.broadcasted_iota(jnp.int32, (1, rows), 1)
    start = jnp.zeros((1, rows), jnp.int32)
    for end in ends:
        start = jnp.where(spot >= end, end, start)
    return (spot - start).astype(F32)


def normed(values):
    centre = jnp.mean(values, axis=-1, keepdims=True)
    shifted = values - centre
    spread = jnp.mean(shifted * shifted, axis=-1, keepdims=True)
    scale = lax.rsqrt(spread + EPSILON)
    return shifted * scale, scale


def norm_back(unit, scale, grad, gain):
    u = grad * gain
    mean_u = jnp.mean(u, axis=-1, keepdims=True)
    mean_un = jnp.mean(u * unit, axis=-1, keepdims=True)
    return scale * (u - mean_u - unit * mean_un)


def project_kernel(
    width, need, give, len_any, roster_any, x_ref, w_ref, gain_ref, freq_ref, *refs
):
    q_out, kv_out, h_out, cos_out, sin_out = refs[:5]
    proj, len_ref, roster_ref, sems = refs[5:]
    rows = x_ref.shape[0]
    fetch_docs(len_any, roster_any, len_ref, roster_ref, sems.at[0], sems.at[1])
    need(5)
    ends = doc_bounds(len_ref)
    place = place_row(ends, roster_ref[lax.axis_index("seq")] * rows, rows)
    angles = place * freq_ref[...]
    cos_table = jnp.cos(angles)
    sin_table = jnp.sin(angles)
    cos_out[...] = cos_table
    sin_out[...] = sin_table
    give(3, 4)
    need(2, 4)
    gain = gain_ref[...].reshape(1, -1)

    def strip(i, carry):
        at = pl.ds(i * STRIP, STRIP)
        unit, unused = normed(x_ref[at, :].astype(F32))
        h_out[at, :] = (unit * gain).astype(BF16)
        return carry

    lax.fori_loop(0, rows // STRIP, strip, 0)
    give(2)
    need(3)
    proj[...] = mm(w_ref[...], h_out[...], NT)
    for at in range(0, 2 * width, HDIM):
        low = proj[at : at + HALF, :]
        high = proj[at + HALF : at + HDIM, :]
        turned_low = (low * cos_out[...] - high * sin_out[...]).astype(BF16)
        turned_high = (high * cos_out[...] + low * sin_out[...]).astype(BF16)
        if at < width:
            q_out[at : at + HALF, :] = (turned_low.astype(F32) * HDIM**-0.5).astype(BF16)
            q_out[at + HALF : at + HDIM, :] = (turned_high.astype(F32) * HDIM**-0.5).astype(BF16)
        else:
            kv_out[at - width : at - width + HALF, :] = turned_low
            kv_out[at - width + HALF : at - width + HDIM, :] = turned_high
    kv_out[width:, :] = proj[2 * width :, :].astype(BF16)


def project(doc_lengths, roster, tokens, gain, qkv_t):
    rows, model = tokens.shape
    width = qkv_t.shape[0] // 3
    freq = (ROPE_THETA ** -(np.arange(HALF) * (2.0 / HDIM))).astype(np.float32)[:, None]
    return call(
        "project",
        functools.partial(project_kernel, width),
        kinds((doc_lengths, roster), "raw") + kinds((tokens, qkv_t, gain, jnp.asarray(freq)), "h"),
        [
            ((width, rows), BF16, "v"),
            ((2 * width, rows), BF16, "v"),
            ((rows, model), BF16, "v"),
            ((HALF, rows), F32, "v"),
            ((HALF, rows), F32, "v"),
        ],
        [pltpu.VMEM((3 * width, rows), F32)]
        + doc_scratch(doc_lengths, roster)
        + [pltpu.SemaphoreType.DMA((2,))],
        lazy=True,
    )


def forward_kernel(first, count, heads, last, len_any, roster_any, q_own, q_pair, *refs):
    kv_refs = refs[:count]
    refs = refs[count:]
    if first:
        state_in, refs = refs[0], refs[1:]
    outs = refs[: 2 if last else 1]
    kv, q_aug, state, len_ref, roster_ref, sems = refs[len(outs) :]
    rows = q_own.shape[1]
    width = heads * HDIM
    me = lax.axis_index("seq")
    copies = [pltpu.make_async_copy(kv_refs[j], kv.at[j], sems.at[j]) for j in range(count)]
    for copy in copies:
        copy.start()
    fetch_docs(len_any, roster_any, len_ref, roster_ref, sems.at[count], sems.at[count + 1])
    ends = doc_bounds(len_ref)
    bases = (roster_ref[me] * rows, roster_ref[me ^ 1] * rows)
    for g, q_ref in enumerate((q_own, q_pair)):
        mark = doc_rows(ends, bases[g], rows).astype(BF16)
        for h in range(heads):
            q_aug[g * heads + h, :HDIM, :] = q_ref[h * HDIM : (h + 1) * HDIM, :]
            q_aug[g * heads + h, HDIM:, :] = mark
    if first:
        state[...] = state_in[...]
    else:
        line = lax.broadcasted_iota(jnp.int32, (2 * heads, AUG, rows), 1)
        state[...] = jnp.where(line >= 72, MASKED, 0.0)
    for copy in copies:
        copy.wait()

    top = lax.broadcasted_iota(jnp.int32, (16, rows), 0) == 0
    ones = jnp.where(top, 1.0, 0.0).astype(BF16)

    def block(j, carry):
        key_base = roster_ref[key_row(j + first, me)] * rows
        ban = ban_rows(ends, key_base, rows).astype(BF16)
        for g in range(2):

            @pl.when(meet(ends, bases[g], key_base, rows))
            def _():
                for h in range(heads):
                    at = g * heads + h
                    keys = jnp.concatenate([kv[j, h * HDIM : (h + 1) * HDIM, :], ban], axis=0)
                    vals = jnp.concatenate(
                        [kv[j, width + h * HDIM : width + (h + 1) * HDIM, :], ones], axis=0
                    )
                    scores = mm(keys, q_aug[at], TN)
                    old = state[at, 72:73, :]
                    new = jnp.maximum(old, jnp.max(scores, axis=0, keepdims=True))
                    probs = jnp.exp(scores - new).astype(BF16)
                    part = mm(vals, probs, NN)
                    fade = jnp.exp(old - new)
                    state[at, :72, :] = state[at, :72, :] * fade + part[:72]
                    state[at, 72:, :] = jnp.broadcast_to(new, (8, rows))

        return carry

    lax.fori_loop(0, count, block, 0)
    if last:
        outs[0][...] = state[:heads]
        outs[1][...] = state[heads:]
    else:
        outs[0][...] = state[...]


def attention_forward(first, last, doc_lengths, roster, q_own, q_pair, blocks, state=None, after=()):
    width, rows = q_own.shape
    heads = width // HDIM
    count = len(blocks)
    half = ((heads, AUG, rows), F32, "v")
    whole = ((2 * heads, AUG, rows), F32, "v")
    given = [] if state is None else [(state, "v")]
    return call(
        "attention_forward",
        functools.partial(forward_kernel, first, count, heads, last),
        [(doc_lengths, "raw"), (roster, "raw"), (q_own, "v"), (q_pair, "v")]
        + kinds(blocks, "free")
        + given,
        [half, half] if last else [whole],
        [
            pltpu.VMEM((count, 2 * width, rows), BF16),
            pltpu.VMEM((2 * heads, AUG, rows), BF16),
            pltpu.VMEM((2 * heads, AUG, rows), F32),
        ]
        + doc_scratch(doc_lengths, roster)
        + [pltpu.SemaphoreType.DMA((count + 2,))],
        16 if count < 8 else 40,
        after,
    )


def backward_kernel(first, count, heads, more, last, len_any, roster_any, *refs):
    q_own, q_pair, g_own, g_pair, o_own, o_pair, t_own, t_pair = refs[:8]
    kv_refs, refs = refs[8 : 8 + count], refs[8 + count :]
    if more:
        dq_in, refs = refs[0], refs[1:]
    outs, refs = refs[:count], refs[count:]
    dq_outs, refs = (refs[:2], refs[2:]) if last else (refs[:1], refs[1:])
    kv, q_aug, delta, dq, dkv, len_ref, roster_ref, sems = refs
    rows = q_own.shape[1]
    width = heads * HDIM
    me = lax.axis_index("seq")
    copies = [pltpu.make_async_copy(kv_refs[j], kv.at[j], sems.at[j]) for j in range(count)]
    for copy in copies:
        copy.start()
    fetch_docs(len_any, roster_any, len_ref, roster_ref, sems.at[count], sems.at[count + 1])
    ends = doc_bounds(len_ref)
    bases = (roster_ref[me] * rows, roster_ref[me ^ 1] * rows)
    for g, (q_ref, g_ref, o_ref) in enumerate(((q_own, g_own, o_own), (q_pair, g_pair, o_pair))):
        mark = doc_rows(ends, bases[g], rows).astype(BF16)
        for h in range(heads):
            part = slice(h * HDIM, (h + 1) * HDIM)
            q_aug[g * heads + h, :HDIM, :] = q_ref[part, :]
            q_aug[g * heads + h, HDIM:, :] = mark
            product = g_ref[part, :].astype(F32) * o_ref[part, :].astype(F32)
            delta[g * heads + h] = jnp.broadcast_to(
                jnp.sum(product, axis=0, keepdims=True), (8, rows)
            )
    if more:
        dq[...] = dq_in[...]
    else:
        dq[...] = jnp.zeros_like(dq)
    for copy in copies:
        copy.wait()

    def block(j, carry):
        key_base = roster_ref[key_row(j + first, me)] * rows
        ban = ban_rows(ends, key_base, rows).astype(BF16)
        dkv[j] = jnp.zeros((2 * width, rows), F32)
        for g, (g_ref, t_ref) in enumerate(((g_own, t_own), (g_pair, t_pair))):

            @pl.when(meet(ends, bases[g], key_base, rows))
            def _():
                for h in range(heads):
                    at = g * heads + h
                    part = slice(h * HDIM, (h + 1) * HDIM)
                    late = slice(width + h * HDIM, width + (h + 1) * HDIM)
                    keys = kv[j, part, :]
                    scores = mm(jnp.concatenate([keys, ban], axis=0), q_aug[at], TN)
                    probs = jnp.exp(scores - t_ref[h, 0:1, :])
                    prob_grads = mm(kv[j, late, :], g_ref[part, :], TN)
                    score_grad = (probs * (prob_grads - delta[at, 0:1, :])).astype(BF16)
                    dkv[j, late, :] += mm(g_ref[part, :], probs.astype(BF16), NT)
                    dkv[j, part, :] += mm(q_aug[at, :HDIM, :], score_grad, NT)
                    dq[at] += mm(keys, score_grad, NN)

        return carry

    lax.fori_loop(0, count, block, 0)
    for j in range(count):
        outs[j][...] = dkv[j].astype(outs[j].dtype)
    if last:
        for h in range(heads):
            part = slice(h * HDIM, (h + 1) * HDIM)
            dq_outs[0][part, :] = dq[h] * HDIM**-0.5
            dq_outs[1][part, :] = (dq[heads + h] * HDIM**-0.5).astype(BF16)
    else:
        dq_outs[0][...] = dq[...]


def attention_backward(first, last, doc_lengths, roster, held, blocks, dq=None, after=()):
    width, rows = held[0].shape
    heads = width // HDIM
    count = len(blocks)
    given = [] if dq is None else [(dq, "v")]
    if last:
        queries = [((width, rows), F32, "v"), ((width, rows), BF16, "v")]
    else:
        queries = [((2 * heads, HDIM, rows), F32, "v")]
    return call(
        "attention_backward",
        functools.partial(backward_kernel, first, count, heads, bool(given), last),
        kinds((doc_lengths, roster), "raw") + kinds(held, "v") + kinds(blocks, "free") + given,
        [((2 * width, rows), BF16 if first else F32, "v")] * count + queries,
        [
            pltpu.VMEM((count, 2 * width, rows), BF16),
            pltpu.VMEM((2 * heads, AUG, rows), BF16),
            pltpu.VMEM((2 * heads, 8, rows), F32),
            pltpu.VMEM((2 * heads, HDIM, rows), F32),
            pltpu.VMEM((count, 2 * width, rows), F32),
        ]
        + doc_scratch(doc_lengths, roster)
        + [pltpu.SemaphoreType.DMA((count + 2,))],
        16 if count < 8 else 40,
        after,
        flops=0 if last else 0,
    )


def join_kernel(heads, own_ref, back_ref, out_ref, total_ref, mine_ref, other_ref):
    rows = own_ref.shape[2]
    for h in range(heads):
        top_own = own_ref[h, 72:73, :]
        top_back = back_ref[h, 72:73, :]
        top = jnp.maximum(top_own, top_back)
        fade_own = jnp.exp(top_own - top)
        fade_back = jnp.exp(top_back - top)
        total = own_ref[h, 64:65, :] * fade_own + back_ref[h, 64:65, :] * fade_back
        share_own = fade_own / total
        share_back = fade_back / total
        value = own_ref[h, :HDIM, :] * share_own + back_ref[h, :HDIM, :] * share_back
        out_ref[h * HDIM : (h + 1) * HDIM, :] = value.astype(BF16)
        total_ref[h] = jnp.broadcast_to(top + jnp.log(total), (8, rows))
    half = rows // 2
    for bit in range(2):

        @pl.when(lax.axis_index("tp") % 2 == bit)
        def _():
            mine_ref[...] = out_ref[:, bit * half : (bit + 1) * half]
            other_ref[...] = out_ref[:, (1 - bit) * half : (2 - bit) * half]


def join(own, back):
    heads, unused, rows = own.shape
    return call(
        "join",
        functools.partial(join_kernel, heads),
        [(own, "v"), (back, "v")],
        [
            ((heads * HDIM, rows), BF16, "v"),
            ((heads, 8, rows), F32, "v"),
            ((heads * HDIM, rows // 2), BF16, "v"),
            ((heads * HDIM, rows // 2), BF16, "v"),
        ],
    )


def pick_kernel(in_any, down_any, w_any, all_ref, w_ref, sems):
    core = lax.axis_index("seq") % 2
    at = 0
    copies = []
    for source in (in_any, down_any, w_any):
        rows = source.shape[0] // 2
        mine = pl.ds(pl.multiple_of(core * rows, rows), rows)
        copies.append((source.at[mine], all_ref.at[pl.ds(at, rows)]))
        at += rows
    copies.append((w_any.at[mine], w_ref))
    copies = [pltpu.make_async_copy(*move, sems.at[n]) for n, move in enumerate(copies)]
    for copy in copies:
        copy.start()
    for copy in copies:
        copy.wait()


def pick(in_t, w_down, w_out):
    rows = (in_t.shape[0] + w_down.shape[0] + w_out.shape[0]) // 2
    model = w_out.shape[1]
    return call(
        "pick",
        pick_kernel,
        kinds((in_t, w_down, w_out), "raw"),
        [((rows, model), BF16, "v"), ((w_out.shape[0] // 2, model), BF16, "v")],
        [pltpu.SemaphoreType.DMA((4,))],
    )


def pile_kernel(*refs):
    out_ref = refs[-1]
    at = 0
    for ref in refs[:-1]:
        out_ref[at : at + ref.shape[0], :] = ref[...]
        at += ref.shape[0]


def pile(values, after):
    rows = sum(value.shape[0] for value in values)
    (out,) = call(
        "pile",
        pile_kernel,
        kinds(values, "v"),
        [((rows, values[0].shape[1]), BF16, "v")],
        (),
        16,
        after,
    )
    return out


def stage_kernel(x_any, cot_any, in_any, down_any, w_any, got_ref, rest_ref, *refs):
    x_ref, cot_ref, w_ref, in_ref, down_ref, sems = refs
    half = x_ref.shape[0]
    core = lax.axis_index("seq") % 2
    tp = lax.axis_index("tp")
    n_tp = w_ref.shape[0] // w_any.shape[0]
    mine = pl.ds(pl.multiple_of(tp % 2 * half, half), half)
    width = w_any.shape[0]
    rows = width // 2
    own = pl.ds(pl.multiple_of(tp * width, width), width)
    moves = [(w_any, w_ref.at[own]), (x_any.at[mine], x_ref), (cot_any.at[mine], cot_ref)]
    sides = ((got_ref, core), (rest_ref, 1 - core))
    first = got_ref.shape[0] - (n_tp - 1) * rows
    for k in range(1, n_tp):
        for source, side in sides:
            spot = pl.multiple_of((tp ^ k) * width + side * rows, rows)
            piece = source.at[pl.ds(first + (k - 1) * rows, rows)]
            moves.append((piece, w_ref.at[pl.ds(spot, rows)]))
    at = 0
    for own, ref in ((in_any, in_ref), (down_any, down_ref)):
        rows = own.shape[0] // 2
        moves.append((own, ref.at[pl.ds(0, 2 * rows)]))
        for source, side in sides:
            spot = pl.multiple_of(2 * rows + side * rows, rows)
            moves.append((source.at[pl.ds(at, rows)], ref.at[pl.ds(spot, rows)]))
        at += rows
    copies = [pltpu.make_async_copy(*move, sems.at[n]) for n, move in enumerate(moves)]
    for copy in copies:
        copy.start()
    for copy in copies:
        copy.wait()


def stage(n_tp, tokens, cotangent, in_t, w_down, w_out, got, rest):
    rows, model = tokens.shape
    return call(
        "stage",
        stage_kernel,
        kinds((tokens, cotangent, in_t, w_down, w_out), "raw") + kinds((got, rest), "v"),
        [
            ((rows // 2, model), BF16, "v"),
            ((rows // 2, model), BF16, "v"),
            ((n_tp * w_out.shape[0], model), BF16, "v"),
            ((2 * in_t.shape[0], model), BF16, "v"),
            ((2 * w_down.shape[0], model), BF16, "v"),
        ],
        [pltpu.SemaphoreType.DMA((7 + 2 * n_tp,))],
    )


def gated(units, first, gate_up, mixed_grad, mixed_out, gate_out):
    rows = math.gcd(units, 96)

    def wave(i, carry):
        spot = pl.ds(first + i * rows, rows)
        at = pl.ds(2 * first + i * rows, rows)
        late = pl.ds(2 * first + units + i * rows, rows)
        gate = gate_up[at, :]
        up = gate_up[late, :]
        back = mixed_grad[spot, :]
        bell = 0.5 * (1.0 + lax.erf(gate * (2.0**-0.5)))
        active = gate * bell
        slope = bell + gate * jnp.exp(-0.5 * gate * gate) * ((2.0 * jnp.pi) ** -0.5)
        mixed_out[spot, :] = (active * up).astype(BF16)
        gate_out[at, :] = (back * up * slope).astype(BF16)
        gate_out[late, :] = (back * active).astype(BF16)
        return carry

    lax.fori_loop(0, units // rows, wave, 0)


def feed_kernel(n_tp, need, give, x_ref, cot_ref, w_ref, in_ref, down_ref, gain_ref, *refs):
    out_refs = refs[:n_tp]
    middle_out, part_out, h_out, mixed_out, gate_out, gain_out = refs[n_tp : n_tp + 6]
    keep_ref, *send_refs = refs[n_tp + 6 : n_tp + 6 + n_tp // 2]
    outs, unit, gate_up, mixed_grad, grad = refs[n_tp + 6 + n_tp // 2 :]
    rows = x_ref.shape[0]
    part = keep_ref.shape[0]
    units = down_ref.shape[0] // 2
    width = out_refs[0].shape[0]
    tp = lax.axis_index("tp")
    for k in range(n_tp):
        at = pl.ds(pl.multiple_of((tp ^ hop(k, n_tp)) * width, width), width)
        outs[at, :] = out_refs[k][...]
    mixed_grad[...] = mm(down_ref[...], cot_ref[...], NT)
    middle_out[...] = mm(outs[...], w_ref[...], TN)
    need(5)
    gain = gain_ref[...].reshape(1, -1)

    def strip(i, carry):
        at = pl.ds(i * 32, 32)
        middle = middle_out[at, :] + x_ref[at, :].astype(F32)
        middle_out[at, :] = middle
        held, unused = normed(middle)
        unit[at, :] = held
        h_out[at, :] = (held * gain).astype(BF16)
        return carry

    lax.fori_loop(0, rows // 32, strip, 0)
    give(0, 2)
    gate_up[...] = mm(in_ref[...], h_out[...], NT)
    for first in (0, units):
        gated(units, first, gate_up, mixed_grad, mixed_out, gate_out)
    give(3, 4)
    grad[...] = mm(gate_out[...], in_ref[...], TN)
    for n, ref in enumerate((keep_ref, *send_refs)):
        at = pl.ds(pl.multiple_of((tp ^ (2 * n)) // 2 * part, part), part)
        ref[...] = grad[at, :].astype(ref.dtype)
        give(6 + n)
    own = pl.ds(pl.multiple_of(tp // 2 * part, part), part)
    part_out[...] = middle_out[own, :]
    give(1)

    def gains(i, carry):
        at = pl.ds(i * 32, 32)
        product = grad[at, :] * unit[at, :]
        return carry + jnp.sum(product.reshape(4, 8, -1), axis=0)

    gain_out[...] = lax.fori_loop(0, rows // 32, gains, jnp.zeros(gain_out.shape, F32))


def feed(gain, staged, outs):
    rows, model = staged[0].shape
    n_tp = len(outs)
    units = staged[4].shape[0]
    part = 2 * rows // n_tp
    return call(
        "feed",
        functools.partial(feed_kernel, n_tp),
        kinds(staged, "v") + [(gain, "h")] + kinds(outs, "v"),
        [
            ((rows, model), F32, "v"),
            ((part, model), F32, "v"),
            ((rows, model), BF16, "v"),
            ((units, rows), BF16, "v"),
            ((2 * units, rows), BF16, "v"),
            ((8, model), F32, "v"),
            ((part, model), F32, "v"),
        ]
        + [((part, model), BF16, "v")] * (n_tp // 2 - 1),
        [
            pltpu.VMEM((n_tp * outs[0].shape[0], rows), BF16),
            pltpu.VMEM((rows, model), F32),
            pltpu.VMEM((2 * units, rows), F32),
            pltpu.VMEM((units, rows), F32),
            pltpu.VMEM((rows, model), F32),
        ],
        24,
        lazy=True,
    )


def branch_kernel(n_tp, count, need, give, middle_ref, cot_ref, gain_ref, w_ref, *refs):
    arrived = refs[:count]
    grad_out, branch_out = refs[count : count + 2]
    piece_refs = refs[count + 2 :]
    width = piece_refs[0].shape[1]
    tp = lax.axis_index("tp")
    need(0, 1, 2, 4)
    total = arrived[0][...]
    for ref in arrived[1:]:
        total = total + ref[...].astype(F32)
    unit, scale = normed(middle_ref[...])
    gain = gain_ref[...].reshape(1, -1)
    value = cot_ref[...].astype(F32) + norm_back(unit, scale, total, gain)
    grad_out[...] = value
    branch_out[...] = value.astype(BF16)
    give(0, 1)
    need(3)
    for k in range(n_tp):
        at = pl.ds(pl.multiple_of((tp ^ k) * width, width), width)
        piece_refs[k][...] = mm(branch_out[...], w_ref[at, :], NT).astype(BF16)


def branch(n_tp, middle_part, cotangent, gain, w_full, arrived, after):
    part, model = arrived[0].shape
    width = w_full.shape[0] // n_tp
    return call(
        "branch",
        functools.partial(branch_kernel, n_tp, len(arrived)),
        [(middle_part, "v"), (cotangent, part)]
        + [(gain, "h"), (w_full, "v"), (arrived[0], "v")]
        + kinds(arrived[1:], "v"),
        [((part, model), F32, "v"), ((part, model), BF16, "v")]
        + [((part, width), BF16, "v")] * n_tp,
        (),
        16,
        after,
        True,
    )


def lay_kernel(n_tp, *refs):
    out_ref, held = refs[n_tp:]
    part = refs[0].shape[0]
    tp = lax.axis_index("tp")
    for k in range(n_tp):
        at = pl.ds(pl.multiple_of(slot(tp ^ hop(k, n_tp), n_tp) * part, part), part)
        held[at, :] = refs[k][...].astype(F32)
    out_ref[...] = held[...].T.astype(BF16)


def lay_turned(pieces, after):
    part, width = pieces[0].shape
    rows = part * len(pieces)
    (out,) = call(
        "lay_turned",
        functools.partial(lay_kernel, len(pieces)),
        kinds(pieces, "v"),
        [((width, rows), BF16, "v")],
        [pltpu.VMEM((rows, width), F32)],
        16,
        after,
    )
    return out


def stack_kernel(n_tp, *refs):
    out_ref = refs[n_tp]
    part = refs[0].shape[0]
    tp = lax.axis_index("tp")
    for k in range(n_tp):
        at = pl.ds(pl.multiple_of(slot(tp ^ hop(k, n_tp), n_tp) * part, part), part)
        out_ref[at, :] = refs[k][...]


def stack_parts(pieces, after=(), flops=0):
    part, model = pieces[0].shape
    (out,) = call(
        "stack_parts",
        functools.partial(stack_kernel, len(pieces)),
        kinds(pieces, "v"),
        [((part * len(pieces), model), pieces[0].dtype, "h")],
        (),
        16,
        after,
        flops=flops,
    )
    return out


def turn_back(out_ref, first, value, cos_table, sin_table):
    for at in range(0, value.shape[0], HDIM):
        low = value[at : at + HALF]
        high = value[at + HALF : at + HDIM]
        spot = first + at
        out_ref[spot : spot + HALF, :] = (low * cos_table + high * sin_table).astype(BF16)
        out_ref[spot + HALF : spot + HDIM, :] = (high * cos_table - low * sin_table).astype(BF16)


def unproject_kernel(
    count, n_tp, need, give, x_ref, w_ref, cos_ref, sin_ref, two_ref, dq_ref, dq_back, *refs
):
    dkv_refs = refs[:count]
    proj_out = refs[count]
    part_refs = refs[count + 1 : count + 1 + n_tp]
    grad, dkv = refs[count + 1 + n_tp :]
    rows, model = x_ref.shape
    part = rows // n_tp
    width = dq_ref.shape[0]
    tp = lax.axis_index("tp")
    need(2, 3)
    cos_table = cos_ref[...]
    sin_table = sin_ref[...]
    turn_back(proj_out, 0, dq_ref[...] + dq_back[...].astype(F32), cos_table, sin_table)
    total = dkv_refs[0][...]
    for ref in dkv_refs[1:]:
        total = total + ref[...].astype(F32)
    dkv[...] = total
    turn_back(proj_out, width, dkv[:width, :], cos_table, sin_table)
    proj_out[2 * width :, :] = dkv[width:, :].astype(BF16)
    need(1)
    grad[...] = mm(proj_out[...], w_ref[...], TN)
    need(0, 4)

    def gains(i, carry):
        at = pl.ds(i * STRIP, STRIP)
        unit, unused = normed(x_ref[at, :].astype(F32))
        product = grad[at, :] * unit
        return carry + jnp.sum(product.reshape(STRIP // 8, 8, -1), axis=0)

    gain = lax.fori_loop(0, rows // STRIP, gains, jnp.zeros((8, model), F32))
    line = lax.broadcasted_iota(jnp.int32, (16, model), 0)
    gain_two = jnp.sum(two_ref[...], axis=0, keepdims=True)
    gain = jnp.sum(gain, axis=0, keepdims=True)
    gain = jnp.where(line == 0, gain, jnp.where(line == 1, gain_two, 0.0))
    for k in range(n_tp):
        at = pl.ds(pl.multiple_of(slot(tp ^ k, n_tp) * part, part), part)
        part_refs[k][:part, :] = grad[at, :].astype(part_refs[k].dtype)
        part_refs[k][part:, :] = gain.astype(part_refs[k].dtype)


def unproject(n_tp, tokens, qkv_t, cos_table, sin_table, gain_two_part, dq, dq_back, dkvs, after):
    rows, model = tokens.shape
    part = rows // n_tp
    return call(
        "unproject",
        functools.partial(unproject_kernel, len(dkvs), n_tp),
        kinds((tokens, qkv_t, cos_table, sin_table, gain_two_part), "v")
        + kinds((dq, dq_back, *dkvs), "v"),
        [((qkv_t.shape[0], rows), BF16, "v"), ((part + 16, model), F32, "v")]
        + [((part + 16, model), BF16, "v")] * (n_tp - 1),
        [pltpu.VMEM((rows, model), F32), pltpu.VMEM(dkvs[0].shape, F32)],
        16,
        after,
        True,
    )


def input_kernel(x_ref, gain_ref, grad_ref, sum_ref, out_ref, gain_out):
    part, model = grad_ref.shape
    total = sum_ref[...]
    unit, scale = normed(x_ref[...].astype(F32))
    gain = gain_ref[...].reshape(1, -1)
    value = grad_ref[...] + norm_back(unit, scale, total[:part], gain)
    out_ref[...] = value.astype(BF16)
    gain_out[...] = total[part : part + 8]


def input_side(tokens, gain, middle_grad, summed, after):
    part, model = middle_grad.shape
    return call(
        "input_side",
        input_kernel,
        [(tokens, part), (gain, "h"), (middle_grad, "v"), (summed, "v")],
        [((part, model), BF16, "v"), ((8, model), F32, "v")],
        (),
        16,
        after,
    )


def early_kernel(mixed_ref, gate_ref, cot_ref, h_ref, in_ref, down_ref, h_pair, *refs):
    keep_ref, send_ref, gate_up, mixed_grad, mixed, gate = refs
    units = down_ref.shape[0]
    half = h_ref.shape[0]
    bit = lax.axis_index("tp") % 2
    mine = pl.ds(pl.multiple_of(bit * half, half), half)
    other = pl.ds(pl.multiple_of((1 - bit) * half, half), half)
    gate_up[...] = mm(in_ref[...], h_pair[...], NT)
    mixed_grad[...] = mm(down_ref[...], cot_ref[other, :], NT)
    gated(units, 0, gate_up, mixed_grad, mixed, gate)
    width = keep_ref.shape[1]
    core = lax.axis_index("seq") % 2
    for ref, side in ((send_ref, 1 - core), (keep_ref, core)):
        columns = pl.ds(pl.multiple_of(side * width, width), width)
        down = mm(mixed_ref[:units, :], cot_ref[mine, columns], NN)
        down = down + mm(mixed[...], cot_ref[other, columns], NN)
        ref[:units, :] = down.astype(ref.dtype)
        both = mm(gate_ref[: 2 * units, :], h_ref[:, columns], NN)
        both = both + mm(gate[...], h_pair[:, columns], NN)
        ref[units:, :] = both.astype(ref.dtype)


def early_grads(mixed, gate_grad, cotangent, h_two, in_t, w_down, h_pair, after):
    units, model = w_down.shape
    half = h_two.shape[0]
    return call(
        "early_grads",
        early_kernel,
        kinds((mixed, gate_grad, cotangent, h_two, in_t, w_down, h_pair), "v"),
        [((3 * units, model // 2), F32, "v"), ((3 * units, model // 2), BF16, "v")],
        [
            pltpu.VMEM((2 * units, half), F32),
            pltpu.VMEM((units, half), F32),
            pltpu.VMEM((units, half), BF16),
            pltpu.VMEM((2 * units, half), BF16),
        ],
        24,
        after,
    )


def late_kernel(n_tp, proj_ref, h_ref, out_ref, *refs):
    branch_refs = refs[:n_tp]
    keep_ref, send_ref, branch_full = refs[n_tp:]
    part = branch_refs[0].shape[0]
    half = keep_ref.shape[1]
    wide = proj_ref.shape[0]
    tp = lax.axis_index("tp")
    core = lax.axis_index("seq") % 2
    for k in range(n_tp):
        at = pl.ds(pl.multiple_of(slot(tp ^ hop(k, n_tp), n_tp) * part, part), part)
        branch_full[at, :] = branch_refs[k][...]
    for ref, side in ((send_ref, 1 - core), (keep_ref, core)):
        columns = pl.ds(pl.multiple_of(side * half, half), half)
        ref[:wide, :] = mm(proj_ref[...], h_ref[:, columns], NN).astype(ref.dtype)
        ref[wide:, :] = mm(out_ref[...], branch_full[:, columns], NN).astype(ref.dtype)


def late_grads(proj_grad, h_one, out_b, branches, after):
    rows, model = h_one.shape
    wide = proj_grad.shape[0] + out_b.shape[0]
    return call(
        "late_grads",
        functools.partial(late_kernel, len(branches)),
        [(proj_grad, "v"), (h_one, "v"), (out_b, "v"), (branches[0], "v")]
        + kinds(branches[1:], "v"),
        [((wide, model // 2), F32, "v"), ((wide, model // 2), BF16, "v")],
        [pltpu.VMEM((rows, model), BF16)],
        16,
        after,
    )


def spread_kernel(count, *refs):
    given, outs, held = refs[: -count - 1], refs[-count - 1 : -1], refs[-1]
    piece = outs[0].shape[0]
    chip = lax.axis_index("seq") // 2
    at = 0
    for keep_ref, back_ref in zip(given[::2], given[1::2]):
        rows = keep_ref.shape[0]
        held[at : at + rows, :] = keep_ref[...] + back_ref[...].astype(F32)
        at += rows
    if at < held.shape[0]:
        held[at:, :] = jnp.zeros((held.shape[0] - at, held.shape[1]), F32)
    for k in range(count):
        at = pl.ds(pl.multiple_of((chip ^ k) * piece, piece), piece)
        outs[k][...] = held[at, :].astype(outs[k].dtype)


def spread(count, *pairs):
    half = pairs[0][0].shape[1]
    rows = sum(keep.shape[0] for keep, unused in pairs)
    piece = -(-rows // (8 * count)) * 8
    return call(
        "spread",
        functools.partial(spread_kernel, count),
        [(array, "v") for pair in pairs for array in pair],
        [((piece, half), F32, "v")] + [((piece, half), BF16, "v")] * (count - 1),
        [pltpu.VMEM((count * piece, half), F32)],
    )


def piece_kernel(count, gain_ref, *refs):
    out_ref = refs[count]
    half = out_ref.shape[1]
    total = refs[0][...]
    for ref in refs[1:count]:
        total = total + ref[...].astype(F32)
    line = lax.broadcasted_iota(jnp.int32, (16, half), 0)
    gains = jnp.zeros((16, half), F32)
    for at in range(4):
        row = gain_ref[at // 2 : at // 2 + 1, at % 2 * half : (at % 2 + 1) * half]
        gains = jnp.where(line == at, row, gains)
    out_ref[...] = jnp.concatenate([total, gains], axis=0).astype(BF16)


def sum_piece(gains, pieces, after=()):
    piece, half = pieces[0].shape
    (out,) = call(
        "sum_piece",
        functools.partial(piece_kernel, len(pieces)),
        [(gains, "v")] + kinds(pieces, "v"),
        [((piece + 16, half), BF16, "v")],
        (),
        16,
        after,
    )
    return out


def collect_kernel(count, *refs):
    out_ref, held = refs[count:]
    piece = refs[0].shape[0] - 16
    wide = count * piece
    chip = lax.axis_index("seq") // 2
    gains = jnp.zeros((16, out_ref.shape[1]), F32)
    for k in range(count):
        at = pl.ds(pl.multiple_of((chip ^ hop(k, count)) * piece, piece), piece)
        whole = refs[k][...].astype(F32)
        held[at, :] = whole[:piece]
        gains = gains + whole[piece:]
    held[wide:, :] = gains
    out_ref[...] = held[...].astype(BF16)


def collect(pieces, after=()):
    piece, half = pieces[0].shape
    wide = (piece - 16) * len(pieces) + 16
    (out,) = call(
        "collect",
        functools.partial(collect_kernel, len(pieces)),
        kinds(pieces, "v"),
        [((wide, half), BF16, "v")],
        [pltpu.VMEM((wide, half), F32)],
        16,
        after,
    )
    return out


def write_half(sizes, source, side, out_refs, held, sems):
    half = source.shape[1]
    columns = pl.ds(pl.multiple_of(side * half, half), half)
    at = 0
    copies = []
    for n, (ref, size) in enumerate(zip(out_refs, sizes)):
        rows = pl.ds(at, size)
        held[rows, :] = source[rows, :].astype(F32)
        copies.append(pltpu.make_async_copy(held.at[rows], ref.at[:, columns], sems.at[n]))
        copies[-1].start()
        at += size
    return copies


def own_kernel(sizes, own_ref, *refs):
    out_refs, held, sems = refs[:-2], refs[-2], refs[-1]
    core = lax.axis_index("seq") % 2
    for copy in write_half(sizes, own_ref, core, out_refs, held, sems):
        copy.wait()


def pair_kernel(sizes, own_ref, pair_ref, *refs):
    refs = refs[len(sizes) :]
    out_refs, gain_refs = refs[: len(sizes)], refs[len(sizes) : len(sizes) + 2]
    held, sems = refs[-2:]
    core = lax.axis_index("seq") % 2
    copies = write_half(sizes, pair_ref, 1 - core, out_refs, held, sems)
    half = own_ref.shape[1]
    first = own_ref.shape[0] - 16
    gains = own_ref[first:, :].astype(F32) + pair_ref[first:, :].astype(F32)
    for at, ref in zip((0, 2), gain_refs):
        ref[pl.ds(0, half)] = gains[at]
        ref[pl.ds(half, half)] = gains[at + 1]
    for copy in copies:
        copy.wait()


def half_scratch(sizes, half):
    return [pltpu.VMEM((sum(sizes), half), F32), pltpu.SemaphoreType.DMA((len(sizes),))]


def begin(own, sizes):
    half = own.shape[1]
    return call(
        "own_half",
        functools.partial(own_kernel, sizes),
        [(own, "v")],
        [((size, 2 * half), F32, "raw") for size in sizes],
        half_scratch(sizes, half),
    )


def finish(begun, own, pair, sizes):
    half = own.shape[1]
    return call(
        "pair_half",
        functools.partial(pair_kernel, sizes),
        [(own, "v"), (pair, "v")] + kinds(begun, "raw"),
        [((size, 2 * half), F32, "raw") for size in sizes] + [((2 * half,), F32, "h")] * 2,
        half_scratch(sizes, half),
        alias={2 + n: n for n in range(len(sizes))},
    )


def down_kernel(mixed_ref, w_ref, middle_ref, keep_ref, *refs):
    send_refs, total = refs[:-1], refs[-1]
    part = keep_ref.shape[0]
    tp = lax.axis_index("tp")
    total[...] = mm(mixed_ref[...], w_ref[...], TN)
    own = pl.ds(pl.multiple_of(tp // 2 * part, part), part)
    keep_ref[...] = total[own, :] + middle_ref[own, :]
    for n, ref in enumerate(send_refs):
        at = pl.ds(pl.multiple_of((tp ^ (2 * n + 2)) // 2 * part, part), part)
        ref[...] = total[at, :].astype(ref.dtype)


def down(n_tp, mixed, w_both, middle, after):
    rows, model = middle.shape
    part = 2 * rows // n_tp
    return call(
        "down",
        down_kernel,
        kinds((mixed, w_both, middle), "v"),
        [((part, model), F32, "v")] + [((part, model), BF16, "v")] * (n_tp // 2 - 1),
        [pltpu.VMEM((rows, model), F32)],
        16,
        after,
    )


def total_kernel(count, *refs):
    total = refs[0][...]
    for ref in refs[1:count]:
        total = total + ref[...].astype(F32)
    refs[count][...] = total.astype(refs[count].dtype)


def total_of(parts, dtype=BF16, kind="v", after=(), flops=0):
    (out,) = call(
        "total_of",
        functools.partial(total_kernel, len(parts)),
        [(parts[0], kind)] + kinds(parts[1:], "v"),
        [(parts[0].shape, dtype, "v")],
        (),
        16,
        after,
        flops=flops,
    )
    return out


def body(
    n_seq,
    n_tp,
    tokens,
    gain_one,
    w_qkv,
    w_out,
    gain_two,
    w_in,
    w_down,
    cotangent,
    doc_lengths,
    roster,
):
    rows, model = tokens.shape
    width = w_qkv.shape[2]
    units = w_in.shape[2]
    count = n_seq // 2
    qkv_t = w_qkv.transpose(1, 2, 0).reshape(3 * width, model)
    in_t = w_in.transpose(1, 2, 0).reshape(2 * units, model)
    over_tp = lambda x, k: swap(x, "tp", k, n_tp)
    over_chips = lambda x, k: swap(x, "seq", 2 * k, n_seq)
    over_cores = lambda x: swap(x, "seq", 1, n_seq)
    everywhere = lambda xs: [xs[0]] + came(n_tp, lambda k: over_tp(xs[k], k))

    def by_steps(part):
        parts = {0: part}
        step = n_tp // 2
        while step:
            parts.update({k ^ step: over_tp(x, step) for k, x in parts.items()})
            step //= 2
        return [parts[hop(n, n_tp)] for n in range(n_tp)]

    docs = (doc_lengths, roster)

    queries, kv, h_one, cos_table, sin_table = project(*docs, tokens, gain_one, qkv_t)
    blocks = [kv] + [over_chips(kv, j) for j in range(1, count)]
    q_pair = over_cores(queries)
    picked, w_half = pick(in_t, w_down, w_out)
    got = [over_tp(picked, 1)] + [over_tp(w_half, k) for k in range(2, n_tp)]

    split = (count + 1) // 2
    (state,) = attention_forward(0, False, *docs, queries, q_pair, blocks[:split])
    state_own, state_pair = attention_forward(
        split, True, *docs, queries, q_pair, blocks[split:], state
    )
    out_b, totals, out_mine, out_other = join(state_own, over_cores(state_pair))
    outs = everywhere([out_other if k % 2 else out_mine for k in range(n_tp)])
    out_pair = over_cores(out_b)
    totals_pair = over_cores(totals)

    got = pile(got, [(state_pair, "v")])
    staged = stage(n_tp, tokens, cotangent, in_t, w_down, w_out, got, over_cores(got))
    middle, middle_part, h_two, mixed, gate_grad, gain_two_part, own, *others = feed(
        gain_two, staged, outs
    )
    arrived = [own] + [over_tp(others[n], 2 * n + 2) for n in range(n_tp // 2 - 1)]
    own, *others = down(n_tp, mixed, staged[4], middle, [(out_pair, "v"), (totals_pair, "v")])
    middle_grad, branch_grad, *pieces = branch(
        n_tp, middle_part, cotangent, gain_two, staged[2], arrived, [(own, "v")]
    )
    early, early_send = early_grads(
        mixed, gate_grad, cotangent, h_two, in_t, w_down, over_tp(h_two, 1), [(branch_grad, "v")]
    )
    early_back = over_cores(early_send)
    out_grad = lay_turned(everywhere(pieces), ())
    grad_pair = over_cores(out_grad)
    branches = by_steps(branch_grad)

    held = (queries, q_pair, out_grad, grad_pair, out_b, out_pair, totals, totals_pair)
    *terms, dq = attention_backward(1, False, *docs, held, blocks[1:], None)
    total = total_of(
        [own] + [over_tp(others[n], 2 * n + 2) for n in range(n_tp // 2 - 1)],
        BF16,
        "v",
        [(dq, "v"), (branches[2], "v")],
    )
    totals_all = by_steps(total)

    dkv, dq_own, dq_pair = attention_backward(
        0, True, *docs, held, blocks[:1], dq, ()
    )
    dkvs = [dkv] + [over_chips(terms[j - 1], j) for j in range(1, count)]

    proj_grad, *parts = unproject(
        n_tp,
        tokens,
        qkv_t,
        cos_table,
        sin_table,
        gain_two_part,
        dq_own,
        over_cores(dq_pair),
        dkvs,
        [(total, "v")],
    )
    layer_out = stack_parts(totals_all, [(proj_grad, "v"), (branches[1], "v"), (branches[3], "v")])
    keep, send = late_grads(proj_grad, h_one, out_b, branches, [(layer_out, "h")])
    own, *others = spread(count, (keep, over_cores(send)), (early, early_back))
    summed = total_of(everywhere(parts), F32, flops=2_000_000_000)
    chip_sum = total_of(
        [own] + came(count, lambda k: over_chips(others[k - 1], k)), F32, "v", ()
    )
    input_part, gains = input_side(tokens, gain_one, middle_grad, summed, [(own, "v")])
    inputs_all = everywhere([input_part] * n_tp)
    piece = sum_piece(gains, [chip_sum], ())
    input_grad = stack_parts(inputs_all, (), 3_000_000_000)
    collected = collect(
        [piece] + came(count, lambda k: over_chips(piece, k)), [(input_grad, "h")]
    )
    sizes = (3 * width, width, units, 2 * units)
    pair = over_cores(collected)
    begun = begin(collected, sizes)
    grad_qkv, grad_out, grad_down, grad_in, grad_one, grad_two = finish(
        begun, collected, pair, sizes
    )

    back = lambda x, n: x.reshape(-1, n, model).transpose(2, 0, 1)
    return (
        layer_out,
        input_grad,
        grad_one,
        back(grad_qkv, width),
        grad_out,
        grad_two,
        back(grad_in, units),
        grad_down,
    )


def solution(mesh):
    placed = (
        P("seq", None),
        P(),
        P(None, None, "tp"),
        P("tp", None),
        P(),
        P(None, None, "tp"),
        P("tp", None),
        P("seq", None),
        P(),
        P(),
    )
    return jax.shard_map(
        functools.partial(body, mesh.shape["seq"], mesh.shape["tp"]),
        mesh=mesh,
        in_specs=placed,
        out_specs=(
            P("seq", None),
            P("seq", None),
            P(),
            P(None, None, "tp"),
            P("tp", None),
            P(),
            P(None, None, "tp"),
            P("tp", None),
        ),
        check_vma=False,
    )
```

```python
import functools
import math

import jax
import jax.numpy as jnp
import numpy as np
from jax import lax
from jax.experimental import pallas as pl
from jax.experimental.pallas import tpu as pltpu
from jax.sharding import PartitionSpec as P

HDIM = 64
HALF = HDIM // 2
EPSILON = 1e-05
ROPE_THETA = 160000.0
MASKED = -1e30
AUG = 80
STRIP = 64
F32 = jnp.float32
BF16 = jnp.bfloat16
HBM = pl.BlockSpec(memory_space=pltpu.HBM)
VMEM = pl.BlockSpec(memory_space=pltpu.VMEM)

NN = (((1,), (0,)), ((), ()))
NT = (((1,), (1,)), ((), ()))
TN = (((0,), (0,)), ((), ()))


def params(mib):
    return pltpu.CompilerParams(vmem_limit_bytes=mib * 2**20)


def slot(tp, n_tp):
    return tp % 2 * (n_tp // 2) + tp // 2


def hop(n, count):
    return (count - n) % count


def came(count, send):
    return [send(hop(n, count)) for n in range(1, count)]


def mm(a, b, dims):
    return lax.dot_general(a, b, dims, preferred_element_type=F32)


def shaped(shape, dtype):
    return jax.ShapeDtypeStruct(shape, dtype)


def kinds(arrays, kind):
    return [(array, kind) for array in arrays]


def pin(array, kind):
    return array if kind in ("v", "free") else pltpu.with_memory_space_constraint(array, pltpu.HBM)


def call(name, kernel, ins, outs, scratch=(), mib=16, after=(), lazy=False, flops=0, alias=None):
    fetched = [i for i, given in enumerate(ins) if given[1] not in ("v", "raw", "free")]
    left = [i for i, out in enumerate(outs) if out[2] == "h"]

    def held(array, kind):
        rows = array.shape[0] if kind == "h" else kind
        return pltpu.VMEM((rows,) + array.shape[1:], array.dtype)

    def run(*refs):
        in_refs = list(refs[: len(ins)])
        at = len(ins) + len(after)
        out_refs = list(refs[at : at + len(outs)])
        at += len(outs)
        own = refs[at : at + len(scratch)]
        at += len(scratch)
        buffers = refs[at : at + len(fetched) + len(left)]
        sems = refs[-1]
        copies = []
        for n, i in enumerate(fetched):
            source = in_refs[i]
            if ins[i][1] != "h":
                rows = ins[i][1]
                n_tp = ins[i][0].shape[0] // rows
                at = pl.multiple_of(slot(lax.axis_index("tp"), n_tp) * rows, rows)
                source = source.at[pl.ds(at, rows)]
            copies.append(pltpu.make_async_copy(source, buffers[n], sems.at[n]))
            in_refs[i] = buffers[n]
        for copy in copies:
            copy.start()
        coming = dict(zip(fetched, copies))
        going = {}
        for n, i in enumerate(left):
            spot = len(fetched) + n
            going[i] = pltpu.make_async_copy(buffers[spot], out_refs[i], sems.at[spot])
            out_refs[i] = buffers[spot]
        gone = []

        def need(*which):
            for i in which:
                if i in coming:
                    coming.pop(i).wait()

        def give(*which):
            for i in which:
                if i in going:
                    gone.append(going.pop(i))
                    gone[-1].start()

        if lazy:
            kernel(need, give, *in_refs, *out_refs, *own)
        else:
            need(*fetched)
            kernel(*in_refs, *out_refs, *own)
        need(*fetched)
        give(*left)
        for copy in gone:
            copy.wait()

    spec = lambda kind: VMEM if kind == "v" else HBM
    count = len(fetched) + len(left)
    return pl.pallas_call(
        run,
        out_shape=tuple(
            shaped(shape, dtype) if kind == "v" else pltpu.HBM(shape, dtype)
            for shape, dtype, kind in outs
        ),
        in_specs=[spec(kind) for unused, kind in ins] + [spec(kind) for unused, kind in after],
        out_specs=tuple(spec(kind) for unused, unused, kind in outs),
        scratch_shapes=list(scratch)
        + [held(*ins[i]) for i in fetched]
        + [pltpu.VMEM(outs[i][0], outs[i][1]) for i in left]
        + [pltpu.SemaphoreType.DMA((max(count, 1),))],
        name=name,
        input_output_aliases=alias or {},
        cost_estimate=pl.CostEstimate(flops=flops, bytes_accessed=0, transcendentals=0)
        if flops
        else None,
        compiler_params=params(mib),
    )(*[pin(*given) for given in ins], *[pin(*given) for given in after])


def swap(x, axis, hop, count):
    return lax.ppermute(x, axis, [(i, i ^ hop) for i in range(count)])


def doc_scratch(doc_lengths, roster):
    return [pltpu.SMEM(doc_lengths.shape, jnp.int32), pltpu.SMEM(roster.shape, jnp.int32)]


def fetch_docs(len_any, roster_any, len_ref, roster_ref, len_sem, roster_sem):
    one = pltpu.make_async_copy(len_any, len_ref, len_sem)
    two = pltpu.make_async_copy(roster_any, roster_ref, roster_sem)
    one.start()
    two.start()
    one.wait()
    two.wait()


def doc_bounds(len_ref):
    ends, total = [], jnp.int32(0)
    for d in range(len_ref.shape[0]):
        total = total + len_ref[d]
        ends.append(total)
    return ends


def doc_of(ends, position):
    found = jnp.int32(0)
    for end in ends:
        found = found + (end <= position).astype(jnp.int32)
    return found


def meet(ends, base_a, base_b, rows):
    low = jnp.maximum(doc_of(ends, base_a), doc_of(ends, base_b))
    high = jnp.minimum(doc_of(ends, base_a + rows - 1), doc_of(ends, base_b + rows - 1))
    return low <= high


def doc_rows(ends, base, rows):
    spot = base + lax.broadcasted_iota(jnp.int32, (16, rows), 1)
    line = lax.broadcasted_iota(jnp.int32, (16, rows), 0)
    held = jnp.zeros((16, rows), F32)
    start = jnp.int32(0)
    for d, end in enumerate(ends):
        inside = (line == d) & (spot >= start) & (spot < end)
        held = jnp.where(inside, 1.0, held)
        start = end
    return held


def ban_rows(ends, base, rows):
    line = lax.broadcasted_iota(jnp.int32, (16, rows), 0)
    held = doc_rows(ends, base, rows)
    return jnp.where((held > 0.5) | (line >= len(ends)), 0.0, MASKED)


def key_row(block, seq_index):
    return seq_index ^ (2 * block)


def place_row(ends, base, rows):
    spot = base + lax.broadcasted_iota(jnp.int32, (1, rows), 1)
    start = jnp.zeros((1, rows), jnp.int32)
    for end in ends:
        start = jnp.where(spot >= end, end, start)
    return (spot - start).astype(F32)


def normed(values):
    centre = jnp.mean(values, axis=-1, keepdims=True)
    shifted = values - centre
    spread = jnp.mean(shifted * shifted, axis=-1, keepdims=True)
    scale = lax.rsqrt(spread + EPSILON)
    return shifted * scale, scale


def norm_back(unit, scale, grad, gain):
    u = grad * gain
    mean_u = jnp.mean(u, axis=-1, keepdims=True)
    mean_un = jnp.mean(u * unit, axis=-1, keepdims=True)
    return scale * (u - mean_u - unit * mean_un)


def project_kernel(
    width, need, give, len_any, roster_any, x_ref, w_ref, gain_ref, freq_ref, *refs
):
    q_out, kv_out, h_out, cos_out, sin_out = refs[:5]
    proj, len_ref, roster_ref, sems = refs[5:]
    rows = x_ref.shape[0]
    fetch_docs(len_any, roster_any, len_ref, roster_ref, sems.at[0], sems.at[1])
    need(5)
    ends = doc_bounds(len_ref)
    place = place_row(ends, roster_ref[lax.axis_index("seq")] * rows, rows)
    angles = place * freq_ref[...]
    cos_table = jnp.cos(angles)
    sin_table = jnp.sin(angles)
    cos_out[...] = cos_table
    sin_out[...] = sin_table
    give(3, 4)
    need(2, 4)
    gain = gain_ref[...].reshape(1, -1)

    def strip(i, carry):
        at = pl.ds(i * STRIP, STRIP)
        unit, unused = normed(x_ref[at, :].astype(F32))
        h_out[at, :] = (unit * gain).astype(BF16)
        return carry

    lax.fori_loop(0, rows // STRIP, strip, 0)
    give(2)
    need(3)
    proj[...] = mm(w_ref[...], h_out[...], NT)
    for at in range(0, 2 * width, HDIM):
        low = proj[at : at + HALF, :]
        high = proj[at + HALF : at + HDIM, :]
        turned_low = (low * cos_out[...] - high * sin_out[...]).astype(BF16)
        turned_high = (high * cos_out[...] + low * sin_out[...]).astype(BF16)
        if at < width:
            q_out[at : at + HALF, :] = (turned_low.astype(F32) * HDIM**-0.5).astype(BF16)
            q_out[at + HALF : at + HDIM, :] = (turned_high.astype(F32) * HDIM**-0.5).astype(BF16)
        else:
            kv_out[at - width : at - width + HALF, :] = turned_low
            kv_out[at - width + HALF : at - width + HDIM, :] = turned_high
    kv_out[width:, :] = proj[2 * width :, :].astype(BF16)


def project(doc_lengths, roster, tokens, gain, qkv_t):
    rows, model = tokens.shape
    width = qkv_t.shape[0] // 3
    freq = (ROPE_THETA ** -(np.arange(HALF) * (2.0 / HDIM))).astype(np.float32)[:, None]
    return call(
        "project",
        functools.partial(project_kernel, width),
        kinds((doc_lengths, roster), "raw") + kinds((tokens, qkv_t, gain, jnp.asarray(freq)), "h"),
        [
            ((width, rows), BF16, "v"),
            ((2 * width, rows), BF16, "v"),
            ((rows, model), BF16, "v"),
            ((HALF, rows), F32, "v"),
            ((HALF, rows), F32, "v"),
        ],
        [pltpu.VMEM((3 * width, rows), F32)]
        + doc_scratch(doc_lengths, roster)
        + [pltpu.SemaphoreType.DMA((2,))],
        lazy=True,
    )


def forward_kernel(first, count, heads, last, len_any, roster_any, q_own, q_pair, *refs):
    kv_refs = refs[:count]
    refs = refs[count:]
    if first:
        state_in, refs = refs[0], refs[1:]
    outs = refs[: 2 if last else 1]
    kv, q_aug, state, len_ref, roster_ref, sems = refs[len(outs) :]
    rows = q_own.shape[1]
    width = heads * HDIM
    me = lax.axis_index("seq")
    copies = [pltpu.make_async_copy(kv_refs[j], kv.at[j], sems.at[j]) for j in range(count)]
    for copy in copies:
        copy.start()
    fetch_docs(len_any, roster_any, len_ref, roster_ref, sems.at[count], sems.at[count + 1])
    ends = doc_bounds(len_ref)
    bases = (roster_ref[me] * rows, roster_ref[me ^ 1] * rows)
    for g, q_ref in enumerate((q_own, q_pair)):
        mark = doc_rows(ends, bases[g], rows).astype(BF16)
        for h in range(heads):
            q_aug[g * heads + h, :HDIM, :] = q_ref[h * HDIM : (h + 1) * HDIM, :]
            q_aug[g * heads + h, HDIM:, :] = mark
    if first:
        state[...] = state_in[...]
    else:
        line = lax.broadcasted_iota(jnp.int32, (2 * heads, AUG, rows), 1)
        state[...] = jnp.where(line >= 72, MASKED, 0.0)
    for copy in copies:
        copy.wait()

    top = lax.broadcasted_iota(jnp.int32, (16, rows), 0) == 0
    ones = jnp.where(top, 1.0, 0.0).astype(BF16)

    def block(j, carry):
        key_base = roster_ref[key_row(j + first, me)] * rows
        ban = ban_rows(ends, key_base, rows).astype(BF16)
        for g in range(2):

            @pl.when(meet(ends, bases[g], key_base, rows))
            def _():
                for h in range(heads):
                    at = g * heads + h
                    keys = jnp.concatenate([kv[j, h * HDIM : (h + 1) * HDIM, :], ban], axis=0)
                    vals = jnp.concatenate(
                        [kv[j, width + h * HDIM : width + (h + 1) * HDIM, :], ones], axis=0
                    )
                    scores = mm(keys, q_aug[at], TN)
                    old = state[at, 72:73, :]
                    new = jnp.maximum(old, jnp.max(scores, axis=0, keepdims=True))
                    probs = jnp.exp(scores - new).astype(BF16)
                    part = mm(vals, probs, NN)
                    fade = jnp.exp(old - new)
                    state[at, :72, :] = state[at, :72, :] * fade + part[:72]
                    state[at, 72:, :] = jnp.broadcast_to(new, (8, rows))

        return carry

    lax.fori_loop(0, count, block, 0)
    if last:
        outs[0][...] = state[:heads]
        outs[1][...] = state[heads:]
    else:
        outs[0][...] = state[...]


def attention_forward(first, last, doc_lengths, roster, q_own, q_pair, blocks, state=None, after=()):
    width, rows = q_own.shape
    heads = width // HDIM
    count = len(blocks)
    half = ((heads, AUG, rows), F32, "v")
    whole = ((2 * heads, AUG, rows), F32, "v")
    given = [] if state is None else [(state, "v")]
    return call(
        "attention_forward",
        functools.partial(forward_kernel, first, count, heads, last),
        [(doc_lengths, "raw"), (roster, "raw"), (q_own, "v"), (q_pair, "v")]
        + kinds(blocks, "free")
        + given,
        [half, half] if last else [whole],
        [
            pltpu.VMEM((count, 2 * width, rows), BF16),
            pltpu.VMEM((2 * heads, AUG, rows), BF16),
            pltpu.VMEM((2 * heads, AUG, rows), F32),
        ]
        + doc_scratch(doc_lengths, roster)
        + [pltpu.SemaphoreType.DMA((count + 2,))],
        16 if count < 8 else 40,
        after,
    )


def backward_kernel(first, count, heads, more, last, len_any, roster_any, *refs):
    q_own, q_pair, g_own, g_pair, o_own, o_pair, t_own, t_pair = refs[:8]
    kv_refs, refs = refs[8 : 8 + count], refs[8 + count :]
    if more:
        dq_in, refs = refs[0], refs[1:]
    outs, refs = refs[:count], refs[count:]
    dq_outs, refs = (refs[:2], refs[2:]) if last else (refs[:1], refs[1:])
    kv, q_aug, delta, dq, dkv, len_ref, roster_ref, sems = refs
    rows = q_own.shape[1]
    width = heads * HDIM
    me = lax.axis_index("seq")
    copies = [pltpu.make_async_copy(kv_refs[j], kv.at[j], sems.at[j]) for j in range(count)]
    for copy in copies:
        copy.start()
    fetch_docs(len_any, roster_any, len_ref, roster_ref, sems.at[count], sems.at[count + 1])
    ends = doc_bounds(len_ref)
    bases = (roster_ref[me] * rows, roster_ref[me ^ 1] * rows)
    for g, (q_ref, g_ref, o_ref) in enumerate(((q_own, g_own, o_own), (q_pair, g_pair, o_pair))):
        mark = doc_rows(ends, bases[g], rows).astype(BF16)
        for h in range(heads):
            part = slice(h * HDIM, (h + 1) * HDIM)
            q_aug[g * heads + h, :HDIM, :] = q_ref[part, :]
            q_aug[g * heads + h, HDIM:, :] = mark
            product = g_ref[part, :].astype(F32) * o_ref[part, :].astype(F32)
            delta[g * heads + h] = jnp.broadcast_to(
                jnp.sum(product, axis=0, keepdims=True), (8, rows)
            )
    if more:
        dq[...] = dq_in[...]
    else:
        dq[...] = jnp.zeros_like(dq)
    for copy in copies:
        copy.wait()

    def block(j, carry):
        key_base = roster_ref[key_row(j + first, me)] * rows
        ban = ban_rows(ends, key_base, rows).astype(BF16)
        dkv[j] = jnp.zeros((2 * width, rows), F32)
        for g, (g_ref, t_ref) in enumerate(((g_own, t_own), (g_pair, t_pair))):

            @pl.when(meet(ends, bases[g], key_base, rows))
            def _():
                for h in range(heads):
                    at = g * heads + h
                    part = slice(h * HDIM, (h + 1) * HDIM)
                    late = slice(width + h * HDIM, width + (h + 1) * HDIM)
                    keys = kv[j, part, :]
                    scores = mm(jnp.concatenate([keys, ban], axis=0), q_aug[at], TN)
                    probs = jnp.exp(scores - t_ref[h, 0:1, :])
                    prob_grads = mm(kv[j, late, :], g_ref[part, :], TN)
                    score_grad = (probs * (prob_grads - delta[at, 0:1, :])).astype(BF16)
                    dkv[j, late, :] += mm(g_ref[part, :], probs.astype(BF16), NT)
                    dkv[j, part, :] += mm(q_aug[at, :HDIM, :], score_grad, NT)
                    dq[at] += mm(keys, score_grad, NN)

        return carry

    lax.fori_loop(0, count, block, 0)
    for j in range(count):
        outs[j][...] = dkv[j].astype(outs[j].dtype)
    if last:
        for h in range(heads):
            part = slice(h * HDIM, (h + 1) * HDIM)
            dq_outs[0][part, :] = dq[h] * HDIM**-0.5
            dq_outs[1][part, :] = (dq[heads + h] * HDIM**-0.5).astype(BF16)
    else:
        dq_outs[0][...] = dq[...]


def attention_backward(first, last, doc_lengths, roster, held, blocks, dq=None, after=()):
    width, rows = held[0].shape
    heads = width // HDIM
    count = len(blocks)
    given = [] if dq is None else [(dq, "v")]
    if last:
        queries = [((width, rows), F32, "v"), ((width, rows), BF16, "v")]
    else:
        queries = [((2 * heads, HDIM, rows), F32, "v")]
    return call(
        "attention_backward",
        functools.partial(backward_kernel, first, count, heads, bool(given), last),
        kinds((doc_lengths, roster), "raw") + kinds(held, "v") + kinds(blocks, "free") + given,
        [((2 * width, rows), BF16 if first else F32, "v")] * count + queries,
        [
            pltpu.VMEM((count, 2 * width, rows), BF16),
            pltpu.VMEM((2 * heads, AUG, rows), BF16),
            pltpu.VMEM((2 * heads, 8, rows), F32),
            pltpu.VMEM((2 * heads, HDIM, rows), F32),
            pltpu.VMEM((count, 2 * width, rows), F32),
        ]
        + doc_scratch(doc_lengths, roster)
        + [pltpu.SemaphoreType.DMA((count + 2,))],
        16 if count < 8 else 40,
        after,
        flops=0 if last else 0,
    )


def join_kernel(heads, own_ref, back_ref, out_ref, total_ref, mine_ref, other_ref):
    rows = own_ref.shape[2]
    for h in range(heads):
        top_own = own_ref[h, 72:73, :]
        top_back = back_ref[h, 72:73, :]
        top = jnp.maximum(top_own, top_back)
        fade_own = jnp.exp(top_own - top)
        fade_back = jnp.exp(top_back - top)
        total = own_ref[h, 64:65, :] * fade_own + back_ref[h, 64:65, :] * fade_back
        share_own = fade_own / total
        share_back = fade_back / total
        value = own_ref[h, :HDIM, :] * share_own + back_ref[h, :HDIM, :] * share_back
        out_ref[h * HDIM : (h + 1) * HDIM, :] = value.astype(BF16)
        total_ref[h] = jnp.broadcast_to(top + jnp.log(total), (8, rows))
    half = rows // 2
    for bit in range(2):

        @pl.when(lax.axis_index("tp") % 2 == bit)
        def _():
            mine_ref[...] = out_ref[:, bit * half : (bit + 1) * half]
            other_ref[...] = out_ref[:, (1 - bit) * half : (2 - bit) * half]


def join(own, back):
    heads, unused, rows = own.shape
    return call(
        "join",
        functools.partial(join_kernel, heads),
        [(own, "v"), (back, "v")],
        [
            ((heads * HDIM, rows), BF16, "v"),
            ((heads, 8, rows), F32, "v"),
            ((heads * HDIM, rows // 2), BF16, "v"),
            ((heads * HDIM, rows // 2), BF16, "v"),
        ],
    )


def pick_kernel(in_any, down_any, w_any, all_ref, w_ref, sems):
    core = lax.axis_index("seq") % 2
    at = 0
    copies = []
    for source in (in_any, down_any, w_any):
        rows = source.shape[0] // 2
        mine = pl.ds(pl.multiple_of(core * rows, rows), rows)
        copies.append((source.at[mine], all_ref.at[pl.ds(at, rows)]))
        at += rows
    copies.append((w_any.at[mine], w_ref))
    copies = [pltpu.make_async_copy(*move, sems.at[n]) for n, move in enumerate(copies)]
    for copy in copies:
        copy.start()
    for copy in copies:
        copy.wait()


def pick(in_t, w_down, w_out):
    rows = (in_t.shape[0] + w_down.shape[0] + w_out.shape[0]) // 2
    model = w_out.shape[1]
    return call(
        "pick",
        pick_kernel,
        kinds((in_t, w_down, w_out), "raw"),
        [((rows, model), BF16, "v"), ((w_out.shape[0] // 2, model), BF16, "v")],
        [pltpu.SemaphoreType.DMA((4,))],
    )


def pile_kernel(*refs):
    out_ref = refs[-1]
    at = 0
    for ref in refs[:-1]:
        out_ref[at : at + ref.shape[0], :] = ref[...]
        at += ref.shape[0]


def pile(values, after):
    rows = sum(value.shape[0] for value in values)
    (out,) = call(
        "pile",
        pile_kernel,
        kinds(values, "v"),
        [((rows, values[0].shape[1]), BF16, "v")],
        (),
        16,
        after,
    )
    return out


def stage_kernel(x_any, cot_any, in_any, down_any, w_any, got_ref, rest_ref, *refs):
    x_ref, cot_ref, w_ref, in_ref, down_ref, sems = refs
    half = x_ref.shape[0]
    core = lax.axis_index("seq") % 2
    tp = lax.axis_index("tp")
    n_tp = w_ref.shape[0] // w_any.shape[0]
    mine = pl.ds(pl.multiple_of(tp % 2 * half, half), half)
    width = w_any.shape[0]
    rows = width // 2
    own = pl.ds(pl.multiple_of(tp * width, width), width)
    moves = [(w_any, w_ref.at[own]), (x_any.at[mine], x_ref), (cot_any.at[mine], cot_ref)]
    sides = ((got_ref, core), (rest_ref, 1 - core))
    first = got_ref.shape[0] - (n_tp - 1) * rows
    for k in range(1, n_tp):
        for source, side in sides:
            spot = pl.multiple_of((tp ^ k) * width + side * rows, rows)
            piece = source.at[pl.ds(first + (k - 1) * rows, rows)]
            moves.append((piece, w_ref.at[pl.ds(spot, rows)]))
    at = 0
    for own, ref in ((in_any, in_ref), (down_any, down_ref)):
        rows = own.shape[0] // 2
        moves.append((own, ref.at[pl.ds(0, 2 * rows)]))
        for source, side in sides:
            spot = pl.multiple_of(2 * rows + side * rows, rows)
            moves.append((source.at[pl.ds(at, rows)], ref.at[pl.ds(spot, rows)]))
        at += rows
    copies = [pltpu.make_async_copy(*move, sems.at[n]) for n, move in enumerate(moves)]
    for copy in copies:
        copy.start()
    for copy in copies:
        copy.wait()


def stage(n_tp, tokens, cotangent, in_t, w_down, w_out, got, rest):
    rows, model = tokens.shape
    return call(
        "stage",
        stage_kernel,
        kinds((tokens, cotangent, in_t, w_down, w_out), "raw") + kinds((got, rest), "v"),
        [
            ((rows // 2, model), BF16, "v"),
            ((rows // 2, model), BF16, "v"),
            ((n_tp * w_out.shape[0], model), BF16, "v"),
            ((2 * in_t.shape[0], model), BF16, "v"),
            ((2 * w_down.shape[0], model), BF16, "v"),
        ],
        [pltpu.SemaphoreType.DMA((7 + 2 * n_tp,))],
    )


def gated(units, first, gate_up, mixed_grad, mixed_out, gate_out):
    rows = math.gcd(units, 96)

    def wave(i, carry):
        spot = pl.ds(first + i * rows, rows)
        at = pl.ds(2 * first + i * rows, rows)
        late = pl.ds(2 * first + units + i * rows, rows)
        gate = gate_up[at, :]
        up = gate_up[late, :]
        back = mixed_grad[spot, :]
        bell = 0.5 * (1.0 + lax.erf(gate * (2.0**-0.5)))
        active = gate * bell
        slope = bell + gate * jnp.exp(-0.5 * gate * gate) * ((2.0 * jnp.pi) ** -0.5)
        mixed_out[spot, :] = (active * up).astype(BF16)
        gate_out[at, :] = (back * up * slope).astype(BF16)
        gate_out[late, :] = (back * active).astype(BF16)
        return carry

    lax.fori_loop(0, units // rows, wave, 0)


def feed_kernel(n_tp, need, give, x_ref, cot_ref, w_ref, in_ref, down_ref, gain_ref, *refs):
    out_refs = refs[:n_tp]
    middle_out, part_out, h_out, mixed_out, gate_out, gain_out = refs[n_tp : n_tp + 6]
    keep_ref, *send_refs = refs[n_tp + 6 : n_tp + 6 + n_tp // 2]
    outs, unit, gate_up, mixed_grad, grad = refs[n_tp + 6 + n_tp // 2 :]
    rows = x_ref.shape[0]
    part = keep_ref.shape[0]
    units = down_ref.shape[0] // 2
    width = out_refs[0].shape[0]
    tp = lax.axis_index("tp")
    for k in range(n_tp):
        at = pl.ds(pl.multiple_of((tp ^ hop(k, n_tp)) * width, width), width)
        outs[at, :] = out_refs[k][...]
    mixed_grad[...] = mm(down_ref[...], cot_ref[...], NT)
    middle_out[...] = mm(outs[...], w_ref[...], TN)
    need(5)
    gain = gain_ref[...].reshape(1, -1)

    def strip(i, carry):
        at = pl.ds(i * 32, 32)
        middle = middle_out[at, :] + x_ref[at, :].astype(F32)
        middle_out[at, :] = middle
        held, unused = normed(middle)
        unit[at, :] = held
        h_out[at, :] = (held * gain).astype(BF16)
        return carry

    lax.fori_loop(0, rows // 32, strip, 0)
    give(0, 2)
    gate_up[...] = mm(in_ref[...], h_out[...], NT)
    for first in (0, units):
        gated(units, first, gate_up, mixed_grad, mixed_out, gate_out)
    give(3, 4)
    grad[...] = mm(gate_out[...], in_ref[...], TN)
    for n, ref in enumerate((keep_ref, *send_refs)):
        at = pl.ds(pl.multiple_of((tp ^ (2 * n)) // 2 * part, part), part)
        ref[...] = grad[at, :].astype(ref.dtype)
        give(6 + n)
    own = pl.ds(pl.multiple_of(tp // 2 * part, part), part)
    part_out[...] = middle_out[own, :]
    give(1)

    def gains(i, carry):
        at = pl.ds(i * 32, 32)
        product = grad[at, :] * unit[at, :]
        return carry + jnp.sum(product.reshape(4, 8, -1), axis=0)

    gain_out[...] = lax.fori_loop(0, rows // 32, gains, jnp.zeros(gain_out.shape, F32))


def feed(gain, staged, outs):
    rows, model = staged[0].shape
    n_tp = len(outs)
    units = staged[4].shape[0]
    part = 2 * rows // n_tp
    return call(
        "feed",
        functools.partial(feed_kernel, n_tp),
        kinds(staged, "v") + [(gain, "h")] + kinds(outs, "v"),
        [
            ((rows, model), F32, "v"),
            ((part, model), F32, "v"),
            ((rows, model), BF16, "v"),
            ((units, rows), BF16, "v"),
            ((2 * units, rows), BF16, "v"),
            ((8, model), F32, "v"),
            ((part, model), F32, "v"),
        ]
        + [((part, model), BF16, "v")] * (n_tp // 2 - 1),
        [
            pltpu.VMEM((n_tp * outs[0].shape[0], rows), BF16),
            pltpu.VMEM((rows, model), F32),
            pltpu.VMEM((2 * units, rows), F32),
            pltpu.VMEM((units, rows), F32),
            pltpu.VMEM((rows, model), F32),
        ],
        24,
        lazy=True,
    )


def branch_kernel(n_tp, count, need, give, middle_ref, cot_ref, gain_ref, w_ref, *refs):
    arrived = refs[:count]
    grad_out, branch_out = refs[count : count + 2]
    piece_refs = refs[count + 2 :]
    width = piece_refs[0].shape[1]
    tp = lax.axis_index("tp")
    need(0, 1, 2, 4)
    total = arrived[0][...]
    for ref in arrived[1:]:
        total = total + ref[...].astype(F32)
    unit, scale = normed(middle_ref[...])
    gain = gain_ref[...].reshape(1, -1)
    value = cot_ref[...].astype(F32) + norm_back(unit, scale, total, gain)
    grad_out[...] = value
    branch_out[...] = value.astype(BF16)
    give(0, 1)
    need(3)
    for k in range(n_tp):
        at = pl.ds(pl.multiple_of((tp ^ k) * width, width), width)
        piece_refs[k][...] = mm(branch_out[...], w_ref[at, :], NT).astype(BF16)


def branch(n_tp, middle_part, cotangent, gain, w_full, arrived, after):
    part, model = arrived[0].shape
    width = w_full.shape[0] // n_tp
    return call(
        "branch",
        functools.partial(branch_kernel, n_tp, len(arrived)),
        [(middle_part, "v"), (cotangent, part)]
        + [(gain, "h"), (w_full, "v"), (arrived[0], "v")]
        + kinds(arrived[1:], "v"),
        [((part, model), F32, "v"), ((part, model), BF16, "v")]
        + [((part, width), BF16, "v")] * n_tp,
        (),
        16,
        after,
        True,
    )


def lay_kernel(n_tp, *refs):
    out_ref, held = refs[n_tp:]
    part = refs[0].shape[0]
    tp = lax.axis_index("tp")
    for k in range(n_tp):
        at = pl.ds(pl.multiple_of(slot(tp ^ hop(k, n_tp), n_tp) * part, part), part)
        held[at, :] = refs[k][...].astype(F32)
    out_ref[...] = held[...].T.astype(BF16)


def lay_turned(pieces, after):
    part, width = pieces[0].shape
    rows = part * len(pieces)
    (out,) = call(
        "lay_turned",
        functools.partial(lay_kernel, len(pieces)),
        kinds(pieces, "v"),
        [((width, rows), BF16, "v")],
        [pltpu.VMEM((rows, width), F32)],
        16,
        after,
    )
    return out


def lay_rows(out_ref, n_tp, places, refs):
    part = out_ref.shape[0] // n_tp
    tp = lax.axis_index("tp")
    for ks, ref in zip(places, refs):
        for n, k in enumerate(ks):
            at = pl.ds(pl.multiple_of(slot(tp ^ k, n_tp) * part, part), part)
            out_ref[at, :] = ref[n * part : (n + 1) * part, :]


def stack_kernel(n_tp, places, *refs):
    lay_rows(refs[-1], n_tp, places, refs[:-1])


def stack_parts(n_tp, pieces, places, after=(), flops=0):
    part, model = pieces[0].shape
    (out,) = call(
        "stack_parts",
        functools.partial(stack_kernel, n_tp, places),
        kinds(pieces, "v"),
        [((part * n_tp, model), pieces[0].dtype, "h")],
        (),
        16,
        after,
        flops=flops,
    )
    return out


def turn_back(out_ref, first, value, cos_table, sin_table):
    for at in range(0, value.shape[0], HDIM):
        low = value[at : at + HALF]
        high = value[at + HALF : at + HDIM]
        spot = first + at
        out_ref[spot : spot + HALF, :] = (low * cos_table + high * sin_table).astype(BF16)
        out_ref[spot + HALF : spot + HDIM, :] = (high * cos_table - low * sin_table).astype(BF16)


def unproject_kernel(
    count, n_tp, need, give, x_ref, w_ref, cos_ref, sin_ref, two_ref, dq_ref, dq_back, *refs
):
    dkv_refs = refs[:count]
    proj_out = refs[count]
    part_refs = refs[count + 1 : count + 1 + n_tp]
    grad, dkv = refs[count + 1 + n_tp :]
    rows, model = x_ref.shape
    part = rows // n_tp
    width = dq_ref.shape[0]
    tp = lax.axis_index("tp")
    need(2, 3)
    cos_table = cos_ref[...]
    sin_table = sin_ref[...]
    turn_back(proj_out, 0, dq_ref[...] + dq_back[...].astype(F32), cos_table, sin_table)
    total = dkv_refs[0][...]
    for ref in dkv_refs[1:]:
        total = total + ref[...].astype(F32)
    dkv[...] = total
    turn_back(proj_out, width, dkv[:width, :], cos_table, sin_table)
    proj_out[2 * width :, :] = dkv[width:, :].astype(BF16)
    need(1)
    grad[...] = mm(proj_out[...], w_ref[...], TN)
    need(0, 4)

    def gains(i, carry):
        at = pl.ds(i * STRIP, STRIP)
        unit, unused = normed(x_ref[at, :].astype(F32))
        product = grad[at, :] * unit
        return carry + jnp.sum(product.reshape(STRIP // 8, 8, -1), axis=0)

    gain = lax.fori_loop(0, rows // STRIP, gains, jnp.zeros((8, model), F32))
    line = lax.broadcasted_iota(jnp.int32, (16, model), 0)
    gain_two = jnp.sum(two_ref[...], axis=0, keepdims=True)
    gain = jnp.sum(gain, axis=0, keepdims=True)
    gain = jnp.where(line == 0, gain, jnp.where(line == 1, gain_two, 0.0))
    for k in range(n_tp):
        at = pl.ds(pl.multiple_of(slot(tp ^ k, n_tp) * part, part), part)
        part_refs[k][:part, :] = grad[at, :].astype(part_refs[k].dtype)
        part_refs[k][part:, :] = gain.astype(part_refs[k].dtype)


def unproject(n_tp, tokens, qkv_t, cos_table, sin_table, gain_two_part, dq, dq_back, dkvs, after):
    rows, model = tokens.shape
    part = rows // n_tp
    return call(
        "unproject",
        functools.partial(unproject_kernel, len(dkvs), n_tp),
        kinds((tokens, qkv_t, cos_table, sin_table, gain_two_part), "v")
        + kinds((dq, dq_back, *dkvs), "v"),
        [((qkv_t.shape[0], rows), BF16, "v"), ((part + 16, model), F32, "v")]
        + [((part + 16, model), BF16, "v")] * (n_tp - 1),
        [pltpu.VMEM((rows, model), F32), pltpu.VMEM(dkvs[0].shape, F32)],
        16,
        after,
        True,
    )


def input_kernel(x_ref, gain_ref, grad_ref, sum_ref, out_ref, gain_out):
    part, model = grad_ref.shape
    total = sum_ref[...]
    unit, scale = normed(x_ref[...].astype(F32))
    gain = gain_ref[...].reshape(1, -1)
    value = grad_ref[...] + norm_back(unit, scale, total[:part], gain)
    out_ref[...] = value.astype(BF16)
    gain_out[...] = total[part : part + 8]


def input_side(tokens, gain, middle_grad, summed, after):
    part, model = middle_grad.shape
    return call(
        "input_side",
        input_kernel,
        [(tokens, part), (gain, "h"), (middle_grad, "v"), (summed, "v")],
        [((part, model), BF16, "v"), ((8, model), F32, "v")],
        (),
        16,
        after,
    )


def early_kernel(mixed_ref, gate_ref, cot_ref, h_ref, in_ref, down_ref, h_pair, *refs):
    keep_ref, send_ref, gate_up, mixed_grad, mixed, gate = refs
    units = down_ref.shape[0]
    half = h_ref.shape[0]
    bit = lax.axis_index("tp") % 2
    mine = pl.ds(pl.multiple_of(bit * half, half), half)
    other = pl.ds(pl.multiple_of((1 - bit) * half, half), half)
    gate_up[...] = mm(in_ref[...], h_pair[...], NT)
    mixed_grad[...] = mm(down_ref[...], cot_ref[other, :], NT)
    gated(units, 0, gate_up, mixed_grad, mixed, gate)
    width = keep_ref.shape[1]
    core = lax.axis_index("seq") % 2
    for ref, side in ((send_ref, 1 - core), (keep_ref, core)):
        columns = pl.ds(pl.multiple_of(side * width, width), width)
        down = mm(mixed_ref[:units, :], cot_ref[mine, columns], NN)
        down = down + mm(mixed[...], cot_ref[other, columns], NN)
        ref[:units, :] = down.astype(ref.dtype)
        both = mm(gate_ref[: 2 * units, :], h_ref[:, columns], NN)
        both = both + mm(gate[...], h_pair[:, columns], NN)
        ref[units:, :] = both.astype(ref.dtype)


def early_grads(mixed, gate_grad, cotangent, h_two, in_t, w_down, h_pair, after):
    units, model = w_down.shape
    half = h_two.shape[0]
    return call(
        "early_grads",
        early_kernel,
        kinds((mixed, gate_grad, cotangent, h_two, in_t, w_down, h_pair), "v"),
        [((3 * units, model // 2), F32, "v"), ((3 * units, model // 2), BF16, "v")],
        [
            pltpu.VMEM((2 * units, half), F32),
            pltpu.VMEM((units, half), F32),
            pltpu.VMEM((units, half), BF16),
            pltpu.VMEM((2 * units, half), BF16),
        ],
        24,
        after,
    )


def late_kernel(n_tp, places, proj_ref, h_ref, out_ref, *refs):
    branch_refs = refs[: len(places)]
    keep_ref, send_ref, branch_full = refs[len(places) :]
    half = keep_ref.shape[1]
    wide = proj_ref.shape[0]
    core = lax.axis_index("seq") % 2
    lay_rows(branch_full, n_tp, places, branch_refs)
    for ref, side in ((send_ref, 1 - core), (keep_ref, core)):
        columns = pl.ds(pl.multiple_of(side * half, half), half)
        ref[:wide, :] = mm(proj_ref[...], h_ref[:, columns], NN).astype(ref.dtype)
        ref[wide:, :] = mm(out_ref[...], branch_full[:, columns], NN).astype(ref.dtype)


def late_grads(n_tp, proj_grad, h_one, out_b, branches, places, after):
    rows, model = h_one.shape
    wide = proj_grad.shape[0] + out_b.shape[0]
    return call(
        "late_grads",
        functools.partial(late_kernel, n_tp, places),
        [(proj_grad, "v"), (h_one, "v"), (out_b, "v"), (branches[0], "v")]
        + kinds(branches[1:], "v"),
        [((wide, model // 2), F32, "v"), ((wide, model // 2), BF16, "v")],
        [pltpu.VMEM((rows, model), BF16)],
        16,
        after,
    )


def spread_kernel(count, *refs):
    given, outs, held = refs[: -count - 1], refs[-count - 1 : -1], refs[-1]
    piece = outs[0].shape[0]
    chip = lax.axis_index("seq") // 2
    at = 0
    for keep_ref, back_ref in zip(given[::2], given[1::2]):
        rows = keep_ref.shape[0]
        held[at : at + rows, :] = keep_ref[...] + back_ref[...].astype(F32)
        at += rows
    if at < held.shape[0]:
        held[at:, :] = jnp.zeros((held.shape[0] - at, held.shape[1]), F32)
    for k in range(count):
        at = pl.ds(pl.multiple_of((chip ^ k) * piece, piece), piece)
        outs[k][...] = held[at, :].astype(outs[k].dtype)


def spread(count, *pairs):
    half = pairs[0][0].shape[1]
    rows = sum(keep.shape[0] for keep, unused in pairs)
    piece = -(-rows // (8 * count)) * 8
    return call(
        "spread",
        functools.partial(spread_kernel, count),
        [(array, "v") for pair in pairs for array in pair],
        [((piece, half), F32, "v")] + [((piece, half), BF16, "v")] * (count - 1),
        [pltpu.VMEM((count * piece, half), F32)],
    )


def piece_kernel(count, gain_ref, *refs):
    out_ref = refs[count]
    half = out_ref.shape[1]
    total = refs[0][...]
    for ref in refs[1:count]:
        total = total + ref[...].astype(F32)
    line = lax.broadcasted_iota(jnp.int32, (16, half), 0)
    gains = jnp.zeros((16, half), F32)
    for at in range(4):
        row = gain_ref[at // 2 : at // 2 + 1, at % 2 * half : (at % 2 + 1) * half]
        gains = jnp.where(line == at, row, gains)
    out_ref[...] = jnp.concatenate([total, gains], axis=0).astype(BF16)


def sum_piece(gains, pieces, after=()):
    piece, half = pieces[0].shape
    (out,) = call(
        "sum_piece",
        functools.partial(piece_kernel, len(pieces)),
        [(gains, "v")] + kinds(pieces, "v"),
        [((piece + 16, half), BF16, "v")],
        (),
        16,
        after,
    )
    return out


def collect_kernel(count, *refs):
    out_ref, held = refs[count:]
    piece = refs[0].shape[0] - 16
    wide = count * piece
    chip = lax.axis_index("seq") // 2
    gains = jnp.zeros((16, out_ref.shape[1]), F32)
    for k in range(count):
        at = pl.ds(pl.multiple_of((chip ^ hop(k, count)) * piece, piece), piece)
        whole = refs[k][...].astype(F32)
        held[at, :] = whole[:piece]
        gains = gains + whole[piece:]
    held[wide:, :] = gains
    out_ref[...] = held[...].astype(BF16)


def collect(pieces, after=()):
    piece, half = pieces[0].shape
    wide = (piece - 16) * len(pieces) + 16
    (out,) = call(
        "collect",
        functools.partial(collect_kernel, len(pieces)),
        kinds(pieces, "v"),
        [((wide, half), BF16, "v")],
        [pltpu.VMEM((wide, half), F32)],
        16,
        after,
    )
    return out


def write_half(sizes, source, side, out_refs, held, sems):
    half = source.shape[1]
    columns = pl.ds(pl.multiple_of(side * half, half), half)
    at = 0
    copies = []
    for n, (ref, size) in enumerate(zip(out_refs, sizes)):
        rows = pl.ds(at, size)
        held[rows, :] = source[rows, :].astype(F32)
        copies.append(pltpu.make_async_copy(held.at[rows], ref.at[:, columns], sems.at[n]))
        copies[-1].start()
        at += size
    return copies


def own_kernel(sizes, own_ref, *refs):
    out_refs, held, sems = refs[:-2], refs[-2], refs[-1]
    core = lax.axis_index("seq") % 2
    for copy in write_half(sizes, own_ref, core, out_refs, held, sems):
        copy.wait()


def pair_kernel(sizes, own_ref, pair_ref, *refs):
    refs = refs[len(sizes) :]
    out_refs, gain_refs = refs[: len(sizes)], refs[len(sizes) : len(sizes) + 2]
    held, sems = refs[-2:]
    core = lax.axis_index("seq") % 2
    copies = write_half(sizes, pair_ref, 1 - core, out_refs, held, sems)
    half = own_ref.shape[1]
    first = own_ref.shape[0] - 16
    gains = own_ref[first:, :].astype(F32) + pair_ref[first:, :].astype(F32)
    for at, ref in zip((0, 2), gain_refs):
        ref[pl.ds(0, half)] = gains[at]
        ref[pl.ds(half, half)] = gains[at + 1]
    for copy in copies:
        copy.wait()


def finish(own, over_cores, sizes):
    half = own.shape[1]
    shapes = [((size, 2 * half), F32, "raw") for size in sizes]
    scratch = [pltpu.VMEM((sum(sizes), half), F32), pltpu.SemaphoreType.DMA((len(sizes),))]
    pair = over_cores(own)
    begun = call("own_half", functools.partial(own_kernel, sizes), [(own, "v")], shapes, scratch)
    return call(
        "pair_half",
        functools.partial(pair_kernel, sizes),
        [(own, "v"), (pair, "v")] + kinds(begun, "raw"),
        shapes + [((2 * half,), F32, "h")] * 2,
        scratch,
        alias={2 + n: n for n in range(len(sizes))},
    )


def down_kernel(mixed_ref, w_ref, middle_ref, keep_ref, *refs):
    send_refs, total = refs[:-1], refs[-1]
    part = keep_ref.shape[0]
    tp = lax.axis_index("tp")
    total[...] = mm(mixed_ref[...], w_ref[...], TN)
    own = pl.ds(pl.multiple_of(tp // 2 * part, part), part)
    keep_ref[...] = total[own, :] + middle_ref[own, :]
    for n, ref in enumerate(send_refs):
        at = pl.ds(pl.multiple_of((tp ^ (2 * n + 2)) // 2 * part, part), part)
        ref[...] = total[at, :].astype(ref.dtype)


def down(n_tp, mixed, w_both, middle, after):
    rows, model = middle.shape
    part = 2 * rows // n_tp
    return call(
        "down",
        down_kernel,
        kinds((mixed, w_both, middle), "v"),
        [((part, model), F32, "v")] + [((part, model), BF16, "v")] * (n_tp // 2 - 1),
        [pltpu.VMEM((rows, model), F32)],
        16,
        after,
    )


def total_kernel(count, *refs):
    total = refs[0][...]
    for ref in refs[1:count]:
        total = total + ref[...].astype(F32)
    refs[count][...] = total.astype(refs[count].dtype)


def total_of(parts, dtype=BF16, kind="v", after=(), flops=0):
    (out,) = call(
        "total_of",
        functools.partial(total_kernel, len(parts)),
        [(parts[0], kind)] + kinds(parts[1:], "v"),
        [(parts[0].shape, dtype, "v")],
        (),
        16,
        after,
        flops=flops,
    )
    return out


def body(
    n_seq,
    n_tp,
    tokens,
    gain_one,
    w_qkv,
    w_out,
    gain_two,
    w_in,
    w_down,
    cotangent,
    doc_lengths,
    roster,
):
    rows, model = tokens.shape
    width = w_qkv.shape[2]
    units = w_in.shape[2]
    count = n_seq // 2
    qkv_t = w_qkv.transpose(1, 2, 0).reshape(3 * width, model)
    in_t = w_in.transpose(1, 2, 0).reshape(2 * units, model)
    over_tp = lambda x, k: swap(x, "tp", k, n_tp)
    over_chips = lambda x, k: swap(x, "seq", 2 * k, n_seq)
    over_cores = lambda x: swap(x, "seq", 1, n_seq)
    everywhere = lambda xs: [xs[0]] + came(n_tp, lambda k: over_tp(xs[k], k))

    def by_steps(part):
        held, places, step = [part], [(0,)], n_tp // 2
        while step:
            joined = pile(held, ()) if len(held) > 1 else part
            ks = tuple(k ^ step for group in places for k in group)
            held, places, step = held + [over_tp(joined, step)], places + [ks], step // 2
        return held, tuple(places)

    singly = tuple((hop(n, n_tp),) for n in range(n_tp))
    docs = (doc_lengths, roster)

    queries, kv, h_one, cos_table, sin_table = project(*docs, tokens, gain_one, qkv_t)
    blocks = [kv] + [over_chips(kv, j) for j in range(1, count)]
    q_pair = over_cores(queries)
    picked, w_half = pick(in_t, w_down, w_out)
    got = [over_tp(picked, 1)] + [over_tp(w_half, k) for k in range(2, n_tp)]

    split = (count + 1) // 2
    (state,) = attention_forward(0, False, *docs, queries, q_pair, blocks[:split])
    state_own, state_pair = attention_forward(
        split, True, *docs, queries, q_pair, blocks[split:], state
    )
    out_b, totals, out_mine, out_other = join(state_own, over_cores(state_pair))
    outs = everywhere([out_other if k % 2 else out_mine for k in range(n_tp)])
    out_pair = over_cores(out_b)
    totals_pair = over_cores(totals)

    got = pile(got, [(state_pair, "v")])
    staged = stage(n_tp, tokens, cotangent, in_t, w_down, w_out, got, over_cores(got))
    middle, middle_part, h_two, mixed, gate_grad, gain_two_part, own, *others = feed(
        gain_two, staged, outs
    )
    arrived = [own] + [over_tp(others[n], 2 * n + 2) for n in range(n_tp // 2 - 1)]
    own, *others = down(n_tp, mixed, staged[4], middle, [(out_pair, "v"), (totals_pair, "v")])
    middle_grad, branch_grad, *pieces = branch(
        n_tp, middle_part, cotangent, gain_two, staged[2], arrived, [(own, "v")]
    )
    early, early_send = early_grads(
        mixed, gate_grad, cotangent, h_two, in_t, w_down, over_tp(h_two, 1), [(branch_grad, "v")]
    )
    early_back = over_cores(early_send)
    out_grad = lay_turned(everywhere(pieces), ())
    grad_pair = over_cores(out_grad)
    branches, branch_places = by_steps(branch_grad)

    held = (queries, q_pair, out_grad, grad_pair, out_b, out_pair, totals, totals_pair)
    *terms, dq = attention_backward(1, False, *docs, held, blocks[1:], None)
    total = total_of(
        [own] + [over_tp(others[n], 2 * n + 2) for n in range(n_tp // 2 - 1)],
        BF16,
        "v",
        [(dq, "v"), (branches[1], "v")],
    )
    totals_all, total_places = by_steps(total)

    dkv, dq_own, dq_pair = attention_backward(
        0, True, *docs, held, blocks[:1], dq, ()
    )
    dkvs = [dkv] + [over_chips(terms[j - 1], j) for j in range(1, count)]

    proj_grad, *parts = unproject(
        n_tp,
        tokens,
        qkv_t,
        cos_table,
        sin_table,
        gain_two_part,
        dq_own,
        over_cores(dq_pair),
        dkvs,
        [(total, "v")],
    )
    layer_out = stack_parts(n_tp, totals_all, total_places)
    keep, send = late_grads(
        n_tp, proj_grad, h_one, out_b, branches, branch_places, [(totals_all[1], "v")]
    )
    own, *others = spread(count, (keep, over_cores(send)), (early, early_back))
    ways = everywhere(parts)
    summed = total_of([ways[0]] + [ways[i] for i in (1, 3, 2)], F32, flops=2_000_000_000)
    chip_sum = total_of(
        [own] + came(count, lambda k: over_chips(others[k - 1], k)), F32, "v", ()
    )
    input_part, gains = input_side(tokens, gain_one, middle_grad, summed, [(own, "v")])
    inputs_all = everywhere([input_part] * n_tp)
    piece = sum_piece(gains, [chip_sum], ())
    input_grad = stack_parts(n_tp, inputs_all, singly, (), 3_000_000_000)
    collected = collect(
        [piece] + came(count, lambda k: over_chips(piece, k)), [(input_grad, "h"), (layer_out, "h")]
    )
    grad_qkv, grad_out, grad_down, grad_in, grad_one, grad_two = finish(
        collected, over_cores, (3 * width, width, units, 2 * units)
    )

    back = lambda x, n: x.reshape(-1, n, model).transpose(2, 0, 1)
    return (
        layer_out,
        input_grad,
        grad_one,
        back(grad_qkv, width),
        grad_out,
        grad_two,
        back(grad_in, units),
        grad_down,
    )


def solution(mesh):
    placed = (
        P("seq", None),
        P(),
        P(None, None, "tp"),
        P("tp", None),
        P(),
        P(None, None, "tp"),
        P("tp", None),
        P("seq", None),
        P(),
        P(),
    )
    return jax.shard_map(
        functools.partial(body, mesh.shape["seq"], mesh.shape["tp"]),
        mesh=mesh,
        in_specs=placed,
        out_specs=(
            P("seq", None),
            P("seq", None),
            P(),
            P(None, None, "tp"),
            P("tp", None),
            P(),
            P(None, None, "tp"),
            P("tp", None),
        ),
        check_vma=False,
    )
```

```python
import functools
import math

import jax
import jax.numpy as jnp
import numpy as np
from jax import lax
from jax.experimental import pallas as pl
from jax.experimental.pallas import tpu as pltpu
from jax.sharding import PartitionSpec as P

HDIM = 64
HALF = HDIM // 2
EPSILON = 1e-05
ROPE_THETA = 160000.0
MASKED = -1e30
AUG = 80
STRIP = 64
F32 = jnp.float32
BF16 = jnp.bfloat16
HBM = pl.BlockSpec(memory_space=pltpu.HBM)
VMEM = pl.BlockSpec(memory_space=pltpu.VMEM)

NN = (((1,), (0,)), ((), ()))
NT = (((1,), (1,)), ((), ()))
TN = (((0,), (0,)), ((), ()))


def params(mib):
    return pltpu.CompilerParams(vmem_limit_bytes=mib * 2**20)


def slot(tp, n_tp):
    return tp % 2 * (n_tp // 2) + tp // 2


def hop(n, count):
    return (count - n) % count


def came(count, send):
    return [send(hop(n, count)) for n in range(1, count)]


def mm(a, b, dims):
    return lax.dot_general(a, b, dims, preferred_element_type=F32)


def shaped(shape, dtype):
    return jax.ShapeDtypeStruct(shape, dtype)


def kinds(arrays, kind):
    return [(array, kind) for array in arrays]


def pin(array, kind):
    return array if kind in ("v", "free") else pltpu.with_memory_space_constraint(array, pltpu.HBM)


def call(name, kernel, ins, outs, scratch=(), mib=16, after=(), lazy=False, flops=0, alias=None):
    fetched = [i for i, given in enumerate(ins) if given[1] not in ("v", "raw", "free")]
    left = [i for i, out in enumerate(outs) if out[2] == "h"]

    def held(array, kind):
        rows = array.shape[0] if kind == "h" else kind
        return pltpu.VMEM((rows,) + array.shape[1:], array.dtype)

    def run(*refs):
        in_refs = list(refs[: len(ins)])
        at = len(ins) + len(after)
        out_refs = list(refs[at : at + len(outs)])
        at += len(outs)
        own = refs[at : at + len(scratch)]
        at += len(scratch)
        buffers = refs[at : at + len(fetched) + len(left)]
        sems = refs[-1]
        copies = []
        for n, i in enumerate(fetched):
            source = in_refs[i]
            if ins[i][1] != "h":
                rows = ins[i][1]
                n_tp = ins[i][0].shape[0] // rows
                at = pl.multiple_of(slot(lax.axis_index("tp"), n_tp) * rows, rows)
                source = source.at[pl.ds(at, rows)]
            copies.append(pltpu.make_async_copy(source, buffers[n], sems.at[n]))
            in_refs[i] = buffers[n]
        for copy in copies:
            copy.start()
        coming = dict(zip(fetched, copies))
        going = {}
        for n, i in enumerate(left):
            spot = len(fetched) + n
            going[i] = pltpu.make_async_copy(buffers[spot], out_refs[i], sems.at[spot])
            out_refs[i] = buffers[spot]
        gone = []

        def need(*which):
            for i in which:
                if i in coming:
                    coming.pop(i).wait()

        def give(*which):
            for i in which:
                if i in going:
                    gone.append(going.pop(i))
                    gone[-1].start()

        if lazy:
            kernel(need, give, *in_refs, *out_refs, *own)
        else:
            need(*fetched)
            kernel(*in_refs, *out_refs, *own)
        need(*fetched)
        give(*left)
        for copy in gone:
            copy.wait()

    spec = lambda kind: VMEM if kind == "v" else HBM
    count = len(fetched) + len(left)
    return pl.pallas_call(
        run,
        out_shape=tuple(
            shaped(shape, dtype) if kind == "v" else pltpu.HBM(shape, dtype)
            for shape, dtype, kind in outs
        ),
        in_specs=[spec(kind) for unused, kind in ins] + [spec(kind) for unused, kind in after],
        out_specs=tuple(spec(kind) for unused, unused, kind in outs),
        scratch_shapes=list(scratch)
        + [held(*ins[i]) for i in fetched]
        + [pltpu.VMEM(outs[i][0], outs[i][1]) for i in left]
        + [pltpu.SemaphoreType.DMA((max(count, 1),))],
        name=name,
        input_output_aliases=alias or {},
        cost_estimate=pl.CostEstimate(flops=flops, bytes_accessed=0, transcendentals=0)
        if flops
        else None,
        compiler_params=params(mib),
    )(*[pin(*given) for given in ins], *[pin(*given) for given in after])


def swap(x, axis, hop, count):
    return lax.ppermute(x, axis, [(i, i ^ hop) for i in range(count)])


def doc_scratch(doc_lengths, roster):
    return [pltpu.SMEM(doc_lengths.shape, jnp.int32), pltpu.SMEM(roster.shape, jnp.int32)]


def fetch_docs(len_any, roster_any, len_ref, roster_ref, len_sem, roster_sem):
    one = pltpu.make_async_copy(len_any, len_ref, len_sem)
    two = pltpu.make_async_copy(roster_any, roster_ref, roster_sem)
    one.start()
    two.start()
    one.wait()
    two.wait()


def doc_bounds(len_ref):
    ends, total = [], jnp.int32(0)
    for d in range(len_ref.shape[0]):
        total = total + len_ref[d]
        ends.append(total)
    return ends


def doc_of(ends, position):
    found = jnp.int32(0)
    for end in ends:
        found = found + (end <= position).astype(jnp.int32)
    return found


def meet(ends, base_a, base_b, rows):
    low = jnp.maximum(doc_of(ends, base_a), doc_of(ends, base_b))
    high = jnp.minimum(doc_of(ends, base_a + rows - 1), doc_of(ends, base_b + rows - 1))
    return low <= high


def doc_rows(ends, base, rows):
    spot = base + lax.broadcasted_iota(jnp.int32, (16, rows), 1)
    line = lax.broadcasted_iota(jnp.int32, (16, rows), 0)
    held = jnp.zeros((16, rows), F32)
    start = jnp.int32(0)
    for d, end in enumerate(ends):
        inside = (line == d) & (spot >= start) & (spot < end)
        held = jnp.where(inside, 1.0, held)
        start = end
    return held


def ban_rows(ends, base, rows):
    line = lax.broadcasted_iota(jnp.int32, (16, rows), 0)
    held = doc_rows(ends, base, rows)
    return jnp.where((held > 0.5) | (line >= len(ends)), 0.0, MASKED)


def key_row(block, seq_index):
    return seq_index ^ (2 * block)


def place_row(ends, base, rows):
    spot = base + lax.broadcasted_iota(jnp.int32, (1, rows), 1)
    start = jnp.zeros((1, rows), jnp.int32)
    for end in ends:
        start = jnp.where(spot >= end, end, start)
    return (spot - start).astype(F32)


def normed(values):
    centre = jnp.mean(values, axis=-1, keepdims=True)
    shifted = values - centre
    spread = jnp.mean(shifted * shifted, axis=-1, keepdims=True)
    scale = lax.rsqrt(spread + EPSILON)
    return shifted * scale, scale


def norm_back(unit, scale, grad, gain):
    u = grad * gain
    mean_u = jnp.mean(u, axis=-1, keepdims=True)
    mean_un = jnp.mean(u * unit, axis=-1, keepdims=True)
    return scale * (u - mean_u - unit * mean_un)


def project_kernel(
    width, need, give, len_any, roster_any, x_ref, w_ref, gain_ref, freq_ref, *refs
):
    q_out, kv_out, h_out, cos_out, sin_out, unit_out = refs[:6]
    proj, len_ref, roster_ref, sems = refs[6:]
    rows = x_ref.shape[0]
    fetch_docs(len_any, roster_any, len_ref, roster_ref, sems.at[0], sems.at[1])
    need(5)
    ends = doc_bounds(len_ref)
    place = place_row(ends, roster_ref[lax.axis_index("seq")] * rows, rows)
    angles = place * freq_ref[...]
    cos_table = jnp.cos(angles)
    sin_table = jnp.sin(angles)
    cos_out[...] = cos_table
    sin_out[...] = sin_table
    give(3, 4)
    need(2, 4)
    gain = gain_ref[...].reshape(1, -1)

    def strip(i, carry):
        at = pl.ds(i * STRIP, STRIP)
        unit, unused = normed(x_ref[at, :].astype(F32))
        unit_out[at, :] = unit
        h_out[at, :] = (unit * gain).astype(BF16)
        return carry

    lax.fori_loop(0, rows // STRIP, strip, 0)
    give(2)
    need(3)
    proj[...] = mm(w_ref[...], h_out[...], NT)
    for at in range(0, 2 * width, HDIM):
        low = proj[at : at + HALF, :]
        high = proj[at + HALF : at + HDIM, :]
        turned_low = (low * cos_out[...] - high * sin_out[...]).astype(BF16)
        turned_high = (high * cos_out[...] + low * sin_out[...]).astype(BF16)
        if at < width:
            q_out[at : at + HALF, :] = (turned_low.astype(F32) * HDIM**-0.5).astype(BF16)
            q_out[at + HALF : at + HDIM, :] = (turned_high.astype(F32) * HDIM**-0.5).astype(BF16)
        else:
            kv_out[at - width : at - width + HALF, :] = turned_low
            kv_out[at - width + HALF : at - width + HDIM, :] = turned_high
    kv_out[width:, :] = proj[2 * width :, :].astype(BF16)


def project(doc_lengths, roster, tokens, gain, qkv_t):
    rows, model = tokens.shape
    width = qkv_t.shape[0] // 3
    freq = (ROPE_THETA ** -(np.arange(HALF) * (2.0 / HDIM))).astype(np.float32)[:, None]
    return call(
        "project",
        functools.partial(project_kernel, width),
        kinds((doc_lengths, roster), "raw") + kinds((tokens, qkv_t, gain, jnp.asarray(freq)), "h"),
        [
            ((width, rows), BF16, "v"),
            ((2 * width, rows), BF16, "v"),
            ((rows, model), BF16, "v"),
            ((HALF, rows), F32, "v"),
            ((HALF, rows), F32, "v"),
            ((rows, model), F32, "v"),
        ],
        [pltpu.VMEM((3 * width, rows), F32)]
        + doc_scratch(doc_lengths, roster)
        + [pltpu.SemaphoreType.DMA((2,))],
        lazy=True,
    )


def forward_kernel(first, count, heads, last, len_any, roster_any, q_own, q_pair, *refs):
    kv_refs = refs[:count]
    refs = refs[count:]
    if first:
        state_in, refs = refs[0], refs[1:]
    outs = refs[: 2 if last else 1]
    kv, q_aug, state, len_ref, roster_ref, sems = refs[len(outs) :]
    rows = q_own.shape[1]
    width = heads * HDIM
    me = lax.axis_index("seq")
    copies = [pltpu.make_async_copy(kv_refs[j], kv.at[j], sems.at[j]) for j in range(count)]
    for copy in copies:
        copy.start()
    fetch_docs(len_any, roster_any, len_ref, roster_ref, sems.at[count], sems.at[count + 1])
    ends = doc_bounds(len_ref)
    bases = (roster_ref[me] * rows, roster_ref[me ^ 1] * rows)
    for g, q_ref in enumerate((q_own, q_pair)):
        mark = doc_rows(ends, bases[g], rows).astype(BF16)
        for h in range(heads):
            q_aug[g * heads + h, :HDIM, :] = q_ref[h * HDIM : (h + 1) * HDIM, :]
            q_aug[g * heads + h, HDIM:, :] = mark
    if first:
        state[...] = state_in[...]
    else:
        line = lax.broadcasted_iota(jnp.int32, (2 * heads, AUG, rows), 1)
        state[...] = jnp.where(line >= 72, MASKED, 0.0)
    for copy in copies:
        copy.wait()

    top = lax.broadcasted_iota(jnp.int32, (16, rows), 0) == 0
    ones = jnp.where(top, 1.0, 0.0).astype(BF16)

    def block(j, carry):
        key_base = roster_ref[key_row(j + first, me)] * rows
        ban = ban_rows(ends, key_base, rows).astype(BF16)
        for g in range(2):

            @pl.when(meet(ends, bases[g], key_base, rows))
            def _():
                for h in range(heads):
                    at = g * heads + h
                    keys = jnp.concatenate([kv[j, h * HDIM : (h + 1) * HDIM, :], ban], axis=0)
                    vals = jnp.concatenate(
                        [kv[j, width + h * HDIM : width + (h + 1) * HDIM, :], ones], axis=0
                    )
                    scores = mm(keys, q_aug[at], TN)
                    old = state[at, 72:73, :]
                    new = jnp.maximum(old, jnp.max(scores, axis=0, keepdims=True))
                    probs = jnp.exp(scores - new).astype(BF16)
                    part = mm(vals, probs, NN)
                    fade = jnp.exp(old - new)
                    state[at, :72, :] = state[at, :72, :] * fade + part[:72]
                    state[at, 72:, :] = jnp.broadcast_to(new, (8, rows))

        return carry

    lax.fori_loop(0, count, block, 0)
    if last:
        outs[0][...] = state[:heads]
        outs[1][...] = state[heads:]
    else:
        outs[0][...] = state[...]


def attention_forward(first, last, doc_lengths, roster, q_own, q_pair, blocks, state=None, after=()):
    width, rows = q_own.shape
    heads = width // HDIM
    count = len(blocks)
    half = ((heads, AUG, rows), F32, "v")
    whole = ((2 * heads, AUG, rows), F32, "v")
    given = [] if state is None else [(state, "v")]
    return call(
        "attention_forward",
        functools.partial(forward_kernel, first, count, heads, last),
        [(doc_lengths, "raw"), (roster, "raw"), (q_own, "v"), (q_pair, "v")]
        + kinds(blocks, "free")
        + given,
        [half, half] if last else [whole],
        [
            pltpu.VMEM((count, 2 * width, rows), BF16),
            pltpu.VMEM((2 * heads, AUG, rows), BF16),
            pltpu.VMEM((2 * heads, AUG, rows), F32),
        ]
        + doc_scratch(doc_lengths, roster)
        + [pltpu.SemaphoreType.DMA((count + 2,))],
        16 if count < 8 else 40,
        after,
    )


def backward_kernel(first, count, heads, more, last, len_any, roster_any, *refs):
    q_own, q_pair, g_own, g_pair, o_own, o_pair, t_own, t_pair = refs[:8]
    kv_refs, refs = refs[8 : 8 + count], refs[8 + count :]
    if more:
        dq_in, refs = refs[0], refs[1:]
    outs, refs = refs[:count], refs[count:]
    dq_outs, refs = (refs[:2], refs[2:]) if last else (refs[:1], refs[1:])
    kv, q_aug, delta, dq, dkv, len_ref, roster_ref, sems = refs
    rows = q_own.shape[1]
    width = heads * HDIM
    me = lax.axis_index("seq")
    copies = [pltpu.make_async_copy(kv_refs[j], kv.at[j], sems.at[j]) for j in range(count)]
    for copy in copies:
        copy.start()
    fetch_docs(len_any, roster_any, len_ref, roster_ref, sems.at[count], sems.at[count + 1])
    ends = doc_bounds(len_ref)
    bases = (roster_ref[me] * rows, roster_ref[me ^ 1] * rows)
    for g, (q_ref, g_ref, o_ref) in enumerate(((q_own, g_own, o_own), (q_pair, g_pair, o_pair))):
        mark = doc_rows(ends, bases[g], rows).astype(BF16)
        for h in range(heads):
            part = slice(h * HDIM, (h + 1) * HDIM)
            q_aug[g * heads + h, :HDIM, :] = q_ref[part, :]
            q_aug[g * heads + h, HDIM:, :] = mark
            product = g_ref[part, :].astype(F32) * o_ref[part, :].astype(F32)
            delta[g * heads + h] = jnp.broadcast_to(
                jnp.sum(product, axis=0, keepdims=True), (8, rows)
            )
    if more:
        dq[...] = dq_in[...]
    else:
        dq[...] = jnp.zeros_like(dq)
    for copy in copies:
        copy.wait()

    def block(j, carry):
        key_base = roster_ref[key_row(j + first, me)] * rows
        ban = ban_rows(ends, key_base, rows).astype(BF16)
        dkv[j] = jnp.zeros((2 * width, rows), F32)
        for g, (g_ref, t_ref) in enumerate(((g_own, t_own), (g_pair, t_pair))):

            @pl.when(meet(ends, bases[g], key_base, rows))
            def _():
                for h in range(heads):
                    at = g * heads + h
                    part = slice(h * HDIM, (h + 1) * HDIM)
                    late = slice(width + h * HDIM, width + (h + 1) * HDIM)
                    keys = kv[j, part, :]
                    scores = mm(jnp.concatenate([keys, ban], axis=0), q_aug[at], TN)
                    probs = jnp.exp(scores - t_ref[h, 0:1, :])
                    prob_grads = mm(kv[j, late, :], g_ref[part, :], TN)
                    score_grad = (probs * (prob_grads - delta[at, 0:1, :])).astype(BF16)
                    dkv[j, late, :] += mm(g_ref[part, :], probs.astype(BF16), NT)
                    dkv[j, part, :] += mm(q_aug[at, :HDIM, :], score_grad, NT)
                    dq[at] += mm(keys, score_grad, NN)

        return carry

    lax.fori_loop(0, count, block, 0)
    for j in range(count):
        outs[j][...] = dkv[j].astype(outs[j].dtype)
    if last:
        for h in range(heads):
            part = slice(h * HDIM, (h + 1) * HDIM)
            dq_outs[0][part, :] = dq[h] * HDIM**-0.5
            dq_outs[1][part, :] = (dq[heads + h] * HDIM**-0.5).astype(BF16)
    else:
        dq_outs[0][...] = dq[...]


def attention_backward(first, last, doc_lengths, roster, held, blocks, dq=None, after=()):
    width, rows = held[0].shape
    heads = width // HDIM
    count = len(blocks)
    given = [] if dq is None else [(dq, "v")]
    if last:
        queries = [((width, rows), F32, "v"), ((width, rows), BF16, "v")]
    else:
        queries = [((2 * heads, HDIM, rows), F32, "v")]
    return call(
        "attention_backward",
        functools.partial(backward_kernel, first, count, heads, bool(given), last),
        kinds((doc_lengths, roster), "raw") + kinds(held, "v") + kinds(blocks, "free") + given,
        [((2 * width, rows), BF16 if first else F32, "v")] * count + queries,
        [
            pltpu.VMEM((count, 2 * width, rows), BF16),
            pltpu.VMEM((2 * heads, AUG, rows), BF16),
            pltpu.VMEM((2 * heads, 8, rows), F32),
            pltpu.VMEM((2 * heads, HDIM, rows), F32),
            pltpu.VMEM((count, 2 * width, rows), F32),
        ]
        + doc_scratch(doc_lengths, roster)
        + [pltpu.SemaphoreType.DMA((count + 2,))],
        16 if count < 8 else 40,
        after,
        flops=0 if last else 0,
    )


def join_kernel(heads, own_ref, back_ref, out_ref, total_ref, mine_ref, other_ref):
    rows = own_ref.shape[2]
    for h in range(heads):
        top_own = own_ref[h, 72:73, :]
        top_back = back_ref[h, 72:73, :]
        top = jnp.maximum(top_own, top_back)
        fade_own = jnp.exp(top_own - top)
        fade_back = jnp.exp(top_back - top)
        total = own_ref[h, 64:65, :] * fade_own + back_ref[h, 64:65, :] * fade_back
        share_own = fade_own / total
        share_back = fade_back / total
        value = own_ref[h, :HDIM, :] * share_own + back_ref[h, :HDIM, :] * share_back
        out_ref[h * HDIM : (h + 1) * HDIM, :] = value.astype(BF16)
        total_ref[h] = jnp.broadcast_to(top + jnp.log(total), (8, rows))
    half = rows // 2
    for bit in range(2):

        @pl.when(lax.axis_index("tp") % 2 == bit)
        def _():
            mine_ref[...] = out_ref[:, bit * half : (bit + 1) * half]
            other_ref[...] = out_ref[:, (1 - bit) * half : (2 - bit) * half]


def join(own, back):
    heads, unused, rows = own.shape
    return call(
        "join",
        functools.partial(join_kernel, heads),
        [(own, "v"), (back, "v")],
        [
            ((heads * HDIM, rows), BF16, "v"),
            ((heads, 8, rows), F32, "v"),
            ((heads * HDIM, rows // 2), BF16, "v"),
            ((heads * HDIM, rows // 2), BF16, "v"),
        ],
    )


def pick_kernel(in_any, down_any, w_any, all_ref, w_ref, sems):
    core = lax.axis_index("seq") % 2
    at = 0
    copies = []
    for source in (in_any, down_any, w_any):
        rows = source.shape[0] // 2
        mine = pl.ds(pl.multiple_of(core * rows, rows), rows)
        copies.append((source.at[mine], all_ref.at[pl.ds(at, rows)]))
        at += rows
    copies.append((w_any.at[mine], w_ref))
    copies = [pltpu.make_async_copy(*move, sems.at[n]) for n, move in enumerate(copies)]
    for copy in copies:
        copy.start()
    for copy in copies:
        copy.wait()


def pick(in_t, w_down, w_out, after=()):
    rows = (in_t.shape[0] + w_down.shape[0] + w_out.shape[0]) // 2
    model = w_out.shape[1]
    return call(
        "pick",
        pick_kernel,
        kinds((in_t, w_down, w_out), "raw"),
        [((rows, model), BF16, "v"), ((w_out.shape[0] // 2, model), BF16, "v")],
        [pltpu.SemaphoreType.DMA((4,))],
        16,
        after,
    )


def pile_kernel(*refs):
    out_ref = refs[-1]
    at = 0
    for ref in refs[:-1]:
        out_ref[at : at + ref.shape[0], :] = ref[...]
        at += ref.shape[0]


def pile(values, after):
    rows = sum(value.shape[0] for value in values)
    (out,) = call(
        "pile",
        pile_kernel,
        kinds(values, "v"),
        [((rows, values[0].shape[1]), BF16, "v")],
        (),
        16,
        after,
    )
    return out


def stage_kernel(
    x_any, cot_any, in_any, down_any, w_any, one_any, two_any, got_ref, rest_ref, *refs
):
    x_ref, cot_ref, w_ref, in_ref, down_ref, x_part, cot_part, one_ref, two_ref, sems = refs
    half = x_ref.shape[0]
    core = lax.axis_index("seq") % 2
    tp = lax.axis_index("tp")
    n_tp = w_ref.shape[0] // w_any.shape[0]
    mine = pl.ds(pl.multiple_of(tp % 2 * half, half), half)
    width = w_any.shape[0]
    rows = width // 2
    own = pl.ds(pl.multiple_of(tp * width, width), width)
    part = x_part.shape[0]
    kept = pl.ds(pl.multiple_of(slot(tp, n_tp) * part, part), part)
    moves = [(w_any, w_ref.at[own]), (x_any.at[mine], x_ref), (cot_any.at[mine], cot_ref)]
    moves += [(x_any.at[kept], x_part), (cot_any.at[kept], cot_part)]
    moves += [(one_any, one_ref), (two_any, two_ref)]
    sides = ((got_ref, core), (rest_ref, 1 - core))
    first = got_ref.shape[0] - (n_tp - 1) * rows
    for k in range(1, n_tp):
        for source, side in sides:
            spot = pl.multiple_of((tp ^ k) * width + side * rows, rows)
            piece = source.at[pl.ds(first + (k - 1) * rows, rows)]
            moves.append((piece, w_ref.at[pl.ds(spot, rows)]))
    at = 0
    for own, ref in ((in_any, in_ref), (down_any, down_ref)):
        rows = own.shape[0] // 2
        moves.append((own, ref.at[pl.ds(0, 2 * rows)]))
        for source, side in sides:
            spot = pl.multiple_of(2 * rows + side * rows, rows)
            moves.append((source.at[pl.ds(at, rows)], ref.at[pl.ds(spot, rows)]))
        at += rows
    copies = [pltpu.make_async_copy(*move, sems.at[n]) for n, move in enumerate(moves)]
    for copy in copies:
        copy.start()
    for copy in copies:
        copy.wait()


def stage(n_tp, tokens, cotangent, in_t, w_down, w_out, gain_one, gain_two, got, rest):
    rows, model = tokens.shape
    return call(
        "stage",
        stage_kernel,
        kinds((tokens, cotangent, in_t, w_down, w_out, gain_one, gain_two), "raw")
        + kinds((got, rest), "v"),
        [
            ((rows // 2, model), BF16, "v"),
            ((rows // 2, model), BF16, "v"),
            ((n_tp * w_out.shape[0], model), BF16, "v"),
            ((2 * in_t.shape[0], model), BF16, "v"),
            ((2 * w_down.shape[0], model), BF16, "v"),
            ((rows // n_tp, model), BF16, "v"),
            ((rows // n_tp, model), BF16, "v"),
            ((model,), F32, "v"),
            ((model,), F32, "v"),
        ],
        [pltpu.SemaphoreType.DMA((11 + 2 * n_tp,))],
    )


def gated(units, first, gate_up, mixed_grad, mixed_out, gate_out):
    rows = math.gcd(units, 96)

    def wave(i, carry):
        spot = pl.ds(first + i * rows, rows)
        at = pl.ds(2 * first + i * rows, rows)
        late = pl.ds(2 * first + units + i * rows, rows)
        gate = gate_up[at, :]
        up = gate_up[late, :]
        back = mixed_grad[spot, :]
        bell = 0.5 * (1.0 + lax.erf(gate * (2.0**-0.5)))
        active = gate * bell
        slope = bell + gate * jnp.exp(-0.5 * gate * gate) * ((2.0 * jnp.pi) ** -0.5)
        mixed_out[spot, :] = (active * up).astype(BF16)
        gate_out[at, :] = (back * up * slope).astype(BF16)
        gate_out[late, :] = (back * active).astype(BF16)
        return carry

    lax.fori_loop(0, units // rows, wave, 0)


def feed_kernel(n_tp, need, give, x_ref, cot_ref, w_ref, in_ref, down_ref, gain_ref, *refs):
    out_refs = refs[:n_tp]
    middle_out, part_out, h_out, mixed_out, gate_out, gain_out = refs[n_tp : n_tp + 6]
    keep_ref, *send_refs = refs[n_tp + 6 : n_tp + 6 + n_tp // 2]
    outs, unit, gate_up, mixed_grad, grad = refs[n_tp + 6 + n_tp // 2 :]
    rows = x_ref.shape[0]
    part = keep_ref.shape[0]
    units = down_ref.shape[0] // 2
    width = out_refs[0].shape[0]
    tp = lax.axis_index("tp")
    for k in range(n_tp):
        at = pl.ds(pl.multiple_of((tp ^ hop(k, n_tp)) * width, width), width)
        outs[at, :] = out_refs[k][...]
    mixed_grad[...] = mm(down_ref[...], cot_ref[...], NT)
    middle_out[...] = mm(outs[...], w_ref[...], TN)
    need(5)
    gain = gain_ref[...].reshape(1, -1)

    def strip(i, carry):
        at = pl.ds(i * 32, 32)
        middle = middle_out[at, :] + x_ref[at, :].astype(F32)
        middle_out[at, :] = middle
        held, unused = normed(middle)
        unit[at, :] = held
        h_out[at, :] = (held * gain).astype(BF16)
        return carry

    lax.fori_loop(0, rows // 32, strip, 0)
    give(0, 2)
    gate_up[...] = mm(in_ref[...], h_out[...], NT)
    for first in (0, units):
        gated(units, first, gate_up, mixed_grad, mixed_out, gate_out)
    give(3, 4)
    grad[...] = mm(gate_out[...], in_ref[...], TN)
    for n, ref in enumerate((keep_ref, *send_refs)):
        at = pl.ds(pl.multiple_of((tp ^ (2 * n)) // 2 * part, part), part)
        ref[...] = grad[at, :].astype(ref.dtype)
        give(6 + n)
    own = pl.ds(pl.multiple_of(tp // 2 * part, part), part)
    part_out[...] = middle_out[own, :]
    give(1)

    def gains(i, carry):
        at = pl.ds(i * 32, 32)
        product = grad[at, :] * unit[at, :]
        return carry + jnp.sum(product.reshape(4, 8, -1), axis=0)

    gain_out[...] = lax.fori_loop(0, rows // 32, gains, jnp.zeros(gain_out.shape, F32))


def feed(gain, staged, outs):
    rows, model = staged[0].shape
    n_tp = len(outs)
    units = staged[4].shape[0]
    part = 2 * rows // n_tp
    return call(
        "feed",
        functools.partial(feed_kernel, n_tp),
        kinds((*staged, gain, *outs), "v"),
        [
            ((rows, model), F32, "v"),
            ((part, model), F32, "v"),
            ((rows, model), BF16, "v"),
            ((units, rows), BF16, "v"),
            ((2 * units, rows), BF16, "v"),
            ((8, model), F32, "v"),
            ((part, model), F32, "v"),
        ]
        + [((part, model), BF16, "v")] * (n_tp // 2 - 1),
        [
            pltpu.VMEM((n_tp * outs[0].shape[0], rows), BF16),
            pltpu.VMEM((rows, model), F32),
            pltpu.VMEM((2 * units, rows), F32),
            pltpu.VMEM((units, rows), F32),
            pltpu.VMEM((rows, model), F32),
        ],
        24,
        lazy=True,
    )


def branch_kernel(n_tp, count, need, give, middle_ref, cot_ref, gain_ref, w_ref, *refs):
    arrived = refs[:count]
    grad_out, branch_out = refs[count : count + 2]
    piece_refs = refs[count + 2 :]
    width = piece_refs[0].shape[1]
    tp = lax.axis_index("tp")
    need(0, 1, 2, 4)
    total = arrived[0][...]
    for ref in arrived[1:]:
        total = total + ref[...].astype(F32)
    unit, scale = normed(middle_ref[...])
    gain = gain_ref[...].reshape(1, -1)
    value = cot_ref[...].astype(F32) + norm_back(unit, scale, total, gain)
    grad_out[...] = value
    branch_out[...] = value.astype(BF16)
    give(0, 1)
    need(3)
    for k in range(n_tp):
        at = pl.ds(pl.multiple_of((tp ^ k) * width, width), width)
        piece_refs[k][...] = mm(branch_out[...], w_ref[at, :], NT).astype(BF16)


def branch(n_tp, middle_part, cotangent, gain, w_full, arrived, after):
    part, model = arrived[0].shape
    width = w_full.shape[0] // n_tp
    return call(
        "branch",
        functools.partial(branch_kernel, n_tp, len(arrived)),
        [(middle_part, "v"), (cotangent, "v")]
        + [(gain, "v"), (w_full, "v"), (arrived[0], "v")]
        + kinds(arrived[1:], "v"),
        [((part, model), F32, "v"), ((part, model), BF16, "v")]
        + [((part, width), BF16, "v")] * n_tp,
        (),
        16,
        after,
        True,
    )


def lay_kernel(n_tp, *refs):
    out_ref, held = refs[n_tp:]
    part = refs[0].shape[0]
    tp = lax.axis_index("tp")
    for k in range(n_tp):
        at = pl.ds(pl.multiple_of(slot(tp ^ hop(k, n_tp), n_tp) * part, part), part)
        held[at, :] = refs[k][...].astype(F32)
    out_ref[...] = held[...].T.astype(BF16)


def lay_turned(pieces, after):
    part, width = pieces[0].shape
    rows = part * len(pieces)
    (out,) = call(
        "lay_turned",
        functools.partial(lay_kernel, len(pieces)),
        kinds(pieces, "v"),
        [((width, rows), BF16, "v")],
        [pltpu.VMEM((rows, width), F32)],
        16,
        after,
    )
    return out


def lay_rows(out_ref, n_tp, places, refs):
    part = out_ref.shape[0] // n_tp
    tp = lax.axis_index("tp")
    for ks, ref in zip(places, refs):
        for n, k in enumerate(ks):
            at = pl.ds(pl.multiple_of(slot(tp ^ k, n_tp) * part, part), part)
            out_ref[at, :] = ref[n * part : (n + 1) * part, :]


def stack_kernel(n_tp, places, *refs):
    lay_rows(refs[-1], n_tp, places, refs[:-1])


def stack_parts(n_tp, pieces, places, after=(), flops=0):
    part, model = pieces[0].shape
    (out,) = call(
        "stack_parts",
        functools.partial(stack_kernel, n_tp, places),
        kinds(pieces, "v"),
        [((part * n_tp, model), pieces[0].dtype, "h")],
        (),
        16,
        after,
        flops=flops,
    )
    return out


def turn_back(out_ref, first, value, cos_table, sin_table):
    for at in range(0, value.shape[0], HDIM):
        low = value[at : at + HALF]
        high = value[at + HALF : at + HDIM]
        spot = first + at
        out_ref[spot : spot + HALF, :] = (low * cos_table + high * sin_table).astype(BF16)
        out_ref[spot + HALF : spot + HDIM, :] = (high * cos_table - low * sin_table).astype(BF16)


def unproject_kernel(
    count, n_tp, need, give, x_ref, w_ref, cos_ref, sin_ref, two_ref, dq_ref, dq_back, *refs
):
    dkv_refs = refs[:count]
    proj_out = refs[count]
    part_refs = refs[count + 1 : count + 1 + n_tp]
    grad, dkv = refs[count + 1 + n_tp :]
    rows, model = x_ref.shape
    part = rows // n_tp
    width = dq_ref.shape[0]
    tp = lax.axis_index("tp")
    need(2, 3)
    cos_table = cos_ref[...]
    sin_table = sin_ref[...]
    turn_back(proj_out, 0, dq_ref[...] + dq_back[...].astype(F32), cos_table, sin_table)
    total = dkv_refs[0][...]
    for ref in dkv_refs[1:]:
        total = total + ref[...].astype(F32)
    dkv[...] = total
    turn_back(proj_out, width, dkv[:width, :], cos_table, sin_table)
    proj_out[2 * width :, :] = dkv[width:, :].astype(BF16)
    need(1)
    grad[...] = mm(proj_out[...], w_ref[...], TN)
    need(0, 4)

    def gains(i, carry):
        at = pl.ds(i * STRIP, STRIP)
        product = grad[at, :] * x_ref[at, :]
        return carry + jnp.sum(product.reshape(STRIP // 8, 8, -1), axis=0)

    gain = lax.fori_loop(0, rows // STRIP, gains, jnp.zeros((8, model), F32))
    line = lax.broadcasted_iota(jnp.int32, (16, model), 0)
    gain_two = jnp.sum(two_ref[...], axis=0, keepdims=True)
    gain = jnp.sum(gain, axis=0, keepdims=True)
    gain = jnp.where(line == 0, gain, jnp.where(line == 1, gain_two, 0.0))
    for k in range(n_tp):
        at = pl.ds(pl.multiple_of(slot(tp ^ k, n_tp) * part, part), part)
        part_refs[k][:part, :] = grad[at, :].astype(part_refs[k].dtype)
        part_refs[k][part:, :] = gain.astype(part_refs[k].dtype)


def unproject(n_tp, tokens, qkv_t, cos_table, sin_table, gain_two_part, dq, dq_back, dkvs, after):
    rows, model = tokens.shape
    part = rows // n_tp
    return call(
        "unproject",
        functools.partial(unproject_kernel, len(dkvs), n_tp),
        kinds((tokens, qkv_t, cos_table, sin_table, gain_two_part), "v")
        + kinds((dq, dq_back, *dkvs), "v"),
        [((qkv_t.shape[0], rows), BF16, "v"), ((part + 16, model), F32, "v")]
        + [((part + 16, model), BF16, "v")] * (n_tp - 1),
        [pltpu.VMEM((rows, model), F32), pltpu.VMEM(dkvs[0].shape, F32)],
        16,
        after,
        True,
    )


def input_kernel(x_ref, gain_ref, grad_ref, sum_ref, out_ref, gain_out):
    part, model = grad_ref.shape
    total = sum_ref[...]
    unit, scale = normed(x_ref[...].astype(F32))
    gain = gain_ref[...].reshape(1, -1)
    value = grad_ref[...] + norm_back(unit, scale, total[:part], gain)
    out_ref[...] = value.astype(BF16)
    gain_out[...] = total[part : part + 8]


def input_side(tokens, gain, middle_grad, summed, after):
    part, model = middle_grad.shape
    return call(
        "input_side",
        input_kernel,
        kinds((tokens, gain, middle_grad, summed), "v"),
        [((part, model), BF16, "v"), ((8, model), F32, "v")],
        (),
        16,
        after,
    )


def early_kernel(mixed_ref, gate_ref, cot_ref, h_ref, in_ref, down_ref, h_pair, *refs):
    keep_ref, send_ref, gate_up, mixed_grad, mixed, gate = refs
    units = down_ref.shape[0]
    half = h_ref.shape[0]
    bit = lax.axis_index("tp") % 2
    mine = pl.ds(pl.multiple_of(bit * half, half), half)
    other = pl.ds(pl.multiple_of((1 - bit) * half, half), half)
    gate_up[...] = mm(in_ref[...], h_pair[...], NT)
    mixed_grad[...] = mm(down_ref[...], cot_ref[other, :], NT)
    gated(units, 0, gate_up, mixed_grad, mixed, gate)
    width = keep_ref.shape[1]
    core = lax.axis_index("seq") % 2
    for ref, side in ((send_ref, 1 - core), (keep_ref, core)):
        columns = pl.ds(pl.multiple_of(side * width, width), width)
        down = mm(mixed_ref[:units, :], cot_ref[mine, columns], NN)
        down = down + mm(mixed[...], cot_ref[other, columns], NN)
        ref[:units, :] = down.astype(ref.dtype)
        both = mm(gate_ref[: 2 * units, :], h_ref[:, columns], NN)
        both = both + mm(gate[...], h_pair[:, columns], NN)
        ref[units:, :] = both.astype(ref.dtype)


def early_grads(mixed, gate_grad, cotangent, h_two, in_t, w_down, h_pair, after):
    units, model = w_down.shape
    half = h_two.shape[0]
    return call(
        "early_grads",
        early_kernel,
        kinds((mixed, gate_grad, cotangent, h_two, in_t, w_down, h_pair), "v"),
        [((3 * units, model // 2), F32, "v"), ((3 * units, model // 2), BF16, "v")],
        [
            pltpu.VMEM((2 * units, half), F32),
            pltpu.VMEM((units, half), F32),
            pltpu.VMEM((units, half), BF16),
            pltpu.VMEM((2 * units, half), BF16),
        ],
        24,
        after,
    )


def late_kernel(n_tp, places, proj_ref, h_ref, out_ref, *refs):
    branch_refs = refs[: len(places)]
    keep_ref, send_ref, branch_full = refs[len(places) :]
    half = keep_ref.shape[1]
    wide = proj_ref.shape[0]
    core = lax.axis_index("seq") % 2
    lay_rows(branch_full, n_tp, places, branch_refs)
    for ref, side in ((send_ref, 1 - core), (keep_ref, core)):
        columns = pl.ds(pl.multiple_of(side * half, half), half)
        ref[:wide, :] = mm(proj_ref[...], h_ref[:, columns], NN).astype(ref.dtype)
        ref[wide:, :] = mm(out_ref[...], branch_full[:, columns], NN).astype(ref.dtype)


def late_grads(n_tp, proj_grad, h_one, out_b, branches, places, after):
    rows, model = h_one.shape
    wide = proj_grad.shape[0] + out_b.shape[0]
    return call(
        "late_grads",
        functools.partial(late_kernel, n_tp, places),
        [(proj_grad, "v"), (h_one, "v"), (out_b, "v"), (branches[0], "v")]
        + kinds(branches[1:], "v"),
        [((wide, model // 2), F32, "v"), ((wide, model // 2), BF16, "v")],
        [pltpu.VMEM((rows, model), BF16)],
        16,
        after,
    )


def spread_kernel(count, *refs):
    given, outs, held = refs[: -count - 1], refs[-count - 1 : -1], refs[-1]
    piece = outs[0].shape[0]
    chip = lax.axis_index("seq") // 2
    at = 0
    for keep_ref, back_ref in zip(given[::2], given[1::2]):
        rows = keep_ref.shape[0]
        held[at : at + rows, :] = keep_ref[...] + back_ref[...].astype(F32)
        at += rows
    if at < held.shape[0]:
        held[at:, :] = jnp.zeros((held.shape[0] - at, held.shape[1]), F32)
    for k in range(count):
        at = pl.ds(pl.multiple_of((chip ^ k) * piece, piece), piece)
        outs[k][...] = held[at, :].astype(outs[k].dtype)


def spread(count, *pairs):
    half = pairs[0][0].shape[1]
    rows = sum(keep.shape[0] for keep, unused in pairs)
    piece = -(-rows // (8 * count)) * 8
    return call(
        "spread",
        functools.partial(spread_kernel, count),
        [(array, "v") for pair in pairs for array in pair],
        [((piece, half), F32, "v")] + [((piece, half), BF16, "v")] * (count - 1),
        [pltpu.VMEM((count * piece, half), F32)],
    )


def piece_kernel(count, gain_ref, *refs):
    out_ref = refs[count]
    half = out_ref.shape[1]
    total = refs[0][...]
    for ref in refs[1:count]:
        total = total + ref[...].astype(F32)
    line = lax.broadcasted_iota(jnp.int32, (16, half), 0)
    gains = jnp.zeros((16, half), F32)
    for at in range(4):
        row = gain_ref[at // 2 : at // 2 + 1, at % 2 * half : (at % 2 + 1) * half]
        gains = jnp.where(line == at, row, gains)
    out_ref[...] = jnp.concatenate([total, gains], axis=0).astype(BF16)


def sum_piece(gains, pieces, after=()):
    piece, half = pieces[0].shape
    (out,) = call(
        "sum_piece",
        functools.partial(piece_kernel, len(pieces)),
        [(gains, "v")] + kinds(pieces, "v"),
        [((piece + 16, half), BF16, "v")],
        (),
        16,
        after,
    )
    return out


def collect_kernel(count, *refs):
    out_ref, held = refs[count:]
    piece = refs[0].shape[0] - 16
    wide = count * piece
    chip = lax.axis_index("seq") // 2
    gains = jnp.zeros((16, out_ref.shape[1]), F32)
    for k in range(count):
        at = pl.ds(pl.multiple_of((chip ^ hop(k, count)) * piece, piece), piece)
        whole = refs[k][...].astype(F32)
        held[at, :] = whole[:piece]
        gains = gains + whole[piece:]
    held[wide:, :] = gains
    out_ref[...] = held[...].astype(BF16)


def collect(pieces, after=()):
    piece, half = pieces[0].shape
    wide = (piece - 16) * len(pieces) + 16
    (out,) = call(
        "collect",
        functools.partial(collect_kernel, len(pieces)),
        kinds(pieces, "v"),
        [((wide, half), BF16, "v")],
        [pltpu.VMEM((wide, half), F32)],
        16,
        after,
    )
    return out


def write_half(sizes, source, side, out_refs, held, sems):
    half = source.shape[1]
    columns = pl.ds(pl.multiple_of(side * half, half), half)
    at = 0
    copies = []
    for n, (ref, size) in enumerate(zip(out_refs, sizes)):
        rows = pl.ds(at, size)
        held[rows, :] = source[rows, :].astype(F32)
        for part in range(2):
            some = pl.ds(at + part * (size // 2), size // 2)
            target = ref.at[pl.ds(part * (size // 2), size // 2), columns]
            copies.append(pltpu.make_async_copy(held.at[some], target, sems.at[2 * n + part]))
            copies[-1].start()
        at += size
    return copies


def own_kernel(sizes, own_ref, *refs):
    out_refs, held, sems = refs[:-2], refs[-2], refs[-1]
    core = lax.axis_index("seq") % 2
    for copy in write_half(sizes, own_ref, core, out_refs, held, sems):
        copy.wait()


def pair_kernel(sizes, own_ref, pair_ref, *refs):
    refs = refs[len(sizes) :]
    out_refs, gain_refs = refs[: len(sizes)], refs[len(sizes) : len(sizes) + 2]
    held, sems = refs[-2:]
    core = lax.axis_index("seq") % 2
    copies = write_half(sizes, pair_ref, 1 - core, out_refs, held, sems)
    half = own_ref.shape[1]
    first = own_ref.shape[0] - 16
    gains = own_ref[first:, :].astype(F32) + pair_ref[first:, :].astype(F32)
    for at, ref in zip((0, 2), gain_refs):
        ref[pl.ds(0, half)] = gains[at]
        ref[pl.ds(half, half)] = gains[at + 1]
    for copy in copies:
        copy.wait()


def finish(own, over_cores, sizes):
    half = own.shape[1]
    shapes = [((size, 2 * half), F32, "raw") for size in sizes]
    scratch = [pltpu.VMEM((sum(sizes), half), F32), pltpu.SemaphoreType.DMA((2 * len(sizes),))]
    pair = over_cores(own)
    begun = call("own_half", functools.partial(own_kernel, sizes), [(own, "v")], shapes, scratch)
    return call(
        "pair_half",
        functools.partial(pair_kernel, sizes),
        [(own, "v"), (pair, "v")] + kinds(begun, "raw"),
        shapes + [((2 * half,), F32, "h")] * 2,
        scratch,
        alias={2 + n: n for n in range(len(sizes))},
    )


def down_kernel(mixed_ref, w_ref, middle_ref, keep_ref, *refs):
    send_refs, total = refs[:-1], refs[-1]
    part = keep_ref.shape[0]
    tp = lax.axis_index("tp")
    total[...] = mm(mixed_ref[...], w_ref[...], TN)
    own = pl.ds(pl.multiple_of(tp // 2 * part, part), part)
    keep_ref[...] = total[own, :] + middle_ref[own, :]
    for n, ref in enumerate(send_refs):
        at = pl.ds(pl.multiple_of((tp ^ (2 * n + 2)) // 2 * part, part), part)
        ref[...] = total[at, :].astype(ref.dtype)


def down(n_tp, mixed, w_both, middle, after):
    rows, model = middle.shape
    part = 2 * rows // n_tp
    return call(
        "down",
        down_kernel,
        kinds((mixed, w_both, middle), "v"),
        [((part, model), F32, "v")] + [((part, model), BF16, "v")] * (n_tp // 2 - 1),
        [pltpu.VMEM((rows, model), F32)],
        16,
        after,
    )


def total_kernel(count, *refs):
    total = refs[0][...]
    for ref in refs[1:count]:
        total = total + ref[...].astype(F32)
    refs[count][...] = total.astype(refs[count].dtype)


def total_of(parts, dtype=BF16, kind="v", after=(), flops=0):
    (out,) = call(
        "total_of",
        functools.partial(total_kernel, len(parts)),
        [(parts[0], kind)] + kinds(parts[1:], "v"),
        [(parts[0].shape, dtype, "v")],
        (),
        16,
        after,
        flops=flops,
    )
    return out


def body(
    n_seq,
    n_tp,
    tokens,
    gain_one,
    w_qkv,
    w_out,
    gain_two,
    w_in,
    w_down,
    cotangent,
    doc_lengths,
    roster,
):
    rows, model = tokens.shape
    width = w_qkv.shape[2]
    units = w_in.shape[2]
    count = n_seq // 2
    qkv_t = w_qkv.transpose(1, 2, 0).reshape(3 * width, model)
    in_t = w_in.transpose(1, 2, 0).reshape(2 * units, model)
    over_tp = lambda x, k: swap(x, "tp", k, n_tp)
    over_chips = lambda x, k: swap(x, "seq", 2 * k, n_seq)
    over_cores = lambda x: swap(x, "seq", 1, n_seq)
    everywhere = lambda xs: [xs[0]] + came(n_tp, lambda k: over_tp(xs[k], k))

    def by_steps(part, after=()):
        held, places, step = [part], [(0,)], n_tp // 2
        while step:
            joined = pile(held, after) if len(held) > 1 else part
            ks = tuple(k ^ step for group in places for k in group)
            held, places, step = held + [over_tp(joined, step)], places + [ks], step // 2
        return held, tuple(places)

    singly = tuple((hop(n, n_tp),) for n in range(n_tp))
    docs = (doc_lengths, roster)

    queries, kv, h_one, cos_table, sin_table, unit_one = project(*docs, tokens, gain_one, qkv_t)
    blocks = [kv] + [over_chips(kv, j) for j in range(1, count)]
    q_pair = over_cores(queries)

    picked, w_half = pick(in_t, w_down, w_out, ())
    got = [over_tp(picked, 1)] + [over_tp(w_half, k) for k in range(2, n_tp)]
    split = (count + 1) // 2
    (state,) = attention_forward(0, False, *docs, queries, q_pair, blocks[:split])
    state_own, state_pair = attention_forward(
        split, True, *docs, queries, q_pair, blocks[split:], state
    )
    out_b, totals, out_mine, out_other = join(state_own, over_cores(state_pair))
    outs = everywhere([out_other if k % 2 else out_mine for k in range(n_tp)])
    out_pair = over_cores(out_b)
    totals_pair = over_cores(totals)

    got = pile(got, [(state_pair, "v")])
    *staged, x_part, cot_part, gain_one, gain_two = stage(
        n_tp, tokens, cotangent, in_t, w_down, w_out, gain_one, gain_two, got, over_cores(got)
    )
    middle, middle_part, h_two, mixed, gate_grad, gain_two_part, own, *others = feed(
        gain_two, staged, outs
    )
    arrived = [own] + [over_tp(others[n], 2 * n + 2) for n in range(n_tp // 2 - 1)]
    own, *others = down(n_tp, mixed, staged[4], middle, [(out_pair, "v"), (totals_pair, "v")])
    middle_grad, branch_grad, *pieces = branch(
        n_tp, middle_part, cot_part, gain_two, staged[2], arrived, [(own, "v")]
    )
    early, early_send = early_grads(
        mixed, gate_grad, cotangent, h_two, in_t, w_down, over_tp(h_two, 1), [(branch_grad, "v")]
    )
    early_back = over_cores(early_send)
    out_grad = lay_turned(everywhere(pieces), ())
    grad_pair = over_cores(out_grad)
    branches, branch_places = by_steps(branch_grad)

    held = (queries, q_pair, out_grad, grad_pair, out_b, out_pair, totals, totals_pair)
    *terms, dq = attention_backward(1, False, *docs, held, blocks[1:], None)
    total = total_of(
        [own] + [over_tp(others[n], 2 * n + 2) for n in range(n_tp // 2 - 1)],
        BF16,
        "v",
        [(dq, "v"), (branches[1], "v")],
    )

    dkv, dq_own, dq_pair = attention_backward(
        0, True, *docs, held, blocks[:1], dq, ()
    )
    dkvs = [dkv] + [over_chips(terms[j - 1], j) for j in range(count - 1, 0, -1)]

    proj_grad, *parts = unproject(
        n_tp,
        unit_one,
        qkv_t,
        cos_table,
        sin_table,
        gain_two_part,
        dq_own,
        over_cores(dq_pair),
        dkvs,
        [(total, "v")],
    )
    ways = everywhere(parts)
    totals_all, total_places = by_steps(total, ())
    keep, send = late_grads(
        n_tp, proj_grad, h_one, out_b, branches, branch_places, [(totals_all[1], "v")]
    )
    own, *others = spread(count, (keep, over_cores(send)), (early, early_back))
    summed = total_of([ways[0]] + [ways[i] for i in (1, 3, 2)], F32, flops=2_000_000_000)
    chip_sum = total_of(
        [own] + came(count, lambda k: over_chips(others[k - 1], k)), F32, "v", ()
    )
    layer_out = stack_parts(n_tp, totals_all, total_places)
    input_part, gains = input_side(x_part, gain_one, middle_grad, summed, [(own, "v")])
    inputs_all = everywhere([input_part] * n_tp)
    piece = sum_piece(gains, [chip_sum], ())
    input_grad = stack_parts(n_tp, inputs_all, singly, (), 3_000_000_000)
    collected = collect(
        [piece] + came(count, lambda k: over_chips(piece, k)), [(input_grad, "h"), (layer_out, "h")]
    )
    grad_qkv, grad_out, grad_down, grad_in, grad_one, grad_two = finish(
        collected, over_cores, (3 * width, width, units, 2 * units)
    )

    back = lambda x, n: x.reshape(-1, n, model).transpose(2, 0, 1)
    return (
        layer_out,
        input_grad,
        grad_one,
        back(grad_qkv, width),
        grad_out,
        grad_two,
        back(grad_in, units),
        grad_down,
    )


def solution(mesh):
    placed = (
        P("seq", None),
        P(),
        P(None, None, "tp"),
        P("tp", None),
        P(),
        P(None, None, "tp"),
        P("tp", None),
        P("seq", None),
        P(),
        P(),
    )
    return jax.shard_map(
        functools.partial(body, mesh.shape["seq"], mesh.shape["tp"]),
        mesh=mesh,
        in_specs=placed,
        out_specs=(
            P("seq", None),
            P("seq", None),
            P(),
            P(None, None, "tp"),
            P("tp", None),
            P(),
            P(None, None, "tp"),
            P("tp", None),
        ),
        check_vma=False,
    )
```

```python
import functools
import math

import jax
import jax.numpy as jnp
import numpy as np
from jax import lax
from jax.experimental import pallas as pl
from jax.experimental.pallas import tpu as pltpu
from jax.sharding import PartitionSpec as P

HDIM = 64
HALF = HDIM // 2
EPSILON = 1e-05
ROPE_THETA = 160000.0
MASKED = -1e30
AUG = 80
STRIP = 64
F32 = jnp.float32
BF16 = jnp.bfloat16
HBM = pl.BlockSpec(memory_space=pltpu.HBM)
VMEM = pl.BlockSpec(memory_space=pltpu.VMEM)

NN = (((1,), (0,)), ((), ()))
NT = (((1,), (1,)), ((), ()))
TN = (((0,), (0,)), ((), ()))


def params(mib):
    return pltpu.CompilerParams(vmem_limit_bytes=mib * 2**20)


def slot(tp, n_tp):
    return tp % 2 * (n_tp // 2) + tp // 2


def hop(n, count):
    return (count - n) % count


def came(count, send):
    return [send(hop(n, count)) for n in range(1, count)]


def mm(a, b, dims):
    return lax.dot_general(a, b, dims, preferred_element_type=F32)


def shaped(shape, dtype):
    return jax.ShapeDtypeStruct(shape, dtype)


def kinds(arrays, kind):
    return [(array, kind) for array in arrays]


def pin(array, kind):
    return array if kind in ("v", "free") else pltpu.with_memory_space_constraint(array, pltpu.HBM)


def call(name, kernel, ins, outs, scratch=(), mib=16, after=(), lazy=False, flops=0, alias=None):
    fetched = [i for i, given in enumerate(ins) if given[1] not in ("v", "raw", "free")]
    left = [i for i, out in enumerate(outs) if out[2] == "h"]

    def held(array, kind):
        rows = array.shape[0] if kind == "h" else kind
        return pltpu.VMEM((rows,) + array.shape[1:], array.dtype)

    def run(*refs):
        in_refs = list(refs[: len(ins)])
        at = len(ins) + len(after)
        out_refs = list(refs[at : at + len(outs)])
        at += len(outs)
        own = refs[at : at + len(scratch)]
        at += len(scratch)
        buffers = refs[at : at + len(fetched) + len(left)]
        sems = refs[-1]
        copies = []
        for n, i in enumerate(fetched):
            source = in_refs[i]
            if ins[i][1] != "h":
                rows = ins[i][1]
                n_tp = ins[i][0].shape[0] // rows
                at = pl.multiple_of(slot(lax.axis_index("tp"), n_tp) * rows, rows)
                source = source.at[pl.ds(at, rows)]
            copies.append(pltpu.make_async_copy(source, buffers[n], sems.at[n]))
            in_refs[i] = buffers[n]
        for copy in copies:
            copy.start()
        coming = dict(zip(fetched, copies))
        going = {}
        for n, i in enumerate(left):
            spot = len(fetched) + n
            going[i] = pltpu.make_async_copy(buffers[spot], out_refs[i], sems.at[spot])
            out_refs[i] = buffers[spot]
        gone = []

        def need(*which):
            for i in which:
                if i in coming:
                    coming.pop(i).wait()

        def give(*which):
            for i in which:
                if i in going:
                    gone.append(going.pop(i))
                    gone[-1].start()

        if lazy:
            kernel(need, give, *in_refs, *out_refs, *own)
        else:
            need(*fetched)
            kernel(*in_refs, *out_refs, *own)
        need(*fetched)
        give(*left)
        for copy in gone:
            copy.wait()

    spec = lambda kind: VMEM if kind == "v" else HBM
    count = len(fetched) + len(left)
    return pl.pallas_call(
        run,
        out_shape=tuple(
            shaped(shape, dtype) if kind == "v" else pltpu.HBM(shape, dtype)
            for shape, dtype, kind in outs
        ),
        in_specs=[spec(kind) for unused, kind in ins] + [spec(kind) for unused, kind in after],
        out_specs=tuple(spec(kind) for unused, unused, kind in outs),
        scratch_shapes=list(scratch)
        + [held(*ins[i]) for i in fetched]
        + [pltpu.VMEM(outs[i][0], outs[i][1]) for i in left]
        + [pltpu.SemaphoreType.DMA((max(count, 1),))],
        name=name,
        input_output_aliases=alias or {},
        cost_estimate=pl.CostEstimate(flops=flops, bytes_accessed=0, transcendentals=0)
        if flops
        else None,
        compiler_params=params(mib),
    )(*[pin(*given) for given in ins], *[pin(*given) for given in after])


def swap(x, axis, hop, count):
    return lax.ppermute(x, axis, [(i, i ^ hop) for i in range(count)])


def doc_scratch(doc_lengths, roster):
    return [pltpu.SMEM(doc_lengths.shape, jnp.int32), pltpu.SMEM(roster.shape, jnp.int32)]


def fetch_docs(len_any, roster_any, len_ref, roster_ref, len_sem, roster_sem):
    one = pltpu.make_async_copy(len_any, len_ref, len_sem)
    two = pltpu.make_async_copy(roster_any, roster_ref, roster_sem)
    one.start()
    two.start()
    one.wait()
    two.wait()


def doc_bounds(len_ref):
    ends, total = [], jnp.int32(0)
    for d in range(len_ref.shape[0]):
        total = total + len_ref[d]
        ends.append(total)
    return ends


def doc_of(ends, position):
    found = jnp.int32(0)
    for end in ends:
        found = found + (end <= position).astype(jnp.int32)
    return found


def meet(ends, base_a, base_b, rows):
    low = jnp.maximum(doc_of(ends, base_a), doc_of(ends, base_b))
    high = jnp.minimum(doc_of(ends, base_a + rows - 1), doc_of(ends, base_b + rows - 1))
    return low <= high


def doc_rows(ends, base, rows):
    spot = base + lax.broadcasted_iota(jnp.int32, (16, rows), 1)
    line = lax.broadcasted_iota(jnp.int32, (16, rows), 0)
    held = jnp.zeros((16, rows), F32)
    start = jnp.int32(0)
    for d, end in enumerate(ends):
        inside = (line == d) & (spot >= start) & (spot < end)
        held = jnp.where(inside, 1.0, held)
        start = end
    return held


def ban_rows(ends, base, rows):
    line = lax.broadcasted_iota(jnp.int32, (16, rows), 0)
    held = doc_rows(ends, base, rows)
    return jnp.where((held > 0.5) | (line >= len(ends)), 0.0, MASKED)


def key_row(block, seq_index):
    return seq_index ^ (2 * block)


def place_row(ends, base, rows):
    spot = base + lax.broadcasted_iota(jnp.int32, (1, rows), 1)
    start = jnp.zeros((1, rows), jnp.int32)
    for end in ends:
        start = jnp.where(spot >= end, end, start)
    return (spot - start).astype(F32)


def normed(values):
    centre = jnp.mean(values, axis=-1, keepdims=True)
    shifted = values - centre
    spread = jnp.mean(shifted * shifted, axis=-1, keepdims=True)
    scale = lax.rsqrt(spread + EPSILON)
    return shifted * scale, scale


def norm_back(unit, scale, grad, gain):
    u = grad * gain
    mean_u = jnp.mean(u, axis=-1, keepdims=True)
    mean_un = jnp.mean(u * unit, axis=-1, keepdims=True)
    return scale * (u - mean_u - unit * mean_un)


def project_kernel(
    width, need, give, len_any, roster_any, x_ref, w_ref, gain_ref, freq_ref, *refs
):
    q_out, kv_out, h_out, cos_out, sin_out, unit_out = refs[:6]
    proj, len_ref, roster_ref, sems = refs[6:]
    rows = x_ref.shape[0]
    fetch_docs(len_any, roster_any, len_ref, roster_ref, sems.at[0], sems.at[1])
    need(5)
    ends = doc_bounds(len_ref)
    place = place_row(ends, roster_ref[lax.axis_index("seq")] * rows, rows)
    angles = place * freq_ref[...]
    cos_table = jnp.cos(angles)
    sin_table = jnp.sin(angles)
    cos_out[...] = cos_table
    sin_out[...] = sin_table
    give(3, 4)
    need(2, 4)
    gain = gain_ref[...].reshape(1, -1)

    def strip(i, carry):
        at = pl.ds(i * STRIP, STRIP)
        unit, unused = normed(x_ref[at, :].astype(F32))
        unit_out[at, :] = unit
        h_out[at, :] = (unit * gain).astype(BF16)
        return carry

    lax.fori_loop(0, rows // STRIP, strip, 0)
    give(2)
    need(3)
    proj[...] = mm(w_ref[...], h_out[...], NT)
    for at in range(0, 2 * width, HDIM):
        low = proj[at : at + HALF, :]
        high = proj[at + HALF : at + HDIM, :]
        turned_low = (low * cos_out[...] - high * sin_out[...]).astype(BF16)
        turned_high = (high * cos_out[...] + low * sin_out[...]).astype(BF16)
        if at < width:
            q_out[at : at + HALF, :] = (turned_low.astype(F32) * HDIM**-0.5).astype(BF16)
            q_out[at + HALF : at + HDIM, :] = (turned_high.astype(F32) * HDIM**-0.5).astype(BF16)
        else:
            kv_out[at - width : at - width + HALF, :] = turned_low
            kv_out[at - width + HALF : at - width + HDIM, :] = turned_high
    kv_out[width:, :] = proj[2 * width :, :].astype(BF16)


def project(doc_lengths, roster, tokens, gain, qkv_t):
    rows, model = tokens.shape
    width = qkv_t.shape[0] // 3
    freq = (ROPE_THETA ** -(np.arange(HALF) * (2.0 / HDIM))).astype(np.float32)[:, None]
    return call(
        "project",
        functools.partial(project_kernel, width),
        kinds((doc_lengths, roster), "raw") + kinds((tokens, qkv_t, gain, jnp.asarray(freq)), "h"),
        [
            ((width, rows), BF16, "v"),
            ((2 * width, rows), BF16, "v"),
            ((rows, model), BF16, "v"),
            ((HALF, rows), F32, "v"),
            ((HALF, rows), F32, "v"),
            ((rows, model), F32, "v"),
        ],
        [pltpu.VMEM((3 * width, rows), F32)]
        + doc_scratch(doc_lengths, roster)
        + [pltpu.SemaphoreType.DMA((2,))],
        lazy=True,
    )


def forward_kernel(first, count, heads, last, len_any, roster_any, q_own, q_pair, *refs):
    kv_refs = refs[:count]
    refs = refs[count:]
    if first:
        state_in, refs = refs[0], refs[1:]
    outs = refs[: 2 if last else 1]
    kv, q_aug, state, len_ref, roster_ref, sems = refs[len(outs) :]
    rows = q_own.shape[1]
    width = heads * HDIM
    me = lax.axis_index("seq")
    copies = [pltpu.make_async_copy(kv_refs[j], kv.at[j], sems.at[j]) for j in range(count)]
    for copy in copies:
        copy.start()
    fetch_docs(len_any, roster_any, len_ref, roster_ref, sems.at[count], sems.at[count + 1])
    ends = doc_bounds(len_ref)
    bases = (roster_ref[me] * rows, roster_ref[me ^ 1] * rows)
    for g, q_ref in enumerate((q_own, q_pair)):
        mark = doc_rows(ends, bases[g], rows).astype(BF16)
        for h in range(heads):
            q_aug[g * heads + h, :HDIM, :] = q_ref[h * HDIM : (h + 1) * HDIM, :]
            q_aug[g * heads + h, HDIM:, :] = mark
    if first:
        state[...] = state_in[...]
    else:
        line = lax.broadcasted_iota(jnp.int32, (2 * heads, AUG, rows), 1)
        state[...] = jnp.where(line >= 72, MASKED, 0.0)
    for copy in copies:
        copy.wait()

    top = lax.broadcasted_iota(jnp.int32, (16, rows), 0) == 0
    ones = jnp.where(top, 1.0, 0.0).astype(BF16)

    def block(j, carry):
        key_base = roster_ref[key_row(j + first, me)] * rows
        ban = ban_rows(ends, key_base, rows).astype(BF16)
        for g in range(2):

            @pl.when(meet(ends, bases[g], key_base, rows))
            def _():
                for h in range(heads):
                    at = g * heads + h
                    keys = jnp.concatenate([kv[j, h * HDIM : (h + 1) * HDIM, :], ban], axis=0)
                    vals = jnp.concatenate(
                        [kv[j, width + h * HDIM : width + (h + 1) * HDIM, :], ones], axis=0
                    )
                    scores = mm(keys, q_aug[at], TN)
                    old = state[at, 72:73, :]
                    new = jnp.maximum(old, jnp.max(scores, axis=0, keepdims=True))
                    probs = jnp.exp(scores - new).astype(BF16)
                    part = mm(vals, probs, NN)
                    fade = jnp.exp(old - new)
                    state[at, :72, :] = state[at, :72, :] * fade + part[:72]
                    state[at, 72:, :] = jnp.broadcast_to(new, (8, rows))

        return carry

    lax.fori_loop(0, count, block, 0)
    if last:
        outs[0][...] = state[:heads]
        outs[1][...] = state[heads:]
    else:
        outs[0][...] = state[...]


def attention_forward(first, last, doc_lengths, roster, q_own, q_pair, blocks, state=None, after=()):
    width, rows = q_own.shape
    heads = width // HDIM
    count = len(blocks)
    half = ((heads, AUG, rows), F32, "v")
    whole = ((2 * heads, AUG, rows), F32, "v")
    given = [] if state is None else [(state, "v")]
    return call(
        "attention_forward",
        functools.partial(forward_kernel, first, count, heads, last),
        [(doc_lengths, "raw"), (roster, "raw"), (q_own, "v"), (q_pair, "v")]
        + kinds(blocks, "free")
        + given,
        [half, half] if last else [whole],
        [
            pltpu.VMEM((count, 2 * width, rows), BF16),
            pltpu.VMEM((2 * heads, AUG, rows), BF16),
            pltpu.VMEM((2 * heads, AUG, rows), F32),
        ]
        + doc_scratch(doc_lengths, roster)
        + [pltpu.SemaphoreType.DMA((count + 2,))],
        16 if count < 8 else 40,
        after,
    )


def backward_kernel(first, count, heads, more, last, len_any, roster_any, *refs):
    q_own, q_pair, g_own, g_pair, o_own, o_pair, t_own, t_pair = refs[:8]
    kv_refs, refs = refs[8 : 8 + count], refs[8 + count :]
    if more:
        dq_in, refs = refs[0], refs[1:]
    outs, refs = refs[:count], refs[count:]
    dq_outs, refs = (refs[:2], refs[2:]) if last else (refs[:1], refs[1:])
    kv, q_aug, delta, dq, dkv, len_ref, roster_ref, sems = refs
    rows = q_own.shape[1]
    width = heads * HDIM
    me = lax.axis_index("seq")
    copies = [pltpu.make_async_copy(kv_refs[j], kv.at[j], sems.at[j]) for j in range(count)]
    for copy in copies:
        copy.start()
    fetch_docs(len_any, roster_any, len_ref, roster_ref, sems.at[count], sems.at[count + 1])
    ends = doc_bounds(len_ref)
    bases = (roster_ref[me] * rows, roster_ref[me ^ 1] * rows)
    for g, (q_ref, g_ref, o_ref) in enumerate(((q_own, g_own, o_own), (q_pair, g_pair, o_pair))):
        mark = doc_rows(ends, bases[g], rows).astype(BF16)
        for h in range(heads):
            part = slice(h * HDIM, (h + 1) * HDIM)
            q_aug[g * heads + h, :HDIM, :] = q_ref[part, :]
            q_aug[g * heads + h, HDIM:, :] = mark
            product = g_ref[part, :].astype(F32) * o_ref[part, :].astype(F32)
            delta[g * heads + h] = jnp.broadcast_to(
                jnp.sum(product, axis=0, keepdims=True), (8, rows)
            )
    if more:
        dq[...] = dq_in[...]
    else:
        dq[...] = jnp.zeros_like(dq)
    for copy in copies:
        copy.wait()

    def block(j, carry):
        key_base = roster_ref[key_row(j + first, me)] * rows
        ban = ban_rows(ends, key_base, rows).astype(BF16)
        dkv[j] = jnp.zeros((2 * width, rows), F32)
        for g, (g_ref, t_ref) in enumerate(((g_own, t_own), (g_pair, t_pair))):

            @pl.when(meet(ends, bases[g], key_base, rows))
            def _():
                for h in range(heads):
                    at = g * heads + h
                    part = slice(h * HDIM, (h + 1) * HDIM)
                    late = slice(width + h * HDIM, width + (h + 1) * HDIM)
                    keys = kv[j, part, :]
                    scores = mm(jnp.concatenate([keys, ban], axis=0), q_aug[at], TN)
                    probs = jnp.exp(scores - t_ref[h, 0:1, :])
                    prob_grads = mm(kv[j, late, :], g_ref[part, :], TN)
                    score_grad = (probs * (prob_grads - delta[at, 0:1, :])).astype(BF16)
                    dkv[j, late, :] += mm(g_ref[part, :], probs.astype(BF16), NT)
                    dkv[j, part, :] += mm(q_aug[at, :HDIM, :], score_grad, NT)
                    dq[at] += mm(keys, score_grad, NN)

        return carry

    lax.fori_loop(0, count, block, 0)
    for j in range(count):
        outs[j][...] = dkv[j].astype(outs[j].dtype)
    if last:
        for h in range(heads):
            part = slice(h * HDIM, (h + 1) * HDIM)
            dq_outs[0][part, :] = dq[h] * HDIM**-0.5
            dq_outs[1][part, :] = (dq[heads + h] * HDIM**-0.5).astype(BF16)
    else:
        dq_outs[0][...] = dq[...]


def attention_backward(first, last, doc_lengths, roster, held, blocks, dq=None, after=()):
    width, rows = held[0].shape
    heads = width // HDIM
    count = len(blocks)
    given = [] if dq is None else [(dq, "v")]
    if last:
        queries = [((width, rows), F32, "v"), ((width, rows), BF16, "v")]
    else:
        queries = [((2 * heads, HDIM, rows), F32, "v")]
    return call(
        "attention_backward",
        functools.partial(backward_kernel, first, count, heads, bool(given), last),
        kinds((doc_lengths, roster), "raw") + kinds(held, "v") + kinds(blocks, "free") + given,
        [((2 * width, rows), BF16 if first else F32, "v")] * count + queries,
        [
            pltpu.VMEM((count, 2 * width, rows), BF16),
            pltpu.VMEM((2 * heads, AUG, rows), BF16),
            pltpu.VMEM((2 * heads, 8, rows), F32),
            pltpu.VMEM((2 * heads, HDIM, rows), F32),
            pltpu.VMEM((count, 2 * width, rows), F32),
        ]
        + doc_scratch(doc_lengths, roster)
        + [pltpu.SemaphoreType.DMA((count + 2,))],
        16 if count < 8 else 40,
        after,
        flops=0 if last else 0,
    )


def join_kernel(heads, own_ref, back_ref, out_ref, total_ref, mine_ref, other_ref):
    rows = own_ref.shape[2]
    for h in range(heads):
        top_own = own_ref[h, 72:73, :]
        top_back = back_ref[h, 72:73, :]
        top = jnp.maximum(top_own, top_back)
        fade_own = jnp.exp(top_own - top)
        fade_back = jnp.exp(top_back - top)
        total = own_ref[h, 64:65, :] * fade_own + back_ref[h, 64:65, :] * fade_back
        share_own = fade_own / total
        share_back = fade_back / total
        value = own_ref[h, :HDIM, :] * share_own + back_ref[h, :HDIM, :] * share_back
        out_ref[h * HDIM : (h + 1) * HDIM, :] = value.astype(BF16)
        total_ref[h] = jnp.broadcast_to(top + jnp.log(total), (8, rows))
    half = rows // 2
    for bit in range(2):

        @pl.when(lax.axis_index("tp") % 2 == bit)
        def _():
            mine_ref[...] = out_ref[:, bit * half : (bit + 1) * half]
            other_ref[...] = out_ref[:, (1 - bit) * half : (2 - bit) * half]


def join(own, back):
    heads, unused, rows = own.shape
    return call(
        "join",
        functools.partial(join_kernel, heads),
        [(own, "v"), (back, "v")],
        [
            ((heads * HDIM, rows), BF16, "v"),
            ((heads, 8, rows), F32, "v"),
            ((heads * HDIM, rows // 2), BF16, "v"),
            ((heads * HDIM, rows // 2), BF16, "v"),
        ],
    )


def pick_kernel(in_any, down_any, w_any, all_ref, w_ref, sems):
    core = lax.axis_index("seq") % 2
    at = 0
    copies = []
    for source in (in_any, down_any, w_any):
        rows = source.shape[0] // 2
        mine = pl.ds(pl.multiple_of(core * rows, rows), rows)
        copies.append((source.at[mine], all_ref.at[pl.ds(at, rows)]))
        at += rows
    copies.append((w_any.at[mine], w_ref))
    copies = [pltpu.make_async_copy(*move, sems.at[n]) for n, move in enumerate(copies)]
    for copy in copies:
        copy.start()
    for copy in copies:
        copy.wait()


def pick(in_t, w_down, w_out, after=()):
    rows = (in_t.shape[0] + w_down.shape[0] + w_out.shape[0]) // 2
    model = w_out.shape[1]
    return call(
        "pick",
        pick_kernel,
        kinds((in_t, w_down, w_out), "raw"),
        [((rows, model), BF16, "v"), ((w_out.shape[0] // 2, model), BF16, "v")],
        [pltpu.SemaphoreType.DMA((4,))],
        16,
        after,
    )


def pile_kernel(*refs):
    out_ref = refs[-1]
    at = 0
    for ref in refs[:-1]:
        out_ref[at : at + ref.shape[0], :] = ref[...]
        at += ref.shape[0]


def pile(values, after):
    rows = sum(value.shape[0] for value in values)
    (out,) = call(
        "pile",
        pile_kernel,
        kinds(values, "v"),
        [((rows, values[0].shape[1]), BF16, "v")],
        (),
        16,
        after,
    )
    return out


def stage_kernel(
    x_any, cot_any, in_any, down_any, w_any, one_any, two_any, got_ref, rest_ref, *refs
):
    x_ref, cot_ref, w_ref, in_ref, down_ref, x_part, cot_part, one_ref, two_ref, sems = refs
    half = x_ref.shape[0]
    core = lax.axis_index("seq") % 2
    tp = lax.axis_index("tp")
    n_tp = w_ref.shape[0] // w_any.shape[0]
    mine = pl.ds(pl.multiple_of(tp % 2 * half, half), half)
    width = w_any.shape[0]
    rows = width // 2
    own = pl.ds(pl.multiple_of(tp * width, width), width)
    part = x_part.shape[0]
    kept = pl.ds(pl.multiple_of(slot(tp, n_tp) * part, part), part)
    moves = [(w_any, w_ref.at[own]), (x_any.at[mine], x_ref), (cot_any.at[mine], cot_ref)]
    moves += [(x_any.at[kept], x_part), (cot_any.at[kept], cot_part)]
    moves += [(one_any, one_ref), (two_any, two_ref)]
    sides = ((got_ref, core), (rest_ref, 1 - core))
    first = got_ref.shape[0] - (n_tp - 1) * rows
    for k in range(1, n_tp):
        for source, side in sides:
            spot = pl.multiple_of((tp ^ k) * width + side * rows, rows)
            piece = source.at[pl.ds(first + (k - 1) * rows, rows)]
            moves.append((piece, w_ref.at[pl.ds(spot, rows)]))
    at = 0
    for own, ref in ((in_any, in_ref), (down_any, down_ref)):
        rows = own.shape[0] // 2
        moves.append((own, ref.at[pl.ds(0, 2 * rows)]))
        for source, side in sides:
            spot = pl.multiple_of(2 * rows + side * rows, rows)
            moves.append((source.at[pl.ds(at, rows)], ref.at[pl.ds(spot, rows)]))
        at += rows
    copies = [pltpu.make_async_copy(*move, sems.at[n]) for n, move in enumerate(moves)]
    for copy in copies:
        copy.start()
    for copy in copies:
        copy.wait()


def stage(n_tp, tokens, cotangent, in_t, w_down, w_out, gain_one, gain_two, got, rest):
    rows, model = tokens.shape
    return call(
        "stage",
        stage_kernel,
        kinds((tokens, cotangent, in_t, w_down, w_out, gain_one, gain_two), "raw")
        + kinds((got, rest), "v"),
        [
            ((rows // 2, model), BF16, "v"),
            ((rows // 2, model), BF16, "v"),
            ((n_tp * w_out.shape[0], model), BF16, "v"),
            ((2 * in_t.shape[0], model), BF16, "v"),
            ((2 * w_down.shape[0], model), BF16, "v"),
            ((rows // n_tp, model), BF16, "v"),
            ((rows // n_tp, model), BF16, "v"),
            ((model,), F32, "v"),
            ((model,), F32, "v"),
        ],
        [pltpu.SemaphoreType.DMA((11 + 2 * n_tp,))],
    )


def gated(units, first, gate_up, mixed_grad, mixed_out, gate_out):
    rows = math.gcd(units, 96)

    def wave(i, carry):
        spot = pl.ds(first + i * rows, rows)
        at = pl.ds(2 * first + i * rows, rows)
        late = pl.ds(2 * first + units + i * rows, rows)
        gate = gate_up[at, :]
        up = gate_up[late, :]
        back = mixed_grad[spot, :]
        bell = 0.5 * (1.0 + lax.erf(gate * (2.0**-0.5)))
        active = gate * bell
        slope = bell + gate * jnp.exp(-0.5 * gate * gate) * ((2.0 * jnp.pi) ** -0.5)
        mixed_out[spot, :] = (active * up).astype(BF16)
        gate_out[at, :] = (back * up * slope).astype(BF16)
        gate_out[late, :] = (back * active).astype(BF16)
        return carry

    lax.fori_loop(0, units // rows, wave, 0)


def feed_kernel(n_tp, need, give, x_ref, cot_ref, w_ref, in_ref, down_ref, gain_ref, *refs):
    out_refs = refs[:n_tp]
    middle_out, part_out, h_out, mixed_out, gate_out, gain_out = refs[n_tp : n_tp + 6]
    keep_ref, *send_refs = refs[n_tp + 6 : n_tp + 6 + n_tp // 2]
    outs, unit, gate_up, mixed_grad, grad = refs[n_tp + 6 + n_tp // 2 :]
    rows = x_ref.shape[0]
    part = keep_ref.shape[0]
    units = down_ref.shape[0] // 2
    width = out_refs[0].shape[0]
    tp = lax.axis_index("tp")
    for k in range(n_tp):
        at = pl.ds(pl.multiple_of((tp ^ hop(k, n_tp)) * width, width), width)
        outs[at, :] = out_refs[k][...]
    mixed_grad[...] = mm(down_ref[...], cot_ref[...], NT)
    middle_out[...] = mm(outs[...], w_ref[...], TN)
    need(5)
    gain = gain_ref[...].reshape(1, -1)

    def strip(i, carry):
        at = pl.ds(i * 32, 32)
        middle = middle_out[at, :] + x_ref[at, :].astype(F32)
        middle_out[at, :] = middle
        held, unused = normed(middle)
        unit[at, :] = held
        h_out[at, :] = (held * gain).astype(BF16)
        return carry

    lax.fori_loop(0, rows // 32, strip, 0)
    give(0, 2)
    gate_up[...] = mm(in_ref[...], h_out[...], NT)
    for first in (0, units):
        gated(units, first, gate_up, mixed_grad, mixed_out, gate_out)
    give(3, 4)
    grad[...] = mm(gate_out[...], in_ref[...], TN)
    for n, ref in enumerate((keep_ref, *send_refs)):
        at = pl.ds(pl.multiple_of((tp ^ (2 * n)) // 2 * part, part), part)
        ref[...] = grad[at, :].astype(ref.dtype)
        give(6 + n)
    own = pl.ds(pl.multiple_of(tp // 2 * part, part), part)
    part_out[...] = middle_out[own, :]
    give(1)

    def gains(i, carry):
        at = pl.ds(i * 32, 32)
        product = grad[at, :] * unit[at, :]
        return carry + jnp.sum(product.reshape(4, 8, -1), axis=0)

    gain_out[...] = lax.fori_loop(0, rows // 32, gains, jnp.zeros(gain_out.shape, F32))


def feed(gain, staged, outs):
    rows, model = staged[0].shape
    n_tp = len(outs)
    units = staged[4].shape[0]
    part = 2 * rows // n_tp
    return call(
        "feed",
        functools.partial(feed_kernel, n_tp),
        kinds((*staged, gain, *outs), "v"),
        [
            ((rows, model), F32, "v"),
            ((part, model), F32, "v"),
            ((rows, model), BF16, "v"),
            ((units, rows), BF16, "v"),
            ((2 * units, rows), BF16, "v"),
            ((8, model), F32, "v"),
            ((part, model), F32, "v"),
        ]
        + [((part, model), BF16, "v")] * (n_tp // 2 - 1),
        [
            pltpu.VMEM((n_tp * outs[0].shape[0], rows), BF16),
            pltpu.VMEM((rows, model), F32),
            pltpu.VMEM((2 * units, rows), F32),
            pltpu.VMEM((units, rows), F32),
            pltpu.VMEM((rows, model), F32),
        ],
        24,
        lazy=True,
    )


def branch_kernel(n_tp, count, need, give, middle_ref, cot_ref, gain_ref, w_ref, *refs):
    arrived = refs[:count]
    grad_out, branch_out = refs[count : count + 2]
    piece_refs = refs[count + 2 :]
    width = piece_refs[0].shape[1]
    tp = lax.axis_index("tp")
    need(0, 1, 2, 4)
    total = arrived[0][...]
    for ref in arrived[1:]:
        total = total + ref[...].astype(F32)
    unit, scale = normed(middle_ref[...])
    gain = gain_ref[...].reshape(1, -1)
    value = cot_ref[...].astype(F32) + norm_back(unit, scale, total, gain)
    grad_out[...] = value
    branch_out[...] = value.astype(BF16)
    give(0, 1)
    need(3)
    for k in range(n_tp):
        at = pl.ds(pl.multiple_of((tp ^ k) * width, width), width)
        piece_refs[k][...] = mm(branch_out[...], w_ref[at, :], NT).astype(BF16)


def branch(n_tp, middle_part, cotangent, gain, w_full, arrived, after):
    part, model = arrived[0].shape
    width = w_full.shape[0] // n_tp
    return call(
        "branch",
        functools.partial(branch_kernel, n_tp, len(arrived)),
        [(middle_part, "v"), (cotangent, "v")]
        + [(gain, "v"), (w_full, "v"), (arrived[0], "v")]
        + kinds(arrived[1:], "v"),
        [((part, model), F32, "v"), ((part, model), BF16, "v")]
        + [((part, width), BF16, "v")] * n_tp,
        (),
        16,
        after,
        True,
    )


def lay_kernel(n_tp, *refs):
    out_ref, held = refs[n_tp:]
    part = refs[0].shape[0]
    tp = lax.axis_index("tp")
    for k in range(n_tp):
        at = pl.ds(pl.multiple_of(slot(tp ^ hop(k, n_tp), n_tp) * part, part), part)
        held[at, :] = refs[k][...].astype(F32)
    out_ref[...] = held[...].T.astype(BF16)


def lay_turned(pieces, after):
    part, width = pieces[0].shape
    rows = part * len(pieces)
    (out,) = call(
        "lay_turned",
        functools.partial(lay_kernel, len(pieces)),
        kinds(pieces, "v"),
        [((width, rows), BF16, "v")],
        [pltpu.VMEM((rows, width), F32)],
        16,
        after,
    )
    return out


def lay_rows(out_ref, n_tp, places, refs):
    part = out_ref.shape[0] // n_tp
    tp = lax.axis_index("tp")
    for ks, ref in zip(places, refs):
        for n, k in enumerate(ks):
            at = pl.ds(pl.multiple_of(slot(tp ^ k, n_tp) * part, part), part)
            out_ref[at, :] = ref[n * part : (n + 1) * part, :]


def stack_kernel(n_tp, places, *refs):
    lay_rows(refs[-1], n_tp, places, refs[:-1])


def stack_parts(n_tp, pieces, places, after=(), flops=0):
    part, model = pieces[0].shape
    (out,) = call(
        "stack_parts",
        functools.partial(stack_kernel, n_tp, places),
        kinds(pieces, "v"),
        [((part * n_tp, model), pieces[0].dtype, "h")],
        (),
        16,
        after,
        flops=flops,
    )
    return out


def turn_back(out_ref, first, value, cos_table, sin_table):
    for at in range(0, value.shape[0], HDIM):
        low = value[at : at + HALF]
        high = value[at + HALF : at + HDIM]
        spot = first + at
        out_ref[spot : spot + HALF, :] = (low * cos_table + high * sin_table).astype(BF16)
        out_ref[spot + HALF : spot + HDIM, :] = (high * cos_table - low * sin_table).astype(BF16)


def unproject_kernel(
    count, n_tp, need, give, x_ref, w_ref, cos_ref, sin_ref, two_ref, dq_ref, dq_back, *refs
):
    dkv_refs = refs[:count]
    proj_out = refs[count]
    part_refs = refs[count + 1 : count + 1 + n_tp]
    grad, dkv = refs[count + 1 + n_tp :]
    rows, model = x_ref.shape
    part = rows // n_tp
    width = dq_ref.shape[0]
    tp = lax.axis_index("tp")
    need(2, 3)
    cos_table = cos_ref[...]
    sin_table = sin_ref[...]
    turn_back(proj_out, 0, dq_ref[...] + dq_back[...].astype(F32), cos_table, sin_table)
    total = dkv_refs[0][...]
    for ref in dkv_refs[1:]:
        total = total + ref[...].astype(F32)
    dkv[...] = total
    turn_back(proj_out, width, dkv[:width, :], cos_table, sin_table)
    proj_out[2 * width :, :] = dkv[width:, :].astype(BF16)
    need(1)
    grad[...] = mm(proj_out[...], w_ref[...], TN)
    need(0, 4)

    def gains(i, carry):
        at = pl.ds(i * STRIP, STRIP)
        product = grad[at, :] * x_ref[at, :]
        return carry + jnp.sum(product.reshape(STRIP // 8, 8, -1), axis=0)

    gain = lax.fori_loop(0, rows // STRIP, gains, jnp.zeros((8, model), F32))
    line = lax.broadcasted_iota(jnp.int32, (16, model), 0)
    gain_two = jnp.sum(two_ref[...], axis=0, keepdims=True)
    gain = jnp.sum(gain, axis=0, keepdims=True)
    gain = jnp.where(line == 0, gain, jnp.where(line == 1, gain_two, 0.0))
    for k in range(n_tp):
        at = pl.ds(pl.multiple_of(slot(tp ^ k, n_tp) * part, part), part)
        part_refs[k][:part, :] = grad[at, :].astype(part_refs[k].dtype)
        part_refs[k][part:, :] = gain.astype(part_refs[k].dtype)


def unproject(n_tp, tokens, qkv_t, cos_table, sin_table, gain_two_part, dq, dq_back, dkvs, after):
    rows, model = tokens.shape
    part = rows // n_tp
    return call(
        "unproject",
        functools.partial(unproject_kernel, len(dkvs), n_tp),
        kinds((tokens, qkv_t, cos_table, sin_table, gain_two_part), "v")
        + kinds((dq, dq_back, *dkvs), "v"),
        [((qkv_t.shape[0], rows), BF16, "v"), ((part + 16, model), F32, "v")]
        + [((part + 16, model), BF16, "v")] * (n_tp - 1),
        [pltpu.VMEM((rows, model), F32), pltpu.VMEM(dkvs[0].shape, F32)],
        16,
        after,
        True,
    )


def input_kernel(x_ref, gain_ref, grad_ref, sum_ref, out_ref, gain_out):
    part, model = grad_ref.shape
    total = sum_ref[...]
    unit, scale = normed(x_ref[...].astype(F32))
    gain = gain_ref[...].reshape(1, -1)
    value = grad_ref[...] + norm_back(unit, scale, total[:part], gain)
    out_ref[...] = value.astype(BF16)
    gain_out[...] = total[part : part + 8]


def input_side(tokens, gain, middle_grad, summed, after):
    part, model = middle_grad.shape
    return call(
        "input_side",
        input_kernel,
        kinds((tokens, gain, middle_grad, summed), "v"),
        [((part, model), BF16, "v"), ((8, model), F32, "v")],
        (),
        16,
        after,
    )


def early_kernel(mixed_ref, gate_ref, cot_ref, h_ref, in_ref, down_ref, h_pair, *refs):
    keep_ref, send_ref, gate_up, mixed_grad, mixed, gate = refs
    units = down_ref.shape[0]
    half = h_ref.shape[0]
    bit = lax.axis_index("tp") % 2
    mine = pl.ds(pl.multiple_of(bit * half, half), half)
    other = pl.ds(pl.multiple_of((1 - bit) * half, half), half)
    gate_up[...] = mm(in_ref[...], h_pair[...], NT)
    mixed_grad[...] = mm(down_ref[...], cot_ref[other, :], NT)
    gated(units, 0, gate_up, mixed_grad, mixed, gate)
    width = keep_ref.shape[1]
    core = lax.axis_index("seq") % 2
    for ref, side in ((send_ref, 1 - core), (keep_ref, core)):
        columns = pl.ds(pl.multiple_of(side * width, width), width)
        down = mm(mixed_ref[:units, :], cot_ref[mine, columns], NN)
        down = down + mm(mixed[...], cot_ref[other, columns], NN)
        ref[:units, :] = down.astype(ref.dtype)
        both = mm(gate_ref[: 2 * units, :], h_ref[:, columns], NN)
        both = both + mm(gate[...], h_pair[:, columns], NN)
        ref[units:, :] = both.astype(ref.dtype)


def early_grads(mixed, gate_grad, cotangent, h_two, in_t, w_down, h_pair, after):
    units, model = w_down.shape
    half = h_two.shape[0]
    return call(
        "early_grads",
        early_kernel,
        kinds((mixed, gate_grad, cotangent, h_two, in_t, w_down, h_pair), "v"),
        [((3 * units, model // 2), F32, "v"), ((3 * units, model // 2), BF16, "v")],
        [
            pltpu.VMEM((2 * units, half), F32),
            pltpu.VMEM((units, half), F32),
            pltpu.VMEM((units, half), BF16),
            pltpu.VMEM((2 * units, half), BF16),
        ],
        24,
        after,
    )


def late_kernel(n_tp, places, proj_ref, h_ref, out_ref, *refs):
    branch_refs = refs[: len(places)]
    keep_ref, send_ref, branch_full = refs[len(places) :]
    half = keep_ref.shape[1]
    wide = proj_ref.shape[0]
    core = lax.axis_index("seq") % 2
    lay_rows(branch_full, n_tp, places, branch_refs)
    for ref, side in ((send_ref, 1 - core), (keep_ref, core)):
        columns = pl.ds(pl.multiple_of(side * half, half), half)
        ref[:wide, :] = mm(proj_ref[...], h_ref[:, columns], NN).astype(ref.dtype)
        ref[wide:, :] = mm(out_ref[...], branch_full[:, columns], NN).astype(ref.dtype)


def late_grads(n_tp, proj_grad, h_one, out_b, branches, places, after):
    rows, model = h_one.shape
    wide = proj_grad.shape[0] + out_b.shape[0]
    return call(
        "late_grads",
        functools.partial(late_kernel, n_tp, places),
        [(proj_grad, "v"), (h_one, "v"), (out_b, "v"), (branches[0], "v")]
        + kinds(branches[1:], "v"),
        [((wide, model // 2), F32, "v"), ((wide, model // 2), BF16, "v")],
        [pltpu.VMEM((rows, model), BF16)],
        16,
        after,
    )


def spread_kernel(count, *refs):
    given, outs, held = refs[: -count - 1], refs[-count - 1 : -1], refs[-1]
    piece = outs[0].shape[0]
    chip = lax.axis_index("seq") // 2
    at = 0
    for keep_ref, back_ref in zip(given[::2], given[1::2]):
        rows = keep_ref.shape[0]
        held[at : at + rows, :] = keep_ref[...] + back_ref[...].astype(F32)
        at += rows
    if at < held.shape[0]:
        held[at:, :] = jnp.zeros((held.shape[0] - at, held.shape[1]), F32)
    for k in range(count):
        at = pl.ds(pl.multiple_of((chip ^ k) * piece, piece), piece)
        outs[k][...] = held[at, :].astype(outs[k].dtype)


def spread(count, *pairs):
    half = pairs[0][0].shape[1]
    rows = sum(keep.shape[0] for keep, unused in pairs)
    piece = -(-rows // (8 * count)) * 8
    return call(
        "spread",
        functools.partial(spread_kernel, count),
        [(array, "v") for pair in pairs for array in pair],
        [((piece, half), F32, "v")] + [((piece, half), BF16, "v")] * (count - 1),
        [pltpu.VMEM((count * piece, half), F32)],
    )


def piece_kernel(count, gain_ref, *refs):
    out_ref = refs[count]
    half = out_ref.shape[1]
    total = refs[0][...]
    for ref in refs[1:count]:
        total = total + ref[...].astype(F32)
    line = lax.broadcasted_iota(jnp.int32, (16, half), 0)
    gains = jnp.zeros((16, half), F32)
    for at in range(4):
        row = gain_ref[at // 2 : at // 2 + 1, at % 2 * half : (at % 2 + 1) * half]
        gains = jnp.where(line == at, row, gains)
    out_ref[...] = jnp.concatenate([total, gains], axis=0).astype(BF16)


def sum_piece(gains, pieces, after=()):
    piece, half = pieces[0].shape
    (out,) = call(
        "sum_piece",
        functools.partial(piece_kernel, len(pieces)),
        [(gains, "v")] + kinds(pieces, "v"),
        [((piece + 16, half), BF16, "v")],
        (),
        16,
        after,
    )
    return out


def collect_kernel(count, *refs):
    out_ref, held = refs[count:]
    piece = refs[0].shape[0] - 16
    wide = count * piece
    chip = lax.axis_index("seq") // 2
    gains = jnp.zeros((16, out_ref.shape[1]), F32)
    for k in range(count):
        at = pl.ds(pl.multiple_of((chip ^ hop(k, count)) * piece, piece), piece)
        whole = refs[k][...].astype(F32)
        held[at, :] = whole[:piece]
        gains = gains + whole[piece:]
    held[wide:, :] = gains
    out_ref[...] = held[...].astype(BF16)


def collect(pieces, after=()):
    piece, half = pieces[0].shape
    wide = (piece - 16) * len(pieces) + 16
    (out,) = call(
        "collect",
        functools.partial(collect_kernel, len(pieces)),
        kinds(pieces, "v"),
        [((wide, half), BF16, "v")],
        [pltpu.VMEM((wide, half), F32)],
        16,
        after,
    )
    return out


def write_half(sizes, source, side, out_refs, held, sems):
    half = source.shape[1]
    columns = pl.ds(pl.multiple_of(side * half, half), half)
    at = 0
    copies = []
    for n, (ref, size) in enumerate(zip(out_refs, sizes)):
        rows = pl.ds(at, size)
        held[rows, :] = source[rows, :].astype(F32)
        for part in range(2):
            some = pl.ds(at + part * (size // 2), size // 2)
            target = ref.at[pl.ds(part * (size // 2), size // 2), columns]
            copies.append(pltpu.make_async_copy(held.at[some], target, sems.at[2 * n + part]))
            copies[-1].start()
        at += size
    return copies


def own_kernel(sizes, own_ref, *refs):
    out_refs, held, sems = refs[:-2], refs[-2], refs[-1]
    core = lax.axis_index("seq") % 2
    for copy in write_half(sizes, own_ref, core, out_refs, held, sems):
        copy.wait()


def pair_kernel(sizes, own_ref, pair_ref, *refs):
    refs = refs[len(sizes) :]
    out_refs, gain_refs = refs[: len(sizes)], refs[len(sizes) : len(sizes) + 2]
    held, sems = refs[-2:]
    core = lax.axis_index("seq") % 2
    copies = write_half(sizes, pair_ref, 1 - core, out_refs, held, sems)
    half = own_ref.shape[1]
    first = own_ref.shape[0] - 16
    gains = own_ref[first:, :].astype(F32) + pair_ref[first:, :].astype(F32)
    for at, ref in zip((0, 2), gain_refs):
        ref[pl.ds(0, half)] = gains[at]
        ref[pl.ds(half, half)] = gains[at + 1]
    for copy in copies:
        copy.wait()


def finish(own, over_cores, sizes):
    half = own.shape[1]
    shapes = [((size, 2 * half), F32, "raw") for size in sizes]
    scratch = [pltpu.VMEM((sum(sizes), half), F32), pltpu.SemaphoreType.DMA((2 * len(sizes),))]
    pair = over_cores(own)
    begun = call("own_half", functools.partial(own_kernel, sizes), [(own, "v")], shapes, scratch)
    return call(
        "pair_half",
        functools.partial(pair_kernel, sizes),
        [(own, "v"), (pair, "v")] + kinds(begun, "raw"),
        shapes + [((2 * half,), F32, "h")] * 2,
        scratch,
        alias={2 + n: n for n in range(len(sizes))},
    )


def down_kernel(mixed_ref, w_ref, middle_ref, keep_ref, *refs):
    send_refs, total = refs[:-1], refs[-1]
    part = keep_ref.shape[0]
    tp = lax.axis_index("tp")
    total[...] = mm(mixed_ref[...], w_ref[...], TN)
    own = pl.ds(pl.multiple_of(tp // 2 * part, part), part)
    keep_ref[...] = total[own, :] + middle_ref[own, :]
    for n, ref in enumerate(send_refs):
        at = pl.ds(pl.multiple_of((tp ^ (2 * n + 2)) // 2 * part, part), part)
        ref[...] = total[at, :].astype(ref.dtype)


def down(n_tp, mixed, w_both, middle, after):
    rows, model = middle.shape
    part = 2 * rows // n_tp
    return call(
        "down",
        down_kernel,
        kinds((mixed, w_both, middle), "v"),
        [((part, model), F32, "v")] + [((part, model), BF16, "v")] * (n_tp // 2 - 1),
        [pltpu.VMEM((rows, model), F32)],
        16,
        after,
    )


def total_kernel(count, *refs):
    total = refs[0][...]
    for ref in refs[1:count]:
        total = total + ref[...].astype(F32)
    refs[count][...] = total.astype(refs[count].dtype)


def total_of(parts, dtype=BF16, kind="v", after=(), flops=0):
    (out,) = call(
        "total_of",
        functools.partial(total_kernel, len(parts)),
        [(parts[0], kind)] + kinds(parts[1:], "v"),
        [(parts[0].shape, dtype, "v")],
        (),
        16,
        after,
        flops=flops,
    )
    return out


def body(
    n_seq,
    n_tp,
    tokens,
    gain_one,
    w_qkv,
    w_out,
    gain_two,
    w_in,
    w_down,
    cotangent,
    doc_lengths,
    roster,
):
    rows, model = tokens.shape
    width = w_qkv.shape[2]
    units = w_in.shape[2]
    count = n_seq // 2
    qkv_t = w_qkv.transpose(1, 2, 0).reshape(3 * width, model)
    in_t = w_in.transpose(1, 2, 0).reshape(2 * units, model)
    over_tp = lambda x, k: swap(x, "tp", k, n_tp)
    over_chips = lambda x, k: swap(x, "seq", 2 * k, n_seq)
    over_cores = lambda x: swap(x, "seq", 1, n_seq)
    everywhere = lambda xs: [xs[0]] + came(n_tp, lambda k: over_tp(xs[k], k))

    def by_steps(part, after=()):
        held, places, step = [part], [(0,)], n_tp // 2
        while step:
            joined = pile(held, after) if len(held) > 1 else part
            ks = tuple(k ^ step for group in places for k in group)
            held, places, step = held + [over_tp(joined, step)], places + [ks], step // 2
        return held, tuple(places)

    singly = tuple((hop(n, n_tp),) for n in range(n_tp))
    docs = (doc_lengths, roster)

    queries, kv, h_one, cos_table, sin_table, unit_one = project(*docs, tokens, gain_one, qkv_t)
    blocks = [kv] + [over_chips(kv, j) for j in range(1, count)]
    q_pair = over_cores(queries)

    picked, w_half = pick(in_t, w_down, w_out, ())
    got = [over_tp(picked, 1)] + [over_tp(w_half, k) for k in range(2, n_tp)]
    split = (count + 1) // 2
    (state,) = attention_forward(0, False, *docs, queries, q_pair, blocks[:split])
    state_own, state_pair = attention_forward(
        split, True, *docs, queries, q_pair, blocks[split:], state
    )
    out_b, totals, out_mine, out_other = join(state_own, over_cores(state_pair))
    outs = everywhere([out_other if k % 2 else out_mine for k in range(n_tp)])
    out_pair = over_cores(out_b)
    totals_pair = over_cores(totals)

    got = pile(got, [(state_pair, "v")])
    *staged, x_part, cot_part, gain_one, gain_two = stage(
        n_tp, tokens, cotangent, in_t, w_down, w_out, gain_one, gain_two, got, over_cores(got)
    )
    middle, middle_part, h_two, mixed, gate_grad, gain_two_part, own, *others = feed(
        gain_two, staged, outs
    )
    arrived = [own] + [over_tp(others[n], 2 * n + 2) for n in range(n_tp // 2 - 1)]
    own, *others = down(n_tp, mixed, staged[4], middle, [(out_pair, "v"), (totals_pair, "v")])
    middle_grad, branch_grad, *pieces = branch(
        n_tp, middle_part, cot_part, gain_two, staged[2], arrived, [(own, "v")]
    )
    early, early_send = early_grads(
        mixed, gate_grad, cotangent, h_two, in_t, w_down, over_tp(h_two, 1), [(branch_grad, "v")]
    )
    early_back = over_cores(early_send)
    out_grad = lay_turned(everywhere(pieces), ())
    grad_pair = over_cores(out_grad)
    branches, branch_places = by_steps(branch_grad)

    held = (queries, q_pair, out_grad, grad_pair, out_b, out_pair, totals, totals_pair)
    *terms, dq = attention_backward(1, False, *docs, held, blocks[1:], None)
    total = total_of(
        [own] + [over_tp(others[n], 2 * n + 2) for n in range(n_tp // 2 - 1)],
        BF16,
        "v",
        [(dq, "v"), (branches[1], "v")],
    )

    dkv, dq_own, dq_pair = attention_backward(
        0, True, *docs, held, blocks[:1], dq, ()
    )
    dkvs = [dkv] + [over_chips(terms[j - 1], j) for j in range(count - 1, 0, -1)]

    proj_grad, *parts = unproject(
        n_tp,
        unit_one,
        qkv_t,
        cos_table,
        sin_table,
        gain_two_part,
        dq_own,
        over_cores(dq_pair),
        dkvs,
        [(total, "v")],
    )
    ways = everywhere(parts)
    totals_all, total_places = by_steps(total, [(ways[3], "v")])
    keep, send = late_grads(
        n_tp, proj_grad, h_one, out_b, branches, branch_places, [(totals_all[1], "v")]
    )
    own, *others = spread(count, (keep, over_cores(send)), (early, early_back))
    summed = total_of([ways[0]] + [ways[i] for i in (3, 2, 1)], F32, flops=2_000_000_000)
    chip_sum = total_of(
        [own] + came(count, lambda k: over_chips(others[k - 1], k)), F32, "v", ()
    )
    layer_out = stack_parts(n_tp, totals_all, total_places)
    input_part, gains = input_side(x_part, gain_one, middle_grad, summed, [(own, "v")])
    inputs_all = everywhere([input_part] * n_tp)
    piece = sum_piece(gains, [chip_sum], ())
    input_grad = stack_parts(n_tp, inputs_all, singly, (), 3_000_000_000)
    collected = collect(
        [piece] + came(count, lambda k: over_chips(piece, k)), [(input_grad, "h"), (layer_out, "h")]
    )
    grad_qkv, grad_out, grad_down, grad_in, grad_one, grad_two = finish(
        collected, over_cores, (3 * width, width, units, 2 * units)
    )

    back = lambda x, n: x.reshape(-1, n, model).transpose(2, 0, 1)
    return (
        layer_out,
        input_grad,
        grad_one,
        back(grad_qkv, width),
        grad_out,
        grad_two,
        back(grad_in, units),
        grad_down,
    )


def solution(mesh):
    placed = (
        P("seq", None),
        P(),
        P(None, None, "tp"),
        P("tp", None),
        P(),
        P(None, None, "tp"),
        P("tp", None),
        P("seq", None),
        P(),
        P(),
    )
    return jax.shard_map(
        functools.partial(body, mesh.shape["seq"], mesh.shape["tp"]),
        mesh=mesh,
        in_specs=placed,
        out_specs=(
            P("seq", None),
            P("seq", None),
            P(),
            P(None, None, "tp"),
            P("tp", None),
            P(),
            P(None, None, "tp"),
            P("tp", None),
        ),
        check_vma=False,
    )
```
